32 devices in a mesh: wide: 16 (over z, x, core), lat: 2 (over y).
Axes of the slice: x: 2, y: 2, z: 4, core: 2. Of those that a mesh axis runs over, the one named last changes fastest.
Arguments:
- block_input: bfloat16 [16, 4, 641, 1152], P('wide', None, None, 'lat'), may hold values from -6 to 6
- noise_fields: bfloat16 [16, 4, 8, 1152], P('wide', None, None, 'lat'), may hold values from -6 to 6
- filter_taps: float32 [18, 3, 3, 5], P('lat'), may hold values from -1.5 to 1.5
- rollout: int32 [16], P('wide'), may hold values from 1 to 4
- cotangent: bfloat16 [16, 4, 641, 1152], P('wide', None, None, 'lat'), may hold values from -6 to 6
- params: bfloat16 [2897920], P('wide'), may hold values from -2 to 2, as said below
Outputs:
- block_output: bfloat16 [16, 4, 641, 1152], P('wide', None, None, 'lat')
- input_grad: float32 [16, 4, 641, 1152], P('wide', None, None, 'lat')
- param_grad: float32 [2897920], P('wide')
The draws below stay inside these ranges and needn't reach their ends.
Inputs may be any that keep to these rules, and one draw needn't show every extreme that they name: `params`: entries from 2896679 on are padding.
All inputs are finite; a program needn't handle non-finite values.
Results may differ from the reference program's by a relative error of at most 0.0061.
Values may be sent and summed in bfloat16 or wider, within the bound.
A program may use at most 256 MiB of HBM per device.

```python
import jax
import jax.numpy as jnp
from jax import lax

C = 641
HID = 1282
NOISE = 8
NLON = 64
K = 3
TAPS = 5
STEPS = 4
BATCH = 16
NLAT = 18
CELLS = 1152
CIN = 649
PADDED = 2897920


def draw_params(key, part):
    key = jax.random.fold_in(key, 11)
    key_base = jax.random.fold_in(key, 1)
    key_gain = jax.random.fold_in(key, 2)
    base = jnp.clip(jax.random.normal(key_base, (PADDED,), jnp.float32), -4.0, 4.0)
    spread = jax.random.uniform(key_gain, (PADDED,), jnp.float32, -1.0, 1.0)
    index = jnp.arange(PADDED)
    lengths = [C, C, C * K * CIN, C, C, C, C * HID, HID, HID * C, C]
    kinds = [0, 1, 2, 1, 0, 1, 3, 1, 4, 1]
    result = jnp.zeros((PADDED,), jnp.float32)
    offset = 0
    for length, which in zip(lengths, kinds):
        inside = (index >= offset) & (index < offset + length)
        if which == 0:
            values = 1.0 + 0.4 * spread
        elif which == 1:
            values = 0.3 * base
        elif which == 2:
            values = base * (K * CIN) ** (-0.5)
        elif which == 3:
            values = base * C ** (-0.5)
        else:
            values = base * HID ** (-0.5)
        result = jnp.where(inside, values, result)
        offset = offset + length
    result = jnp.where(index >= offset, 0.1 * spread, result)
    return result.astype(jnp.bfloat16)


def set_ends(values, stream_key, low, largest):
    longest = values.shape.index(max(values.shape))
    spots = []
    for shift in (0, 1):
        where = [jax.random.randint(jax.random.fold_in(stream_key, axis), (), 0, length) for axis, length in enumerate(values.shape)]
        where[longest] = (where[longest] + shift) % values.shape[longest]
        spots.append(tuple(where))
    return values.at[spots[0]].set(low).at[spots[1]].set(largest)


def block_scale(own_key, extent, cuts, smallest, high):
    level, own = 1.0, jax.random.fold_in(own_key, 6)
    for position, shards_of in cuts:
        heights = jnp.exp(jax.random.uniform(jax.random.fold_in(own, position), (shards_of,), jnp.float32, smallest / len(cuts), high / len(cuts)))
        level = level * jnp.repeat(heights, extent[position] // shards_of).reshape([-1 if axis == position else 1 for axis in range(len(extent))])
    return level


def centred(rng, extent, scale, bound, cuts=(), held_as=jnp.bfloat16):
    level = block_scale(rng, extent, cuts, -0.22, 0.18) if cuts else 1.0
    values = jax.random.normal(rng, extent, jnp.float32) * scale * level
    return jnp.minimum(jnp.maximum(values, -bound), bound).astype(held_as)


def setup_inputs(seed: int = 0) -> dict:
    streams_of = jax.random.split(jax.random.key(seed), 7)
    block_input = centred(streams_of[0], (BATCH, STEPS, C, CELLS), 1.0, 6.0, ((0, 16), (3, 2)))
    noise_fields = centred(streams_of[1], (BATCH, STEPS, NOISE, CELLS), 1.0, 6.0, ((0, 16), (3, 2)))
    filter_taps = centred(streams_of[2], (NLAT, K, 3, TAPS), 0.25, 1.5, ((0, 2),), jnp.float32)
    rollout = set_ends(jax.random.randint(streams_of[3], (BATCH,), 1, STEPS + 1), jax.random.fold_in(streams_of[3], 1), 1, STEPS).astype(jnp.int32)
    cotangent = centred(streams_of[4], (BATCH, STEPS, C, CELLS), 1.0, 6.0, ((0, 16), (3, 2)))
    params = draw_params(jax.random.fold_in(streams_of[6], 71), 0)
    return dict(block_input=block_input, noise_fields=noise_fields, filter_taps=filter_taps, rollout=rollout, cotangent=cotangent, params=params)


@jax.custom_vjp
def low(v):
    return lax.optimization_barrier(v.astype(jnp.bfloat16)).astype(jnp.float32)

@jax.custom_vjp
def low_back(v):
    return v

def low_keep(v):
    return (low(v), None)

def low_pass(kept, grad):
    return (grad,)

def back_keep(v):
    return (v, None)

def back_low(kept, grad):
    return (low(grad),)
low.defvjp(low_keep, low_pass)
low_back.defvjp(back_keep, back_low)

def unpack_params(flat_params):
    lengths = [C, C, C * K * CIN, C, C, C, C * HID, HID, HID * C, C]
    pieces = []
    offset = 0
    for length in lengths:
        pieces.append(flat_params[offset:offset + length])
        offset = offset + length
    return (pieces[0], pieces[1], pieces[2].reshape(C, K * CIN), pieces[3], pieces[4], pieces[5], pieces[6].reshape(C, HID), pieces[7], pieces[8].reshape(HID, C), pieces[9])

def layer_norm(values, gain, bias):
    centre = lax.optimization_barrier(jnp.mean(values, 0))
    spread = lax.optimization_barrier(jnp.mean(jnp.square(values - centre), 0))
    return (values - centre) * lax.rsqrt(spread + 1e-05) * gain[:, None] + bias[:, None]

def tap_sum(fields, taps_table):
    chans = fields.shape[0]
    grid = fields.reshape(chans, NLAT, NLON)
    padded = jnp.pad(grid, ((0, 0), (1, 1), (0, 0)))
    result = jnp.zeros((K, chans, NLAT, NLON), jnp.float32)
    half_taps = TAPS // 2
    for lat_off in range(3):
        rows = padded[:, lat_off:lat_off + NLAT, :]
        for lon_off in range(TAPS):
            moved = jnp.roll(rows, half_taps - lon_off, axis=2)
            coef = jnp.transpose(taps_table[:, :, lat_off, lon_off])
            result = result + coef[:, None, :, None] * moved[None]
    return result.reshape(K * chans, NLAT * NLON)

def matmul(left, right):
    return jnp.dot(left, right, preferred_element_type=jnp.float32, precision=lax.Precision.HIGHEST)

def block(flat_params, x_values, noise_values, taps_table, live_mask):
    gain_one, bias_one, disco_weight, disco_bias, gain_two, bias_two, up_weight, up_bias, down_weight, down_bias = unpack_params(flat_params)
    normed_one = layer_norm(x_values, gain_one, bias_one)
    noisy = low(jnp.concatenate([normed_one, noise_values], 0))
    basis_out = low(tap_sum(noisy, taps_table))
    disco = low_back(matmul(disco_weight, basis_out) + disco_bias[:, None])
    residual = x_values + disco
    normed_two = low(layer_norm(residual, gain_two, bias_two))
    pre_act = low_back(matmul(up_weight.T, normed_two) + up_bias[:, None])
    hidden = low(jax.nn.gelu(pre_act, approximate=False))
    branch = low_back(matmul(down_weight.T, hidden) + down_bias[:, None])
    return live_mask * (residual + branch)

def reference(block_input, noise_fields, filter_taps, rollout, cotangent, params):
    param_values = params.astype(jnp.float32)
    taps_table = filter_taps.astype(jnp.float32)
    step_ids = jnp.arange(STEPS, dtype=jnp.int32)
    live = (step_ids[None, :] < rollout[:, None]).astype(jnp.float32).reshape(BATCH * STEPS)
    x_items = block_input.reshape(BATCH * STEPS, C, CELLS)
    noise_items = noise_fields.reshape(BATCH * STEPS, NOISE, CELLS)
    cot_items = cotangent.reshape(BATCH * STEPS, C, CELLS)

    def one_item(grad_total, item_data):
        x_item, noise_item, cot_item, mask_item = item_data
        noise_values = noise_item.astype(jnp.float32)

        def forward(flat_params, x_values):
            return block(flat_params, x_values, noise_values, taps_table, mask_item)
        output, pullback = jax.vjp(forward, param_values, x_item.astype(jnp.float32))
        param_part, input_part = pullback(cot_item.astype(jnp.float32))
        return (grad_total + param_part, (output.astype(jnp.bfloat16), input_part))
    start = jnp.zeros((PADDED,), jnp.float32)
    param_grad, (outputs, input_grads) = lax.scan(one_item, start, (x_items, noise_items, cot_items, live))
    block_output = outputs.reshape(BATCH, STEPS, C, CELLS)
    input_grad = input_grads.reshape(BATCH, STEPS, C, CELLS)
    return (block_output, input_grad, param_grad)
```

```python
from functools import partial

import jax
import jax.numpy as jnp
from jax import lax
from jax.experimental import pallas as pl
from jax.experimental.pallas import tpu as pltpu
from jax.sharding import PartitionSpec as P

HID = 1282
BF = jnp.bfloat16
F32 = jnp.float32
EPS = 1e-05
NEAR = 256
MESH = pl.DeviceIdType.MESH


def up_to(size, unit):
    return -(-size // unit) * unit


def mm(left, right, dims=(1, 0)):
    return lax.dot_general(
        left, right, (((dims[0],), (dims[1],)), ((), ())), preferred_element_type=F32
    )


class Sizes:
    def __init__(self, block_input, noise_fields, filter_taps):
        self.steps = block_input.shape[0] * block_input.shape[1]
        self.chans = block_input.shape[2]
        self.noise = noise_fields.shape[2]
        self.inputs = self.chans + self.noise
        self.rows = filter_taps.shape[0]
        self.basis = filter_taps.shape[1]
        self.taps = filter_taps.shape[3]
        self.cells = block_input.shape[3]
        self.lons = self.cells // self.rows
        self.chan_pad = up_to(self.inputs + 1, 16)
        self.chan_main = self.chans // 128 * 128
        self.rest = self.chan_pad - self.chan_main
        self.hid = HID
        self.hid_pad = up_to(HID + 1, 16)
        self.mix = self.basis * self.chan_pad
        self.main = (self.rows - 1) * self.lons
        self.width = self.steps * self.cells
        self.tail = self.steps * self.main


def block_kernel(
    sz, x_hbm, noise_ref, cot_hbm, halo_ref, taps_ref, live_ref, norm_ref, mix_hbm, mixt_hbm,
    up_hbm, down_hbm, out_hbm, grad_hbm, dmix_hbm, dup_hbm, ddown_hbm, dnorm_ref,
    xs, gs, basis_s, normed_s, act_s, gd_s, grad_s, stage, noisy_s, filt_s, filt_e,
    edge_s, mix_s, up_s, down_s,
    in_sem, w_sem, out_sem, send_sem, recv_sem,
):
    chans, cp, cm, rest = sz.chans, sz.chan_pad, sz.chan_main, sz.rest
    hp, lons, main, tail = sz.hid_pad, sz.lons, sz.main, sz.tail
    pair = 2 * lons
    lat = lax.axis_index("lat")
    lat_count = lax.axis_size("lat")
    has_up = lat > 0
    has_down = lat < lat_count - 1

    def fetch(step, slot):
        return (
            pltpu.make_async_copy(x_hbm.at[step], stage.at[slot], in_sem.at[slot, 0]),
            pltpu.make_async_copy(cot_hbm.at[step], stage.at[2 + slot], in_sem.at[slot, 1]),
        )

    for step in range(2):
        for copy in fetch(step, step):
            copy.start()
    weights = [
        pltpu.make_async_copy(src, dst, w_sem.at[i])
        for i, (src, dst) in enumerate(((mix_hbm, mix_s), (up_hbm, up_s), (down_hbm, down_s)))
    ]
    for copy in weights:
        copy.start()
    mixt_s = normed_s.at[:, pl.ds(0, mixt_hbm.shape[1])]
    mixt_copy = pltpu.make_async_copy(mixt_hbm, mixt_s, w_sem.at[3])

    row_in = lax.broadcasted_iota(jnp.int32, (lons, pair), 0)
    lane = lax.broadcasted_iota(jnp.int32, (lons, pair), 1)
    lane_in = lane % lons
    left_half = lane < lons
    half_taps = sz.taps // 2
    circ = []
    circ_t = []
    for t in range(sz.taps):
        circ.append(row_in == (lane_in + (t - half_taps + lons)) % lons)
        circ_t.append(lane_in == (row_in + (t - half_taps + lons)) % lons)
    tap_stride = sz.basis * 3 * sz.taps

    def tap_block(ext_row_a, a_a, ext_row_b, a_b, k, masks):
        block = jnp.zeros((lons, pair), F32)
        for t in range(sz.taps):
            va = F32(0) if a_a is None else taps_ref[ext_row_a * tap_stride + (k * 3 + a_a) * sz.taps + t]
            vb = F32(0) if a_b is None else taps_ref[ext_row_b * tap_stride + (k * 3 + a_b) * sz.taps + t]
            block = jnp.where(masks[t], jnp.where(left_half, va, vb), block)
        return block.astype(BF)

    def inside(a):
        return a if 0 <= a <= 2 else None

    windows = (sz.rows - 1) // 2
    last = sz.rows - 1

    def build_filters(backward):
        def build(index, _):
            m = index // sz.basis
            k = index % sz.basis
            cols = pl.ds(pl.multiple_of(k * pair, pair), pair)
            for ri in range(4):
                if backward:
                    block = tap_block(
                        2 * m + ri, inside(2 - ri), 2 * m + ri, inside(3 - ri), k, circ_t
                    )
                else:
                    block = tap_block(
                        2 * m + 1, inside(ri), 2 * m + 2, inside(ri - 1), k, circ
                    )
                filt_s[m, pl.ds(ri * lons, lons), cols] = block
            return 0

        def build_last(k, _):
            cols = pl.ds(pl.multiple_of(k * pair, pair), pair)
            for ri in range(4):
                ext = min(last + ri, last + 2) if backward else last + 1
                a = inside(2 - ri) if backward else inside(ri)
                masks = circ_t if backward else circ
                for odd in range(2):
                    filt_e[pl.ds((odd * 4 + ri) * lons, lons), cols] = tap_block(
                        ext, None if odd else a, ext, a if odd else None, k, masks
                    )
            return 0

        lax.fori_loop(0, windows * sz.basis, build, 0)
        lax.fori_loop(0, sz.basis, build_last, 0)

    build_filters(False)

    gain_one, bias_one = norm_ref[0], norm_ref[1]
    gain_two, bias_two = norm_ref[2], norm_ref[3]

    def wide(vec, lanes):
        if lanes <= 128:
            return vec[:, :lanes]
        return jnp.concatenate([vec] * (lanes // 128) + ([vec[:, : lanes % 128]] if lanes % 128 else []), 1)

    def stats(values):
        centre = jnp.sum(values, 0, keepdims=True) * (1.0 / chans)
        shifted = values - centre
        spread = jnp.sum(jnp.square(shifted), 0, keepdims=True) * (1.0 / chans)
        return shifted, lax.rsqrt(spread + EPS)

    def norm_one(values, lanes):
        shifted, inv = stats(values)
        return shifted * inv * wide(gain_one[:chans], lanes) + wide(bias_one[:chans], lanes)

    halos = []
    for side, there in ((0, has_up), (1, has_down)):
        fields = halo_ref[side].astype(F32)
        width = fields.shape[1]
        normed = norm_one(fields[:chans], width)
        noise = fields[chans : sz.inputs]
        full = jnp.concatenate(
            [normed, noise, jnp.zeros((cp - sz.inputs, width), F32)], 0
        )
        edge_s[side] = jnp.where(there, full, 0.0).astype(BF)

    def halo_part(source, step):
        return source[:, step * lons : (step + 1) * lons]

    ones_row = (lax.broadcasted_iota(jnp.int32, (rest, pair), 0) == sz.inputs - cm).astype(F32)

    def run_filter(slot, store):
        for m in range(windows):
            window = noisy_s[slot, :, m * pair : m * pair + 2 * pair]
            result = mm(window, filt_s[m])
            for k in range(sz.basis):
                store(m, k, result[:, k * pair : (k + 1) * pair])

    def run_last(store):
        window = jnp.concatenate(
            [noisy_s[slot, :, windows * pair : windows * pair + 2 * pair] for slot in range(2)], 1
        )
        result = mm(window, filt_e[...])
        for k in range(sz.basis):
            store(k, result[:, k * pair : (k + 1) * pair])

    def put_basis(lanes, k, part, ones):
        basis_s[k * cm : (k + 1) * cm, lanes] = part[:cm].astype(BF)
        low = part[cm:]
        if ones and k == 0:
            low = low + ones_row
        start = sz.basis * cm + k * rest
        basis_s[start : start + rest, lanes] = low.astype(BF)

    zero_lanes = jnp.zeros((cp, lons), BF)
    pad_rows = jnp.zeros((cp - chans, sz.cells), F32)
    pad_pair = jnp.zeros((cp - chans, pair), F32)
    pairs = sz.steps // 2

    def prepare(two, _):
        both = pl.ds(pl.multiple_of(tail + two * pair, pair), pair)
        near = pl.ds(pl.multiple_of(two * pair, pair), pair)
        for slot in range(2):
            step = 2 * two + slot
            for copy in fetch(step, slot):
                copy.wait()
            fields = stage[slot].astype(F32)
            normed = norm_one(fields, sz.cells)
            noise = noise_ref[step].astype(F32)
            own = jnp.concatenate(
                [normed, noise, jnp.zeros((cp - sz.inputs, sz.cells), F32)], 0
            ).astype(BF)
            noisy_s[slot] = jnp.concatenate(
                [
                    halo_part(edge_s[0, :, near], slot),
                    own,
                    halo_part(edge_s[1, :, near], slot),
                    zero_lanes,
                ],
                1,
            )
            lanes = pl.ds(pl.multiple_of(step * main, main), main)
            xs[:, lanes] = jnp.concatenate([fields, pad_rows], 0)[:, :main].astype(BF)
            masked = jnp.concatenate([stage[2 + slot].astype(F32), pad_rows], 0)[:, :main]
            gs[:, lanes] = (masked * live_ref[:, lanes]).astype(BF)

            def keep(m, k, part, step=step):
                start = pl.multiple_of(step * main + m * pair, pair)
                put_basis(pl.ds(start, pair), k, part, True)

            run_filter(slot, keep)
        x_tail = jnp.concatenate([stage[s, :, main:] for s in range(2)], 1).astype(F32)
        xs[:, both] = jnp.concatenate([x_tail, pad_pair], 0).astype(BF)
        g_tail = jnp.concatenate([stage[2 + s, :, main:] for s in range(2)], 1).astype(F32)
        g_tail = jnp.concatenate([g_tail, pad_pair], 0)
        gs[:, both] = (g_tail * live_ref[:, both]).astype(BF)
        run_last(lambda k, part: put_basis(both, k, part, True))

        @pl.when(two + 1 < pairs)
        def _():
            for slot in range(2):
                for copy in fetch(2 * two + 2 + slot, slot):
                    copy.start()

        return 0

    lax.fori_loop(0, pairs, prepare, 0)
    barrier = pltpu.get_barrier_semaphore()

    @pl.when(has_up)
    def _():
        pl.semaphore_signal(barrier, inc=1, device_id={"lat": lat - 1}, device_id_type=MESH)

    @pl.when(has_down)
    def _():
        pl.semaphore_signal(barrier, inc=1, device_id={"lat": lat + 1}, device_id_type=MESH)

    for copy in weights:
        copy.wait()
    dnorm_ref[...] = jnp.zeros_like(dnorm_ref)

    def fold(values):
        total = values[:, :128]
        for i in range(1, values.shape[1] // 128):
            total = total + values[:, i * 128 : (i + 1) * 128]
        return total

    chunks = sz.width // NEAR
    per_step = main // NEAR
    tail_chunk = tail // NEAR
    steps_per_tail = NEAR // lons

    def split_store(chunk, put):
        @pl.when(chunk < tail_chunk)
        def _():
            start = pl.multiple_of((chunk % per_step) * NEAR, NEAR)
            put(chunk // per_step, pl.ds(start, NEAR), slice(0, NEAR))

        @pl.when(chunk >= tail_chunk)
        def _():
            for part in range(steps_per_tail):
                put(
                    (chunk - tail_chunk) * steps_per_tail + part,
                    pl.ds(main, lons),
                    slice(part * lons, (part + 1) * lons),
                )

    def out_copy(step):
        return pltpu.make_async_copy(stage.at[step], out_hbm.at[step], out_sem.at[0, step])

    def grad_copy(step):
        return pltpu.make_async_copy(grad_s.at[step], grad_hbm.at[step], out_sem.at[1, step])

    tail_total = chunks - tail_chunk

    def forward_chunk(index, _):
        chunk = lax.rem(index + tail_chunk, chunks)
        lanes = pl.ds(pl.multiple_of(chunk * NEAR, NEAR), NEAR)
        residual = xs[:, lanes].astype(F32) + mm(mix_s[:, : sz.mix], basis_s[:, lanes])
        centre = jnp.sum(residual[:chans], 0, keepdims=True) * (1.0 / chans)
        shifted = residual - centre
        spread = jnp.sum(jnp.square(shifted[:chans]), 0, keepdims=True) * (1.0 / chans)
        inv = lax.rsqrt(spread + EPS)
        hat = shifted * inv
        normed = (hat * wide(gain_two, NEAR) + wide(bias_two, NEAR)).astype(BF)
        normed_s[:, lanes] = normed
        grad_low = gs[:, lanes]
        pre = mm(up_s[:, :hp], normed, (0, 0))
        grad_hidden = mm(down_s[:, :cp], grad_low)
        phi = 0.5 + 0.5 * lax.erf(pre * 0.7071067811865476)
        density = jnp.exp(pre * pre * -0.5) * 0.3989422804014327
        hidden = pre * phi
        grad_pre = (grad_hidden * (phi + pre * density)).astype(BF)
        low_rows = hp - HID // 16 * 16
        low = lax.broadcasted_iota(jnp.int32, (low_rows, NEAR), 0) == HID - (hp - low_rows)
        hidden = jnp.concatenate(
            [hidden[: hp - low_rows], jnp.where(low, 1.0, hidden[hp - low_rows :])], 0
        ).astype(BF)
        act_s[:hp, lanes] = hidden
        act_s[hp:, lanes] = grad_pre
        branch = mm(down_s[:, :cp], hidden, (0, 0))
        output = ((residual + branch)[:chans] * live_ref[:, lanes]).astype(BF)

        def put_out(step, where, part):
            stage[step, :, where] = output[:, part]

        split_store(chunk, put_out)

        grad_normed = mm(up_s[:, :hp], grad_pre)
        dnorm_ref[2] += fold(grad_normed * hat)
        dnorm_ref[3] += fold(grad_normed)
        scaled = grad_normed * wide(gain_two, NEAR)
        mean_one = jnp.sum(scaled[:chans], 0, keepdims=True) * (1.0 / chans)
        mean_two = jnp.sum((scaled * hat)[:chans], 0, keepdims=True) * (1.0 / chans)
        grad_resid = grad_low.astype(F32) + inv * (scaled - mean_one - hat * mean_two)
        gd_s[:, lanes] = grad_resid.astype(BF)

        def put_grad(step, where, part):
            grad_s[step, :, where] = grad_resid[:chans, part]

        split_store(chunk, put_grad)

        @pl.when((chunk < tail_chunk) & (lax.rem(chunk, per_step) == per_step - 1))
        def _():
            out_copy(chunk // per_step).start()

        return 0

    lax.fori_loop(0, chunks, forward_chunk, 0)

    rim = pl.ds(0, sz.steps * lons)
    noisy_s[0, :, rim] = jnp.concatenate(
        [gd_s[:, step * main : step * main + lons] for step in range(sz.steps)], 1
    )
    noisy_s[1, :, rim] = gd_s[:, tail:]
    pl.semaphore_wait(barrier, has_up.astype(jnp.int32) + has_down.astype(jnp.int32))

    def send(side, to):
        return pltpu.make_async_remote_copy(
            src_ref=noisy_s.at[side, :, rim],
            dst_ref=edge_s.at[1 - side],
            send_sem=send_sem.at[side],
            recv_sem=recv_sem.at[1 - side],
            device_id={"lat": to},
            device_id_type=MESH,
        )

    @pl.when(has_up)
    def _():
        send(0, lat - 1).start()

    @pl.when(has_down)
    def _():
        send(1, lat + 1).start()

    def blocks(total, size):
        return [(i, min(size, total - i)) for i in range(0, total, size)]

    for start, size in blocks(hp, 512):
        up_s[:, start : start + size] = mm(
            normed_s[...], act_s[hp + start : hp + start + size, :], (1, 1)
        ).astype(BF)
    dup_copy = pltpu.make_async_copy(up_s, dup_hbm, w_sem.at[1])
    dup_copy.start()
    mixt_copy.start()
    for start, size in blocks(hp, 432):
        rows = pl.ds(start, size)
        down_s[rows, :cp] = mm(act_s[rows, :], gs[...], (1, 1)).astype(BF)
    ddown_copy = pltpu.make_async_copy(down_s, ddown_hbm, w_sem.at[2])
    ddown_copy.start()
    for start, size in blocks(sz.mix, 512):
        mix_s[:, start : start + size] = mm(
            gd_s[...], basis_s[start : start + size, :], (1, 1)
        ).astype(BF)
    dmix_copy = pltpu.make_async_copy(mix_s, dmix_hbm, w_sem.at[0])
    dmix_copy.start()

    build_filters(True)

    @pl.when(has_up)
    def _():
        send(0, lat - 1).wait_send()
        send(1, lat - 1).wait_recv()

    @pl.when(has_down)
    def _():
        send(1, lat + 1).wait_send()
        send(0, lat + 1).wait_recv()

    def adjoint(two, _):
        both = pl.ds(pl.multiple_of(tail + two * pair, pair), pair)
        near = pl.ds(pl.multiple_of(two * pair, pair), pair)
        for slot in range(2):
            step = 2 * two + slot
            noisy_s[slot] = jnp.concatenate(
                [
                    halo_part(edge_s[0, :, near], slot),
                    gd_s[:, pl.ds(pl.multiple_of(step * main, main), main)],
                    halo_part(gd_s[:, both], slot),
                    halo_part(edge_s[1, :, near], slot),
                    zero_lanes,
                ],
                1,
            )

            def keep_grad(m, k, part, step=step):
                start = pl.multiple_of(step * main + m * pair, pair)
                put_basis(pl.ds(start, pair), k, part, False)

            run_filter(slot, keep_grad)
        run_last(lambda k, part: put_basis(both, k, part, False))
        return 0

    lax.fori_loop(0, pairs, adjoint, 0)
    mixt_copy.wait()

    def backward_chunk(index, _):
        chunk = lax.rem(index + tail_chunk, chunks)
        lanes = pl.ds(pl.multiple_of(chunk * NEAR, NEAR), NEAR)
        grad_first = mm(normed_s[:, : sz.mix], basis_s[:, lanes])[:chans]
        shifted, inv = stats(xs[:, lanes].astype(F32)[:chans])
        hat = shifted * inv
        dnorm_ref[0, :chans] += fold(grad_first * hat)
        dnorm_ref[1, :chans] += fold(grad_first)
        scaled = grad_first * wide(gain_one[:chans], NEAR)
        mean_one = jnp.sum(scaled, 0, keepdims=True) * (1.0 / chans)
        mean_two = jnp.sum(scaled * hat, 0, keepdims=True) * (1.0 / chans)
        added = inv * (scaled - mean_one - hat * mean_two)

        def put_grad(step, where, part):
            grad_s[step, :, where] += added[:, part]

        split_store(chunk, put_grad)

        @pl.when((chunk < tail_chunk) & (lax.rem(chunk, per_step) == per_step - 1))
        def _():
            grad_copy(chunk // per_step).start()

        return 0

    lax.fori_loop(0, chunks, backward_chunk, 0)
    for step in range(sz.steps):
        out_copy(step).wait()
        grad_copy(step).wait()
    for copy in (ddown_copy, dup_copy, dmix_copy):
        copy.wait()


def shift_rows(values, axis, down):
    count = lax.axis_size(axis)
    if down:
        pairs = [(i, i + 1) for i in range(count - 1)]
    else:
        pairs = [(i + 1, i) for i in range(count - 1)]
    return lax.ppermute(values, axis, pairs)


def run_block(sz, x_items, noise_items, cot_items, filter_taps, live, norms, mix, mixt, up, down):
    cp, hp = sz.chan_pad, sz.hid_pad
    lons = sz.lons

    def edge(first):
        lanes = slice(0, lons) if first else slice(sz.cells - lons, sz.cells)
        rows = jnp.concatenate([x_items[:, :, lanes], noise_items[:, :, lanes]], 1)
        rows = jnp.transpose(rows, (1, 0, 2)).reshape(sz.inputs, sz.steps * lons)
        return jnp.pad(rows, ((0, cp - sz.inputs), (0, 0)))

    halo = jnp.stack([shift_rows(edge(False), "lat", True), shift_rows(edge(True), "lat", False)])
    taps_ext = jnp.concatenate(
        [
            shift_rows(filter_taps[-1:], "lat", True),
            filter_taps,
            shift_rows(filter_taps[:1], "lat", False),
        ],
        0,
    ).reshape(-1)
    live_lanes = jnp.concatenate([jnp.repeat(live, sz.main), jnp.repeat(live, lons)])[None]
    any_spec = pl.BlockSpec(memory_space=pl.ANY)
    vmem = pl.BlockSpec(memory_space=pltpu.VMEM)
    mix_lanes = up_to(sz.mix, 128)
    up_lanes = up_to(hp, 128)
    down_lanes = up_to(cp, 128)
    windows = (sz.rows - 1) // 2
    lon = lons
    flops = 2 * sz.width * (3 * sz.mix * cp + 6 * hp * cp)
    return pl.pallas_call(
        partial(block_kernel, sz),
        name="block",
        out_shape=[
            jax.ShapeDtypeStruct(x_items.shape, BF),
            jax.ShapeDtypeStruct(x_items.shape, F32),
            jax.ShapeDtypeStruct((cp, mix_lanes), BF),
            jax.ShapeDtypeStruct((cp, up_lanes), BF),
            jax.ShapeDtypeStruct((hp, down_lanes), BF),
            jax.ShapeDtypeStruct((4, cp, 128), F32),
        ],
        in_specs=[
            any_spec, vmem, any_spec, vmem, pl.BlockSpec(memory_space=pltpu.SMEM), vmem, vmem,
            any_spec, any_spec, any_spec, any_spec,
        ],
        out_specs=[any_spec] * 5 + [vmem],
        scratch_shapes=[
            pltpu.VMEM((cp, sz.width), BF),
            pltpu.VMEM((cp, sz.width), BF),
            pltpu.VMEM((sz.mix, sz.width), BF),
            pltpu.VMEM((cp, sz.width), BF),
            pltpu.VMEM((2 * hp, sz.width), BF),
            pltpu.VMEM((cp, sz.width), BF),
            pltpu.VMEM((sz.steps, sz.chans, sz.cells), F32),
            pltpu.VMEM((4, sz.chans, sz.cells), BF),
            pltpu.VMEM((2, cp, (sz.rows + 3) * lon), BF),
            pltpu.VMEM((windows, 4 * lon, sz.basis * 2 * lon), BF),
            pltpu.VMEM((8 * lon, sz.basis * 2 * lon), BF),
            pltpu.VMEM((2, cp, sz.steps * lon), BF),
            pltpu.VMEM((cp, mix_lanes), BF),
            pltpu.VMEM((cp, up_lanes), BF),
            pltpu.VMEM((hp, down_lanes), BF),
            pltpu.SemaphoreType.DMA((2, 2)),
            pltpu.SemaphoreType.DMA((4,)),
            pltpu.SemaphoreType.DMA((2, sz.steps)),
            pltpu.SemaphoreType.DMA((2,)),
            pltpu.SemaphoreType.DMA((2,)),
        ],
        compiler_params=pltpu.CompilerParams(
            collective_id=0, has_side_effects=True, vmem_limit_bytes=63 * 1024 * 1024
        ),
        cost_estimate=pl.CostEstimate(flops=flops, bytes_accessed=40_000_000, transcendentals=0),
    )(x_items, noise_items, cot_items, halo, taps_ext, live_lanes, norms, mix, mixt, up, down)


def unpack(sz, flat):
    chans, hid, inputs, basis = sz.chans, sz.hid, sz.inputs, sz.basis
    cm, rest, cp, hp = sz.chan_main, sz.rest, sz.chan_pad, sz.hid_pad
    lengths = [chans, chans, chans * basis * inputs, chans, chans, chans, chans * hid, hid,
               hid * chans, chans]
    pieces = []
    offset = 0
    for length in lengths:
        pieces.append(flat[offset : offset + length])
        offset = offset + length

    def column(vec, ones=None):
        vec = jnp.pad(vec.astype(F32), (0, cp - chans))
        if ones is not None:
            vec = vec.at[ones].set(1.0)
        return jnp.broadcast_to(vec[:, None], (cp, 128))

    norms = jnp.stack(
        [column(pieces[0]), column(pieces[1]), column(pieces[4]), column(pieces[5], chans)]
    )
    disco = pieces[2].reshape(chans, basis, inputs)

    def packed(values, bias):
        values = jnp.pad(values, ((0, cp - values.shape[0]), (0, 0), (0, cp - values.shape[2])))
        head = values[:, :, :cm].reshape(cp, basis * cm)
        low = values[:, :, cm:].reshape(cp, basis * rest)
        if bias is not None:
            low = low.at[:chans, inputs - cm].set(bias)
        full = jnp.concatenate([head, low], 1)
        return jnp.pad(full, ((0, 0), (0, up_to(full.shape[1], 128) - full.shape[1])))

    mix = packed(disco, pieces[3])
    mixt = packed(jnp.transpose(disco, (2, 1, 0))[:chans], None)
    up = pieces[6].reshape(chans, hid)
    up = jnp.concatenate([up, pieces[7][None]], 0)
    up = jnp.pad(up, ((0, cp - chans - 1), (0, up_to(hp, 128) - hid)))
    down = jnp.concatenate([pieces[8].reshape(hid, chans), pieces[9][None]], 0)
    down = jnp.pad(down, ((0, hp - hid - 1), (0, up_to(cp, 128) - chans)))
    return norms, mix, mixt, up, down


def shards(block_input, noise_fields, filter_taps, rollout, cotangent, params):
    sz = Sizes(block_input, noise_fields, filter_taps)
    chans, cm, rest = sz.chans, sz.chan_main, sz.rest
    flat = lax.all_gather(params, "wide", axis=0, tiled=True)
    norms, mix, mixt, up, down = unpack(sz, flat)
    dates, step_total = block_input.shape[:2]
    step_ids = jnp.arange(step_total, dtype=jnp.int32)
    live = (step_ids[None, :] < rollout[:, None]).astype(F32).reshape(sz.steps)
    items = (sz.steps, chans, sz.cells)
    out, grad, dmix, dup, ddown, dnorm = run_block(
        sz,
        block_input.reshape(items),
        noise_fields.reshape(sz.steps, sz.noise, sz.cells),
        cotangent.reshape(items),
        filter_taps,
        live,
        norms,
        mix,
        mixt,
        up,
        down,
    )
    dvec = jnp.sum(dnorm, 2).astype(BF)[:, :chans]
    low = dmix[:chans, sz.basis * cm : sz.mix].reshape(chans, sz.basis, rest)
    ddisco = jnp.concatenate(
        [dmix[:chans, : sz.basis * cm].reshape(chans, sz.basis, cm), low[:, :, : sz.inputs - cm]], 2
    )
    parts = [
        dvec[0], dvec[1], ddisco, low[:, 0, sz.inputs - cm], dvec[2], dvec[3],
        dup[:chans, :HID], dup[chans, :HID], ddown[:HID, :chans], ddown[HID, :chans],
    ]
    padded = params.shape[0] * lax.axis_size("wide")
    parts = [part.reshape(-1) for part in parts]
    used = sum(part.shape[0] for part in parts)
    flat_grad = jnp.concatenate(parts + [jnp.zeros((padded - used,), BF)])
    mine = lax.psum_scatter(flat_grad, "wide", scatter_dimension=0, tiled=True)
    param_grad = lax.psum(mine.astype(F32), "lat")
    return (out.reshape(block_input.shape), grad.reshape(block_input.shape), param_grad)


def solution(mesh):
    in_specs = (
        P("wide", None, None, "lat"),
        P("wide", None, None, "lat"),
        P("lat", None, None, None),
        P("wide"),
        P("wide", None, None, "lat"),
        P("wide"),
    )
    out_specs = (P("wide", None, None, "lat"), P("wide", None, None, "lat"), P("wide"))
    return jax.shard_map(shards, mesh=mesh, in_specs=in_specs, out_specs=out_specs, check_vma=False)
```

```python
from functools import partial

import jax
import jax.numpy as jnp
from jax import lax
from jax.experimental import pallas as pl
from jax.experimental.pallas import tpu as pltpu
from jax.sharding import PartitionSpec as P

HID = 1282
BF = jnp.bfloat16
F32 = jnp.float32
EPS = 1e-05
NEAR = 256
MESH = pl.DeviceIdType.MESH


def up_to(size, unit):
    return -(-size // unit) * unit


def mm(left, right, dims=(1, 0)):
    return lax.dot_general(
        left, right, (((dims[0],), (dims[1],)), ((), ())), preferred_element_type=F32
    )


class Sizes:
    def __init__(self, block_input, noise_fields, filter_taps):
        self.steps = block_input.shape[0] * block_input.shape[1]
        self.chans = block_input.shape[2]
        self.noise = noise_fields.shape[2]
        self.inputs = self.chans + self.noise
        self.rows = filter_taps.shape[0]
        self.basis = filter_taps.shape[1]
        self.taps = filter_taps.shape[3]
        self.cells = block_input.shape[3]
        self.lons = self.cells // self.rows
        self.chan_pad = up_to(self.inputs + 1, 16)
        self.chan_main = self.chans // 128 * 128
        self.rest = self.chan_pad - self.chan_main
        self.hid = HID
        self.hid_pad = up_to(HID + 1, 16)
        self.mix = self.basis * self.chan_pad
        self.main = (self.rows - 1) * self.lons
        self.width = self.steps * self.cells
        self.tail = self.steps * self.main


def block_kernel(
    sz, x_hbm, noise_ref, cot_hbm, halo_ref, taps_ref, live_ref, norm_ref, mix_hbm, mixt_hbm,
    up_hbm, down_hbm, out_hbm, grad_hbm, dmix_hbm, dup_hbm, ddown_hbm, dnorm_ref,
    xs, gs, basis_s, normed_s, act_s, gd_s, grad_s, stage, noisy_s, filt_s, filt_e,
    edge_s, mix_s, up_s, down_s,
    in_sem, w_sem, out_sem, send_sem, recv_sem,
):
    chans, cp, cm, rest = sz.chans, sz.chan_pad, sz.chan_main, sz.rest
    hp, lons, main, tail = sz.hid_pad, sz.lons, sz.main, sz.tail
    pair = 2 * lons
    lat = lax.axis_index("lat")
    lat_count = lax.axis_size("lat")
    has_up = lat > 0
    has_down = lat < lat_count - 1

    def fetch(step, slot):
        return (
            pltpu.make_async_copy(x_hbm.at[step], stage.at[slot], in_sem.at[slot, 0]),
            pltpu.make_async_copy(cot_hbm.at[step], stage.at[2 + slot], in_sem.at[slot, 1]),
        )

    for step in range(2):
        for copy in fetch(step, step):
            copy.start()
    weights = [
        pltpu.make_async_copy(src, dst, w_sem.at[i])
        for i, (src, dst) in enumerate(((mix_hbm, mix_s), (up_hbm, up_s), (down_hbm, down_s)))
    ]
    for copy in weights:
        copy.start()
    mixt_s = normed_s.at[:, pl.ds(0, mixt_hbm.shape[1])]
    mixt_copy = pltpu.make_async_copy(mixt_hbm, mixt_s, w_sem.at[3])

    row_in = lax.broadcasted_iota(jnp.int32, (lons, pair), 0)
    lane = lax.broadcasted_iota(jnp.int32, (lons, pair), 1)
    lane_in = lane % lons
    left_half = lane < lons
    half_taps = sz.taps // 2
    circ = []
    circ_t = []
    for t in range(sz.taps):
        circ.append(row_in == (lane_in + (t - half_taps + lons)) % lons)
        circ_t.append(lane_in == (row_in + (t - half_taps + lons)) % lons)
    tap_stride = sz.basis * 3 * sz.taps

    def tap_block(ext_row_a, a_a, ext_row_b, a_b, k, masks):
        block = jnp.zeros((lons, pair), F32)
        for t in range(sz.taps):
            va = F32(0) if a_a is None else taps_ref[ext_row_a * tap_stride + (k * 3 + a_a) * sz.taps + t]
            vb = F32(0) if a_b is None else taps_ref[ext_row_b * tap_stride + (k * 3 + a_b) * sz.taps + t]
            block = jnp.where(masks[t], jnp.where(left_half, va, vb), block)
        return block.astype(BF)

    def inside(a):
        return a if 0 <= a <= 2 else None

    windows = (sz.rows - 1) // 2
    last = sz.rows - 1

    def build_filters(backward):
        def build(index, _):
            m = index // sz.basis
            k = index % sz.basis
            cols = pl.ds(pl.multiple_of(k * pair, pair), pair)
            for ri in range(4):
                if backward:
                    block = tap_block(
                        2 * m + ri, inside(2 - ri), 2 * m + ri, inside(3 - ri), k, circ_t
                    )
                else:
                    block = tap_block(
                        2 * m + 1, inside(ri), 2 * m + 2, inside(ri - 1), k, circ
                    )
                filt_s[m, pl.ds(ri * lons, lons), cols] = block
            return 0

        def build_last(k, _):
            cols = pl.ds(pl.multiple_of(k * pair, pair), pair)
            for ri in range(4):
                ext = min(last + ri, last + 2) if backward else last + 1
                a = inside(2 - ri) if backward else inside(ri)
                masks = circ_t if backward else circ
                for odd in range(2):
                    filt_e[pl.ds((odd * 4 + ri) * lons, lons), cols] = tap_block(
                        ext, None if odd else a, ext, a if odd else None, k, masks
                    )
            return 0

        lax.fori_loop(0, windows * sz.basis, build, 0)
        lax.fori_loop(0, sz.basis, build_last, 0)

    build_filters(False)

    gain_one, bias_one = norm_ref[0], norm_ref[1]
    gain_two, bias_two = norm_ref[2], norm_ref[3]

    def wide(vec, lanes):
        if lanes <= 128:
            return vec[:, :lanes]
        return jnp.concatenate([vec] * (lanes // 128) + ([vec[:, : lanes % 128]] if lanes % 128 else []), 1)

    def stats(values):
        centre = jnp.sum(values, 0, keepdims=True) * (1.0 / chans)
        shifted = values - centre
        spread = jnp.sum(jnp.square(shifted), 0, keepdims=True) * (1.0 / chans)
        return shifted, lax.rsqrt(spread + EPS)

    def norm_one(values, lanes):
        shifted, inv = stats(values)
        return shifted * inv * wide(gain_one[:chans], lanes) + wide(bias_one[:chans], lanes)

    halos = []
    for side, there in ((0, has_up), (1, has_down)):
        fields = halo_ref[side].astype(F32)
        width = fields.shape[1]
        normed = norm_one(fields[:chans], width)
        noise = fields[chans : sz.inputs]
        full = jnp.concatenate(
            [normed, noise, jnp.zeros((cp - sz.inputs, width), F32)], 0
        )
        edge_s[side] = jnp.where(there, full, 0.0).astype(BF)

    def halo_part(source, step):
        return source[:, step * lons : (step + 1) * lons]

    ones_row = (lax.broadcasted_iota(jnp.int32, (rest, pair), 0) == sz.inputs - cm).astype(F32)

    def run_filter(slot, store):
        for m in range(windows):
            window = noisy_s[slot, :, m * pair : m * pair + 2 * pair]
            result = mm(window, filt_s[m])
            for k in range(sz.basis):
                store(m, k, result[:, k * pair : (k + 1) * pair])

    def run_last(store):
        window = jnp.concatenate(
            [noisy_s[slot, :, windows * pair : windows * pair + 2 * pair] for slot in range(2)], 1
        )
        result = mm(window, filt_e[...])
        for k in range(sz.basis):
            store(k, result[:, k * pair : (k + 1) * pair])

    def put_basis(lanes, k, part, ones):
        basis_s[k * cm : (k + 1) * cm, lanes] = part[:cm].astype(BF)
        low = part[cm:]
        if ones and k == 0:
            low = low + ones_row
        start = sz.basis * cm + k * rest
        basis_s[start : start + rest, lanes] = low.astype(BF)

    zero_lanes = jnp.zeros((cp, lons), BF)
    pad_rows = jnp.zeros((cp - chans, sz.cells), F32)
    pad_pair = jnp.zeros((cp - chans, pair), F32)
    pairs = sz.steps // 2

    def prepare(two, _):
        both = pl.ds(pl.multiple_of(tail + two * pair, pair), pair)
        near = pl.ds(pl.multiple_of(two * pair, pair), pair)
        for slot in range(2):
            step = 2 * two + slot
            for copy in fetch(step, slot):
                copy.wait()
            fields = stage[slot].astype(F32)
            normed = norm_one(fields, sz.cells)
            noise = noise_ref[step].astype(F32)
            own = jnp.concatenate(
                [normed, noise, jnp.zeros((cp - sz.inputs, sz.cells), F32)], 0
            ).astype(BF)
            noisy_s[slot] = jnp.concatenate(
                [
                    halo_part(edge_s[0, :, near], slot),
                    own,
                    halo_part(edge_s[1, :, near], slot),
                    zero_lanes,
                ],
                1,
            )
            lanes = pl.ds(pl.multiple_of(step * main, main), main)
            xs[:, lanes] = jnp.concatenate([fields, pad_rows], 0)[:, :main].astype(BF)
            masked = jnp.concatenate([stage[2 + slot].astype(F32), pad_rows], 0)[:, :main]
            gs[:, lanes] = (masked * live_ref[:, lanes]).astype(BF)

            def keep(m, k, part, step=step):
                start = pl.multiple_of(step * main + m * pair, pair)
                put_basis(pl.ds(start, pair), k, part, True)

            run_filter(slot, keep)
        x_tail = jnp.concatenate([stage[s, :, main:] for s in range(2)], 1).astype(F32)
        xs[:, both] = jnp.concatenate([x_tail, pad_pair], 0).astype(BF)
        g_tail = jnp.concatenate([stage[2 + s, :, main:] for s in range(2)], 1).astype(F32)
        g_tail = jnp.concatenate([g_tail, pad_pair], 0)
        gs[:, both] = (g_tail * live_ref[:, both]).astype(BF)
        run_last(lambda k, part: put_basis(both, k, part, True))

        @pl.when(two + 1 < pairs)
        def _():
            for slot in range(2):
                for copy in fetch(2 * two + 2 + slot, slot):
                    copy.start()

        return 0

    lax.fori_loop(0, pairs, prepare, 0)
    barrier = pltpu.get_barrier_semaphore()

    @pl.when(has_up)
    def _():
        pl.semaphore_signal(barrier, inc=1, device_id={"lat": lat - 1}, device_id_type=MESH)

    @pl.when(has_down)
    def _():
        pl.semaphore_signal(barrier, inc=1, device_id={"lat": lat + 1}, device_id_type=MESH)

    for copy in weights:
        copy.wait()
    dnorm_ref[...] = jnp.zeros_like(dnorm_ref)

    def fold(values):
        total = values[:, :128]
        for i in range(1, values.shape[1] // 128):
            total = total + values[:, i * 128 : (i + 1) * 128]
        return total

    chunks = sz.width // NEAR
    per_step = main // NEAR
    tail_chunk = tail // NEAR
    steps_per_tail = NEAR // lons

    def split_store(chunk, put):
        @pl.when(chunk < tail_chunk)
        def _():
            start = pl.multiple_of((chunk % per_step) * NEAR, NEAR)
            put(chunk // per_step, pl.ds(start, NEAR), slice(0, NEAR))

        @pl.when(chunk >= tail_chunk)
        def _():
            for part in range(steps_per_tail):
                put(
                    (chunk - tail_chunk) * steps_per_tail + part,
                    pl.ds(main, lons),
                    slice(part * lons, (part + 1) * lons),
                )

    def out_copy(step):
        return pltpu.make_async_copy(stage.at[step], out_hbm.at[step], out_sem.at[0, step])

    def grad_copy(step):
        return pltpu.make_async_copy(grad_s.at[step], grad_hbm.at[step], out_sem.at[1, step])

    tail_total = chunks - tail_chunk

    def forward_chunk(index, _):
        chunk = lax.rem(index + tail_chunk, chunks)
        lanes = pl.ds(pl.multiple_of(chunk * NEAR, NEAR), NEAR)
        residual = xs[:, lanes].astype(F32) + mm(mix_s[:, : sz.mix], basis_s[:, lanes])
        centre = jnp.sum(residual[:chans], 0, keepdims=True) * (1.0 / chans)
        shifted = residual - centre
        spread = jnp.sum(jnp.square(shifted[:chans]), 0, keepdims=True) * (1.0 / chans)
        inv = lax.rsqrt(spread + EPS)
        hat = shifted * inv
        normed = (hat * wide(gain_two, NEAR) + wide(bias_two, NEAR)).astype(BF)
        normed_s[:, lanes] = normed
        grad_low = gs[:, lanes]
        pre = mm(up_s[:, :hp], normed, (0, 0))
        grad_hidden = mm(down_s[:, :cp], grad_low)
        phi = 0.5 + 0.5 * lax.erf(pre * 0.7071067811865476)
        density = jnp.exp(pre * pre * -0.5) * 0.3989422804014327
        hidden = pre * phi
        grad_pre = (grad_hidden * (phi + pre * density)).astype(BF)
        low_rows = hp - HID // 16 * 16
        low = lax.broadcasted_iota(jnp.int32, (low_rows, NEAR), 0) == HID - (hp - low_rows)
        hidden = jnp.concatenate(
            [hidden[: hp - low_rows], jnp.where(low, 1.0, hidden[hp - low_rows :])], 0
        ).astype(BF)
        act_s[:hp, lanes] = hidden
        act_s[hp:, lanes] = grad_pre
        branch = mm(down_s[:, :cp], hidden, (0, 0))
        output = ((residual + branch)[:chans] * live_ref[:, lanes]).astype(BF)

        def put_out(step, where, part):
            stage[step, :, where] = output[:, part]

        split_store(chunk, put_out)

        grad_normed = mm(up_s[:, :hp], grad_pre)
        dnorm_ref[2] += fold(grad_normed * hat)
        dnorm_ref[3] += fold(grad_normed)
        scaled = grad_normed * wide(gain_two, NEAR)
        mean_one = jnp.sum(scaled[:chans], 0, keepdims=True) * (1.0 / chans)
        mean_two = jnp.sum((scaled * hat)[:chans], 0, keepdims=True) * (1.0 / chans)
        grad_resid = grad_low.astype(F32) + inv * (scaled - mean_one - hat * mean_two)
        gd_s[:, lanes] = grad_resid.astype(BF)

        def put_grad(step, where, part):
            grad_s[step, :, where] = grad_resid[:chans, part]

        split_store(chunk, put_grad)

        @pl.when((chunk < tail_chunk) & (lax.rem(chunk, per_step) == per_step - 1))
        def _():
            out_copy(chunk // per_step).start()

        return 0

    lax.fori_loop(0, chunks, forward_chunk, 0)

    rim = pl.ds(0, sz.steps * lons)
    noisy_s[0, :, rim] = jnp.concatenate(
        [gd_s[:, step * main : step * main + lons] for step in range(sz.steps)], 1
    )
    noisy_s[1, :, rim] = gd_s[:, tail:]
    pl.semaphore_wait(barrier, has_up.astype(jnp.int32) + has_down.astype(jnp.int32))

    def send(side, to):
        return pltpu.make_async_remote_copy(
            src_ref=noisy_s.at[side, :, rim],
            dst_ref=edge_s.at[1 - side],
            send_sem=send_sem.at[side],
            recv_sem=recv_sem.at[1 - side],
            device_id={"lat": to},
            device_id_type=MESH,
        )

    @pl.when(has_up)
    def _():
        send(0, lat - 1).start()

    @pl.when(has_down)
    def _():
        send(1, lat + 1).start()

    def blocks(total, size):
        return [(i, min(size, total - i)) for i in range(0, total, size)]

    for start, size in blocks(hp, 512):
        up_s[:, start : start + size] = mm(
            normed_s[...], act_s[hp + start : hp + start + size, :], (1, 1)
        ).astype(BF)
    dup_copy = pltpu.make_async_copy(up_s, dup_hbm, w_sem.at[1])
    dup_copy.start()
    mixt_copy.start()
    for start, size in blocks(hp, 432):
        rows = pl.ds(start, size)
        down_s[rows, :cp] = mm(act_s[rows, :], gs[...], (1, 1)).astype(BF)
    ddown_copy = pltpu.make_async_copy(down_s, ddown_hbm, w_sem.at[2])
    ddown_copy.start()
    for start, size in blocks(sz.mix, 512):
        mix_s[:, start : start + size] = mm(
            gd_s[...], basis_s[start : start + size, :], (1, 1)
        ).astype(BF)
    dmix_copy = pltpu.make_async_copy(mix_s, dmix_hbm, w_sem.at[0])
    dmix_copy.start()

    build_filters(True)

    @pl.when(has_up)
    def _():
        send(0, lat - 1).wait_send()
        send(1, lat - 1).wait_recv()

    @pl.when(has_down)
    def _():
        send(1, lat + 1).wait_send()
        send(0, lat + 1).wait_recv()

    def adjoint(two, _):
        both = pl.ds(pl.multiple_of(tail + two * pair, pair), pair)
        near = pl.ds(pl.multiple_of(two * pair, pair), pair)
        for slot in range(2):
            step = 2 * two + slot
            noisy_s[slot] = jnp.concatenate(
                [
                    halo_part(edge_s[0, :, near], slot),
                    gd_s[:, pl.ds(pl.multiple_of(step * main, main), main)],
                    halo_part(gd_s[:, both], slot),
                    halo_part(edge_s[1, :, near], slot),
                    zero_lanes,
                ],
                1,
            )

            def keep_grad(m, k, part, step=step):
                start = pl.multiple_of(step * main + m * pair, pair)
                put_basis(pl.ds(start, pair), k, part, False)

            run_filter(slot, keep_grad)
        run_last(lambda k, part: put_basis(both, k, part, False))
        return 0

    lax.fori_loop(0, pairs, adjoint, 0)
    mixt_copy.wait()

    def backward_chunk(index, _):
        chunk = lax.rem(index + tail_chunk, chunks)
        lanes = pl.ds(pl.multiple_of(chunk * NEAR, NEAR), NEAR)
        grad_first = mm(normed_s[:, : sz.mix], basis_s[:, lanes])[:chans]
        shifted, inv = stats(xs[:, lanes].astype(F32)[:chans])
        hat = shifted * inv
        dnorm_ref[0, :chans] += fold(grad_first * hat)
        dnorm_ref[1, :chans] += fold(grad_first)
        scaled = grad_first * wide(gain_one[:chans], NEAR)
        mean_one = jnp.sum(scaled, 0, keepdims=True) * (1.0 / chans)
        mean_two = jnp.sum(scaled * hat, 0, keepdims=True) * (1.0 / chans)
        added = inv * (scaled - mean_one - hat * mean_two)

        def put_grad(step, where, part):
            grad_s[step, :, where] += added[:, part]

        split_store(chunk, put_grad)

        @pl.when((chunk < tail_chunk) & (lax.rem(chunk, per_step) == per_step - 1))
        def _():
            grad_copy(chunk // per_step).start()

        return 0

    lax.fori_loop(0, chunks, backward_chunk, 0)
    for step in range(sz.steps):
        out_copy(step).wait()
        grad_copy(step).wait()
    for copy in (ddown_copy, dup_copy, dmix_copy):
        copy.wait()


def shift_rows(values, axis, down):
    count = lax.axis_size(axis)
    if down:
        pairs = [(i, i + 1) for i in range(count - 1)]
    else:
        pairs = [(i + 1, i) for i in range(count - 1)]
    return lax.ppermute(values, axis, pairs)


def lane_index(rows):
    return lax.broadcasted_iota(jnp.int32, (rows, 128), 1)


def window(flat, start, rows):
    first = start >> 7
    shift = start & 127
    low = flat[pl.ds(first, rows), :]
    high = flat[pl.ds(first + 1, rows), :]
    mixed = jnp.where(lane_index(rows) >= shift, low, high)
    return pltpu.roll(mixed, (128 - shift) & 127, 1)


def gather_kernel(
    sz, parts, params_hbm, x_hbm, noise_ref,
    halo_ref, norm_ref, mix_ref, mixt_ref, up_ref, down_ref,
    got, flat, lines, x_s, rim_s, edge_s,
    in_sem, z_send, z_recv, x_send, x_recv, y_send, y_recv, c_send, c_recv, e_send, e_recv,
):
    chans, cp, cm, rest, lons = sz.chans, sz.chan_pad, sz.chan_main, sz.rest, sz.lons
    rows, own_rows, shared, split = parts
    wide = lax.axis_index("wide")
    lat = lax.axis_index("lat")
    lat_count = lax.axis_size("lat")
    total = lax.axis_size("wide")
    heights = total // 4
    core = wide % 2
    side = (wide // 2) % 2
    height = wide // 4
    half = lat % 2
    has_up = lat > 0
    has_down = lat < lat_count - 1

    def spot(h, s, c):
        return 4 * ((h + heights) % heights) + 2 * s + c

    x_copy = pltpu.make_async_copy(x_hbm, x_s, in_sem.at[0])
    x_copy.start()
    own_copy = pltpu.make_async_copy(params_hbm, got.at[wide], in_sem.at[1])
    own_copy.start()

    barrier = pltpu.get_barrier_semaphore()

    def hello(w, l):
        pl.semaphore_signal(barrier, inc=1, device_id=(w, l), device_id_type=MESH)

    for i in range(1, heights):
        hello(spot(height + i, side, core), lat)
    hello(spot(height, 1 - side, core), lat)
    hello(spot(height, side, 1 - core), lat)

    @pl.when(has_up)
    def _():
        hello(wide, lat - 1)

    @pl.when(has_down)
    def _():
        hello(wide, lat + 1)

    pl.semaphore_wait(
        barrier, heights + 1 + has_up.astype(jnp.int32) + has_down.astype(jnp.int32)
    )
    own_copy.wait()

    whole = pl.ds(0, rows)
    mine = pl.ds(pl.multiple_of(half * split, 16), split + shared)
    lead = pl.ds(pl.multiple_of(half * (split + shared), 16), split)
    other = pl.ds(pl.multiple_of((1 - half) * (split + shared), 16), split)

    def message(shard, where, to_wide, to_lat, send, recv):
        return pltpu.make_async_remote_copy(
            src_ref=got.at[shard, where],
            dst_ref=got.at[shard, where],
            send_sem=send,
            recv_sem=recv,
            device_id=(to_wide, to_lat),
            device_id_type=MESH,
        )

    started = []

    def start(copy):
        copy.start()
        started.append(copy)

    def along(i):
        return message(wide, mine, spot(height + i, side, core), lat, z_send.at[i - 1], z_recv.at[i - 1])

    def arrive(shard, where, sem):
        message(shard, where, wide, lat, z_send.at[0], sem).wait_recv()

    def across(j, shard):
        return message(shard, mine, spot(height, 1 - side, core), lat, x_send.at[j], x_recv.at[j])

    def over(j, shard):
        return message(shard, lead, wide, lat + 1 - 2 * half, y_send.at[j], y_recv.at[j])

    def beside(j, shard, where):
        return message(shard, where, spot(height, side, 1 - core), lat, c_send.at[j], c_recv.at[j])

    for i in range(1, heights):
        start(along(i))
    start(across(0, wide))
    start(beside(0, wide, whole))

    x_copy.wait()
    blank = jnp.zeros((cp - sz.inputs, sz.steps * lons), F32)
    for edge, lanes in ((0, slice(0, lons)), (1, slice(sz.cells - lons, sz.cells))):
        fields = jnp.concatenate([x_s[t, :, lanes] for t in range(sz.steps)], 1).astype(F32)
        noise = jnp.concatenate([noise_ref[t, :, lanes] for t in range(sz.steps)], 1).astype(F32)
        rim_s[edge] = jnp.concatenate([fields, noise, blank], 0).astype(BF)

    def rim(edge, to):
        return pltpu.make_async_remote_copy(
            src_ref=rim_s.at[edge],
            dst_ref=edge_s.at[1 - edge],
            send_sem=e_send.at[edge],
            recv_sem=e_recv.at[1 - edge],
            device_id=(wide, to),
            device_id_type=MESH,
        )

    @pl.when(has_up)
    def _():
        rim(0, lat - 1).start()

    @pl.when(has_down)
    def _():
        rim(1, lat + 1).start()

    for i in range(1, heights):
        shard = spot(height - i, side, core)
        arrive(shard, mine, z_recv.at[i - 1])
        start(across(i, shard))
        start(over(i - 1, shard))
        start(beside(i, shard, mine))
    for j in range(heights):
        shard = spot(height - j, 1 - side, core)
        arrive(shard, mine, x_recv.at[j])
        start(over(heights - 1 + j, shard))
        start(beside(heights + j, shard, mine))
    for j in range(2 * heights - 1):
        near = j < heights - 1
        shard = spot(height - (j + 1), side, core) if near else spot(height - (j - heights + 1), 1 - side, core)
        arrive(shard, other, y_recv.at[j])
        start(beside(2 * heights + j, shard, other))
    arrive(spot(height, side, 1 - core), whole, c_recv.at[0])
    for j in range(1, 2 * heights):
        near = j < heights
        shard = spot(height - j, side, 1 - core) if near else spot(height - (j - heights), 1 - side, 1 - core)
        arrive(shard, mine, c_recv.at[j])
    for j in range(2 * heights - 1):
        near = j < heights - 1
        shard = (
            spot(height - (j + 1), side, 1 - core)
            if near
            else spot(height - (j - heights + 1), 1 - side, 1 - core)
        )
        arrive(shard, other, c_recv.at[2 * heights + j])
    for copy in started:
        copy.wait_send()

    @pl.when(has_up)
    def _():
        rim(0, lat - 1).wait_send()
        rim(1, lat - 1).wait_recv()

    @pl.when(has_down)
    def _():
        rim(1, lat + 1).wait_send()
        rim(0, lat + 1).wait_recv()

    halo_ref[...] = edge_s[...]

    for shard in range(total):
        flat[pl.ds(shard * own_rows, own_rows), :] = got[shard, :own_rows].astype(F32)
    unpack_kernel(sz, flat, lines, norm_ref, mix_ref, mixt_ref, up_ref, down_ref)


def lines_of(flat, lines, first, length, count, group):
    step = 32

    def some(base, size):
        held = [window(flat, first + (base + j) * length, group) for j in range(size)]
        for j in range(size):
            lines[pl.ds(pl.multiple_of((base + j) * group, 8), group), :] = held[j]

    def body(i, _):
        some(i * step, step)
        return 0

    lax.fori_loop(0, count // step, body, 0)
    some(count // step * step, count % step)


def unpack_kernel(sz, flat, lines, norm_ref, mix_ref, mixt_ref, up_ref, down_ref):
    chans, cp, cm, rest, hid, hp = sz.chans, sz.chan_pad, sz.chan_main, sz.rest, sz.hid, sz.hid_pad
    basis, inputs = sz.basis, sz.inputs
    at_disco = 2 * chans
    at_bias = at_disco + chans * basis * inputs
    at_up = at_bias + 3 * chans
    at_down = at_up + (chans + 1) * hid

    def column(start):
        held = window(flat, start, 8)
        full = jnp.concatenate(
            [jnp.broadcast_to(held[s : s + 1], (128, 128)).T for s in range(up_to(cp, 128) // 128)], 0
        )[:cp]
        row = lax.broadcasted_iota(jnp.int32, (cp, 128), 0)
        return jnp.where(row < chans, full, 0.0), row

    for i, start in enumerate((0, chans, at_bias + chans, at_bias + 2 * chans)):
        value, row = column(start)
        norm_ref[i] = jnp.where(row == chans, 1.0, value) if i == 3 else value
    disco_bias, _ = column(at_bias)

    groups = 8
    lines_of(flat, lines, at_disco, inputs, chans * basis, groups)
    stride = basis * groups
    lane = lane_index(chans)
    low = jnp.where(lane == inputs - cm, disco_bias[:chans], 0.0)
    blank = jnp.zeros((cp - cm, 128), BF)

    def put(ref, lanes, value, size):
        whole = size // 16 * 16
        ref[:whole, lanes] = value[:whole].astype(BF)
        tail = jnp.concatenate(
            [value[whole:size], jnp.zeros((up_to(size, 16) - size, 128), F32)], 0
        )
        ref[whole : up_to(size, 16), lanes] = tail.astype(BF)

    for k in range(basis):
        for s in range(cm // 128):
            value = lines[pl.ds(k * groups + s, chans, stride=stride), :]
            put(mix_ref, slice(k * cm + s * 128, k * cm + s * 128 + 128), value, chans)
        value = lines[pl.ds(k * groups + cm // 128, chans, stride=stride), :]
        value = jnp.where(lane < inputs - cm, value, 0.0)
        low = low + (pltpu.roll(value, k * rest, 1) if k else value)
    put(mix_ref, slice(basis * cm, basis * cm + 128), low, chans)

    for k in range(basis):
        for s in range(cm // 128):
            for r in range(cm // 128):
                block = mix_ref[r * 128 : r * 128 + 128, k * cm + s * 128 : k * cm + s * 128 + 128]
                mixt_ref[s * 128 : s * 128 + 128, k * cm + r * 128 : k * cm + r * 128 + 128] = (
                    block.astype(F32).T.astype(BF)
                )
    for r in range(cm // 128):
        block = low[r * 128 : r * 128 + 128].T
        for k in range(basis):
            mixt_ref[cm:cp, k * cm + r * 128 : k * cm + r * 128 + 128] = block[
                k * rest : (k + 1) * rest
            ].astype(BF)
    for s in range(cm // 128):
        block = jnp.concatenate(
            [
                mix_ref[cm:cp, k * cm + s * 128 : k * cm + s * 128 + 128].astype(F32)
                for k in range(basis)
            ]
            + [jnp.zeros((128 - basis * rest, 128), F32)],
            0,
        )
        mixt_ref[s * 128 : s * 128 + 128, basis * cm : basis * cm + 128] = block.T.astype(BF)
    corner = mix_ref[cm:cp, basis * cm : basis * cm + 128].astype(F32)
    corner = jnp.where(lane_index(cp - cm) % rest == 0, corner, 0.0)
    row = lax.broadcasted_iota(jnp.int32, (cp - cm, 128), 0)
    mixt_ref[cm:cp, basis * cm : basis * cm + 128] = jnp.where(row < chans - cm, corner, 0.0).astype(BF)

    groups = 16
    lines_of(flat, lines, at_up, hid, chans + 1, groups)
    for s in range(up_ref.shape[1] // 128):
        value = lines[pl.ds(s, chans + 1, stride=groups), :]
        keep = hid - s * 128
        if keep < 128:
            value = jnp.where(lane_index(chans + 1) < keep, value, 0.0)
        put(up_ref, slice(s * 128, s * 128 + 128), value, chans + 1)
    groups = 8
    lines_of(flat, lines, at_down, chans, hid + 1, groups)
    for s in range(down_ref.shape[1] // 128):
        value = lines[pl.ds(s, hid + 1, stride=groups), :]
        keep = chans - s * 128
        if keep < 128:
            value = jnp.where(lane_index(hid + 1) < keep, value, 0.0)
        put(down_ref, slice(s * 128, s * 128 + 128), value, hid + 1)
    for ref, size in ((mix_ref, up_to(chans, 16)), (up_ref, up_to(chans + 1, 16)), (down_ref, up_to(hid + 1, 16))):
        if size < ref.shape[0]:
            ref[size:, :] = jnp.zeros((ref.shape[0] - size, ref.shape[1]), BF)


def run_gather(sz, params, x_items, noise_items, total):
    cp, hp = sz.chan_pad, sz.hid_pad
    own_rows = params.shape[0] // 128
    rows = up_to(own_rows, 16)
    split = rows * 7 // 20 // 16 * 16
    shared = rows - 2 * split
    held = jnp.pad(params.reshape(own_rows, 128), ((0, rows - own_rows), (0, 0)))
    heights = total // 4
    any_spec = pl.BlockSpec(memory_space=pl.ANY)
    vmem = pl.BlockSpec(memory_space=pltpu.VMEM)
    edges = (2, cp, sz.steps * sz.lons)
    line_rows = max(sz.chans * sz.basis * 8, (sz.chans + 1) * 16, (sz.hid + 1) * 8)
    dma = pltpu.SemaphoreType.DMA
    return pl.pallas_call(
        partial(gather_kernel, sz, (rows, own_rows, shared, split)),
        name="gather",
        out_shape=[
            jax.ShapeDtypeStruct(edges, BF),
            jax.ShapeDtypeStruct((4, cp, 128), F32),
            jax.ShapeDtypeStruct((cp, up_to(sz.mix, 128)), BF),
            jax.ShapeDtypeStruct((cp, up_to(sz.mix, 128)), BF),
            jax.ShapeDtypeStruct((cp, up_to(hp, 128)), BF),
            jax.ShapeDtypeStruct((hp, up_to(cp, 128)), BF),
        ],
        in_specs=[any_spec, any_spec, vmem],
        out_specs=[vmem] * 6,
        scratch_shapes=[
            pltpu.VMEM((total, rows, 128), BF),
            pltpu.VMEM((up_to(total * own_rows + 24, 8), 128), F32),
            pltpu.VMEM((line_rows, 128), F32),
            pltpu.VMEM(x_items.shape, BF),
            pltpu.VMEM(edges, BF),
            pltpu.VMEM(edges, BF),
            dma((2,)),
            dma((heights,)), dma((heights,)),
            dma((heights,)), dma((heights,)),
            dma((2 * heights,)), dma((2 * heights,)),
            dma((4 * heights,)), dma((4 * heights,)),
            dma((2,)), dma((2,)),
        ],
        compiler_params=pltpu.CompilerParams(
            collective_id=1, has_side_effects=True, vmem_limit_bytes=60 * 1024 * 1024
        ),
    )(held, x_items, noise_items)


def run_block(
    sz, x_items, noise_items, cot_items, filter_taps, live, halo, norms, mix, mixt, up, down
):
    cp, hp = sz.chan_pad, sz.hid_pad
    lons = sz.lons

    taps_ext = jnp.concatenate(
        [
            shift_rows(filter_taps[-1:], "lat", True),
            filter_taps,
            shift_rows(filter_taps[:1], "lat", False),
        ],
        0,
    ).reshape(-1)
    live_lanes = jnp.concatenate([jnp.repeat(live, sz.main), jnp.repeat(live, lons)])[None]
    any_spec = pl.BlockSpec(memory_space=pl.ANY)
    vmem = pl.BlockSpec(memory_space=pltpu.VMEM)
    mix_lanes = up_to(sz.mix, 128)
    up_lanes = up_to(hp, 128)
    down_lanes = up_to(cp, 128)
    windows = (sz.rows - 1) // 2
    lon = lons
    flops = 2 * sz.width * (3 * sz.mix * cp + 6 * hp * cp)
    return pl.pallas_call(
        partial(block_kernel, sz),
        name="block",
        out_shape=[
            jax.ShapeDtypeStruct(x_items.shape, BF),
            jax.ShapeDtypeStruct(x_items.shape, F32),
            jax.ShapeDtypeStruct((cp, mix_lanes), BF),
            jax.ShapeDtypeStruct((cp, up_lanes), BF),
            jax.ShapeDtypeStruct((hp, down_lanes), BF),
            jax.ShapeDtypeStruct((4, cp, 128), F32),
        ],
        in_specs=[
            any_spec, vmem, any_spec, vmem, pl.BlockSpec(memory_space=pltpu.SMEM), vmem, vmem,
            any_spec, any_spec, any_spec, any_spec,
        ],
        out_specs=[any_spec] * 5 + [vmem],
        scratch_shapes=[
            pltpu.VMEM((cp, sz.width), BF),
            pltpu.VMEM((cp, sz.width), BF),
            pltpu.VMEM((sz.mix, sz.width), BF),
            pltpu.VMEM((cp, sz.width), BF),
            pltpu.VMEM((2 * hp, sz.width), BF),
            pltpu.VMEM((cp, sz.width), BF),
            pltpu.VMEM((sz.steps, sz.chans, sz.cells), F32),
            pltpu.VMEM((4, sz.chans, sz.cells), BF),
            pltpu.VMEM((2, cp, (sz.rows + 3) * lon), BF),
            pltpu.VMEM((windows, 4 * lon, sz.basis * 2 * lon), BF),
            pltpu.VMEM((8 * lon, sz.basis * 2 * lon), BF),
            pltpu.VMEM((2, cp, sz.steps * lon), BF),
            pltpu.VMEM((cp, mix_lanes), BF),
            pltpu.VMEM((cp, up_lanes), BF),
            pltpu.VMEM((hp, down_lanes), BF),
            pltpu.SemaphoreType.DMA((2, 2)),
            pltpu.SemaphoreType.DMA((4,)),
            pltpu.SemaphoreType.DMA((2, sz.steps)),
            pltpu.SemaphoreType.DMA((2,)),
            pltpu.SemaphoreType.DMA((2,)),
        ],
        compiler_params=pltpu.CompilerParams(
            collective_id=0, has_side_effects=True, vmem_limit_bytes=63 * 1024 * 1024
        ),
        cost_estimate=pl.CostEstimate(flops=flops, bytes_accessed=40_000_000, transcendentals=0),
    )(x_items, noise_items, cot_items, halo, taps_ext, live_lanes, norms, mix, mixt, up, down)


def merge(flat, start, length, value, rows):
    first = start >> 7
    shift = start & 127
    lane = lane_index(rows)
    place = lax.broadcasted_iota(jnp.int32, (rows, 128), 0) * 128 + lane
    moved = pltpu.roll(value, shift, 1)
    late = pltpu.roll(moved, 1, 0)
    inside = (place >= shift) & (place < shift + length)
    return jnp.where(inside, jnp.where(lane >= shift, moved, late), flat[pl.ds(first, rows), :])


def flatten_lines(flat, lines, first, length, count, group):
    step = 16

    def some(base, size):
        held = []
        for j in range(size):
            at = base + 2 * j
            value = lines[pl.ds(pl.multiple_of(at * group, 8), group), :]
            held.append(merge(flat, first + at * length, length, value, group))
        for j in range(size):
            at = base + 2 * j
            flat[pl.ds((first + at * length) >> 7, group), :] = held[j]

    for odd in range(2):
        lot = (count - odd + 1) // 2

        def body(i, _, odd=odd):
            some(i * (2 * step) + odd, step)
            return 0

        lax.fori_loop(0, lot // step, body, 0)
        some(lot // step * step * 2 + odd, lot % step)


def pack_kernel(sz, dmix_ref, dup_ref, ddown_ref, dnorm_ref, flat, lines):
    chans, cp, cm, rest, hid = sz.chans, sz.chan_pad, sz.chan_main, sz.rest, sz.hid
    basis, inputs = sz.basis, sz.inputs
    at_disco = 2 * chans
    at_bias = at_disco + chans * basis * inputs
    at_up = at_bias + 3 * chans
    at_down = at_up + (chans + 1) * hid
    used = at_down + (hid + 1) * chans

    groups = 8
    stride = basis * groups
    low = dmix_ref[:, basis * cm : basis * cm + 128].astype(F32)
    for k in range(basis):
        for s in range(cm // 128):
            value = dmix_ref[:, k * cm + s * 128 : k * cm + s * 128 + 128].astype(F32)
            lines[pl.ds(k * groups + s, chans, stride=stride), :] = value[:chans]
        value = pltpu.roll(low, 128 - k * rest, 1) if k else low
        lines[pl.ds(k * groups + cm // 128, chans, stride=stride), :] = value[:chans]
    flatten_lines(flat, lines, at_disco, inputs, chans * basis, groups)

    groups = 16
    for s in range(up_to(hid, 128) // 128):
        value = dup_ref[:, s * 128 : s * 128 + 128].astype(F32)
        lines[pl.ds(s, chans + 1, stride=groups), :] = value[: chans + 1]
    flatten_lines(flat, lines, at_up, hid, chans + 1, groups)

    groups = 8
    for s in range(up_to(chans, 128) // 128):
        value = ddown_ref[:, s * 128 : s * 128 + 128].astype(F32)
        lines[pl.ds(s, hid + 1, stride=groups), :] = value[: hid + 1]
    flatten_lines(flat, lines, at_down, chans, hid + 1, groups)

    def across(columns, pick):
        parts = []
        for s in range(8):
            size = min(128, cp - s * 128)
            if size <= 0:
                parts.append(jnp.zeros((1, 128), F32))
                continue
            block = columns[s * 128 : s * 128 + size]
            if size < 128:
                block = jnp.concatenate([block, jnp.zeros((128 - size, 128), F32)], 0)
            parts.append(pick(block.T))
        return jnp.concatenate(parts, 0)

    def total(block):
        return jnp.sum(block, 0, keepdims=True)

    spots = (0, chans, at_bias + chans, at_bias + 2 * chans)
    pieces = [(start, across(dnorm_ref[i], total)) for i, start in enumerate(spots)]
    bias_row = inputs - cm
    pieces.append((at_bias, across(low, lambda block: block[bias_row : bias_row + 1])))
    for start, value in pieces:
        flat[pl.ds(start // 128, 8), :] = merge(flat, start, chans, value, 8)
    begin = used // 128
    rows = flat.shape[0] - begin
    place = lax.broadcasted_iota(jnp.int32, (rows, 128), 0) * 128 + lane_index(rows)
    flat[begin:, :] = jnp.where(place < used % 128, flat[begin:, :], 0.0)


def reduce_kernel(
    sz, parts, dmix_ref, dup_ref, ddown_ref, dnorm_ref, out_ref,
    flat, lines, sums, beside_s, beside_r, over_s, over_r, xa_s, xa_r, xb_s, xb_r,
    za_s, za_r, zb_s, zb_r, fa_s, fa_r, fb_r,
    c_send, c_recv, y_send, y_recv, x_send, x_recv, z_send, z_recv, f_send, f_recv,
):
    rows, own_rows, shared, split = parts
    wide = lax.axis_index("wide")
    lat = lax.axis_index("lat")
    total = lax.axis_size("wide")
    heights = total // 4
    core = wide % 2
    side = (wide // 2) % 2
    height = wide // 4
    half = lat % 2
    mate = lat + 1 - 2 * half

    def spot(h, s, c):
        return 4 * (h % heights) + 2 * s + c

    barrier = pltpu.get_barrier_semaphore()

    def hello(w, l):
        pl.semaphore_signal(barrier, inc=1, device_id=(w, l), device_id_type=MESH)

    for i in range(1, heights):
        hello(spot(height + i, side, core), lat)
    hello(spot(height, 1 - side, core), lat)
    hello(spot(height, side, 1 - core), lat)
    hello(wide, mate)
    pack_kernel(sz, dmix_ref, dup_ref, ddown_ref, dnorm_ref, flat, lines)
    pl.semaphore_wait(barrier, heights + 2)

    shares = pl.ds(split, shared)
    lead = pl.ds(pl.multiple_of(half * (split + shared), 16), split)
    other = pl.ds(pl.multiple_of((1 - half) * (split + shared), 16), split)
    columns = [(height + j, 1 - side) for j in range(heights)]
    columns += [(height + j, side) for j in range(heights)]
    started = []

    def copy(src, dst, send, recv, to_wide, to_lat):
        return pltpu.make_async_remote_copy(
            src_ref=src, dst_ref=dst, send_sem=send, recv_sem=recv,
            device_id=(to_wide, to_lat), device_id_type=MESH,
        )

    def go(message):
        message.start()
        started.append(message)

    def to_core(j):
        return copy(beside_s.at[j], beside_r.at[j], c_send.at[j], c_recv.at[j], spot(height, side, 1 - core), lat)

    def to_mate(j):
        return copy(over_s.at[j], over_r.at[j], y_send.at[j], y_recv.at[j], wide, mate)

    def to_side(src, dst, j, part):
        return copy(src.at[j], dst.at[j], x_send.at[j, part], x_recv.at[j, part], spot(height, 1 - side, core), lat)

    def to_height(src, dst, i, part):
        return copy(
            src.at[i - 1], dst.at[i - 1], z_send.at[i - 1, part], z_recv.at[i - 1, part],
            spot(height + i, side, core), lat,
        )

    for j, (h, s) in enumerate(columns):
        away = spot(h, s, 1 - core)
        beside_s[j] = flat[pl.ds(away * own_rows, rows), :].astype(BF)
        go(to_core(j))
    for j, (h, s) in enumerate(columns):
        mine = spot(h, s, core)
        sums[j] = flat[pl.ds(mine * own_rows, rows), :]
    for j in range(2 * heights):
        to_core(j).wait_recv()
        sums[j] += beside_r[j].astype(F32)
        over_s[j] = sums[j, other].astype(BF)
        go(to_mate(j))
        if j < heights:
            xa_s[j] = sums[j, shares].astype(BF)
            go(to_side(xa_s, xa_r, j, 0))
    for j in range(heights):
        to_mate(j).wait_recv()
        xb_s[j] = (sums[j, lead] + over_r[j].astype(F32)).astype(BF)
        go(to_side(xb_s, xb_r, j, 1))
    order = list(range(1, heights)) + [0]
    for i in order:
        j = heights + i
        to_side(xa_s, xa_r, i, 0).wait_recv()
        sums[j, shares] += xa_r[i].astype(F32)
        if i:
            za_s[i - 1] = sums[j, shares].astype(BF)
            go(to_height(za_s, za_r, i, 0))
    for i in order:
        j = heights + i
        to_mate(j).wait_recv()
        to_side(xb_s, xb_r, i, 1).wait_recv()
        sums[j, lead] += over_r[j].astype(F32) + xb_r[i].astype(F32)
        if i:
            zb_s[i - 1] = sums[j, lead].astype(BF)
            go(to_height(zb_s, zb_r, i, 1))
    own = heights
    for i in range(1, heights):
        to_height(za_s, za_r, i, 0).wait_recv()
        sums[own, shares] += za_r[i - 1].astype(F32)
    fa_s[...] = sums[own, shares].astype(BF)
    last = [
        copy(fa_s, fa_r, f_send.at[0], f_recv.at[0], wide, mate),
        copy(sums.at[own, lead], fb_r, f_send.at[1], f_recv.at[1], wide, mate),
    ]
    go(last[0])
    for i in range(1, heights):
        to_height(zb_s, zb_r, i, 1).wait_recv()
        sums[own, lead] += zb_r[i - 1].astype(F32)
    go(last[1])
    last[0].wait_recv()
    out_ref[shares, :] = fa_s[...].astype(F32) + fa_r[...].astype(F32)
    last[1].wait_recv()
    low, high = sums[own, lead], fb_r[...]
    first = jnp.where(half == 0, low, high)
    second = jnp.where(half == 0, high, low)
    out_ref[:split, :] = first
    out_ref[split + shared :, :] = second[: own_rows - split - shared]
    for message in started:
        message.wait_send()


def run_reduce(sz, own_rows, total, dmix, dup, ddown, dnorm):
    rows = up_to(own_rows, 16)
    split = rows // 4 // 16 * 16
    shared = rows - 2 * split
    heights = total // 4
    vmem = pl.BlockSpec(memory_space=pltpu.VMEM)
    line_rows = max(sz.chans * sz.basis * 8, (sz.chans + 1) * 16, (sz.hid + 1) * 8)
    dma = pltpu.SemaphoreType.DMA
    flat_rows = up_to((total - 1) * own_rows + rows, 8) + 16
    return pl.pallas_call(
        partial(reduce_kernel, sz, (rows, own_rows, shared, split)),
        name="reduce",
        out_shape=jax.ShapeDtypeStruct((own_rows, 128), F32),
        in_specs=[vmem] * 4,
        out_specs=vmem,
        scratch_shapes=[
            pltpu.VMEM((flat_rows, 128), F32),
            pltpu.VMEM((line_rows, 128), F32),
            pltpu.VMEM((2 * heights, rows, 128), F32),
            pltpu.VMEM((2 * heights, rows, 128), BF),
            pltpu.VMEM((2 * heights, rows, 128), BF),
            pltpu.VMEM((2 * heights, split, 128), BF),
            pltpu.VMEM((2 * heights, split, 128), BF),
            pltpu.VMEM((heights, shared, 128), BF),
            pltpu.VMEM((heights, shared, 128), BF),
            pltpu.VMEM((heights, split, 128), BF),
            pltpu.VMEM((heights, split, 128), BF),
            pltpu.VMEM((heights, shared, 128), BF),
            pltpu.VMEM((heights, shared, 128), BF),
            pltpu.VMEM((heights, split, 128), BF),
            pltpu.VMEM((heights, split, 128), BF),
            pltpu.VMEM((shared, 128), BF),
            pltpu.VMEM((shared, 128), BF),
            pltpu.VMEM((split, 128), F32),
            dma((2 * heights,)), dma((2 * heights,)),
            dma((2 * heights,)), dma((2 * heights,)),
            dma((heights, 2)), dma((heights, 2)),
            dma((heights, 2)), dma((heights, 2)),
            dma((2,)), dma((2,)),
        ],
        compiler_params=pltpu.CompilerParams(
            collective_id=2, has_side_effects=True, vmem_limit_bytes=62 * 1024 * 1024
        ),
    )(dmix, dup, ddown, dnorm)


def shards(block_input, noise_fields, filter_taps, rollout, cotangent, params):
    sz = Sizes(block_input, noise_fields, filter_taps)
    chans = sz.chans
    dates, step_total = block_input.shape[:2]
    step_ids = jnp.arange(step_total, dtype=jnp.int32)
    live = (step_ids[None, :] < rollout[:, None]).astype(F32).reshape(sz.steps)
    items = (sz.steps, chans, sz.cells)
    x_items = block_input.reshape(items)
    noise_items = noise_fields.reshape(sz.steps, sz.noise, sz.cells)
    halo, norms, mix, mixt, up, down = run_gather(
        sz, params, x_items, noise_items, lax.axis_size("wide")
    )
    out, grad, dmix, dup, ddown, dnorm = run_block(
        sz,
        x_items,
        noise_items,
        cotangent.reshape(items),
        filter_taps,
        live,
        halo,
        norms,
        mix,
        mixt,
        up,
        down,
    )
    own = run_reduce(sz, params.shape[0] // 128, lax.axis_size("wide"), dmix, dup, ddown, dnorm)
    param_grad = own.reshape(params.shape)
    return (out.reshape(block_input.shape), grad.reshape(block_input.shape), param_grad)


def solution(mesh):
    in_specs = (
        P("wide", None, None, "lat"),
        P("wide", None, None, "lat"),
        P("lat", None, None, None),
        P("wide"),
        P("wide", None, None, "lat"),
        P("wide"),
    )
    out_specs = (P("wide", None, None, "lat"), P("wide", None, None, "lat"), P("wide"))
    return jax.shard_map(shards, mesh=mesh, in_specs=in_specs, out_specs=out_specs, check_vma=False)
```

```python
import math
from functools import partial

import jax
import jax.numpy as jnp
from jax import lax
from jax.experimental import pallas as pl
from jax.experimental.pallas import tpu as pltpu
from jax.sharding import PartitionSpec as P

HID = 1282
BF = jnp.bfloat16
F32 = jnp.float32
EPS = 1e-05
NEAR = 256
MESH = pl.DeviceIdType.MESH


def up_to(size, unit):
    return -(-size // unit) * unit


def mm(left, right, dims=(1, 0)):
    return lax.dot_general(
        left, right, (((dims[0],), (dims[1],)), ((), ())), preferred_element_type=F32
    )


class Sizes:
    def __init__(self, block_input, noise_fields, filter_taps):
        self.steps = block_input.shape[0] * block_input.shape[1]
        self.chans = block_input.shape[2]
        self.noise = noise_fields.shape[2]
        self.inputs = self.chans + self.noise
        self.rows = filter_taps.shape[0]
        self.basis = filter_taps.shape[1]
        self.taps = filter_taps.shape[3]
        self.cells = block_input.shape[3]
        self.lons = self.cells // self.rows
        self.chan_pad = up_to(self.inputs + 1, 16)
        self.chan_main = self.chans // 128 * 128
        self.rest = self.chan_pad - self.chan_main
        self.hid = HID
        self.hid_pad = up_to(HID + 1, 16)
        self.mix = self.basis * self.chan_pad
        self.main = (self.rows - 1) * self.lons
        self.width = self.steps * self.cells
        self.tail = self.steps * self.main


def block_kernel(
    sz, x_hbm, noise_ref, cot_hbm, halo_ref, taps_ref, live_ref, norm_ref, mix_hbm, mixt_hbm,
    up_hbm, down_hbm, out_hbm, grad_hbm, dmix_hbm, dup_hbm, ddown_hbm, dnorm_ref,
    xs, gs, basis_s, normed_s, act_s, gd_s, grad_s, stage, noisy_s, filt_s, filt_e,
    edge_s, mix_s, up_s, down_s,
    in_sem, w_sem, out_sem, send_sem, recv_sem,
):
    chans, cp, cm, rest = sz.chans, sz.chan_pad, sz.chan_main, sz.rest
    hp, lons, main, tail = sz.hid_pad, sz.lons, sz.main, sz.tail
    pair = 2 * lons
    lat = lax.axis_index("lat")
    lat_count = lax.axis_size("lat")
    has_up = lat > 0
    has_down = lat < lat_count - 1

    def fetch(step, slot):
        return (
            pltpu.make_async_copy(x_hbm.at[step], stage.at[slot], in_sem.at[slot, 0]),
            pltpu.make_async_copy(cot_hbm.at[step], stage.at[2 + slot], in_sem.at[slot, 1]),
        )

    for step in range(2):
        for copy in fetch(step, step):
            copy.start()
    weights = [
        pltpu.make_async_copy(src, dst, w_sem.at[i])
        for i, (src, dst) in enumerate(((mix_hbm, mix_s), (up_hbm, up_s), (down_hbm, down_s)))
    ]
    for copy in weights:
        copy.start()
    mixt_s = normed_s.at[:, pl.ds(0, mixt_hbm.shape[1])]
    mixt_copy = pltpu.make_async_copy(mixt_hbm, mixt_s, w_sem.at[3])

    row_in = lax.broadcasted_iota(jnp.int32, (lons, pair), 0)
    lane = lax.broadcasted_iota(jnp.int32, (lons, pair), 1)
    lane_in = lane % lons
    left_half = lane < lons
    half_taps = sz.taps // 2
    circ = []
    circ_t = []
    for t in range(sz.taps):
        circ.append(row_in == (lane_in + (t - half_taps + lons)) % lons)
        circ_t.append(lane_in == (row_in + (t - half_taps + lons)) % lons)
    def tap_block(ext_row_a, a_a, ext_row_b, a_b, k, masks):
        block = jnp.zeros((lons, pair), F32)
        for t in range(sz.taps):
            va = F32(0) if a_a is None else taps_ref[ext_row_a, (k * 3 + a_a) * sz.taps + t]
            vb = F32(0) if a_b is None else taps_ref[ext_row_b, (k * 3 + a_b) * sz.taps + t]
            block = jnp.where(masks[t], jnp.where(left_half, va, vb), block)
        return block.astype(BF)

    def inside(a):
        return a if 0 <= a <= 2 else None

    windows = (sz.rows - 1) // 2
    last = sz.rows - 1

    def build_filters(backward):
        def build(index, _):
            m = index // sz.basis
            k = index % sz.basis
            cols = pl.ds(pl.multiple_of(k * pair, pair), pair)
            for ri in range(4):
                if backward:
                    block = tap_block(
                        2 * m + ri, inside(2 - ri), 2 * m + ri, inside(3 - ri), k, circ_t
                    )
                else:
                    block = tap_block(
                        2 * m + 1, inside(ri), 2 * m + 2, inside(ri - 1), k, circ
                    )
                filt_s[m, pl.ds(ri * lons, lons), cols] = block
            return 0

        def build_last(k, _):
            cols = pl.ds(pl.multiple_of(k * pair, pair), pair)
            for ri in range(4):
                ext = min(last + ri, last + 2) if backward else last + 1
                a = inside(2 - ri) if backward else inside(ri)
                masks = circ_t if backward else circ
                for odd in range(2):
                    filt_e[pl.ds((odd * 4 + ri) * lons, lons), cols] = tap_block(
                        ext, None if odd else a, ext, a if odd else None, k, masks
                    )
            return 0

        lax.fori_loop(0, windows * sz.basis, build, 0)
        lax.fori_loop(0, sz.basis, build_last, 0)

    build_filters(False)

    gain_one, bias_one = norm_ref[0], norm_ref[1]
    gain_two, bias_two = norm_ref[2], norm_ref[3]

    def wide(vec, lanes):
        if lanes <= 128:
            return vec[:, :lanes]
        return jnp.concatenate([vec] * (lanes // 128) + ([vec[:, : lanes % 128]] if lanes % 128 else []), 1)

    def stats(values):
        centre = jnp.sum(values, 0, keepdims=True) * (1.0 / chans)
        shifted = values - centre
        spread = jnp.sum(jnp.square(shifted), 0, keepdims=True) * (1.0 / chans)
        return shifted, lax.rsqrt(spread + EPS)

    def norm_one(values, lanes):
        shifted, inv = stats(values)
        return shifted * inv * wide(gain_one[:chans], lanes) + wide(bias_one[:chans], lanes)

    halos = []
    for side, there in ((0, has_up), (1, has_down)):
        fields = halo_ref[side].astype(F32)
        width = fields.shape[1]
        normed = norm_one(fields[:chans], width)
        noise = fields[chans : sz.inputs]
        full = jnp.concatenate(
            [normed, noise, jnp.zeros((cp - sz.inputs, width), F32)], 0
        )
        edge_s[side] = jnp.where(there, full, 0.0).astype(BF)

    def halo_part(source, step):
        return source[:, step * lons : (step + 1) * lons]

    ones_row = (lax.broadcasted_iota(jnp.int32, (rest, pair), 0) == sz.inputs - cm).astype(F32)

    def run_filter(slot, store):
        for m in range(windows):
            window = noisy_s[slot, :, m * pair : m * pair + 2 * pair]
            result = mm(window, filt_s[m])
            for k in range(sz.basis):
                store(m, k, result[:, k * pair : (k + 1) * pair])

    def run_last(store):
        window = jnp.concatenate(
            [noisy_s[slot, :, windows * pair : windows * pair + 2 * pair] for slot in range(2)], 1
        )
        result = mm(window, filt_e[...])
        for k in range(sz.basis):
            store(k, result[:, k * pair : (k + 1) * pair])

    def put_basis(lanes, k, part, ones):
        basis_s[k * cm : (k + 1) * cm, lanes] = part[:cm].astype(BF)
        low = part[cm:]
        if ones and k == 0:
            low = low + ones_row
        start = sz.basis * cm + k * rest
        basis_s[start : start + rest, lanes] = low.astype(BF)

    zero_lanes = jnp.zeros((cp, lons), BF)
    pad_rows = jnp.zeros((cp - chans, sz.cells), F32)
    pad_pair = jnp.zeros((cp - chans, pair), F32)
    pairs = sz.steps // 2

    def prepare(two, _):
        both = pl.ds(pl.multiple_of(tail + two * pair, pair), pair)
        near = pl.ds(pl.multiple_of(two * pair, pair), pair)
        for slot in range(2):
            step = 2 * two + slot
            for copy in fetch(step, slot):
                copy.wait()
            fields = stage[slot].astype(F32)
            normed = norm_one(fields, sz.cells)
            noise = noise_ref[step].astype(F32)
            own = jnp.concatenate(
                [normed, noise, jnp.zeros((cp - sz.inputs, sz.cells), F32)], 0
            ).astype(BF)
            noisy_s[slot] = jnp.concatenate(
                [
                    halo_part(edge_s[0, :, near], slot),
                    own,
                    halo_part(edge_s[1, :, near], slot),
                    zero_lanes,
                ],
                1,
            )
            lanes = pl.ds(pl.multiple_of(step * main, main), main)
            xs[:, lanes] = jnp.concatenate([fields, pad_rows], 0)[:, :main].astype(BF)
            masked = jnp.concatenate([stage[2 + slot].astype(F32), pad_rows], 0)[:, :main]
            gs[:, lanes] = (masked * live_ref[:, lanes]).astype(BF)

            def keep(m, k, part, step=step):
                start = pl.multiple_of(step * main + m * pair, pair)
                put_basis(pl.ds(start, pair), k, part, True)

            run_filter(slot, keep)
        x_tail = jnp.concatenate([stage[s, :, main:] for s in range(2)], 1).astype(F32)
        xs[:, both] = jnp.concatenate([x_tail, pad_pair], 0).astype(BF)
        g_tail = jnp.concatenate([stage[2 + s, :, main:] for s in range(2)], 1).astype(F32)
        g_tail = jnp.concatenate([g_tail, pad_pair], 0)
        gs[:, both] = (g_tail * live_ref[:, both]).astype(BF)
        run_last(lambda k, part: put_basis(both, k, part, True))

        @pl.when(two + 1 < pairs)
        def _():
            for slot in range(2):
                for copy in fetch(2 * two + 2 + slot, slot):
                    copy.start()

        return 0

    lax.fori_loop(0, pairs, prepare, 0)
    barrier = pltpu.get_barrier_semaphore()

    @pl.when(has_up)
    def _():
        pl.semaphore_signal(barrier, inc=1, device_id={"lat": lat - 1}, device_id_type=MESH)

    @pl.when(has_down)
    def _():
        pl.semaphore_signal(barrier, inc=1, device_id={"lat": lat + 1}, device_id_type=MESH)

    for copy in weights:
        copy.wait()
    dnorm_ref[...] = jnp.zeros_like(dnorm_ref)

    def fold(values):
        total = values[:, :128]
        for i in range(1, values.shape[1] // 128):
            total = total + values[:, i * 128 : (i + 1) * 128]
        return total

    chunks = sz.width // NEAR
    per_step = main // NEAR
    tail_chunk = tail // NEAR
    steps_per_tail = NEAR // lons

    def main_lanes(chunk):
        return pl.ds(pl.multiple_of((chunk % per_step) * NEAR, NEAR), NEAR)

    def put_tail(chunk, put):
        @pl.when(chunk >= tail_chunk)
        def _():
            for part in range(steps_per_tail):
                put(
                    (chunk - tail_chunk) * steps_per_tail + part,
                    pl.ds(main, lons),
                    slice(part * lons, (part + 1) * lons),
                )

    def out_copy(step):
        return pltpu.make_async_copy(stage.at[step], out_hbm.at[step], out_sem.at[0, step])

    def grad_copy(step):
        return pltpu.make_async_copy(grad_s.at[step], grad_hbm.at[step], out_sem.at[1, step])

    def lanes_of(chunk):
        return pl.ds(pl.multiple_of(chunk * NEAR, NEAR), NEAR)

    def order(index):
        return lax.rem(jnp.minimum(index, chunks - 1) + tail_chunk, chunks)

    def forward_first(chunk):
        lanes = lanes_of(chunk)
        residual = xs[:, lanes].astype(F32) + mm(mix_s[:, : sz.mix], basis_s[:, lanes])
        centre = jnp.sum(residual[:chans], 0, keepdims=True) * (1.0 / chans)
        shifted = residual - centre
        spread = jnp.sum(jnp.square(shifted[:chans]), 0, keepdims=True) * (1.0 / chans)
        inv = lax.rsqrt(spread + EPS)
        hat = shifted * inv
        normed_s[:, lanes] = (hat * wide(gain_two, NEAR) + wide(bias_two, NEAR)).astype(BF)
        return residual, centre, inv

    def forward_chunk(index, held):
        residual, centre, inv = held
        chunk = order(index)
        lanes = lanes_of(chunk)
        grad_low = gs[:, lanes]
        pre = mm(up_s[:, :hp], normed_s[:, lanes], (0, 0))
        grad_hidden = mm(down_s[:, :cp], grad_low)
        phi = 0.5 + 0.5 * lax.erf(pre * 0.7071067811865476)
        density = jnp.exp(pre * pre * -0.5) * 0.3989422804014327
        hidden = pre * phi
        grad_pre = (grad_hidden * (phi + pre * density)).astype(BF)
        low_rows = hp - HID // 16 * 16
        low = lax.broadcasted_iota(jnp.int32, (low_rows, NEAR), 0) == HID - (hp - low_rows)
        hidden = jnp.concatenate(
            [hidden[: hp - low_rows], jnp.where(low, 1.0, hidden[hp - low_rows :])], 0
        ).astype(BF)
        act_s[:hp, lanes] = hidden
        act_s[hp:, lanes] = grad_pre
        branch = mm(down_s[:, :cp], hidden, (0, 0))
        output = ((residual + branch)[:chans] * live_ref[:, lanes]).astype(BF)
        hat = (residual - centre) * inv
        grad_normed = mm(up_s[:, :hp], grad_pre)
        ahead = forward_first(order(index + 1))
        dnorm_ref[2] += fold(grad_normed * hat)
        dnorm_ref[3] += fold(grad_normed)
        scaled = grad_normed * wide(gain_two, NEAR)
        mean_one = jnp.sum(scaled[:chans], 0, keepdims=True) * (1.0 / chans)
        mean_two = jnp.sum((scaled * hat)[:chans], 0, keepdims=True) * (1.0 / chans)
        grad_resid = grad_low.astype(F32) + inv * (scaled - mean_one - hat * mean_two)
        gd_s[:, lanes] = grad_resid.astype(BF)

        def put(step, where, part):
            stage[step, :, where] = output[:, part]
            grad_s[step, :, where] = grad_resid[:chans, part]

        put(jnp.minimum(chunk // per_step, sz.steps - 1), main_lanes(chunk), slice(0, NEAR))
        put_tail(chunk, put)

        @pl.when((chunk < tail_chunk) & (lax.rem(chunk, per_step) == per_step - 1))
        def _():
            out_copy(chunk // per_step).start()

        return ahead

    lax.fori_loop(0, chunks, forward_chunk, forward_first(order(0)))

    rim = pl.ds(0, sz.steps * lons)
    noisy_s[0, :, rim] = jnp.concatenate(
        [gd_s[:, step * main : step * main + lons] for step in range(sz.steps)], 1
    )
    noisy_s[1, :, rim] = gd_s[:, tail:]
    pl.semaphore_wait(barrier, has_up.astype(jnp.int32) + has_down.astype(jnp.int32))

    def send(side, to):
        return pltpu.make_async_remote_copy(
            src_ref=noisy_s.at[side, :, rim],
            dst_ref=edge_s.at[1 - side],
            send_sem=send_sem.at[side],
            recv_sem=recv_sem.at[1 - side],
            device_id={"lat": to},
            device_id_type=MESH,
        )

    @pl.when(has_up)
    def _():
        send(0, lat - 1).start()

    @pl.when(has_down)
    def _():
        send(1, lat + 1).start()

    def blocks(total, size):
        return [(i, min(size, total - i)) for i in range(0, total, size)]

    for start, size in blocks(hp, 512):
        up_s[:, start : start + size] = mm(
            normed_s[...], act_s[hp + start : hp + start + size, :], (1, 1)
        ).astype(BF)
    dup_copy = pltpu.make_async_copy(up_s, dup_hbm, w_sem.at[1])
    dup_copy.start()
    mixt_copy.start()
    for start, size in blocks(hp, 432):
        rows = pl.ds(start, size)
        down_s[rows, :cp] = mm(act_s[rows, :], gs[...], (1, 1)).astype(BF)
    ddown_copy = pltpu.make_async_copy(down_s, ddown_hbm, w_sem.at[2])
    ddown_copy.start()
    for start, size in blocks(sz.mix, 512):
        mix_s[:, start : start + size] = mm(
            gd_s[...], basis_s[start : start + size, :], (1, 1)
        ).astype(BF)
    dmix_copy = pltpu.make_async_copy(mix_s, dmix_hbm, w_sem.at[0])
    dmix_copy.start()

    build_filters(True)

    @pl.when(has_up)
    def _():
        send(0, lat - 1).wait_send()
        send(1, lat - 1).wait_recv()

    @pl.when(has_down)
    def _():
        send(1, lat + 1).wait_send()
        send(0, lat + 1).wait_recv()

    def adjoint(two, _):
        both = pl.ds(pl.multiple_of(tail + two * pair, pair), pair)
        near = pl.ds(pl.multiple_of(two * pair, pair), pair)
        for slot in range(2):
            step = 2 * two + slot
            noisy_s[slot] = jnp.concatenate(
                [
                    halo_part(edge_s[0, :, near], slot),
                    gd_s[:, pl.ds(pl.multiple_of(step * main, main), main)],
                    halo_part(gd_s[:, both], slot),
                    halo_part(edge_s[1, :, near], slot),
                    zero_lanes,
                ],
                1,
            )

            def keep_grad(m, k, part, step=step):
                start = pl.multiple_of(step * main + m * pair, pair)
                put_basis(pl.ds(start, pair), k, part, False)

            run_filter(slot, keep_grad)
        run_last(lambda k, part: put_basis(both, k, part, False))
        return 0

    lax.fori_loop(0, pairs, adjoint, 0)
    mixt_copy.wait()

    def backward_chunk(index, _):
        chunk = order(index)
        lanes = lanes_of(chunk)
        grad_first = mm(normed_s[:, : sz.mix], basis_s[:, lanes])[:chans]
        shifted, inv = stats(xs[:, lanes].astype(F32)[:chans])
        hat = shifted * inv
        dnorm_ref[0, :chans] += fold(grad_first * hat)
        dnorm_ref[1, :chans] += fold(grad_first)
        scaled = grad_first * wide(gain_one[:chans], NEAR)
        mean_one = jnp.sum(scaled, 0, keepdims=True) * (1.0 / chans)
        mean_two = jnp.sum(scaled * hat, 0, keepdims=True) * (1.0 / chans)
        added = inv * (scaled - mean_one - hat * mean_two)

        def put_grad(step, where, part):
            grad_s[step, :, where] += added[:, part]

        @pl.when(chunk < tail_chunk)
        def _():
            put_grad(chunk // per_step, main_lanes(chunk), slice(0, NEAR))

        put_tail(chunk, put_grad)

        @pl.when((chunk < tail_chunk) & (lax.rem(chunk, per_step) == per_step - 1))
        def _():
            grad_copy(chunk // per_step).start()

        return 0

    lax.fori_loop(0, chunks, backward_chunk, 0)
    for step in range(sz.steps):
        out_copy(step).wait()
        grad_copy(step).wait()
    for copy in (ddown_copy, dup_copy, dmix_copy):
        copy.wait()


def lane_index(rows):
    return lax.broadcasted_iota(jnp.int32, (rows, 128), 1)


def window(flat, start, rows):
    first = start >> 7
    shift = start & 127
    low = flat[pl.ds(first, rows), :]
    high = flat[pl.ds(first + 1, rows), :]
    mixed = jnp.where(lane_index(rows) >= shift, low, high)
    return pltpu.roll(mixed, (128 - shift) & 127, 1)


def gather_kernel(
    sz, parts, params_ref, x_hbm, noise_ref, taps_ref,
    halo_ref, tap_ref, norm_ref, mix_ref, mixt_ref, up_ref, down_ref,
    got, flat, lines, x_s, rim_s, edge_s, tap_s, tap_r,
    in_sem, z_send, z_recv, x_send, x_recv, y_send, y_recv, c_send, c_recv, e_send, e_recv,
    t_send, t_recv,
):
    chans, cp, cm, rest, lons = sz.chans, sz.chan_pad, sz.chan_main, sz.rest, sz.lons
    rows, own_rows, shared, split = parts
    wide = lax.axis_index("wide")
    lat = lax.axis_index("lat")
    lat_count = lax.axis_size("lat")
    total = lax.axis_size("wide")
    heights = total // 4
    core = wide % 2
    side = (wide // 2) % 2
    height = wide // 4
    half = lat % 2
    has_up = lat > 0
    has_down = lat < lat_count - 1

    def spot(h, s, c):
        return 4 * ((h + heights) % heights) + 2 * s + c

    x_copy = pltpu.make_async_copy(x_hbm, x_s, in_sem)
    x_copy.start()
    got[wide, :own_rows] = params_ref[...]

    barrier = pltpu.get_barrier_semaphore()

    def hello(w, l):
        pl.semaphore_signal(barrier, inc=1, device_id=(w, l), device_id_type=MESH)

    for i in range(1, heights):
        hello(spot(height + i, side, core), lat)
    hello(spot(height, 1 - side, core), lat)
    hello(spot(height, side, 1 - core), lat)

    @pl.when(has_up)
    def _():
        hello(wide, lat - 1)

    @pl.when(has_down)
    def _():
        hello(wide, lat + 1)

    pl.semaphore_wait(
        barrier, heights + 1 + has_up.astype(jnp.int32) + has_down.astype(jnp.int32)
    )

    whole = pl.ds(0, rows)
    mine = pl.ds(pl.multiple_of(half * split, 16), split + shared)
    lead = pl.ds(pl.multiple_of(half * (split + shared), 16), split)
    other = pl.ds(pl.multiple_of((1 - half) * (split + shared), 16), split)

    def message(shard, where, to_wide, to_lat, send, recv):
        return pltpu.make_async_remote_copy(
            src_ref=got.at[shard, where],
            dst_ref=got.at[shard, where],
            send_sem=send,
            recv_sem=recv,
            device_id=(to_wide, to_lat),
            device_id_type=MESH,
        )

    started = []

    def start(copy):
        copy.start()
        started.append(copy)

    def along(i):
        return message(wide, mine, spot(height + i, side, core), lat, z_send.at[i - 1], z_recv.at[i - 1])

    def arrive(shard, where, sem):
        message(shard, where, wide, lat, z_send.at[0], sem).wait_recv()

    def across(j, shard):
        return message(shard, mine, spot(height, 1 - side, core), lat, x_send.at[j], x_recv.at[j])

    def over(j, shard):
        return message(shard, lead, wide, lat + 1 - 2 * half, y_send.at[j], y_recv.at[j])

    def beside(j, shard, where):
        return message(shard, where, spot(height, side, 1 - core), lat, c_send.at[j], c_recv.at[j])

    for i in range(1, heights):
        start(along(i))
    start(across(0, wide))
    start(beside(0, wide, whole))

    x_copy.wait()
    blank = jnp.zeros((cp - sz.inputs, sz.steps * lons), F32)
    for edge, lanes in ((0, slice(0, lons)), (1, slice(sz.cells - lons, sz.cells))):
        fields = jnp.concatenate([x_s[t, :, lanes] for t in range(sz.steps)], 1).astype(F32)
        noise = jnp.concatenate([noise_ref[t, :, lanes] for t in range(sz.steps)], 1).astype(F32)
        rim_s[edge] = jnp.concatenate([fields, noise, blank], 0).astype(BF)

    def rim(edge, to):
        return pltpu.make_async_remote_copy(
            src_ref=rim_s.at[edge],
            dst_ref=edge_s.at[1 - edge],
            send_sem=e_send.at[edge],
            recv_sem=e_recv.at[1 - edge],
            device_id=(wide, to),
            device_id_type=MESH,
        )

    def tap_rim(edge, to):
        return pltpu.make_async_remote_copy(
            src_ref=tap_s.at[edge],
            dst_ref=tap_r.at[1 - edge],
            send_sem=t_send.at[edge],
            recv_sem=t_recv.at[1 - edge],
            device_id=(wide, to),
            device_id_type=MESH,
        )

    tap_total = taps_ref.shape[1]
    for edge, row in ((0, 0), (1, sz.rows - 1)):
        tap_s[edge] = jnp.zeros(tap_s.shape[1:], F32)
        tap_s[edge, :1, :tap_total] = taps_ref[row : row + 1, :]

    @pl.when(has_up)
    def _():
        rim(0, lat - 1).start()
        tap_rim(0, lat - 1).start()

    @pl.when(has_down)
    def _():
        rim(1, lat + 1).start()
        tap_rim(1, lat + 1).start()

    for i in range(1, heights):
        shard = spot(height - i, side, core)
        arrive(shard, mine, z_recv.at[i - 1])
        start(across(i, shard))
        start(over(i - 1, shard))
        start(beside(i, shard, mine))
    for j in range(heights):
        shard = spot(height - j, 1 - side, core)
        arrive(shard, mine, x_recv.at[j])
        start(over(heights - 1 + j, shard))
        start(beside(heights + j, shard, mine))
    for j in range(2 * heights - 1):
        near = j < heights - 1
        shard = spot(height - (j + 1), side, core) if near else spot(height - (j - heights + 1), 1 - side, core)
        arrive(shard, other, y_recv.at[j])
        start(beside(2 * heights + j, shard, other))
    arrive(spot(height, side, 1 - core), whole, c_recv.at[0])
    for j in range(1, 2 * heights):
        near = j < heights
        shard = spot(height - j, side, 1 - core) if near else spot(height - (j - heights), 1 - side, 1 - core)
        arrive(shard, mine, c_recv.at[j])
    for j in range(2 * heights - 1):
        near = j < heights - 1
        shard = (
            spot(height - (j + 1), side, 1 - core)
            if near
            else spot(height - (j - heights + 1), 1 - side, 1 - core)
        )
        arrive(shard, other, c_recv.at[2 * heights + j])
    for copy in started:
        copy.wait_send()

    @pl.when(has_up)
    def _():
        rim(0, lat - 1).wait_send()
        rim(1, lat - 1).wait_recv()
        tap_rim(0, lat - 1).wait_send()
        tap_rim(1, lat - 1).wait_recv()

    @pl.when(has_down)
    def _():
        rim(1, lat + 1).wait_send()
        rim(0, lat + 1).wait_recv()
        tap_rim(1, lat + 1).wait_send()
        tap_rim(0, lat + 1).wait_recv()

    halo_ref[...] = edge_s[...]
    tap_ref[...] = jnp.zeros_like(tap_ref)
    tap_ref[1 : sz.rows + 1, :tap_total] = taps_ref[...]
    tap_ref[:1] = jnp.where(has_up, tap_r[0, :1], 0.0)
    tap_ref[sz.rows + 1 : sz.rows + 2] = jnp.where(has_down, tap_r[1, :1], 0.0)

    for shard in range(total):
        flat[pl.ds(shard * own_rows, own_rows), :] = got[shard, :own_rows].astype(F32)
    unpack_kernel(sz, flat, lines, norm_ref, mix_ref, mixt_ref, up_ref, down_ref)


def period(length):
    return 128 // math.gcd(length, 128)


def in_batches(count, first, length, some, step=16):
    again = period(length)
    spots = [(j, (first + j * length) // 128, (first + j * length) % 128) for j in range(again)]

    def body(i, _):
        for j in range(0, again, step):
            some(i * again, i * (again * length // 128), spots[j : j + step])
        return 0

    whole = count // again
    lax.fori_loop(0, whole, body, 0)
    left = count % again
    for j in range(0, left, step):
        some(whole * again, whole * (again * length // 128), spots[j : min(j + step, left)])


def lines_of(flat, lines, first, length, count, group):
    def some(line, row, spots):
        held = []
        for _, top, shift in spots:
            low = flat[pl.ds(row + top, group), :]
            if shift:
                high = flat[pl.ds(row + top + 1, group), :]
                low = pltpu.roll(jnp.where(lane_index(group) >= shift, low, high), 128 - shift, 1)
            held.append(low)
        for (at, _, _), value in zip(spots, held):
            lines[pl.ds(pl.multiple_of((line + at) * group, 8), group), :] = value

    in_batches(count, first, length, some)


def unpack_kernel(sz, flat, lines, norm_ref, mix_ref, mixt_ref, up_ref, down_ref):
    chans, cp, cm, rest, hid, hp = sz.chans, sz.chan_pad, sz.chan_main, sz.rest, sz.hid, sz.hid_pad
    basis, inputs = sz.basis, sz.inputs
    at_disco = 2 * chans
    at_bias = at_disco + chans * basis * inputs
    at_up = at_bias + 3 * chans
    at_down = at_up + (chans + 1) * hid

    def column(start):
        held = window(flat, start, 8)
        full = jnp.concatenate(
            [jnp.broadcast_to(held[s : s + 1], (128, 128)).T for s in range(up_to(cp, 128) // 128)], 0
        )[:cp]
        row = lax.broadcasted_iota(jnp.int32, (cp, 128), 0)
        return jnp.where(row < chans, full, 0.0), row

    for i, start in enumerate((0, chans, at_bias + chans, at_bias + 2 * chans)):
        value, row = column(start)
        norm_ref[i] = jnp.where(row == chans, 1.0, value) if i == 3 else value
    disco_bias, _ = column(at_bias)

    groups = 8
    lines_of(flat, lines, at_disco, inputs, chans * basis, groups)
    stride = basis * groups
    lane = lane_index(chans)
    low = jnp.where(lane == inputs - cm, disco_bias[:chans], 0.0)
    blank = jnp.zeros((cp - cm, 128), BF)

    def put(ref, lanes, value, size):
        whole = size // 16 * 16
        ref[:whole, lanes] = value[:whole].astype(BF)
        tail = jnp.concatenate(
            [value[whole:size], jnp.zeros((up_to(size, 16) - size, 128), F32)], 0
        )
        ref[whole : up_to(size, 16), lanes] = tail.astype(BF)

    for k in range(basis):
        for s in range(cm // 128):
            value = lines[pl.ds(k * groups + s, chans, stride=stride), :]
            put(mix_ref, slice(k * cm + s * 128, k * cm + s * 128 + 128), value, chans)
        value = lines[pl.ds(k * groups + cm // 128, chans, stride=stride), :]
        value = jnp.where(lane < inputs - cm, value, 0.0)
        low = low + (pltpu.roll(value, k * rest, 1) if k else value)
    put(mix_ref, slice(basis * cm, basis * cm + 128), low, chans)

    for k in range(basis):
        for s in range(cm // 128):
            for r in range(cm // 128):
                block = mix_ref[r * 128 : r * 128 + 128, k * cm + s * 128 : k * cm + s * 128 + 128]
                mixt_ref[s * 128 : s * 128 + 128, k * cm + r * 128 : k * cm + r * 128 + 128] = (
                    block.astype(F32).T.astype(BF)
                )
    for r in range(cm // 128):
        block = low[r * 128 : r * 128 + 128].T
        for k in range(basis):
            mixt_ref[cm:cp, k * cm + r * 128 : k * cm + r * 128 + 128] = block[
                k * rest : (k + 1) * rest
            ].astype(BF)
    for s in range(cm // 128):
        block = jnp.concatenate(
            [
                mix_ref[cm:cp, k * cm + s * 128 : k * cm + s * 128 + 128].astype(F32)
                for k in range(basis)
            ]
            + [jnp.zeros((128 - basis * rest, 128), F32)],
            0,
        )
        mixt_ref[s * 128 : s * 128 + 128, basis * cm : basis * cm + 128] = block.T.astype(BF)
    corner = mix_ref[cm:cp, basis * cm : basis * cm + 128].astype(F32)
    corner = jnp.where(lane_index(cp - cm) % rest == 0, corner, 0.0)
    row = lax.broadcasted_iota(jnp.int32, (cp - cm, 128), 0)
    mixt_ref[cm:cp, basis * cm : basis * cm + 128] = jnp.where(row < chans - cm, corner, 0.0).astype(BF)

    groups = 16
    lines_of(flat, lines, at_up, hid, chans + 1, groups)
    for s in range(up_ref.shape[1] // 128):
        value = lines[pl.ds(s, chans + 1, stride=groups), :]
        keep = hid - s * 128
        if keep < 128:
            value = jnp.where(lane_index(chans + 1) < keep, value, 0.0)
        put(up_ref, slice(s * 128, s * 128 + 128), value, chans + 1)
    groups = 8
    lines_of(flat, lines, at_down, chans, hid + 1, groups)
    for s in range(down_ref.shape[1] // 128):
        value = lines[pl.ds(s, hid + 1, stride=groups), :]
        keep = chans - s * 128
        if keep < 128:
            value = jnp.where(lane_index(hid + 1) < keep, value, 0.0)
        put(down_ref, slice(s * 128, s * 128 + 128), value, hid + 1)
    for ref, size in ((mix_ref, up_to(chans, 16)), (up_ref, up_to(chans + 1, 16)), (down_ref, up_to(hid + 1, 16))):
        if size < ref.shape[0]:
            ref[size:, :] = jnp.zeros((ref.shape[0] - size, ref.shape[1]), BF)


def run_gather(sz, params, x_items, noise_items, filter_taps, total):
    cp, hp = sz.chan_pad, sz.hid_pad
    own_rows = params.shape[0] // 128
    rows = up_to(own_rows, 16)
    split = rows * 7 // 20 // 16 * 16
    shared = rows - 2 * split
    taps = filter_taps.reshape(sz.rows, -1)
    tap_shape = (up_to(sz.rows + 2, 8), up_to(taps.shape[1], 128))
    heights = total // 4
    any_spec = pl.BlockSpec(memory_space=pl.ANY)
    vmem = pl.BlockSpec(memory_space=pltpu.VMEM)
    edges = (2, cp, sz.steps * sz.lons)
    line_rows = max(sz.chans * sz.basis * 8, (sz.chans + 1) * 16, (sz.hid + 1) * 8)
    dma = pltpu.SemaphoreType.DMA
    return pl.pallas_call(
        partial(gather_kernel, sz, (rows, own_rows, shared, split)),
        name="gather",
        out_shape=[
            jax.ShapeDtypeStruct(edges, BF),
            jax.ShapeDtypeStruct(tap_shape, F32),
            jax.ShapeDtypeStruct((4, cp, 128), F32),
            jax.ShapeDtypeStruct((cp, up_to(sz.mix, 128)), BF),
            jax.ShapeDtypeStruct((cp, up_to(sz.mix, 128)), BF),
            jax.ShapeDtypeStruct((cp, up_to(hp, 128)), BF),
            jax.ShapeDtypeStruct((hp, up_to(cp, 128)), BF),
        ],
        in_specs=[vmem, any_spec, vmem, vmem],
        out_specs=[vmem] * 7,
        scratch_shapes=[
            pltpu.VMEM((total, rows, 128), BF),
            pltpu.VMEM((up_to(total * own_rows + 24, 8), 128), F32),
            pltpu.VMEM((line_rows, 128), F32),
            pltpu.VMEM(x_items.shape, BF),
            pltpu.VMEM(edges, BF),
            pltpu.VMEM(edges, BF),
            pltpu.VMEM((2, 8, tap_shape[1]), F32),
            pltpu.VMEM((2, 8, tap_shape[1]), F32),
            dma(()),
            dma((heights,)), dma((heights,)),
            dma((heights,)), dma((heights,)),
            dma((2 * heights,)), dma((2 * heights,)),
            dma((4 * heights,)), dma((4 * heights,)),
            dma((2,)), dma((2,)),
            dma((2,)), dma((2,)),
        ],
        compiler_params=pltpu.CompilerParams(
            collective_id=1, has_side_effects=True, vmem_limit_bytes=60 * 1024 * 1024
        ),
    )(params.reshape(own_rows, 128), x_items, noise_items, taps)


def run_block(
    sz, x_items, noise_items, cot_items, taps_ext, live, halo, norms, mix, mixt, up, down
):
    cp, hp = sz.chan_pad, sz.hid_pad
    lons = sz.lons

    live_lanes = jnp.concatenate([jnp.repeat(live, sz.main), jnp.repeat(live, lons)])[None]
    any_spec = pl.BlockSpec(memory_space=pl.ANY)
    vmem = pl.BlockSpec(memory_space=pltpu.VMEM)
    mix_lanes = up_to(sz.mix, 128)
    up_lanes = up_to(hp, 128)
    down_lanes = up_to(cp, 128)
    windows = (sz.rows - 1) // 2
    lon = lons
    flops = 2 * sz.width * (3 * sz.mix * cp + 6 * hp * cp)
    return pl.pallas_call(
        partial(block_kernel, sz),
        name="block",
        out_shape=[
            jax.ShapeDtypeStruct(x_items.shape, BF),
            jax.ShapeDtypeStruct(x_items.shape, F32),
            jax.ShapeDtypeStruct((cp, mix_lanes), BF),
            jax.ShapeDtypeStruct((cp, up_lanes), BF),
            jax.ShapeDtypeStruct((hp, down_lanes), BF),
            jax.ShapeDtypeStruct((4, cp, 128), F32),
        ],
        in_specs=[
            any_spec, vmem, any_spec, vmem, pl.BlockSpec(memory_space=pltpu.SMEM), vmem, vmem,
            any_spec, any_spec, any_spec, any_spec,
        ],
        out_specs=[any_spec] * 5 + [vmem],
        scratch_shapes=[
            pltpu.VMEM((cp, sz.width), BF),
            pltpu.VMEM((cp, sz.width), BF),
            pltpu.VMEM((sz.mix, sz.width), BF),
            pltpu.VMEM((cp, sz.width), BF),
            pltpu.VMEM((2 * hp, sz.width), BF),
            pltpu.VMEM((cp, sz.width), BF),
            pltpu.VMEM((sz.steps, sz.chans, sz.cells), F32),
            pltpu.VMEM((4, sz.chans, sz.cells), BF),
            pltpu.VMEM((2, cp, (sz.rows + 3) * lon), BF),
            pltpu.VMEM((windows, 4 * lon, sz.basis * 2 * lon), BF),
            pltpu.VMEM((8 * lon, sz.basis * 2 * lon), BF),
            pltpu.VMEM((2, cp, sz.steps * lon), BF),
            pltpu.VMEM((cp, mix_lanes), BF),
            pltpu.VMEM((cp, up_lanes), BF),
            pltpu.VMEM((hp, down_lanes), BF),
            pltpu.SemaphoreType.DMA((2, 2)),
            pltpu.SemaphoreType.DMA((4,)),
            pltpu.SemaphoreType.DMA((2, sz.steps)),
            pltpu.SemaphoreType.DMA((2,)),
            pltpu.SemaphoreType.DMA((2,)),
        ],
        compiler_params=pltpu.CompilerParams(
            collective_id=0, has_side_effects=True, vmem_limit_bytes=63 * 1024 * 1024
        ),
        cost_estimate=pl.CostEstimate(flops=flops, bytes_accessed=40_000_000, transcendentals=0),
    )(x_items, noise_items, cot_items, halo, taps_ext, live_lanes, norms, mix, mixt, up, down)


def merge(old, shift, length, value, rows):
    lane = lane_index(rows)
    place = lax.broadcasted_iota(jnp.int32, (rows, 128), 0) * 128 + lane
    if shift:
        moved = pltpu.roll(value, shift, 1)
        value = jnp.where(lane >= shift, moved, pltpu.roll(moved, 1, 0))
    return jnp.where((place >= shift) & (place < shift + length), value, old)


def flatten_lines(flat, lines, first, length, count, group):
    for odd in range(2):

        def some(line, row, spots, odd=odd):
            spots = [spot for spot in spots if spot[0] % 2 == odd]
            held = []
            for at, top, shift in spots:
                value = lines[pl.ds(pl.multiple_of((line + at) * group, 8), group), :]
                held.append(merge(flat[pl.ds(row + top, group), :], shift, length, value, group))
            for (_, top, _), value in zip(spots, held):
                flat[pl.ds(row + top, group), :] = value

        in_batches(count, first, length, some, 32)


def pack_kernel(sz, dmix_ref, dup_ref, ddown_ref, dnorm_ref, flat, lines):
    chans, cp, cm, rest, hid = sz.chans, sz.chan_pad, sz.chan_main, sz.rest, sz.hid
    basis, inputs = sz.basis, sz.inputs
    at_disco = 2 * chans
    at_bias = at_disco + chans * basis * inputs
    at_up = at_bias + 3 * chans
    at_down = at_up + (chans + 1) * hid
    used = at_down + (hid + 1) * chans

    groups = 8
    stride = basis * groups
    low = dmix_ref[:, basis * cm : basis * cm + 128].astype(F32)
    for k in range(basis):
        for s in range(cm // 128):
            value = dmix_ref[:, k * cm + s * 128 : k * cm + s * 128 + 128].astype(F32)
            lines[pl.ds(k * groups + s, chans, stride=stride), :] = value[:chans]
        value = pltpu.roll(low, 128 - k * rest, 1) if k else low
        lines[pl.ds(k * groups + cm // 128, chans, stride=stride), :] = value[:chans]
    flatten_lines(flat, lines, at_disco, inputs, chans * basis, groups)

    groups = 16
    for s in range(up_to(hid, 128) // 128):
        value = dup_ref[:, s * 128 : s * 128 + 128].astype(F32)
        lines[pl.ds(s, chans + 1, stride=groups), :] = value[: chans + 1]
    flatten_lines(flat, lines, at_up, hid, chans + 1, groups)

    groups = 8
    for s in range(up_to(chans, 128) // 128):
        value = ddown_ref[:, s * 128 : s * 128 + 128].astype(F32)
        lines[pl.ds(s, hid + 1, stride=groups), :] = value[: hid + 1]
    flatten_lines(flat, lines, at_down, chans, hid + 1, groups)

    def across(columns, pick):
        parts = []
        for s in range(8):
            size = min(128, cp - s * 128)
            if size <= 0:
                parts.append(jnp.zeros((1, 128), F32))
                continue
            block = columns[s * 128 : s * 128 + size]
            if size < 128:
                block = jnp.concatenate([block, jnp.zeros((128 - size, 128), F32)], 0)
            parts.append(pick(block.T))
        return jnp.concatenate(parts, 0)

    def total(block):
        return jnp.sum(block, 0, keepdims=True)

    spots = (0, chans, at_bias + chans, at_bias + 2 * chans)
    pieces = [(start, across(dnorm_ref[i], total)) for i, start in enumerate(spots)]
    bias_row = inputs - cm
    pieces.append((at_bias, across(low, lambda block: block[bias_row : bias_row + 1])))
    for start, value in pieces:
        rows = pl.ds(start // 128, 8)
        flat[rows, :] = merge(flat[rows, :], start % 128, chans, value, 8)
    begin = used // 128
    rows = flat.shape[0] - begin
    place = lax.broadcasted_iota(jnp.int32, (rows, 128), 0) * 128 + lane_index(rows)
    flat[begin:, :] = jnp.where(place < used % 128, flat[begin:, :], 0.0)


def reduce_kernel(
    sz, parts, dmix_ref, dup_ref, ddown_ref, dnorm_ref, out_ref,
    flat, lines, sums, beside_s, beside_r, over_s, over_r, xa_s, xa_r, xb_s, xb_r,
    za_s, za_r, zb_s, zb_r, fa_s, fa_r, fb_r,
    c_send, c_recv, y_send, y_recv, x_send, x_recv, z_send, z_recv, f_send, f_recv,
):
    rows, own_rows, shared, split = parts
    wide = lax.axis_index("wide")
    lat = lax.axis_index("lat")
    total = lax.axis_size("wide")
    heights = total // 4
    core = wide % 2
    side = (wide // 2) % 2
    height = wide // 4
    half = lat % 2
    mate = lat + 1 - 2 * half

    def spot(h, s, c):
        return 4 * (h % heights) + 2 * s + c

    barrier = pltpu.get_barrier_semaphore()

    def hello(w, l):
        pl.semaphore_signal(barrier, inc=1, device_id=(w, l), device_id_type=MESH)

    for i in range(1, heights):
        hello(spot(height + i, side, core), lat)
    hello(spot(height, 1 - side, core), lat)
    hello(spot(height, side, 1 - core), lat)
    hello(wide, mate)
    pack_kernel(sz, dmix_ref, dup_ref, ddown_ref, dnorm_ref, flat, lines)
    pl.semaphore_wait(barrier, heights + 2)

    shares = pl.ds(split, shared)
    lead = pl.ds(pl.multiple_of(half * (split + shared), 16), split)
    other = pl.ds(pl.multiple_of((1 - half) * (split + shared), 16), split)
    columns = [(height + j, 1 - side) for j in range(heights)]
    columns += [(height + j, side) for j in range(heights)]
    started = []

    def copy(src, dst, send, recv, to_wide, to_lat):
        return pltpu.make_async_remote_copy(
            src_ref=src, dst_ref=dst, send_sem=send, recv_sem=recv,
            device_id=(to_wide, to_lat), device_id_type=MESH,
        )

    def go(message):
        message.start()
        started.append(message)

    def to_core(j):
        return copy(beside_s.at[j], beside_r.at[j], c_send.at[j], c_recv.at[j], spot(height, side, 1 - core), lat)

    def to_mate(j):
        return copy(over_s.at[j], over_r.at[j], y_send.at[j], y_recv.at[j], wide, mate)

    def to_side(src, dst, j, part):
        return copy(src.at[j], dst.at[j], x_send.at[j, part], x_recv.at[j, part], spot(height, 1 - side, core), lat)

    def to_height(src, dst, i, part):
        return copy(
            src.at[i - 1], dst.at[i - 1], z_send.at[i - 1, part], z_recv.at[i - 1, part],
            spot(height + i, side, core), lat,
        )

    for j, (h, s) in enumerate(columns):
        away = spot(h, s, 1 - core)
        beside_s[j] = flat[pl.ds(away * own_rows, rows), :].astype(BF)
        go(to_core(j))
    for j, (h, s) in enumerate(columns):
        mine = spot(h, s, core)
        sums[j] = flat[pl.ds(mine * own_rows, rows), :]
    for j in range(2 * heights):
        to_core(j).wait_recv()
        sums[j] += beside_r[j].astype(F32)
        over_s[j] = sums[j, other].astype(BF)
        go(to_mate(j))
        if j < heights:
            xa_s[j] = sums[j, shares].astype(BF)
            go(to_side(xa_s, xa_r, j, 0))
    for j in range(heights):
        to_mate(j).wait_recv()
        xb_s[j] = (sums[j, lead] + over_r[j].astype(F32)).astype(BF)
        go(to_side(xb_s, xb_r, j, 1))
    order = list(range(1, heights)) + [0]
    for i in order:
        j = heights + i
        to_side(xa_s, xa_r, i, 0).wait_recv()
        sums[j, shares] += xa_r[i].astype(F32)
        if i:
            za_s[i - 1] = sums[j, shares].astype(BF)
            go(to_height(za_s, za_r, i, 0))
    for i in order:
        j = heights + i
        to_mate(j).wait_recv()
        to_side(xb_s, xb_r, i, 1).wait_recv()
        sums[j, lead] += over_r[j].astype(F32) + xb_r[i].astype(F32)
        if i:
            zb_s[i - 1] = sums[j, lead].astype(BF)
            go(to_height(zb_s, zb_r, i, 1))
    own = heights
    for i in range(1, heights):
        to_height(za_s, za_r, i, 0).wait_recv()
        sums[own, shares] += za_r[i - 1].astype(F32)
    fa_s[...] = sums[own, shares].astype(BF)
    last = [
        copy(fa_s, fa_r, f_send.at[0], f_recv.at[0], wide, mate),
        copy(sums.at[own, lead], fb_r, f_send.at[1], f_recv.at[1], wide, mate),
    ]
    go(last[0])
    for i in range(1, heights):
        to_height(zb_s, zb_r, i, 1).wait_recv()
        sums[own, lead] += zb_r[i - 1].astype(F32)
    go(last[1])
    last[0].wait_recv()
    out_ref[shares, :] = fa_s[...].astype(F32) + fa_r[...].astype(F32)
    last[1].wait_recv()
    low, high = sums[own, lead], fb_r[...]
    first = jnp.where(half == 0, low, high)
    second = jnp.where(half == 0, high, low)
    out_ref[:split, :] = first
    out_ref[split + shared :, :] = second[: own_rows - split - shared]
    for message in started:
        message.wait_send()


def run_reduce(sz, own_rows, total, dmix, dup, ddown, dnorm):
    rows = up_to(own_rows, 16)
    split = rows // 4 // 16 * 16
    shared = rows - 2 * split
    heights = total // 4
    vmem = pl.BlockSpec(memory_space=pltpu.VMEM)
    line_rows = max(sz.chans * sz.basis * 8, (sz.chans + 1) * 16, (sz.hid + 1) * 8)
    dma = pltpu.SemaphoreType.DMA
    flat_rows = up_to((total - 1) * own_rows + rows, 8) + 16
    return pl.pallas_call(
        partial(reduce_kernel, sz, (rows, own_rows, shared, split)),
        name="reduce",
        out_shape=jax.ShapeDtypeStruct((own_rows, 128), F32),
        in_specs=[vmem] * 4,
        out_specs=vmem,
        scratch_shapes=[
            pltpu.VMEM((flat_rows, 128), F32),
            pltpu.VMEM((line_rows, 128), F32),
            pltpu.VMEM((2 * heights, rows, 128), F32),
            pltpu.VMEM((2 * heights, rows, 128), BF),
            pltpu.VMEM((2 * heights, rows, 128), BF),
            pltpu.VMEM((2 * heights, split, 128), BF),
            pltpu.VMEM((2 * heights, split, 128), BF),
            pltpu.VMEM((heights, shared, 128), BF),
            pltpu.VMEM((heights, shared, 128), BF),
            pltpu.VMEM((heights, split, 128), BF),
            pltpu.VMEM((heights, split, 128), BF),
            pltpu.VMEM((heights, shared, 128), BF),
            pltpu.VMEM((heights, shared, 128), BF),
            pltpu.VMEM((heights, split, 128), BF),
            pltpu.VMEM((heights, split, 128), BF),
            pltpu.VMEM((shared, 128), BF),
            pltpu.VMEM((shared, 128), BF),
            pltpu.VMEM((split, 128), F32),
            dma((2 * heights,)), dma((2 * heights,)),
            dma((2 * heights,)), dma((2 * heights,)),
            dma((heights, 2)), dma((heights, 2)),
            dma((heights, 2)), dma((heights, 2)),
            dma((2,)), dma((2,)),
        ],
        compiler_params=pltpu.CompilerParams(
            collective_id=2, has_side_effects=True, vmem_limit_bytes=62 * 1024 * 1024
        ),
    )(dmix, dup, ddown, dnorm)


def shards(block_input, noise_fields, filter_taps, rollout, cotangent, params):
    sz = Sizes(block_input, noise_fields, filter_taps)
    chans = sz.chans
    dates, step_total = block_input.shape[:2]
    step_ids = jnp.arange(step_total, dtype=jnp.int32)
    live = (step_ids[None, :] < rollout[:, None]).astype(F32).reshape(sz.steps)
    items = (sz.steps, chans, sz.cells)
    x_items = block_input.reshape(items)
    noise_items = noise_fields.reshape(sz.steps, sz.noise, sz.cells)
    halo, taps_ext, norms, mix, mixt, up, down = run_gather(
        sz, params, x_items, noise_items, filter_taps, lax.axis_size("wide")
    )
    cotangent, halo = lax.optimization_barrier((cotangent, halo))
    out, grad, dmix, dup, ddown, dnorm = run_block(
        sz,
        x_items,
        noise_items,
        cotangent.reshape(items),
        taps_ext,
        live,
        halo,
        norms,
        mix,
        mixt,
        up,
        down,
    )
    own = run_reduce(sz, params.shape[0] // 128, lax.axis_size("wide"), dmix, dup, ddown, dnorm)
    param_grad = own.reshape(params.shape)
    return (out.reshape(block_input.shape), grad.reshape(block_input.shape), param_grad)


def solution(mesh):
    in_specs = (
        P("wide", None, None, "lat"),
        P("wide", None, None, "lat"),
        P("lat", None, None, None),
        P("wide"),
        P("wide", None, None, "lat"),
        P("wide"),
    )
    out_specs = (P("wide", None, None, "lat"), P("wide", None, None, "lat"), P("wide"))
    return jax.shard_map(shards, mesh=mesh, in_specs=in_specs, out_specs=out_specs, check_vma=False)
```

```python
import math
from functools import partial

import jax
import jax.numpy as jnp
from jax import lax
from jax.experimental import pallas as pl
from jax.experimental.pallas import tpu as pltpu
from jax.sharding import PartitionSpec as P

HID = 1282
BF = jnp.bfloat16
F32 = jnp.float32
EPS = 1e-05
NEAR = 256
MESH = pl.DeviceIdType.MESH


def up_to(size, unit):
    return -(-size // unit) * unit


def mm(left, right, dims=(1, 0)):
    return lax.dot_general(
        left, right, (((dims[0],), (dims[1],)), ((), ())), preferred_element_type=F32
    )


class Sizes:
    def __init__(self, block_input, noise_fields, filter_taps):
        self.steps = block_input.shape[0] * block_input.shape[1]
        self.chans = block_input.shape[2]
        self.noise = noise_fields.shape[2]
        self.inputs = self.chans + self.noise
        self.rows = filter_taps.shape[0]
        self.basis = filter_taps.shape[1]
        self.taps = filter_taps.shape[3]
        self.cells = block_input.shape[3]
        self.lons = self.cells // self.rows
        self.chan_pad = up_to(self.inputs + 1, 16)
        self.chan_main = self.chans // 128 * 128
        self.rest = self.chan_pad - self.chan_main
        self.hid = HID
        self.hid_pad = up_to(HID + 1, 16)
        self.mix = self.basis * self.chan_pad
        self.main = (self.rows - 1) * self.lons
        self.width = self.steps * self.cells
        self.tail = self.steps * self.main


def block_kernel(
    sz, x_hbm, noise_ref, cot_hbm, halo_ref, taps_ref, live_ref, norm_ref, mix_hbm, mixt_hbm,
    up_hbm, down_hbm, out_hbm, grad_hbm, dmix_hbm, dup_hbm, ddown_hbm, dnorm_ref,
    xs, gs, basis_s, normed_s, act_s, gd_s, grad_s, stage, noisy_s, filt_s, filt_e,
    edge_s, mix_s, up_s, down_s,
    in_sem, w_sem, out_sem, send_sem, recv_sem,
):
    chans, cp, cm, rest = sz.chans, sz.chan_pad, sz.chan_main, sz.rest
    hp, lons, main, tail = sz.hid_pad, sz.lons, sz.main, sz.tail
    pair = 2 * lons
    lat = lax.axis_index("lat")
    lat_count = lax.axis_size("lat")
    has_up = lat > 0
    has_down = lat < lat_count - 1

    def fetch(step, slot):
        return (
            pltpu.make_async_copy(x_hbm.at[step], stage.at[slot], in_sem.at[slot, 0]),
            pltpu.make_async_copy(cot_hbm.at[step], stage.at[2 + slot], in_sem.at[slot, 1]),
        )

    for step in range(2):
        for copy in fetch(step, step):
            copy.start()
    weights = [
        pltpu.make_async_copy(src, dst, w_sem.at[i])
        for i, (src, dst) in enumerate(((mix_hbm, mix_s), (up_hbm, up_s), (down_hbm, down_s)))
    ]
    for copy in weights:
        copy.start()
    mixt_s = normed_s.at[:, pl.ds(0, mixt_hbm.shape[1])]
    mixt_copy = pltpu.make_async_copy(mixt_hbm, mixt_s, w_sem.at[3])

    row_in = lax.broadcasted_iota(jnp.int32, (lons, pair), 0)
    lane = lax.broadcasted_iota(jnp.int32, (lons, pair), 1)
    lane_in = lane % lons
    left_half = lane < lons
    half_taps = sz.taps // 2
    circ = []
    circ_t = []
    for t in range(sz.taps):
        circ.append(row_in == (lane_in + (t - half_taps + lons)) % lons)
        circ_t.append(lane_in == (row_in + (t - half_taps + lons)) % lons)
    def tap_block(ext_row_a, a_a, ext_row_b, a_b, k, masks):
        block = jnp.zeros((lons, pair), F32)
        for t in range(sz.taps):
            va = F32(0) if a_a is None else taps_ref[ext_row_a, (k * 3 + a_a) * sz.taps + t]
            vb = F32(0) if a_b is None else taps_ref[ext_row_b, (k * 3 + a_b) * sz.taps + t]
            block = jnp.where(masks[t], jnp.where(left_half, va, vb), block)
        return block.astype(BF)

    def inside(a):
        return a if 0 <= a <= 2 else None

    windows = (sz.rows - 1) // 2
    last = sz.rows - 1

    def build_filters(backward):
        def build(index, _):
            m = index // sz.basis
            k = index % sz.basis
            cols = pl.ds(pl.multiple_of(k * pair, pair), pair)
            for ri in range(4):
                if backward:
                    block = tap_block(
                        2 * m + ri, inside(2 - ri), 2 * m + ri, inside(3 - ri), k, circ_t
                    )
                else:
                    block = tap_block(
                        2 * m + 1, inside(ri), 2 * m + 2, inside(ri - 1), k, circ
                    )
                filt_s[m, pl.ds(ri * lons, lons), cols] = block
            return 0

        def build_last(k, _):
            cols = pl.ds(pl.multiple_of(k * pair, pair), pair)
            for ri in range(4):
                ext = min(last + ri, last + 2) if backward else last + 1
                a = inside(2 - ri) if backward else inside(ri)
                masks = circ_t if backward else circ
                for odd in range(2):
                    filt_e[pl.ds((odd * 4 + ri) * lons, lons), cols] = tap_block(
                        ext, None if odd else a, ext, a if odd else None, k, masks
                    )
            return 0

        lax.fori_loop(0, windows * sz.basis, build, 0)
        lax.fori_loop(0, sz.basis, build_last, 0)

    build_filters(False)

    gain_one, bias_one = norm_ref[0], norm_ref[1]
    gain_two, bias_two = norm_ref[2], norm_ref[3]

    def wide(vec, lanes):
        if lanes <= 128:
            return vec[:, :lanes]
        return jnp.concatenate([vec] * (lanes // 128) + ([vec[:, : lanes % 128]] if lanes % 128 else []), 1)

    def stats(values):
        centre = jnp.sum(values, 0, keepdims=True) * (1.0 / chans)
        shifted = values - centre
        spread = jnp.sum(jnp.square(shifted), 0, keepdims=True) * (1.0 / chans)
        return shifted, lax.rsqrt(spread + EPS)

    def norm_one(values, lanes):
        shifted, inv = stats(values)
        return shifted * inv * wide(gain_one[:chans], lanes) + wide(bias_one[:chans], lanes)

    halos = []
    for side, there in ((0, has_up), (1, has_down)):
        fields = halo_ref[side].astype(F32)
        width = fields.shape[1]
        normed = norm_one(fields[:chans], width)
        noise = fields[chans : sz.inputs]
        full = jnp.concatenate(
            [normed, noise, jnp.zeros((cp - sz.inputs, width), F32)], 0
        )
        edge_s[side] = jnp.where(there, full, 0.0).astype(BF)

    def halo_part(source, step):
        return source[:, step * lons : (step + 1) * lons]

    ones_row = (lax.broadcasted_iota(jnp.int32, (rest, pair), 0) == sz.inputs - cm).astype(F32)

    def run_filter(slot, store):
        for m in range(windows):
            window = noisy_s[slot, :, m * pair : m * pair + 2 * pair]
            result = mm(window, filt_s[m])
            for k in range(sz.basis):
                store(m, k, result[:, k * pair : (k + 1) * pair])

    def run_last(store):
        window = jnp.concatenate(
            [noisy_s[slot, :, windows * pair : windows * pair + 2 * pair] for slot in range(2)], 1
        )
        result = mm(window, filt_e[...])
        for k in range(sz.basis):
            store(k, result[:, k * pair : (k + 1) * pair])

    def put_basis(lanes, k, part, ones):
        basis_s[k * cm : (k + 1) * cm, lanes] = part[:cm].astype(BF)
        low = part[cm:]
        if ones and k == 0:
            low = low + ones_row
        start = sz.basis * cm + k * rest
        basis_s[start : start + rest, lanes] = low.astype(BF)

    zero_lanes = jnp.zeros((cp, lons), BF)
    pad_rows = jnp.zeros((cp - chans, sz.cells), F32)
    pad_pair = jnp.zeros((cp - chans, pair), F32)
    pairs = sz.steps // 2

    def prepare(two, _):
        both = pl.ds(pl.multiple_of(tail + two * pair, pair), pair)
        near = pl.ds(pl.multiple_of(two * pair, pair), pair)
        for slot in range(2):
            step = 2 * two + slot
            for copy in fetch(step, slot):
                copy.wait()
            fields = stage[slot].astype(F32)
            normed = norm_one(fields, sz.cells)
            noise = noise_ref[step].astype(F32)
            own = jnp.concatenate(
                [normed, noise, jnp.zeros((cp - sz.inputs, sz.cells), F32)], 0
            ).astype(BF)
            noisy_s[slot] = jnp.concatenate(
                [
                    halo_part(edge_s[0, :, near], slot),
                    own,
                    halo_part(edge_s[1, :, near], slot),
                    zero_lanes,
                ],
                1,
            )
            lanes = pl.ds(pl.multiple_of(step * main, main), main)
            xs[:, lanes] = jnp.concatenate([fields, pad_rows], 0)[:, :main].astype(BF)
            masked = jnp.concatenate([stage[2 + slot].astype(F32), pad_rows], 0)[:, :main]
            gs[:, lanes] = (masked * live_ref[:, lanes]).astype(BF)

            def keep(m, k, part, step=step):
                start = pl.multiple_of(step * main + m * pair, pair)
                put_basis(pl.ds(start, pair), k, part, True)

            run_filter(slot, keep)
        x_tail = jnp.concatenate([stage[s, :, main:] for s in range(2)], 1).astype(F32)
        xs[:, both] = jnp.concatenate([x_tail, pad_pair], 0).astype(BF)
        g_tail = jnp.concatenate([stage[2 + s, :, main:] for s in range(2)], 1).astype(F32)
        g_tail = jnp.concatenate([g_tail, pad_pair], 0)
        gs[:, both] = (g_tail * live_ref[:, both]).astype(BF)
        run_last(lambda k, part: put_basis(both, k, part, True))

        @pl.when(two + 1 < pairs)
        def _():
            for slot in range(2):
                for copy in fetch(2 * two + 2 + slot, slot):
                    copy.start()

        return 0

    lax.fori_loop(0, pairs, prepare, 0)
    barrier = pltpu.get_barrier_semaphore()

    @pl.when(has_up)
    def _():
        pl.semaphore_signal(barrier, inc=1, device_id={"lat": lat - 1}, device_id_type=MESH)

    @pl.when(has_down)
    def _():
        pl.semaphore_signal(barrier, inc=1, device_id={"lat": lat + 1}, device_id_type=MESH)

    for copy in weights:
        copy.wait()
    dnorm_ref[...] = jnp.zeros_like(dnorm_ref)

    def fold(values):
        total = values[:, :128]
        for i in range(1, values.shape[1] // 128):
            total = total + values[:, i * 128 : (i + 1) * 128]
        return total

    chunks = sz.width // NEAR
    per_step = main // NEAR
    tail_chunk = tail // NEAR
    steps_per_tail = NEAR // lons

    def main_lanes(chunk):
        return pl.ds(pl.multiple_of((chunk % per_step) * NEAR, NEAR), NEAR)

    def put_tail(chunk, put):
        @pl.when(chunk >= tail_chunk)
        def _():
            for part in range(steps_per_tail):
                put(
                    (chunk - tail_chunk) * steps_per_tail + part,
                    pl.ds(main, lons),
                    slice(part * lons, (part + 1) * lons),
                )

    def out_copy(step):
        return pltpu.make_async_copy(stage.at[step], out_hbm.at[step], out_sem.at[0, step])

    def grad_copy(step):
        return pltpu.make_async_copy(grad_s.at[step], grad_hbm.at[step], out_sem.at[1, step])

    def lanes_of(chunk):
        return pl.ds(pl.multiple_of(chunk * NEAR, NEAR), NEAR)

    def order(index):
        return lax.rem(jnp.minimum(index, chunks - 1) + tail_chunk, chunks)

    def forward_first(chunk):
        lanes = lanes_of(chunk)
        residual = xs[:, lanes].astype(F32) + mm(mix_s[:, : sz.mix], basis_s[:, lanes])
        centre = jnp.sum(residual[:chans], 0, keepdims=True) * (1.0 / chans)
        shifted = residual - centre
        spread = jnp.sum(jnp.square(shifted[:chans]), 0, keepdims=True) * (1.0 / chans)
        inv = lax.rsqrt(spread + EPS)
        hat = shifted * inv
        normed_s[:, lanes] = (hat * wide(gain_two, NEAR) + wide(bias_two, NEAR)).astype(BF)
        return residual, centre, inv

    def forward_chunk(index, held):
        residual, centre, inv = held
        chunk = order(index)
        lanes = lanes_of(chunk)
        grad_low = gs[:, lanes]
        pre = mm(up_s[:, :hp], normed_s[:, lanes], (0, 0))
        grad_hidden = mm(down_s[:, :cp], grad_low)
        phi = 0.5 + 0.5 * lax.erf(pre * 0.7071067811865476)
        density = jnp.exp(pre * pre * -0.5) * 0.3989422804014327
        hidden = pre * phi
        grad_pre = (grad_hidden * (phi + pre * density)).astype(BF)
        low_rows = hp - HID // 16 * 16
        low = lax.broadcasted_iota(jnp.int32, (low_rows, NEAR), 0) == HID - (hp - low_rows)
        hidden = jnp.concatenate(
            [hidden[: hp - low_rows], jnp.where(low, 1.0, hidden[hp - low_rows :])], 0
        ).astype(BF)
        act_s[:hp, lanes] = hidden
        act_s[hp:, lanes] = grad_pre
        branch = mm(down_s[:, :cp], hidden, (0, 0))
        output = ((residual + branch)[:chans] * live_ref[:, lanes]).astype(BF)
        hat = (residual - centre) * inv
        grad_normed = mm(up_s[:, :hp], grad_pre)
        ahead = forward_first(order(index + 1))
        dnorm_ref[2] += fold(grad_normed * hat)
        dnorm_ref[3] += fold(grad_normed)
        scaled = grad_normed * wide(gain_two, NEAR)
        mean_one = jnp.sum(scaled[:chans], 0, keepdims=True) * (1.0 / chans)
        mean_two = jnp.sum((scaled * hat)[:chans], 0, keepdims=True) * (1.0 / chans)
        grad_resid = grad_low.astype(F32) + inv * (scaled - mean_one - hat * mean_two)
        gd_s[:, lanes] = grad_resid.astype(BF)

        def put(step, where, part):
            stage[step, :, where] = output[:, part]
            grad_s[step, :, where] = grad_resid[:chans, part]

        put(jnp.minimum(chunk // per_step, sz.steps - 1), main_lanes(chunk), slice(0, NEAR))
        put_tail(chunk, put)

        @pl.when((chunk < tail_chunk) & (lax.rem(chunk, per_step) == per_step - 1))
        def _():
            out_copy(chunk // per_step).start()

        return ahead

    lax.fori_loop(0, chunks, forward_chunk, forward_first(order(0)))

    rim = pl.ds(0, sz.steps * lons)
    noisy_s[0, :, rim] = jnp.concatenate(
        [gd_s[:, step * main : step * main + lons] for step in range(sz.steps)], 1
    )
    noisy_s[1, :, rim] = gd_s[:, tail:]
    pl.semaphore_wait(barrier, has_up.astype(jnp.int32) + has_down.astype(jnp.int32))

    def send(side, to):
        return pltpu.make_async_remote_copy(
            src_ref=noisy_s.at[side, :, rim],
            dst_ref=edge_s.at[1 - side],
            send_sem=send_sem.at[side],
            recv_sem=recv_sem.at[1 - side],
            device_id={"lat": to},
            device_id_type=MESH,
        )

    @pl.when(has_up)
    def _():
        send(0, lat - 1).start()

    @pl.when(has_down)
    def _():
        send(1, lat + 1).start()

    def blocks(total, size):
        return [(i, min(size, total - i)) for i in range(0, total, size)]

    for start, size in blocks(hp, 512):
        up_s[:, start : start + size] = mm(
            normed_s[...], act_s[hp + start : hp + start + size, :], (1, 1)
        ).astype(BF)
    dup_copy = pltpu.make_async_copy(up_s, dup_hbm, w_sem.at[1])
    dup_copy.start()
    mixt_copy.start()
    for start, size in blocks(hp, 432):
        rows = pl.ds(start, size)
        down_s[rows, :cp] = mm(act_s[rows, :], gs[...], (1, 1)).astype(BF)
    ddown_copy = pltpu.make_async_copy(down_s, ddown_hbm, w_sem.at[2])
    ddown_copy.start()
    for start, size in blocks(sz.mix, 512):
        mix_s[:, start : start + size] = mm(
            gd_s[...], basis_s[start : start + size, :], (1, 1)
        ).astype(BF)
    dmix_copy = pltpu.make_async_copy(mix_s, dmix_hbm, w_sem.at[0])
    dmix_copy.start()

    build_filters(True)

    @pl.when(has_up)
    def _():
        send(0, lat - 1).wait_send()
        send(1, lat - 1).wait_recv()

    @pl.when(has_down)
    def _():
        send(1, lat + 1).wait_send()
        send(0, lat + 1).wait_recv()

    def adjoint(two, _):
        both = pl.ds(pl.multiple_of(tail + two * pair, pair), pair)
        near = pl.ds(pl.multiple_of(two * pair, pair), pair)
        for slot in range(2):
            step = 2 * two + slot
            noisy_s[slot] = jnp.concatenate(
                [
                    halo_part(edge_s[0, :, near], slot),
                    gd_s[:, pl.ds(pl.multiple_of(step * main, main), main)],
                    halo_part(gd_s[:, both], slot),
                    halo_part(edge_s[1, :, near], slot),
                    zero_lanes,
                ],
                1,
            )

            def keep_grad(m, k, part, step=step):
                start = pl.multiple_of(step * main + m * pair, pair)
                put_basis(pl.ds(start, pair), k, part, False)

            run_filter(slot, keep_grad)
        run_last(lambda k, part: put_basis(both, k, part, False))
        return 0

    lax.fori_loop(0, pairs, adjoint, 0)
    mixt_copy.wait()

    def backward_chunk(index, _):
        chunk = order(index)
        lanes = lanes_of(chunk)
        grad_first = mm(normed_s[:, : sz.mix], basis_s[:, lanes])[:chans]
        shifted, inv = stats(xs[:, lanes].astype(F32)[:chans])
        hat = shifted * inv
        dnorm_ref[0, :chans] += fold(grad_first * hat)
        dnorm_ref[1, :chans] += fold(grad_first)
        scaled = grad_first * wide(gain_one[:chans], NEAR)
        mean_one = jnp.sum(scaled, 0, keepdims=True) * (1.0 / chans)
        mean_two = jnp.sum(scaled * hat, 0, keepdims=True) * (1.0 / chans)
        added = inv * (scaled - mean_one - hat * mean_two)

        def put_grad(step, where, part):
            grad_s[step, :, where] += added[:, part]

        @pl.when(chunk < tail_chunk)
        def _():
            put_grad(chunk // per_step, main_lanes(chunk), slice(0, NEAR))

        put_tail(chunk, put_grad)

        @pl.when((chunk < tail_chunk) & (lax.rem(chunk, per_step) == per_step - 1))
        def _():
            grad_copy(chunk // per_step).start()

        return 0

    lax.fori_loop(0, chunks, backward_chunk, 0)
    for step in range(sz.steps):
        out_copy(step).wait()
        grad_copy(step).wait()
    for copy in (ddown_copy, dup_copy, dmix_copy):
        copy.wait()


def flip(index, mask):
    for bit in range(mask.bit_length()):
        if mask >> bit & 1:
            index = index + (1 << bit) * (1 - 2 * (index // (1 << bit) % 2))
    return index


def low_bit(mask, bits):
    return (mask & -mask).bit_length() - 1 if mask else bits


def lane_index(rows):
    return lax.broadcasted_iota(jnp.int32, (rows, 128), 1)


def window(flat, start, rows):
    first = start >> 7
    shift = start & 127
    low = flat[pl.ds(first, rows), :]
    high = flat[pl.ds(first + 1, rows), :]
    mixed = jnp.where(lane_index(rows) >= shift, low, high)
    return pltpu.roll(mixed, (128 - shift) & 127, 1)


def gather_kernel(
    sz, parts, params_ref, x_hbm, noise_ref, taps_ref,
    halo_ref, tap_ref, norm_ref, mix_hbm, mixt_hbm, up_hbm, down_hbm,
    got, flat, lines, x_s, rim_s, edge_s, tap_s, tap_r, mix_s, mixt_s, up_s, down_s,
    in_sem, z_send, z_recv, x_send, x_recv, y_send, y_recv, c_send, c_recv, e_send, e_recv,
    t_send, t_recv, out_sem,
):
    chans, cp, cm, rest, lons = sz.chans, sz.chan_pad, sz.chan_main, sz.rest, sz.lons
    rows, own_rows, shared, split = parts
    wide = lax.axis_index("wide")
    lat = lax.axis_index("lat")
    lat_count = lax.axis_size("lat")
    total = lax.axis_size("wide")
    heights = total // 4
    core = wide % 2
    side = (wide // 2) % 2
    height = wide // 4
    half = lat % 2
    has_up = lat > 0
    has_down = lat < lat_count - 1

    bits = heights.bit_length() - 1

    def spot(mask, s, c):
        return 4 * flip(height, mask) + 2 * s + c

    x_copy = pltpu.make_async_copy(x_hbm, x_s, in_sem)
    x_copy.start()
    got[wide, :own_rows] = params_ref[...]

    barrier = pltpu.get_barrier_semaphore()

    def hello(w, l):
        pl.semaphore_signal(barrier, inc=1, device_id=(w, l), device_id_type=MESH)

    for bit in range(bits):
        hello(spot(1 << bit, side, core), lat)
    hello(spot(0, 1 - side, core), lat)
    hello(spot(0, side, 1 - core), lat)

    @pl.when(has_up)
    def _():
        hello(wide, lat - 1)

    @pl.when(has_down)
    def _():
        hello(wide, lat + 1)

    pl.semaphore_wait(
        barrier, bits + 2 + has_up.astype(jnp.int32) + has_down.astype(jnp.int32)
    )

    whole = pl.ds(0, rows)
    mine = pl.ds(pl.multiple_of(half * split, 16), split + shared)
    lead = pl.ds(pl.multiple_of(half * (split + shared), 16), split)
    other = pl.ds(pl.multiple_of((1 - half) * (split + shared), 16), split)

    def message(shard, where, to_wide, to_lat, send, recv):
        return pltpu.make_async_remote_copy(
            src_ref=got.at[shard, where],
            dst_ref=got.at[shard, where],
            send_sem=send,
            recv_sem=recv,
            device_id=(to_wide, to_lat),
            device_id_type=MESH,
        )

    started = []

    def start(copy):
        copy.start()
        started.append(copy)

    def along(mask, bit):
        return message(
            spot(mask, side, core), mine, spot(1 << bit, side, core), lat,
            z_send.at[(mask | 1 << bit) - 1], z_recv.at[(mask | 1 << bit) - 1],
        )

    def arrive(shard, where, sem):
        message(shard, where, wide, lat, z_send.at[0], sem).wait_recv()

    def across(j, shard):
        return message(shard, mine, spot(0, 1 - side, core), lat, x_send.at[j], x_recv.at[j])

    def over(j, shard):
        return message(shard, lead, wide, lat + 1 - 2 * half, y_send.at[j], y_recv.at[j])

    def beside(j, shard, where):
        return message(shard, where, spot(0, side, 1 - core), lat, c_send.at[j], c_recv.at[j])

    for bit in reversed(range(bits)):
        start(along(0, bit))
    start(across(0, wide))
    start(beside(0, wide, whole))

    x_copy.wait()
    blank = jnp.zeros((cp - sz.inputs, sz.steps * lons), F32)
    for edge, lanes in ((0, slice(0, lons)), (1, slice(sz.cells - lons, sz.cells))):
        fields = jnp.concatenate([x_s[t, :, lanes] for t in range(sz.steps)], 1).astype(F32)
        noise = jnp.concatenate([noise_ref[t, :, lanes] for t in range(sz.steps)], 1).astype(F32)
        rim_s[edge] = jnp.concatenate([fields, noise, blank], 0).astype(BF)

    def rim(edge, to):
        return pltpu.make_async_remote_copy(
            src_ref=rim_s.at[edge],
            dst_ref=edge_s.at[1 - edge],
            send_sem=e_send.at[edge],
            recv_sem=e_recv.at[1 - edge],
            device_id=(wide, to),
            device_id_type=MESH,
        )

    def tap_rim(edge, to):
        return pltpu.make_async_remote_copy(
            src_ref=tap_s.at[edge],
            dst_ref=tap_r.at[1 - edge],
            send_sem=t_send.at[edge],
            recv_sem=t_recv.at[1 - edge],
            device_id=(wide, to),
            device_id_type=MESH,
        )

    tap_total = taps_ref.shape[1]
    for edge, row in ((0, 0), (1, sz.rows - 1)):
        tap_s[edge] = jnp.zeros(tap_s.shape[1:], F32)
        tap_s[edge, :1, :tap_total] = taps_ref[row : row + 1, :]

    @pl.when(has_up)
    def _():
        rim(0, lat - 1).start()
        tap_rim(0, lat - 1).start()

    @pl.when(has_down)
    def _():
        rim(1, lat + 1).start()
        tap_rim(1, lat + 1).start()

    for i in range(1, heights):
        shard = spot(i, side, core)
        arrive(shard, mine, z_recv.at[i - 1])
        for bit in reversed(range(low_bit(i, bits))):
            start(along(i, bit))
        start(across(i, shard))
        start(over(i - 1, shard))
        start(beside(i, shard, mine))
    for j in range(heights):
        shard = spot(j, 1 - side, core)
        arrive(shard, mine, x_recv.at[j])
        start(over(heights - 1 + j, shard))
        start(beside(heights + j, shard, mine))

    def late(j, c):
        if j < heights - 1:
            return spot(j + 1, side, c)
        return spot(j - heights + 1, 1 - side, c)

    def widen(shard):
        flat[pl.ds(shard * own_rows, own_rows), :] = got[shard, :own_rows].astype(F32)

    def finish(j):
        shard = late(j, 1 - core)
        arrive(shard, mine, c_recv.at[j + 1])
        arrive(shard, other, c_recv.at[2 * heights + j])
        widen(shard)

    widen(wide)
    arrive(spot(0, side, 1 - core), whole, c_recv.at[0])
    widen(spot(0, side, 1 - core))
    for j in range(2 * heights - 1):
        arrive(late(j, core), other, y_recv.at[j])
        start(beside(2 * heights + j, late(j, core), other))
        widen(late(j, core))
        if j:
            finish(j - 1)
    finish(2 * heights - 2)
    for copy in started:
        copy.wait_send()

    @pl.when(has_up)
    def _():
        rim(0, lat - 1).wait_send()
        rim(1, lat - 1).wait_recv()
        tap_rim(0, lat - 1).wait_send()
        tap_rim(1, lat - 1).wait_recv()

    @pl.when(has_down)
    def _():
        rim(1, lat + 1).wait_send()
        rim(0, lat + 1).wait_recv()
        tap_rim(1, lat + 1).wait_send()
        tap_rim(0, lat + 1).wait_recv()

    halo_ref[...] = edge_s[...]
    tap_ref[...] = jnp.zeros_like(tap_ref)
    tap_ref[1 : sz.rows + 1, :tap_total] = taps_ref[...]
    tap_ref[:1] = jnp.where(has_up, tap_r[0, :1], 0.0)
    tap_ref[sz.rows + 1 : sz.rows + 2] = jnp.where(has_down, tap_r[1, :1], 0.0)

    unpack_kernel(
        sz, flat, lines, norm_ref, mix_s, mixt_s, up_s, down_s,
        [
            pltpu.make_async_copy(src, dst, out_sem.at[i])
            for i, (src, dst) in enumerate(
                ((mix_s, mix_hbm), (mixt_s, mixt_hbm), (up_s, up_hbm), (down_s, down_hbm))
            )
        ],
    )


def period(length):
    return 128 // math.gcd(length, 128)


def in_batches(count, first, length, some, step=16):
    again = period(length)
    spots = [(j, (first + j * length) // 128, (first + j * length) % 128) for j in range(again)]

    def body(i, _):
        for j in range(0, again, step):
            some(i * again, i * (again * length // 128), spots[j : j + step])
        return 0

    whole = count // again
    lax.fori_loop(0, whole, body, 0)
    left = count % again
    for j in range(0, left, step):
        some(whole * again, whole * (again * length // 128), spots[j : min(j + step, left)])


def lines_of(flat, lines, first, length, count, group):
    def some(line, row, spots):
        held = []
        for _, top, shift in spots:
            low = flat[pl.ds(row + top, group), :]
            if shift:
                high = flat[pl.ds(row + top + 1, group), :]
                low = pltpu.roll(jnp.where(lane_index(group) >= shift, low, high), 128 - shift, 1)
            held.append(low)
        for (at, _, _), value in zip(spots, held):
            lines[pl.ds(pl.multiple_of((line + at) * group, 8), group), :] = value

    in_batches(count, first, length, some)


def unpack_kernel(sz, flat, lines, norm_ref, mix_ref, mixt_ref, up_ref, down_ref, copies):
    chans, cp, cm, rest, hid, hp = sz.chans, sz.chan_pad, sz.chan_main, sz.rest, sz.hid, sz.hid_pad
    basis, inputs = sz.basis, sz.inputs
    at_disco = 2 * chans
    at_bias = at_disco + chans * basis * inputs
    at_up = at_bias + 3 * chans
    at_down = at_up + (chans + 1) * hid

    def column(start):
        held = window(flat, start, 8)
        full = jnp.concatenate(
            [jnp.broadcast_to(held[s : s + 1], (128, 128)).T for s in range(up_to(cp, 128) // 128)], 0
        )[:cp]
        row = lax.broadcasted_iota(jnp.int32, (cp, 128), 0)
        return jnp.where(row < chans, full, 0.0), row

    for i, start in enumerate((0, chans, at_bias + chans, at_bias + 2 * chans)):
        value, row = column(start)
        norm_ref[i] = jnp.where(row == chans, 1.0, value) if i == 3 else value
    disco_bias, _ = column(at_bias)

    groups = 8
    lines_of(flat, lines, at_disco, inputs, chans * basis, groups)
    stride = basis * groups
    lane = lane_index(chans)
    low = jnp.where(lane == inputs - cm, disco_bias[:chans], 0.0)
    blank = jnp.zeros((cp - cm, 128), BF)

    def clear(ref, size):
        if size < ref.shape[0]:
            ref[size:, :] = jnp.zeros((ref.shape[0] - size, ref.shape[1]), BF)

    def put(ref, lanes, value, size):
        whole = size // 16 * 16
        ref[:whole, lanes] = value[:whole].astype(BF)
        tail = jnp.concatenate(
            [value[whole:size], jnp.zeros((up_to(size, 16) - size, 128), F32)], 0
        )
        ref[whole : up_to(size, 16), lanes] = tail.astype(BF)

    for k in range(basis):
        for s in range(cm // 128):
            value = lines[pl.ds(k * groups + s, chans, stride=stride), :]
            put(mix_ref, slice(k * cm + s * 128, k * cm + s * 128 + 128), value, chans)
        value = lines[pl.ds(k * groups + cm // 128, chans, stride=stride), :]
        value = jnp.where(lane < inputs - cm, value, 0.0)
        low = low + (pltpu.roll(value, k * rest, 1) if k else value)
    put(mix_ref, slice(basis * cm, basis * cm + 128), low, chans)
    clear(mix_ref, up_to(chans, 16))
    copies[0].start()

    for k in range(basis):
        for s in range(cm // 128):
            for r in range(cm // 128):
                block = mix_ref[r * 128 : r * 128 + 128, k * cm + s * 128 : k * cm + s * 128 + 128]
                mixt_ref[s * 128 : s * 128 + 128, k * cm + r * 128 : k * cm + r * 128 + 128] = (
                    block.astype(F32).T.astype(BF)
                )
    for r in range(cm // 128):
        block = low[r * 128 : r * 128 + 128].T
        for k in range(basis):
            mixt_ref[cm:cp, k * cm + r * 128 : k * cm + r * 128 + 128] = block[
                k * rest : (k + 1) * rest
            ].astype(BF)
    for s in range(cm // 128):
        block = jnp.concatenate(
            [
                mix_ref[cm:cp, k * cm + s * 128 : k * cm + s * 128 + 128].astype(F32)
                for k in range(basis)
            ]
            + [jnp.zeros((128 - basis * rest, 128), F32)],
            0,
        )
        mixt_ref[s * 128 : s * 128 + 128, basis * cm : basis * cm + 128] = block.T.astype(BF)
    corner = mix_ref[cm:cp, basis * cm : basis * cm + 128].astype(F32)
    corner = jnp.where(lane_index(cp - cm) % rest == 0, corner, 0.0)
    row = lax.broadcasted_iota(jnp.int32, (cp - cm, 128), 0)
    mixt_ref[cm:cp, basis * cm : basis * cm + 128] = jnp.where(row < chans - cm, corner, 0.0).astype(BF)
    copies[1].start()

    groups = 16
    lines_of(flat, lines, at_up, hid, chans + 1, groups)
    for s in range(up_ref.shape[1] // 128):
        value = lines[pl.ds(s, chans + 1, stride=groups), :]
        keep = hid - s * 128
        if keep < 128:
            value = jnp.where(lane_index(chans + 1) < keep, value, 0.0)
        put(up_ref, slice(s * 128, s * 128 + 128), value, chans + 1)
    clear(up_ref, up_to(chans + 1, 16))
    copies[2].start()
    groups = 8
    lines_of(flat, lines, at_down, chans, hid + 1, groups)
    for s in range(down_ref.shape[1] // 128):
        value = lines[pl.ds(s, hid + 1, stride=groups), :]
        keep = chans - s * 128
        if keep < 128:
            value = jnp.where(lane_index(hid + 1) < keep, value, 0.0)
        put(down_ref, slice(s * 128, s * 128 + 128), value, hid + 1)
    clear(down_ref, up_to(hid + 1, 16))
    copies[3].start()
    for copy in copies:
        copy.wait()


def run_gather(sz, params, x_items, noise_items, filter_taps, total):
    cp, hp = sz.chan_pad, sz.hid_pad
    own_rows = params.shape[0] // 128
    rows = up_to(own_rows, 16)
    split = rows * 7 // 20 // 16 * 16
    shared = rows - 2 * split
    taps = filter_taps.reshape(sz.rows, -1)
    tap_shape = (up_to(sz.rows + 2, 8), up_to(taps.shape[1], 128))
    heights = total // 4
    any_spec = pl.BlockSpec(memory_space=pl.ANY)
    vmem = pl.BlockSpec(memory_space=pltpu.VMEM)
    edges = (2, cp, sz.steps * sz.lons)
    line_rows = max(sz.chans * sz.basis * 8, (sz.chans + 1) * 16, (sz.hid + 1) * 8)
    dma = pltpu.SemaphoreType.DMA
    return pl.pallas_call(
        partial(gather_kernel, sz, (rows, own_rows, shared, split)),
        name="gather",
        out_shape=[
            jax.ShapeDtypeStruct(edges, BF),
            jax.ShapeDtypeStruct(tap_shape, F32),
            jax.ShapeDtypeStruct((4, cp, 128), F32),
            jax.ShapeDtypeStruct((cp, up_to(sz.mix, 128)), BF),
            jax.ShapeDtypeStruct((cp, up_to(sz.mix, 128)), BF),
            jax.ShapeDtypeStruct((cp, up_to(hp, 128)), BF),
            jax.ShapeDtypeStruct((hp, up_to(cp, 128)), BF),
        ],
        in_specs=[vmem, any_spec, vmem, vmem],
        out_specs=[vmem] * 3 + [any_spec] * 4,
        scratch_shapes=[
            pltpu.VMEM((total, rows, 128), BF),
            pltpu.VMEM((up_to(total * own_rows + 24, 8), 128), F32),
            pltpu.VMEM((line_rows, 128), F32),
            pltpu.VMEM(x_items.shape, BF),
            pltpu.VMEM(edges, BF),
            pltpu.VMEM(edges, BF),
            pltpu.VMEM((2, 8, tap_shape[1]), F32),
            pltpu.VMEM((2, 8, tap_shape[1]), F32),
            pltpu.VMEM((cp, up_to(sz.mix, 128)), BF),
            pltpu.VMEM((cp, up_to(sz.mix, 128)), BF),
            pltpu.VMEM((cp, up_to(hp, 128)), BF),
            pltpu.VMEM((hp, up_to(cp, 128)), BF),
            dma(()),
            dma((heights,)), dma((heights,)),
            dma((heights,)), dma((heights,)),
            dma((2 * heights,)), dma((2 * heights,)),
            dma((4 * heights,)), dma((4 * heights,)),
            dma((2,)), dma((2,)),
            dma((2,)), dma((2,)), dma((4,)),
        ],
        compiler_params=pltpu.CompilerParams(
            collective_id=1, has_side_effects=True, vmem_limit_bytes=60 * 1024 * 1024
        ),
    )(params.reshape(own_rows, 128), x_items, noise_items, taps)


def run_block(
    sz, x_items, noise_items, cot_items, taps_ext, live, halo, norms, mix, mixt, up, down
):
    cp, hp = sz.chan_pad, sz.hid_pad
    lons = sz.lons

    live_lanes = jnp.concatenate([jnp.repeat(live, sz.main), jnp.repeat(live, lons)])[None]
    any_spec = pl.BlockSpec(memory_space=pl.ANY)
    vmem = pl.BlockSpec(memory_space=pltpu.VMEM)
    mix_lanes = up_to(sz.mix, 128)
    up_lanes = up_to(hp, 128)
    down_lanes = up_to(cp, 128)
    windows = (sz.rows - 1) // 2
    lon = lons
    flops = 2 * sz.width * (3 * sz.mix * cp + 6 * hp * cp)
    return pl.pallas_call(
        partial(block_kernel, sz),
        name="block",
        out_shape=[
            jax.ShapeDtypeStruct(x_items.shape, BF),
            jax.ShapeDtypeStruct(x_items.shape, F32),
            jax.ShapeDtypeStruct((cp, mix_lanes), BF),
            jax.ShapeDtypeStruct((cp, up_lanes), BF),
            jax.ShapeDtypeStruct((hp, down_lanes), BF),
            jax.ShapeDtypeStruct((4, cp, 128), F32),
        ],
        in_specs=[
            any_spec, vmem, any_spec, vmem, pl.BlockSpec(memory_space=pltpu.SMEM), vmem, vmem,
            any_spec, any_spec, any_spec, any_spec,
        ],
        out_specs=[any_spec] * 5 + [vmem],
        scratch_shapes=[
            pltpu.VMEM((cp, sz.width), BF),
            pltpu.VMEM((cp, sz.width), BF),
            pltpu.VMEM((sz.mix, sz.width), BF),
            pltpu.VMEM((cp, sz.width), BF),
            pltpu.VMEM((2 * hp, sz.width), BF),
            pltpu.VMEM((cp, sz.width), BF),
            pltpu.VMEM((sz.steps, sz.chans, sz.cells), F32),
            pltpu.VMEM((4, sz.chans, sz.cells), BF),
            pltpu.VMEM((2, cp, (sz.rows + 3) * lon), BF),
            pltpu.VMEM((windows, 4 * lon, sz.basis * 2 * lon), BF),
            pltpu.VMEM((8 * lon, sz.basis * 2 * lon), BF),
            pltpu.VMEM((2, cp, sz.steps * lon), BF),
            pltpu.VMEM((cp, mix_lanes), BF),
            pltpu.VMEM((cp, up_lanes), BF),
            pltpu.VMEM((hp, down_lanes), BF),
            pltpu.SemaphoreType.DMA((2, 2)),
            pltpu.SemaphoreType.DMA((4,)),
            pltpu.SemaphoreType.DMA((2, sz.steps)),
            pltpu.SemaphoreType.DMA((2,)),
            pltpu.SemaphoreType.DMA((2,)),
        ],
        compiler_params=pltpu.CompilerParams(
            collective_id=0, has_side_effects=True, vmem_limit_bytes=63 * 1024 * 1024
        ),
        cost_estimate=pl.CostEstimate(flops=flops, bytes_accessed=40_000_000, transcendentals=0),
    )(x_items, noise_items, cot_items, halo, taps_ext, live_lanes, norms, mix, mixt, up, down)


def merge(old, shift, length, value, rows):
    lane = lane_index(rows)
    place = lax.broadcasted_iota(jnp.int32, (rows, 128), 0) * 128 + lane
    if shift:
        moved = pltpu.roll(value, shift, 1)
        value = jnp.where(lane >= shift, moved, pltpu.roll(moved, 1, 0))
    return jnp.where((place >= shift) & (place < shift + length), value, old)


def flatten_lines(flat, lines, first, length, count, group):
    for odd in range(2):

        def some(line, row, spots, odd=odd):
            spots = [spot for spot in spots if spot[0] % 2 == odd]
            held = []
            for at, top, shift in spots:
                value = lines[pl.ds(pl.multiple_of((line + at) * group, 8), group), :]
                held.append(merge(flat[pl.ds(row + top, group), :], shift, length, value, group))
            for (_, top, _), value in zip(spots, held):
                flat[pl.ds(row + top, group), :] = value

        in_batches(count, first, length, some, 32)


def pack_kernel(sz, dmix_ref, dup_ref, ddown_ref, dnorm_ref, flat, lines, copies, ready):
    chans, cp, cm, rest, hid = sz.chans, sz.chan_pad, sz.chan_main, sz.rest, sz.hid
    basis, inputs = sz.basis, sz.inputs
    at_disco = 2 * chans
    at_bias = at_disco + chans * basis * inputs
    at_up = at_bias + 3 * chans
    at_down = at_up + (chans + 1) * hid
    used = at_down + (hid + 1) * chans

    def across(columns, pick):
        parts = []
        for s in range(8):
            size = min(128, cp - s * 128)
            if size <= 0:
                parts.append(jnp.zeros((1, 128), F32))
                continue
            block = columns[s * 128 : s * 128 + size]
            if size < 128:
                block = jnp.concatenate([block, jnp.zeros((128 - size, 128), F32)], 0)
            parts.append(pick(block.T))
        return jnp.concatenate(parts, 0)

    def total(block):
        return jnp.sum(block, 0, keepdims=True)

    begin = used // 128
    flat[begin:, :] = jnp.zeros((flat.shape[0] - begin, 128), F32)
    spots = (0, chans, at_bias + chans, at_bias + 2 * chans)
    pieces = [(start, across(dnorm_ref[i], total)) for i, start in enumerate(spots)]
    copies[0].wait()
    low = dmix_ref[:, basis * cm : basis * cm + 128].astype(F32)
    bias_row = inputs - cm
    pieces.append((at_bias, across(low, lambda block: block[bias_row : bias_row + 1])))
    for start, value in pieces:
        rows = pl.ds(start // 128, 8)
        flat[rows, :] = merge(flat[rows, :], start % 128, chans, value, 8)

    groups = 8
    stride = basis * groups
    for k in range(basis):
        for s in range(cm // 128):
            value = dmix_ref[:, k * cm + s * 128 : k * cm + s * 128 + 128].astype(F32)
            lines[pl.ds(k * groups + s, chans, stride=stride), :] = value[:chans]
        value = pltpu.roll(low, 128 - k * rest, 1) if k else low
        lines[pl.ds(k * groups + cm // 128, chans, stride=stride), :] = value[:chans]
    flatten_lines(flat, lines, at_disco, inputs, chans * basis, groups)
    ready(at_bias // 128)

    groups = 16
    copies[1].wait()
    for s in range(up_to(hid, 128) // 128):
        value = dup_ref[:, s * 128 : s * 128 + 128].astype(F32)
        lines[pl.ds(s, chans + 1, stride=groups), :] = value[: chans + 1]
    flatten_lines(flat, lines, at_up, hid, chans + 1, groups)
    ready(at_down // 128)

    groups = 8
    copies[2].wait()
    for s in range(up_to(chans, 128) // 128):
        value = ddown_ref[:, s * 128 : s * 128 + 128].astype(F32)
        lines[pl.ds(s, hid + 1, stride=groups), :] = value[: hid + 1]
    flatten_lines(flat, lines, at_down, chans, hid + 1, groups)
    ready(flat.shape[0])


def reduce_kernel(
    sz, parts, dmix_hbm, dup_hbm, ddown_hbm, dnorm_ref, out_ref,
    flat, lines, dmix_s, dup_s, ddown_s, sums, beside_s, beside_r, over_s, over_r, xa_s, xa_r, xb_s, xb_r,
    za_s, za_r, zb_s, zb_r, fa_s, fa_r, fb_r,
    in_sem, c_send, c_recv, y_send, y_recv, x_send, x_recv, z_send, z_recv, f_send, f_recv,
):
    rows, own_rows, shared, split = parts
    wide = lax.axis_index("wide")
    lat = lax.axis_index("lat")
    total = lax.axis_size("wide")
    heights = total // 4
    core = wide % 2
    side = (wide // 2) % 2
    height = wide // 4
    half = lat % 2
    mate = lat + 1 - 2 * half

    bits = heights.bit_length() - 1

    def spot(mask, s, c):
        return 4 * flip(height, mask) + 2 * s + c

    held = (dmix_s, dup_s, ddown_s)
    copies = [
        pltpu.make_async_copy(src, dst, in_sem.at[i])
        for i, (src, dst) in enumerate(zip((dmix_hbm, dup_hbm, ddown_hbm), held))
    ]
    for item in copies:
        item.start()
    barrier = pltpu.get_barrier_semaphore()

    def hello(w, l):
        pl.semaphore_signal(barrier, inc=1, device_id=(w, l), device_id_type=MESH)

    for bit in range(bits):
        hello(spot(1 << bit, side, core), lat)
    hello(spot(0, 1 - side, core), lat)
    hello(spot(0, side, 1 - core), lat)
    hello(wide, mate)
    pl.semaphore_wait(barrier, bits + 3)
    shares = pl.ds(split, shared)
    lead = pl.ds(pl.multiple_of(half * (split + shared), 16), split)
    other = pl.ds(pl.multiple_of((1 - half) * (split + shared), 16), split)
    masks = list(reversed(range(heights)))
    columns = [(mask, 1 - side) for mask in masks] + [(mask, side) for mask in masks]
    started = []

    def copy(src, dst, send, recv, to_wide, to_lat):
        return pltpu.make_async_remote_copy(
            src_ref=src, dst_ref=dst, send_sem=send, recv_sem=recv,
            device_id=(to_wide, to_lat), device_id_type=MESH,
        )

    def go(message):
        message.start()
        started.append(message)

    def to_core(j):
        return copy(beside_s.at[j], beside_r.at[j], c_send.at[j], c_recv.at[j], spot(0, side, 1 - core), lat)

    def to_mate(j):
        return copy(over_s.at[j], over_r.at[j], y_send.at[j], y_recv.at[j], wide, mate)

    def to_side(src, dst, j, part):
        return copy(src.at[j], dst.at[j], x_send.at[j, part], x_recv.at[j, part], spot(0, 1 - side, core), lat)

    def to_height(src, dst, mask, part):
        return copy(
            src.at[mask - 1], dst.at[mask - 1], z_send.at[mask - 1, part], z_recv.at[mask - 1, part],
            spot(mask & -mask, side, core), lat,
        )

    def add_heights(src, dst, mask, part, j, where):
        for bit in range(low_bit(mask, bits)):
            sender = mask | 1 << bit
            to_height(src, dst, sender, part).wait_recv()
            sums[j, where] += dst[sender - 1].astype(F32)

    next_pair = [0]

    def ready(limit):
        while next_pair[0] < 2 * heights:
            two = next_pair[0]
            if (2 * two + 1) * own_rows + rows > limit:
                break
            away = 2 * two + 1 - core
            beside_s[two] = flat[pl.ds(away * own_rows, rows), :].astype(BF)
            go(to_core(two))
            next_pair[0] = two + 1

    pack_kernel(sz, *held, dnorm_ref, flat, lines, copies, ready)
    for j, (mask, s) in enumerate(columns):
        mine = spot(mask, s, core)
        two = mine // 2
        to_core(two).wait_recv()
        sums[j] = flat[pl.ds(mine * own_rows, rows), :] + beside_r[two].astype(F32)
        over_s[j] = sums[j, other].astype(BF)
        go(to_mate(j))
        if j < heights:
            xa_s[j] = sums[j, shares].astype(BF)
            go(to_side(xa_s, xa_r, j, 0))
    for i, mask in enumerate(masks):
        to_mate(i).wait_recv()
        xb_s[i] = (sums[i, lead] + over_r[i].astype(F32)).astype(BF)
        go(to_side(xb_s, xb_r, i, 1))
        j = heights + i
        to_side(xa_s, xa_r, i, 0).wait_recv()
        sums[j, shares] += xa_r[i].astype(F32)
        add_heights(za_s, za_r, mask, 0, j, shares)
        if mask:
            za_s[mask - 1] = sums[j, shares].astype(BF)
            go(to_height(za_s, za_r, mask, 0))
    own = 2 * heights - 1
    fa_s[...] = sums[own, shares].astype(BF)
    last = [
        copy(fa_s, fa_r, f_send.at[0], f_recv.at[0], wide, mate),
        copy(sums.at[own, lead], fb_r, f_send.at[1], f_recv.at[1], wide, mate),
    ]
    go(last[0])
    for i, mask in enumerate(masks):
        j = heights + i
        to_mate(j).wait_recv()
        to_side(xb_s, xb_r, i, 1).wait_recv()
        sums[j, lead] += over_r[j].astype(F32) + xb_r[i].astype(F32)
        add_heights(zb_s, zb_r, mask, 1, j, lead)
        if mask:
            zb_s[mask - 1] = sums[j, lead].astype(BF)
            go(to_height(zb_s, zb_r, mask, 1))
    go(last[1])
    last[0].wait_recv()
    out_ref[shares, :] = fa_s[...].astype(F32) + fa_r[...].astype(F32)
    last[1].wait_recv()
    low, high = sums[own, lead], fb_r[...]
    first = jnp.where(half == 0, low, high)
    second = jnp.where(half == 0, high, low)
    out_ref[:split, :] = first
    out_ref[split + shared :, :] = second[: own_rows - split - shared]
    for message in started:
        message.wait_send()


def run_reduce(sz, own_rows, total, dmix, dup, ddown, dnorm):
    rows = up_to(own_rows, 16)
    split = rows // 4 // 16 * 16
    shared = rows - 2 * split
    heights = total // 4
    vmem = pl.BlockSpec(memory_space=pltpu.VMEM)
    line_rows = max(sz.chans * sz.basis * 8, (sz.chans + 1) * 16, (sz.hid + 1) * 8)
    dma = pltpu.SemaphoreType.DMA
    flat_rows = up_to((total - 1) * own_rows + rows, 8) + 16
    return pl.pallas_call(
        partial(reduce_kernel, sz, (rows, own_rows, shared, split)),
        name="reduce",
        out_shape=jax.ShapeDtypeStruct((own_rows, 128), F32),
        in_specs=[pl.BlockSpec(memory_space=pl.ANY)] * 3 + [vmem],
        out_specs=vmem,
        scratch_shapes=[
            pltpu.VMEM((flat_rows, 128), F32),
            pltpu.VMEM((line_rows, 128), F32),
            pltpu.VMEM(dmix.shape, BF),
            pltpu.VMEM(dup.shape, BF),
            pltpu.VMEM(ddown.shape, BF),
            pltpu.VMEM((2 * heights, rows, 128), F32),
            pltpu.VMEM((2 * heights, rows, 128), BF),
            pltpu.VMEM((2 * heights, rows, 128), BF),
            pltpu.VMEM((2 * heights, split, 128), BF),
            pltpu.VMEM((2 * heights, split, 128), BF),
            pltpu.VMEM((heights, shared, 128), BF),
            pltpu.VMEM((heights, shared, 128), BF),
            pltpu.VMEM((heights, split, 128), BF),
            pltpu.VMEM((heights, split, 128), BF),
            pltpu.VMEM((heights, shared, 128), BF),
            pltpu.VMEM((heights, shared, 128), BF),
            pltpu.VMEM((heights, split, 128), BF),
            pltpu.VMEM((heights, split, 128), BF),
            pltpu.VMEM((shared, 128), BF),
            pltpu.VMEM((shared, 128), BF),
            pltpu.VMEM((split, 128), F32),
            dma((3,)),
            dma((2 * heights,)), dma((2 * heights,)),
            dma((2 * heights,)), dma((2 * heights,)),
            dma((heights, 2)), dma((heights, 2)),
            dma((heights, 2)), dma((heights, 2)),
            dma((2,)), dma((2,)),
        ],
        compiler_params=pltpu.CompilerParams(
            collective_id=2, has_side_effects=True, vmem_limit_bytes=62 * 1024 * 1024
        ),
    )(dmix, dup, ddown, dnorm)


def shards(block_input, noise_fields, filter_taps, rollout, cotangent, params):
    sz = Sizes(block_input, noise_fields, filter_taps)
    chans = sz.chans
    dates, step_total = block_input.shape[:2]
    step_ids = jnp.arange(step_total, dtype=jnp.int32)
    live = (step_ids[None, :] < rollout[:, None]).astype(F32).reshape(sz.steps)
    items = (sz.steps, chans, sz.cells)
    x_items = block_input.reshape(items)
    noise_items = noise_fields.reshape(sz.steps, sz.noise, sz.cells)
    halo, taps_ext, norms, mix, mixt, up, down = run_gather(
        sz, params, x_items, noise_items, filter_taps, lax.axis_size("wide")
    )
    cotangent, halo = lax.optimization_barrier((cotangent, halo))
    out, grad, dmix, dup, ddown, dnorm = run_block(
        sz,
        x_items,
        noise_items,
        cotangent.reshape(items),
        taps_ext,
        live,
        halo,
        norms,
        mix,
        mixt,
        up,
        down,
    )
    own = run_reduce(sz, params.shape[0] // 128, lax.axis_size("wide"), dmix, dup, ddown, dnorm)
    param_grad = own.reshape(params.shape)
    return (out.reshape(block_input.shape), grad.reshape(block_input.shape), param_grad)


def solution(mesh):
    in_specs = (
        P("wide", None, None, "lat"),
        P("wide", None, None, "lat"),
        P("lat", None, None, None),
        P("wide"),
        P("wide", None, None, "lat"),
        P("wide"),
    )
    out_specs = (P("wide", None, None, "lat"), P("wide", None, None, "lat"), P("wide"))
    return jax.shard_map(shards, mesh=mesh, in_specs=in_specs, out_specs=out_specs, check_vma=False)
```

```python
import math
from functools import partial

import jax
import jax.numpy as jnp
from jax import lax
from jax.experimental import pallas as pl
from jax.experimental.pallas import tpu as pltpu
from jax.sharding import PartitionSpec as P

HID = 1282
BF = jnp.bfloat16
F32 = jnp.float32
EPS = 1e-05
NEAR = 256
MESH = pl.DeviceIdType.MESH


def up_to(size, unit):
    return -(-size // unit) * unit


def mm(left, right, dims=(1, 0)):
    return lax.dot_general(
        left, right, (((dims[0],), (dims[1],)), ((), ())), preferred_element_type=F32
    )


class Sizes:
    def __init__(self, block_input, noise_fields, filter_taps):
        self.steps = block_input.shape[0] * block_input.shape[1]
        self.chans = block_input.shape[2]
        self.noise = noise_fields.shape[2]
        self.inputs = self.chans + self.noise
        self.rows = filter_taps.shape[0]
        self.basis = filter_taps.shape[1]
        self.taps = filter_taps.shape[3]
        self.cells = block_input.shape[3]
        self.lons = self.cells // self.rows
        self.chan_pad = up_to(self.inputs + 1, 16)
        self.chan_main = self.chans // 128 * 128
        self.rest = self.chan_pad - self.chan_main
        self.hid = HID
        self.hid_pad = up_to(HID + 1, 16)
        self.mix = self.basis * self.chan_pad
        self.main = (self.rows - 1) * self.lons
        self.width = self.steps * self.cells
        self.tail = self.steps * self.main


def block_kernel(
    sz, x_hbm, noise_ref, cot_hbm, halo_ref, taps_ref, live_ref, norm_ref, mix_hbm, mixt_hbm,
    up_hbm, down_hbm, out_hbm, grad_hbm, dmix_hbm, dup_hbm, ddown_hbm, dnorm_ref,
    xs, gs, basis_s, normed_s, act_s, gd_s, grad_s, stage, noisy_s, filt_s, filt_e,
    edge_s, mix_s, up_s, down_s,
    in_sem, w_sem, out_sem, send_sem, recv_sem,
):
    chans, cp, cm, rest = sz.chans, sz.chan_pad, sz.chan_main, sz.rest
    hp, lons, main, tail = sz.hid_pad, sz.lons, sz.main, sz.tail
    pair = 2 * lons
    lat = lax.axis_index("lat")
    lat_count = lax.axis_size("lat")
    has_up = lat > 0
    has_down = lat < lat_count - 1

    def fetch(step, slot):
        return (
            pltpu.make_async_copy(x_hbm.at[step], stage.at[slot], in_sem.at[slot, 0]),
            pltpu.make_async_copy(cot_hbm.at[step], stage.at[2 + slot], in_sem.at[slot, 1]),
        )

    for step in range(2):
        for copy in fetch(step, step):
            copy.start()
    weights = [
        pltpu.make_async_copy(src, dst, w_sem.at[i])
        for i, (src, dst) in enumerate(((mix_hbm, mix_s), (up_hbm, up_s), (down_hbm, down_s)))
    ]
    for copy in weights:
        copy.start()
    mixt_s = normed_s.at[:, pl.ds(0, mixt_hbm.shape[1])]
    mixt_copy = pltpu.make_async_copy(mixt_hbm, mixt_s, w_sem.at[3])

    row_in = lax.broadcasted_iota(jnp.int32, (lons, pair), 0)
    lane = lax.broadcasted_iota(jnp.int32, (lons, pair), 1)
    lane_in = lane % lons
    left_half = lane < lons
    half_taps = sz.taps // 2
    circ = []
    circ_t = []
    for t in range(sz.taps):
        circ.append(row_in == (lane_in + (t - half_taps + lons)) % lons)
        circ_t.append(lane_in == (row_in + (t - half_taps + lons)) % lons)
    def tap_block(ext_row_a, a_a, ext_row_b, a_b, k, masks):
        block = jnp.zeros((lons, pair), F32)
        for t in range(sz.taps):
            va = F32(0) if a_a is None else taps_ref[ext_row_a, (k * 3 + a_a) * sz.taps + t]
            vb = F32(0) if a_b is None else taps_ref[ext_row_b, (k * 3 + a_b) * sz.taps + t]
            block = jnp.where(masks[t], jnp.where(left_half, va, vb), block)
        return block.astype(BF)

    def inside(a):
        return a if 0 <= a <= 2 else None

    windows = (sz.rows - 1) // 2
    last = sz.rows - 1

    def build_filters(backward):
        def build(index, _):
            m = index // sz.basis
            k = index % sz.basis
            cols = pl.ds(pl.multiple_of(k * pair, pair), pair)
            for ri in range(4):
                if backward:
                    block = tap_block(
                        2 * m + ri, inside(2 - ri), 2 * m + ri, inside(3 - ri), k, circ_t
                    )
                else:
                    block = tap_block(
                        2 * m + 1, inside(ri), 2 * m + 2, inside(ri - 1), k, circ
                    )
                filt_s[m, pl.ds(ri * lons, lons), cols] = block
            return 0

        def build_last(k, _):
            cols = pl.ds(pl.multiple_of(k * pair, pair), pair)
            for ri in range(4):
                ext = min(last + ri, last + 2) if backward else last + 1
                a = inside(2 - ri) if backward else inside(ri)
                masks = circ_t if backward else circ
                for odd in range(2):
                    filt_e[pl.ds((odd * 4 + ri) * lons, lons), cols] = tap_block(
                        ext, None if odd else a, ext, a if odd else None, k, masks
                    )
            return 0

        lax.fori_loop(0, windows * sz.basis, build, 0)
        lax.fori_loop(0, sz.basis, build_last, 0)

    build_filters(False)

    gain_one, bias_one = norm_ref[0], norm_ref[1]
    gain_two, bias_two = norm_ref[2], norm_ref[3]

    def wide(vec, lanes):
        if lanes <= 128:
            return vec[:, :lanes]
        return jnp.concatenate([vec] * (lanes // 128) + ([vec[:, : lanes % 128]] if lanes % 128 else []), 1)

    def stats(values):
        centre = jnp.sum(values, 0, keepdims=True) * (1.0 / chans)
        shifted = values - centre
        spread = jnp.sum(jnp.square(shifted), 0, keepdims=True) * (1.0 / chans)
        return shifted, lax.rsqrt(spread + EPS)

    def norm_one(values, lanes):
        shifted, inv = stats(values)
        return shifted * inv * wide(gain_one[:chans], lanes) + wide(bias_one[:chans], lanes)

    halos = []
    for side, there in ((0, has_up), (1, has_down)):
        fields = halo_ref[side].astype(F32)
        width = fields.shape[1]
        normed = norm_one(fields[:chans], width)
        noise = fields[chans : sz.inputs]
        full = jnp.concatenate(
            [normed, noise, jnp.zeros((cp - sz.inputs, width), F32)], 0
        )
        edge_s[side] = jnp.where(there, full, 0.0).astype(BF)

    def halo_part(source, step):
        return source[:, step * lons : (step + 1) * lons]

    ones_row = (lax.broadcasted_iota(jnp.int32, (rest, pair), 0) == sz.inputs - cm).astype(F32)

    def run_filter(slot, store):
        for m in range(windows):
            window = noisy_s[slot, :, m * pair : m * pair + 2 * pair]
            result = mm(window, filt_s[m])
            for k in range(sz.basis):
                store(m, k, result[:, k * pair : (k + 1) * pair])

    def run_last(store):
        window = jnp.concatenate(
            [noisy_s[slot, :, windows * pair : windows * pair + 2 * pair] for slot in range(2)], 1
        )
        result = mm(window, filt_e[...])
        for k in range(sz.basis):
            store(k, result[:, k * pair : (k + 1) * pair])

    def put_basis(lanes, k, part, ones):
        basis_s[k * cm : (k + 1) * cm, lanes] = part[:cm].astype(BF)
        low = part[cm:]
        if ones and k == 0:
            low = low + ones_row
        start = sz.basis * cm + k * rest
        basis_s[start : start + rest, lanes] = low.astype(BF)

    zero_lanes = jnp.zeros((cp, lons), BF)
    pad_rows = jnp.zeros((cp - chans, sz.cells), F32)
    pad_pair = jnp.zeros((cp - chans, pair), F32)
    pairs = sz.steps // 2

    def prepare(two, _):
        both = pl.ds(pl.multiple_of(tail + two * pair, pair), pair)
        near = pl.ds(pl.multiple_of(two * pair, pair), pair)
        for slot in range(2):
            step = 2 * two + slot
            for copy in fetch(step, slot):
                copy.wait()
            fields = stage[slot].astype(F32)
            normed = norm_one(fields, sz.cells)
            noise = noise_ref[step].astype(F32)
            own = jnp.concatenate(
                [normed, noise, jnp.zeros((cp - sz.inputs, sz.cells), F32)], 0
            ).astype(BF)
            noisy_s[slot] = jnp.concatenate(
                [
                    halo_part(edge_s[0, :, near], slot),
                    own,
                    halo_part(edge_s[1, :, near], slot),
                    zero_lanes,
                ],
                1,
            )
            lanes = pl.ds(pl.multiple_of(step * main, main), main)
            xs[:, lanes] = jnp.concatenate([fields, pad_rows], 0)[:, :main].astype(BF)
            masked = jnp.concatenate([stage[2 + slot].astype(F32), pad_rows], 0)[:, :main]
            gs[:, lanes] = (masked * live_ref[:, lanes]).astype(BF)

            def keep(m, k, part, step=step):
                start = pl.multiple_of(step * main + m * pair, pair)
                put_basis(pl.ds(start, pair), k, part, True)

            run_filter(slot, keep)
        x_tail = jnp.concatenate([stage[s, :, main:] for s in range(2)], 1).astype(F32)
        xs[:, both] = jnp.concatenate([x_tail, pad_pair], 0).astype(BF)
        g_tail = jnp.concatenate([stage[2 + s, :, main:] for s in range(2)], 1).astype(F32)
        g_tail = jnp.concatenate([g_tail, pad_pair], 0)
        gs[:, both] = (g_tail * live_ref[:, both]).astype(BF)
        run_last(lambda k, part: put_basis(both, k, part, True))

        @pl.when(two + 1 < pairs)
        def _():
            for slot in range(2):
                for copy in fetch(2 * two + 2 + slot, slot):
                    copy.start()

        return 0

    lax.fori_loop(0, pairs, prepare, 0)
    barrier = pltpu.get_barrier_semaphore()

    @pl.when(has_up)
    def _():
        pl.semaphore_signal(barrier, inc=1, device_id={"lat": lat - 1}, device_id_type=MESH)

    @pl.when(has_down)
    def _():
        pl.semaphore_signal(barrier, inc=1, device_id={"lat": lat + 1}, device_id_type=MESH)

    for copy in weights:
        copy.wait()
    dnorm_ref[...] = jnp.zeros_like(dnorm_ref)

    def fold(values):
        total = values[:, :128]
        for i in range(1, values.shape[1] // 128):
            total = total + values[:, i * 128 : (i + 1) * 128]
        return total

    chunks = sz.width // NEAR
    per_step = main // NEAR
    tail_chunk = tail // NEAR
    steps_per_tail = NEAR // lons

    def main_lanes(chunk):
        return pl.ds(pl.multiple_of((chunk % per_step) * NEAR, NEAR), NEAR)

    def put_tail(chunk, put):
        @pl.when(chunk >= tail_chunk)
        def _():
            for part in range(steps_per_tail):
                put(
                    (chunk - tail_chunk) * steps_per_tail + part,
                    pl.ds(main, lons),
                    slice(part * lons, (part + 1) * lons),
                )

    def out_copy(step):
        return pltpu.make_async_copy(stage.at[step], out_hbm.at[step], out_sem.at[0, step])

    def grad_copy(step):
        return pltpu.make_async_copy(grad_s.at[step], grad_hbm.at[:, step, :], out_sem.at[1, step])

    def lanes_of(chunk):
        return pl.ds(pl.multiple_of(chunk * NEAR, NEAR), NEAR)

    def order(index):
        return lax.rem(jnp.minimum(index, chunks - 1) + tail_chunk, chunks)

    def forward_first(chunk):
        lanes = lanes_of(chunk)
        residual = xs[:, lanes].astype(F32) + mm(mix_s[:, : sz.mix], basis_s[:, lanes])
        centre = jnp.sum(residual[:chans], 0, keepdims=True) * (1.0 / chans)
        shifted = residual - centre
        spread = jnp.sum(jnp.square(shifted[:chans]), 0, keepdims=True) * (1.0 / chans)
        inv = lax.rsqrt(spread + EPS)
        hat = shifted * inv
        normed_s[:, lanes] = (hat * wide(gain_two, NEAR) + wide(bias_two, NEAR)).astype(BF)
        return residual, centre, inv

    def forward_chunk(index, held):
        residual, centre, inv = held
        chunk = order(index)
        lanes = lanes_of(chunk)
        grad_low = gs[:, lanes]
        pre = mm(up_s[:, :hp], normed_s[:, lanes], (0, 0))
        grad_hidden = mm(down_s[:, :cp], grad_low)
        phi = 0.5 + 0.5 * lax.erf(pre * 0.7071067811865476)
        density = jnp.exp(pre * pre * -0.5) * 0.3989422804014327
        hidden = pre * phi
        grad_pre = (grad_hidden * (phi + pre * density)).astype(BF)
        low_rows = hp - HID // 16 * 16
        low = lax.broadcasted_iota(jnp.int32, (low_rows, NEAR), 0) == HID - (hp - low_rows)
        hidden = jnp.concatenate(
            [hidden[: hp - low_rows], jnp.where(low, 1.0, hidden[hp - low_rows :])], 0
        ).astype(BF)
        act_s[:hp, lanes] = hidden
        act_s[hp:, lanes] = grad_pre
        branch = mm(down_s[:, :cp], hidden, (0, 0))
        output = ((residual + branch)[:chans] * live_ref[:, lanes]).astype(BF)
        hat = (residual - centre) * inv
        grad_normed = mm(up_s[:, :hp], grad_pre)
        ahead = forward_first(order(index + 1))
        dnorm_ref[2] += fold(grad_normed * hat)
        dnorm_ref[3] += fold(grad_normed)
        scaled = grad_normed * wide(gain_two, NEAR)
        mean_one = jnp.sum(scaled[:chans], 0, keepdims=True) * (1.0 / chans)
        mean_two = jnp.sum((scaled * hat)[:chans], 0, keepdims=True) * (1.0 / chans)
        grad_resid = grad_low.astype(F32) + inv * (scaled - mean_one - hat * mean_two)
        gd_s[:, lanes] = grad_resid.astype(BF)

        def put(step, where, part):
            stage[step, :, where] = output[:, part]
            grad_s[step, :, where] = grad_resid[:chans, part]

        put(jnp.minimum(chunk // per_step, sz.steps - 1), main_lanes(chunk), slice(0, NEAR))
        put_tail(chunk, put)

        @pl.when((chunk < tail_chunk) & (lax.rem(chunk, per_step) == per_step - 1))
        def _():
            out_copy(chunk // per_step).start()

        return ahead

    lax.fori_loop(0, chunks, forward_chunk, forward_first(order(0)))

    rim = pl.ds(0, sz.steps * lons)
    noisy_s[0, :, rim] = jnp.concatenate(
        [gd_s[:, step * main : step * main + lons] for step in range(sz.steps)], 1
    )
    noisy_s[1, :, rim] = gd_s[:, tail:]
    pl.semaphore_wait(barrier, has_up.astype(jnp.int32) + has_down.astype(jnp.int32))

    def send(side, to):
        return pltpu.make_async_remote_copy(
            src_ref=noisy_s.at[side, :, rim],
            dst_ref=edge_s.at[1 - side],
            send_sem=send_sem.at[side],
            recv_sem=recv_sem.at[1 - side],
            device_id={"lat": to},
            device_id_type=MESH,
        )

    @pl.when(has_up)
    def _():
        send(0, lat - 1).start()

    @pl.when(has_down)
    def _():
        send(1, lat + 1).start()

    def blocks(total, size):
        return [(i, min(size, total - i)) for i in range(0, total, size)]

    for start, size in blocks(hp, 512):
        up_s[:, start : start + size] = mm(
            normed_s[...], act_s[hp + start : hp + start + size, :], (1, 1)
        ).astype(BF)
    dup_copy = pltpu.make_async_copy(up_s, dup_hbm, w_sem.at[1])
    dup_copy.start()
    mixt_copy.start()
    for start, size in blocks(hp, 432):
        rows = pl.ds(start, size)
        down_s[rows, :cp] = mm(act_s[rows, :], gs[...], (1, 1)).astype(BF)
    ddown_copy = pltpu.make_async_copy(down_s, ddown_hbm, w_sem.at[2])
    ddown_copy.start()
    for start, size in blocks(sz.mix, 512):
        mix_s[:, start : start + size] = mm(
            gd_s[...], basis_s[start : start + size, :], (1, 1)
        ).astype(BF)
    dmix_copy = pltpu.make_async_copy(mix_s, dmix_hbm, w_sem.at[0])
    dmix_copy.start()

    build_filters(True)

    @pl.when(has_up)
    def _():
        send(0, lat - 1).wait_send()
        send(1, lat - 1).wait_recv()

    @pl.when(has_down)
    def _():
        send(1, lat + 1).wait_send()
        send(0, lat + 1).wait_recv()

    def adjoint(two, _):
        both = pl.ds(pl.multiple_of(tail + two * pair, pair), pair)
        near = pl.ds(pl.multiple_of(two * pair, pair), pair)
        for slot in range(2):
            step = 2 * two + slot
            noisy_s[slot] = jnp.concatenate(
                [
                    halo_part(edge_s[0, :, near], slot),
                    gd_s[:, pl.ds(pl.multiple_of(step * main, main), main)],
                    halo_part(gd_s[:, both], slot),
                    halo_part(edge_s[1, :, near], slot),
                    zero_lanes,
                ],
                1,
            )

            def keep_grad(m, k, part, step=step):
                start = pl.multiple_of(step * main + m * pair, pair)
                put_basis(pl.ds(start, pair), k, part, False)

            run_filter(slot, keep_grad)
        run_last(lambda k, part: put_basis(both, k, part, False))
        return 0

    lax.fori_loop(0, pairs, adjoint, 0)
    mixt_copy.wait()

    def backward_chunk(index, _):
        chunk = order(index)
        lanes = lanes_of(chunk)
        grad_first = mm(normed_s[:, : sz.mix], basis_s[:, lanes])[:chans]
        shifted, inv = stats(xs[:, lanes].astype(F32)[:chans])
        hat = shifted * inv
        dnorm_ref[0, :chans] += fold(grad_first * hat)
        dnorm_ref[1, :chans] += fold(grad_first)
        scaled = grad_first * wide(gain_one[:chans], NEAR)
        mean_one = jnp.sum(scaled, 0, keepdims=True) * (1.0 / chans)
        mean_two = jnp.sum(scaled * hat, 0, keepdims=True) * (1.0 / chans)
        added = inv * (scaled - mean_one - hat * mean_two)

        def put_grad(step, where, part):
            grad_s[step, :, where] += added[:, part]

        @pl.when(chunk < tail_chunk)
        def _():
            put_grad(chunk // per_step, main_lanes(chunk), slice(0, NEAR))

        put_tail(chunk, put_grad)

        @pl.when((chunk < tail_chunk) & (lax.rem(chunk, per_step) == per_step - 1))
        def _():
            grad_copy(chunk // per_step).start()

        return 0

    lax.fori_loop(0, chunks, backward_chunk, 0)
    for step in range(sz.steps):
        out_copy(step).wait()
        grad_copy(step).wait()
    for copy in (ddown_copy, dup_copy, dmix_copy):
        copy.wait()


def flip(index, mask):
    for bit in range(mask.bit_length()):
        if mask >> bit & 1:
            index = index + (1 << bit) * (1 - 2 * (index // (1 << bit) % 2))
    return index


def low_bit(mask, bits):
    return (mask & -mask).bit_length() - 1 if mask else bits


def lane_index(rows):
    return lax.broadcasted_iota(jnp.int32, (rows, 128), 1)


def window(flat, start, rows):
    first = start >> 7
    shift = start & 127
    low = flat[pl.ds(first, rows), :]
    high = flat[pl.ds(first + 1, rows), :]
    mixed = jnp.where(lane_index(rows) >= shift, low, high)
    return pltpu.roll(mixed, (128 - shift) & 127, 1)


def gather_kernel(
    sz, parts, params_ref, x_hbm, noise_ref, taps_ref,
    halo_ref, tap_ref, norm_ref, mix_hbm, mixt_hbm, up_hbm, down_hbm,
    got, flat, lines, x_s, rim_s, edge_s, tap_s, tap_r, mix_s, mixt_s, up_s, down_s,
    in_sem, z_send, z_recv, x_send, x_recv, y_send, y_recv, c_send, c_recv, e_send, e_recv,
    t_send, t_recv, out_sem,
):
    chans, cp, cm, rest, lons = sz.chans, sz.chan_pad, sz.chan_main, sz.rest, sz.lons
    rows, own_rows, shared, split = parts
    wide = lax.axis_index("wide")
    lat = lax.axis_index("lat")
    lat_count = lax.axis_size("lat")
    total = lax.axis_size("wide")
    heights = total // 4
    core = wide % 2
    side = (wide // 2) % 2
    height = wide // 4
    half = lat % 2
    has_up = lat > 0
    has_down = lat < lat_count - 1

    bits = heights.bit_length() - 1

    def spot(mask, s, c):
        return 4 * flip(height, mask) + 2 * s + c

    x_copy = pltpu.make_async_copy(x_hbm, x_s, in_sem)
    x_copy.start()
    got[wide, :own_rows] = params_ref[...]

    barrier = pltpu.get_barrier_semaphore()

    def hello(w, l):
        pl.semaphore_signal(barrier, inc=1, device_id=(w, l), device_id_type=MESH)

    for bit in range(bits):
        hello(spot(1 << bit, side, core), lat)
    hello(spot(0, 1 - side, core), lat)
    hello(spot(0, side, 1 - core), lat)

    @pl.when(has_up)
    def _():
        hello(wide, lat - 1)

    @pl.when(has_down)
    def _():
        hello(wide, lat + 1)

    pl.semaphore_wait(
        barrier, bits + 2 + has_up.astype(jnp.int32) + has_down.astype(jnp.int32)
    )

    whole = pl.ds(0, rows)
    mine = pl.ds(pl.multiple_of(half * split, 16), split + shared)
    lead = pl.ds(pl.multiple_of(half * (split + shared), 16), split)
    other = pl.ds(pl.multiple_of((1 - half) * (split + shared), 16), split)

    def message(shard, where, to_wide, to_lat, send, recv):
        return pltpu.make_async_remote_copy(
            src_ref=got.at[shard, where],
            dst_ref=got.at[shard, where],
            send_sem=send,
            recv_sem=recv,
            device_id=(to_wide, to_lat),
            device_id_type=MESH,
        )

    started = []

    def start(copy):
        copy.start()
        started.append(copy)

    def along(mask, bit):
        return message(
            spot(mask, side, core), mine, spot(1 << bit, side, core), lat,
            z_send.at[(mask | 1 << bit) - 1], z_recv.at[(mask | 1 << bit) - 1],
        )

    def arrive(shard, where, sem):
        message(shard, where, wide, lat, z_send.at[0], sem).wait_recv()

    def across(j, shard):
        return message(shard, mine, spot(0, 1 - side, core), lat, x_send.at[j], x_recv.at[j])

    def over(j, shard):
        return message(shard, lead, wide, lat + 1 - 2 * half, y_send.at[j], y_recv.at[j])

    def beside(j, shard, where):
        return message(shard, where, spot(0, side, 1 - core), lat, c_send.at[j], c_recv.at[j])

    for bit in reversed(range(bits)):
        start(along(0, bit))
    start(across(0, wide))
    start(beside(0, wide, whole))

    x_copy.wait()
    blank = jnp.zeros((cp - sz.inputs, sz.steps * lons), F32)
    for edge, lanes in ((0, slice(0, lons)), (1, slice(sz.cells - lons, sz.cells))):
        fields = jnp.concatenate([x_s[t, :, lanes] for t in range(sz.steps)], 1).astype(F32)
        noise = jnp.concatenate([noise_ref[t, :, lanes] for t in range(sz.steps)], 1).astype(F32)
        rim_s[edge] = jnp.concatenate([fields, noise, blank], 0).astype(BF)

    def rim(edge, to):
        return pltpu.make_async_remote_copy(
            src_ref=rim_s.at[edge],
            dst_ref=edge_s.at[1 - edge],
            send_sem=e_send.at[edge],
            recv_sem=e_recv.at[1 - edge],
            device_id=(wide, to),
            device_id_type=MESH,
        )

    def tap_rim(edge, to):
        return pltpu.make_async_remote_copy(
            src_ref=tap_s.at[edge],
            dst_ref=tap_r.at[1 - edge],
            send_sem=t_send.at[edge],
            recv_sem=t_recv.at[1 - edge],
            device_id=(wide, to),
            device_id_type=MESH,
        )

    tap_total = taps_ref.shape[1]
    for edge, row in ((0, 0), (1, sz.rows - 1)):
        tap_s[edge] = jnp.zeros(tap_s.shape[1:], F32)
        tap_s[edge, :1, :tap_total] = taps_ref[row : row + 1, :]

    @pl.when(has_up)
    def _():
        rim(0, lat - 1).start()
        tap_rim(0, lat - 1).start()

    @pl.when(has_down)
    def _():
        rim(1, lat + 1).start()
        tap_rim(1, lat + 1).start()

    late = []

    def pass_on(mask, s, where):
        shard = spot(mask, s, core)
        start(over(len(late), shard))
        late.append((mask, s))
        start(beside(len(late), shard, where))

    def from_across(mask):
        arrive(spot(mask, 1 - side, core), mine, x_recv.at[mask])
        pass_on(mask, 1 - side, mine)

    for i in range(1, heights):
        shard = spot(i, side, core)
        arrive(shard, mine, z_recv.at[i - 1])
        for bit in reversed(range(low_bit(i, bits))):
            start(along(i, bit))
        start(across(i, shard))
        pass_on(i, side, mine)
        from_across(i - 1)
    from_across(heights - 1)

    def widen(shard):
        flat[pl.ds(shard * own_rows, own_rows), :] = got[shard, :own_rows].astype(F32)

    def finish(j):
        shard = spot(*late[j], 1 - core)
        arrive(shard, mine, c_recv.at[j + 1])
        arrive(shard, other, c_recv.at[2 * heights + j])
        widen(shard)

    widen(wide)
    arrive(spot(0, side, 1 - core), whole, c_recv.at[0])
    widen(spot(0, side, 1 - core))
    for j, column in enumerate(late):
        shard = spot(*column, core)
        arrive(shard, other, y_recv.at[j])
        start(beside(2 * heights + j, shard, other))
        widen(shard)
        if j:
            finish(j - 1)
    finish(len(late) - 1)
    for copy in started:
        copy.wait_send()

    @pl.when(has_up)
    def _():
        rim(0, lat - 1).wait_send()
        rim(1, lat - 1).wait_recv()
        tap_rim(0, lat - 1).wait_send()
        tap_rim(1, lat - 1).wait_recv()

    @pl.when(has_down)
    def _():
        rim(1, lat + 1).wait_send()
        rim(0, lat + 1).wait_recv()
        tap_rim(1, lat + 1).wait_send()
        tap_rim(0, lat + 1).wait_recv()

    halo_ref[...] = edge_s[...]
    tap_ref[...] = jnp.zeros_like(tap_ref)
    tap_ref[1 : sz.rows + 1, :tap_total] = taps_ref[...]
    tap_ref[:1] = jnp.where(has_up, tap_r[0, :1], 0.0)
    tap_ref[sz.rows + 1 : sz.rows + 2] = jnp.where(has_down, tap_r[1, :1], 0.0)

    unpack_kernel(
        sz, flat, lines, norm_ref, mix_s, mixt_s, up_s, down_s,
        [
            pltpu.make_async_copy(src, dst, out_sem.at[i])
            for i, (src, dst) in enumerate(
                ((mix_s, mix_hbm), (mixt_s, mixt_hbm), (up_s, up_hbm), (down_s, down_hbm))
            )
        ],
    )


def period(length):
    return 128 // math.gcd(length, 128)


def in_batches(count, first, length, some, step=16):
    again = period(length)
    spots = [(j, (first + j * length) // 128, (first + j * length) % 128) for j in range(again)]

    def body(i, _):
        for j in range(0, again, step):
            some(i * again, i * (again * length // 128), spots[j : j + step])
        return 0

    whole = count // again
    lax.fori_loop(0, whole, body, 0)
    left = count % again
    for j in range(0, left, step):
        some(whole * again, whole * (again * length // 128), spots[j : min(j + step, left)])


def lines_of(flat, lines, first, length, count, group):
    def some(line, row, spots):
        held = []
        for _, top, shift in spots:
            low = flat[pl.ds(row + top, group), :]
            if shift:
                high = flat[pl.ds(row + top + 1, group), :]
                low = pltpu.roll(jnp.where(lane_index(group) >= shift, low, high), 128 - shift, 1)
            held.append(low)
        for (at, _, _), value in zip(spots, held):
            lines[pl.ds(pl.multiple_of((line + at) * group, 8), group), :] = value

    in_batches(count, first, length, some)


def unpack_kernel(sz, flat, lines, norm_ref, mix_ref, mixt_ref, up_ref, down_ref, copies):
    chans, cp, cm, rest, hid, hp = sz.chans, sz.chan_pad, sz.chan_main, sz.rest, sz.hid, sz.hid_pad
    basis, inputs = sz.basis, sz.inputs
    at_disco = 2 * chans
    at_bias = at_disco + chans * basis * inputs
    at_up = at_bias + 3 * chans
    at_down = at_up + (chans + 1) * hid

    def column(start):
        held = window(flat, start, 8)
        full = jnp.concatenate(
            [jnp.broadcast_to(held[s : s + 1], (128, 128)).T for s in range(up_to(cp, 128) // 128)], 0
        )[:cp]
        row = lax.broadcasted_iota(jnp.int32, (cp, 128), 0)
        return jnp.where(row < chans, full, 0.0), row

    for i, start in enumerate((0, chans, at_bias + chans, at_bias + 2 * chans)):
        value, row = column(start)
        norm_ref[i] = jnp.where(row == chans, 1.0, value) if i == 3 else value
    disco_bias, _ = column(at_bias)

    groups = 8
    lines_of(flat, lines, at_disco, inputs, chans * basis, groups)
    stride = basis * groups
    lane = lane_index(chans)
    low = jnp.where(lane == inputs - cm, disco_bias[:chans], 0.0)
    blank = jnp.zeros((cp - cm, 128), BF)

    def clear(ref, size):
        if size < ref.shape[0]:
            ref[size:, :] = jnp.zeros((ref.shape[0] - size, ref.shape[1]), BF)

    def put(ref, lanes, value, size):
        whole = size // 16 * 16
        ref[:whole, lanes] = value[:whole].astype(BF)
        tail = jnp.concatenate(
            [value[whole:size], jnp.zeros((up_to(size, 16) - size, 128), F32)], 0
        )
        ref[whole : up_to(size, 16), lanes] = tail.astype(BF)

    for k in range(basis):
        for s in range(cm // 128):
            value = lines[pl.ds(k * groups + s, chans, stride=stride), :]
            put(mix_ref, slice(k * cm + s * 128, k * cm + s * 128 + 128), value, chans)
        value = lines[pl.ds(k * groups + cm // 128, chans, stride=stride), :]
        value = jnp.where(lane < inputs - cm, value, 0.0)
        low = low + (pltpu.roll(value, k * rest, 1) if k else value)
    put(mix_ref, slice(basis * cm, basis * cm + 128), low, chans)
    clear(mix_ref, up_to(chans, 16))
    copies[0].start()

    for k in range(basis):
        for s in range(cm // 128):
            for r in range(cm // 128):
                block = mix_ref[r * 128 : r * 128 + 128, k * cm + s * 128 : k * cm + s * 128 + 128]
                mixt_ref[s * 128 : s * 128 + 128, k * cm + r * 128 : k * cm + r * 128 + 128] = (
                    block.astype(F32).T.astype(BF)
                )
    for r in range(cm // 128):
        block = low[r * 128 : r * 128 + 128].T
        for k in range(basis):
            mixt_ref[cm:cp, k * cm + r * 128 : k * cm + r * 128 + 128] = block[
                k * rest : (k + 1) * rest
            ].astype(BF)
    for s in range(cm // 128):
        block = jnp.concatenate(
            [
                mix_ref[cm:cp, k * cm + s * 128 : k * cm + s * 128 + 128].astype(F32)
                for k in range(basis)
            ]
            + [jnp.zeros((128 - basis * rest, 128), F32)],
            0,
        )
        mixt_ref[s * 128 : s * 128 + 128, basis * cm : basis * cm + 128] = block.T.astype(BF)
    corner = mix_ref[cm:cp, basis * cm : basis * cm + 128].astype(F32)
    corner = jnp.where(lane_index(cp - cm) % rest == 0, corner, 0.0)
    row = lax.broadcasted_iota(jnp.int32, (cp - cm, 128), 0)
    mixt_ref[cm:cp, basis * cm : basis * cm + 128] = jnp.where(row < chans - cm, corner, 0.0).astype(BF)
    copies[1].start()

    groups = 16
    lines_of(flat, lines, at_up, hid, chans + 1, groups)
    for s in range(up_ref.shape[1] // 128):
        value = lines[pl.ds(s, chans + 1, stride=groups), :]
        keep = hid - s * 128
        if keep < 128:
            value = jnp.where(lane_index(chans + 1) < keep, value, 0.0)
        put(up_ref, slice(s * 128, s * 128 + 128), value, chans + 1)
    clear(up_ref, up_to(chans + 1, 16))
    copies[2].start()
    groups = 8
    lines_of(flat, lines, at_down, chans, hid + 1, groups)
    for s in range(down_ref.shape[1] // 128):
        value = lines[pl.ds(s, hid + 1, stride=groups), :]
        keep = chans - s * 128
        if keep < 128:
            value = jnp.where(lane_index(hid + 1) < keep, value, 0.0)
        put(down_ref, slice(s * 128, s * 128 + 128), value, hid + 1)
    clear(down_ref, up_to(hid + 1, 16))
    copies[3].start()
    for copy in copies:
        copy.wait()


def run_gather(sz, params, x_items, noise_items, filter_taps, total):
    cp, hp = sz.chan_pad, sz.hid_pad
    own_rows = params.shape[0] // 128
    rows = up_to(own_rows, 16)
    split = rows * 7 // 20 // 16 * 16
    shared = rows - 2 * split
    taps = filter_taps.reshape(sz.rows, -1)
    tap_shape = (up_to(sz.rows + 2, 8), up_to(taps.shape[1], 128))
    heights = total // 4
    any_spec = pl.BlockSpec(memory_space=pl.ANY)
    vmem = pl.BlockSpec(memory_space=pltpu.VMEM)
    edges = (2, cp, sz.steps * sz.lons)
    line_rows = max(sz.chans * sz.basis * 8, (sz.chans + 1) * 16, (sz.hid + 1) * 8)
    dma = pltpu.SemaphoreType.DMA
    return pl.pallas_call(
        partial(gather_kernel, sz, (rows, own_rows, shared, split)),
        name="gather",
        out_shape=[
            jax.ShapeDtypeStruct(edges, BF),
            jax.ShapeDtypeStruct(tap_shape, F32),
            jax.ShapeDtypeStruct((4, cp, 128), F32),
            jax.ShapeDtypeStruct((cp, up_to(sz.mix, 128)), BF),
            jax.ShapeDtypeStruct((cp, up_to(sz.mix, 128)), BF),
            jax.ShapeDtypeStruct((cp, up_to(hp, 128)), BF),
            jax.ShapeDtypeStruct((hp, up_to(cp, 128)), BF),
        ],
        in_specs=[vmem, any_spec, vmem, vmem],
        out_specs=[vmem] * 3 + [any_spec] * 4,
        scratch_shapes=[
            pltpu.VMEM((total, rows, 128), BF),
            pltpu.VMEM((up_to(total * own_rows + 24, 8), 128), F32),
            pltpu.VMEM((line_rows, 128), F32),
            pltpu.VMEM(x_items.shape, BF),
            pltpu.VMEM(edges, BF),
            pltpu.VMEM(edges, BF),
            pltpu.VMEM((2, 8, tap_shape[1]), F32),
            pltpu.VMEM((2, 8, tap_shape[1]), F32),
            pltpu.VMEM((cp, up_to(sz.mix, 128)), BF),
            pltpu.VMEM((cp, up_to(sz.mix, 128)), BF),
            pltpu.VMEM((cp, up_to(hp, 128)), BF),
            pltpu.VMEM((hp, up_to(cp, 128)), BF),
            dma(()),
            dma((heights,)), dma((heights,)),
            dma((heights,)), dma((heights,)),
            dma((2 * heights,)), dma((2 * heights,)),
            dma((4 * heights,)), dma((4 * heights,)),
            dma((2,)), dma((2,)),
            dma((2,)), dma((2,)), dma((4,)),
        ],
        compiler_params=pltpu.CompilerParams(
            collective_id=1, has_side_effects=True, vmem_limit_bytes=60 * 1024 * 1024
        ),
    )(params.reshape(own_rows, 128), x_items, noise_items, taps)


def run_block(
    sz, x_items, noise_items, cot_items, taps_ext, live, halo, norms, mix, mixt, up, down
):
    cp, hp = sz.chan_pad, sz.hid_pad
    lons = sz.lons

    live_lanes = jnp.concatenate([jnp.repeat(live, sz.main), jnp.repeat(live, lons)])[None]
    any_spec = pl.BlockSpec(memory_space=pl.ANY)
    vmem = pl.BlockSpec(memory_space=pltpu.VMEM)
    mix_lanes = up_to(sz.mix, 128)
    up_lanes = up_to(hp, 128)
    down_lanes = up_to(cp, 128)
    windows = (sz.rows - 1) // 2
    lon = lons
    flops = 2 * sz.width * (3 * sz.mix * cp + 6 * hp * cp)
    return pl.pallas_call(
        partial(block_kernel, sz),
        name="block",
        out_shape=[
            jax.ShapeDtypeStruct(x_items.shape, BF),
            jax.ShapeDtypeStruct((sz.chans, sz.steps, sz.cells), F32),
            jax.ShapeDtypeStruct((cp, mix_lanes), BF),
            jax.ShapeDtypeStruct((cp, up_lanes), BF),
            jax.ShapeDtypeStruct((hp, down_lanes), BF),
            jax.ShapeDtypeStruct((4, cp, 128), F32),
        ],
        in_specs=[
            any_spec, vmem, any_spec, vmem, pl.BlockSpec(memory_space=pltpu.SMEM), vmem, vmem,
            any_spec, any_spec, any_spec, any_spec,
        ],
        out_specs=[any_spec] * 5 + [vmem],
        scratch_shapes=[
            pltpu.VMEM((cp, sz.width), BF),
            pltpu.VMEM((cp, sz.width), BF),
            pltpu.VMEM((sz.mix, sz.width), BF),
            pltpu.VMEM((cp, sz.width), BF),
            pltpu.VMEM((2 * hp, sz.width), BF),
            pltpu.VMEM((cp, sz.width), BF),
            pltpu.VMEM((sz.steps, sz.chans, sz.cells), F32),
            pltpu.VMEM((4, sz.chans, sz.cells), BF),
            pltpu.VMEM((2, cp, (sz.rows + 3) * lon), BF),
            pltpu.VMEM((windows, 4 * lon, sz.basis * 2 * lon), BF),
            pltpu.VMEM((8 * lon, sz.basis * 2 * lon), BF),
            pltpu.VMEM((2, cp, sz.steps * lon), BF),
            pltpu.VMEM((cp, mix_lanes), BF),
            pltpu.VMEM((cp, up_lanes), BF),
            pltpu.VMEM((hp, down_lanes), BF),
            pltpu.SemaphoreType.DMA((2, 2)),
            pltpu.SemaphoreType.DMA((4,)),
            pltpu.SemaphoreType.DMA((2, sz.steps)),
            pltpu.SemaphoreType.DMA((2,)),
            pltpu.SemaphoreType.DMA((2,)),
        ],
        compiler_params=pltpu.CompilerParams(
            collective_id=0, has_side_effects=True, vmem_limit_bytes=63 * 1024 * 1024
        ),
        cost_estimate=pl.CostEstimate(flops=flops, bytes_accessed=40_000_000, transcendentals=0),
    )(x_items, noise_items, cot_items, halo, taps_ext, live_lanes, norms, mix, mixt, up, down)


def merge(old, shift, length, value, rows):
    lane = lane_index(rows)
    place = lax.broadcasted_iota(jnp.int32, (rows, 128), 0) * 128 + lane
    if shift:
        moved = pltpu.roll(value, shift, 1)
        value = jnp.where(lane >= shift, moved, pltpu.roll(moved, 1, 0))
    return jnp.where((place >= shift) & (place < shift + length), value, old)


def flatten_lines(flat, lines, first, length, count, group):
    for odd in range(2):

        def some(line, row, spots, odd=odd):
            spots = [spot for spot in spots if spot[0] % 2 == odd]
            held = []
            for at, top, shift in spots:
                value = lines[pl.ds(pl.multiple_of((line + at) * group, 8), group), :]
                held.append(merge(flat[pl.ds(row + top, group), :], shift, length, value, group))
            for (_, top, _), value in zip(spots, held):
                flat[pl.ds(row + top, group), :] = value

        in_batches(count, first, length, some, 32)


def pack_kernel(sz, dmix_ref, dup_ref, ddown_ref, dnorm_ref, flat, lines, copies, ready):
    chans, cp, cm, rest, hid = sz.chans, sz.chan_pad, sz.chan_main, sz.rest, sz.hid
    basis, inputs = sz.basis, sz.inputs
    at_disco = 2 * chans
    at_bias = at_disco + chans * basis * inputs
    at_up = at_bias + 3 * chans
    at_down = at_up + (chans + 1) * hid
    used = at_down + (hid + 1) * chans

    def across(columns, pick):
        parts = []
        for s in range(8):
            size = min(128, cp - s * 128)
            if size <= 0:
                parts.append(jnp.zeros((1, 128), F32))
                continue
            block = columns[s * 128 : s * 128 + size]
            if size < 128:
                block = jnp.concatenate([block, jnp.zeros((128 - size, 128), F32)], 0)
            parts.append(pick(block.T))
        return jnp.concatenate(parts, 0)

    def total(block):
        return jnp.sum(block, 0, keepdims=True)

    begin = used // 128
    flat[begin:, :] = jnp.zeros((flat.shape[0] - begin, 128), F32)
    spots = (0, chans, at_bias + chans, at_bias + 2 * chans)
    pieces = [(start, across(dnorm_ref[i], total)) for i, start in enumerate(spots)]
    copies[0].wait()
    low = dmix_ref[:, basis * cm : basis * cm + 128].astype(F32)
    bias_row = inputs - cm
    pieces.append((at_bias, across(low, lambda block: block[bias_row : bias_row + 1])))
    for start, value in pieces:
        rows = pl.ds(start // 128, 8)
        flat[rows, :] = merge(flat[rows, :], start % 128, chans, value, 8)

    groups = 8
    stride = basis * groups
    for k in range(basis):
        for s in range(cm // 128):
            value = dmix_ref[:, k * cm + s * 128 : k * cm + s * 128 + 128].astype(F32)
            lines[pl.ds(k * groups + s, chans, stride=stride), :] = value[:chans]
        value = pltpu.roll(low, 128 - k * rest, 1) if k else low
        lines[pl.ds(k * groups + cm // 128, chans, stride=stride), :] = value[:chans]
    flatten_lines(flat, lines, at_disco, inputs, chans * basis, groups)
    ready(at_bias // 128)

    groups = 16
    copies[1].wait()
    for s in range(up_to(hid, 128) // 128):
        value = dup_ref[:, s * 128 : s * 128 + 128].astype(F32)
        lines[pl.ds(s, chans + 1, stride=groups), :] = value[: chans + 1]
    flatten_lines(flat, lines, at_up, hid, chans + 1, groups)
    ready(at_down // 128)

    groups = 8
    copies[2].wait()
    for s in range(up_to(chans, 128) // 128):
        value = ddown_ref[:, s * 128 : s * 128 + 128].astype(F32)
        lines[pl.ds(s, hid + 1, stride=groups), :] = value[: hid + 1]
    flatten_lines(flat, lines, at_down, chans, hid + 1, groups)
    ready(flat.shape[0])


def reduce_kernel(
    sz, parts, dmix_hbm, dup_hbm, ddown_hbm, dnorm_ref, out_ref,
    flat, lines, dmix_s, dup_s, ddown_s, sums, beside_s, beside_r, over_s, over_r, xa_s, xa_r, xb_s, xb_r,
    za_s, za_r, zb_s, zb_r, fa_s, fa_r, fb_r,
    in_sem, c_send, c_recv, y_send, y_recv, x_send, x_recv, z_send, z_recv, f_send, f_recv,
):
    rows, own_rows, shared, split = parts
    wide = lax.axis_index("wide")
    lat = lax.axis_index("lat")
    total = lax.axis_size("wide")
    heights = total // 4
    core = wide % 2
    side = (wide // 2) % 2
    height = wide // 4
    half = lat % 2
    mate = lat + 1 - 2 * half

    bits = heights.bit_length() - 1

    def spot(mask, s, c):
        return 4 * flip(height, mask) + 2 * s + c

    held = (dmix_s, dup_s, ddown_s)
    copies = [
        pltpu.make_async_copy(src, dst, in_sem.at[i])
        for i, (src, dst) in enumerate(zip((dmix_hbm, dup_hbm, ddown_hbm), held))
    ]
    for item in copies:
        item.start()
    barrier = pltpu.get_barrier_semaphore()

    def hello(w, l):
        pl.semaphore_signal(barrier, inc=1, device_id=(w, l), device_id_type=MESH)

    for bit in range(bits):
        hello(spot(1 << bit, side, core), lat)
    hello(spot(0, 1 - side, core), lat)
    hello(spot(0, side, 1 - core), lat)
    hello(wide, mate)
    pl.semaphore_wait(barrier, bits + 3)
    shares = pl.ds(split, shared)
    lead = pl.ds(pl.multiple_of(half * (split + shared), 16), split)
    other = pl.ds(pl.multiple_of((1 - half) * (split + shared), 16), split)
    masks = list(reversed(range(heights)))
    columns = [(mask, 1 - side) for mask in masks] + [(mask, side) for mask in masks]
    started = []

    def copy(src, dst, send, recv, to_wide, to_lat):
        return pltpu.make_async_remote_copy(
            src_ref=src, dst_ref=dst, send_sem=send, recv_sem=recv,
            device_id=(to_wide, to_lat), device_id_type=MESH,
        )

    def go(message):
        message.start()
        started.append(message)

    def to_core(j):
        return copy(beside_s.at[j], beside_r.at[j], c_send.at[j], c_recv.at[j], spot(0, side, 1 - core), lat)

    def to_mate(j):
        return copy(over_s.at[j], over_r.at[j], y_send.at[j], y_recv.at[j], wide, mate)

    def to_side(src, dst, j, part):
        return copy(src.at[j], dst.at[j], x_send.at[j, part], x_recv.at[j, part], spot(0, 1 - side, core), lat)

    def to_height(src, dst, mask, part):
        return copy(
            src.at[mask - 1], dst.at[mask - 1], z_send.at[mask - 1, part], z_recv.at[mask - 1, part],
            spot(mask & -mask, side, core), lat,
        )

    def add_heights(src, dst, mask, part, j, where):
        for bit in range(low_bit(mask, bits)):
            sender = mask | 1 << bit
            to_height(src, dst, sender, part).wait_recv()
            sums[j, where] += dst[sender - 1].astype(F32)

    next_pair = [0]

    def ready(limit):
        while next_pair[0] < 2 * heights:
            two = next_pair[0]
            if (2 * two + 1) * own_rows + rows > limit:
                break
            away = 2 * two + 1 - core
            beside_s[two] = flat[pl.ds(away * own_rows, rows), :].astype(BF)
            go(to_core(two))
            next_pair[0] = two + 1

    pack_kernel(sz, *held, dnorm_ref, flat, lines, copies, ready)
    for j, (mask, s) in enumerate(columns):
        mine = spot(mask, s, core)
        two = mine // 2
        to_core(two).wait_recv()
        sums[j] = flat[pl.ds(mine * own_rows, rows), :] + beside_r[two].astype(F32)
        over_s[j] = sums[j, other].astype(BF)
        go(to_mate(j))
        if j < heights:
            xa_s[j] = sums[j, shares].astype(BF)
            go(to_side(xa_s, xa_r, j, 0))
    for i, mask in enumerate(masks):
        to_mate(i).wait_recv()
        xb_s[i] = (sums[i, lead] + over_r[i].astype(F32)).astype(BF)
        go(to_side(xb_s, xb_r, i, 1))
        j = heights + i
        to_side(xa_s, xa_r, i, 0).wait_recv()
        sums[j, shares] += xa_r[i].astype(F32)
        add_heights(za_s, za_r, mask, 0, j, shares)
        if mask:
            za_s[mask - 1] = sums[j, shares].astype(BF)
            go(to_height(za_s, za_r, mask, 0))
    own = 2 * heights - 1
    fa_s[...] = sums[own, shares].astype(BF)
    last = [
        copy(fa_s, fa_r, f_send.at[0], f_recv.at[0], wide, mate),
        copy(sums.at[own, lead], fb_r, f_send.at[1], f_recv.at[1], wide, mate),
    ]
    go(last[0])
    for i, mask in enumerate(masks):
        j = heights + i
        to_mate(j).wait_recv()
        to_side(xb_s, xb_r, i, 1).wait_recv()
        sums[j, lead] += over_r[j].astype(F32) + xb_r[i].astype(F32)
        add_heights(zb_s, zb_r, mask, 1, j, lead)
        if mask:
            zb_s[mask - 1] = sums[j, lead].astype(BF)
            go(to_height(zb_s, zb_r, mask, 1))
    go(last[1])
    last[0].wait_recv()
    out_ref[shares, :] = fa_s[...].astype(F32) + fa_r[...].astype(F32)
    last[1].wait_recv()
    low, high = sums[own, lead], fb_r[...]
    first = jnp.where(half == 0, low, high)
    second = jnp.where(half == 0, high, low)
    out_ref[:split, :] = first
    out_ref[split + shared :, :] = second[: own_rows - split - shared]
    for message in started:
        message.wait_send()


def run_reduce(sz, own_rows, total, dmix, dup, ddown, dnorm):
    rows = up_to(own_rows, 16)
    split = rows // 4 // 16 * 16
    shared = rows - 2 * split
    heights = total // 4
    vmem = pl.BlockSpec(memory_space=pltpu.VMEM)
    line_rows = max(sz.chans * sz.basis * 8, (sz.chans + 1) * 16, (sz.hid + 1) * 8)
    dma = pltpu.SemaphoreType.DMA
    flat_rows = up_to((total - 1) * own_rows + rows, 8) + 16
    return pl.pallas_call(
        partial(reduce_kernel, sz, (rows, own_rows, shared, split)),
        name="reduce",
        out_shape=jax.ShapeDtypeStruct((own_rows, 128), F32),
        in_specs=[pl.BlockSpec(memory_space=pl.ANY)] * 3 + [vmem],
        out_specs=vmem,
        scratch_shapes=[
            pltpu.VMEM((flat_rows, 128), F32),
            pltpu.VMEM((line_rows, 128), F32),
            pltpu.VMEM(dmix.shape, BF),
            pltpu.VMEM(dup.shape, BF),
            pltpu.VMEM(ddown.shape, BF),
            pltpu.VMEM((2 * heights, rows, 128), F32),
            pltpu.VMEM((2 * heights, rows, 128), BF),
            pltpu.VMEM((2 * heights, rows, 128), BF),
            pltpu.VMEM((2 * heights, split, 128), BF),
            pltpu.VMEM((2 * heights, split, 128), BF),
            pltpu.VMEM((heights, shared, 128), BF),
            pltpu.VMEM((heights, shared, 128), BF),
            pltpu.VMEM((heights, split, 128), BF),
            pltpu.VMEM((heights, split, 128), BF),
            pltpu.VMEM((heights, shared, 128), BF),
            pltpu.VMEM((heights, shared, 128), BF),
            pltpu.VMEM((heights, split, 128), BF),
            pltpu.VMEM((heights, split, 128), BF),
            pltpu.VMEM((shared, 128), BF),
            pltpu.VMEM((shared, 128), BF),
            pltpu.VMEM((split, 128), F32),
            dma((3,)),
            dma((2 * heights,)), dma((2 * heights,)),
            dma((2 * heights,)), dma((2 * heights,)),
            dma((heights, 2)), dma((heights, 2)),
            dma((heights, 2)), dma((heights, 2)),
            dma((2,)), dma((2,)),
        ],
        compiler_params=pltpu.CompilerParams(
            collective_id=2, has_side_effects=True, vmem_limit_bytes=62 * 1024 * 1024
        ),
    )(dmix, dup, ddown, dnorm)


def shards(block_input, noise_fields, filter_taps, rollout, cotangent, params):
    sz = Sizes(block_input, noise_fields, filter_taps)
    chans = sz.chans
    dates, step_total = block_input.shape[:2]
    step_ids = jnp.arange(step_total, dtype=jnp.int32)
    live = (step_ids[None, :] < rollout[:, None]).astype(F32).reshape(sz.steps)
    items = (sz.steps, chans, sz.cells)
    x_items = block_input.reshape(items)
    noise_items = noise_fields.reshape(sz.steps, sz.noise, sz.cells)
    halo, taps_ext, norms, mix, mixt, up, down = run_gather(
        sz, params, x_items, noise_items, filter_taps, lax.axis_size("wide")
    )
    cotangent, halo = lax.optimization_barrier((cotangent, halo))
    out, grad, dmix, dup, ddown, dnorm = run_block(
        sz,
        x_items,
        noise_items,
        cotangent.reshape(items),
        taps_ext,
        live,
        halo,
        norms,
        mix,
        mixt,
        up,
        down,
    )
    own = run_reduce(sz, params.shape[0] // 128, lax.axis_size("wide"), dmix, dup, ddown, dnorm)
    param_grad = own.reshape(params.shape)
    return (out.reshape(block_input.shape), jnp.transpose(grad, (1, 0, 2)).reshape(block_input.shape), param_grad)


def solution(mesh):
    in_specs = (
        P("wide", None, None, "lat"),
        P("wide", None, None, "lat"),
        P("lat", None, None, None),
        P("wide"),
        P("wide", None, None, "lat"),
        P("wide"),
    )
    out_specs = (P("wide", None, None, "lat"), P("wide", None, None, "lat"), P("wide"))
    return jax.shard_map(shards, mesh=mesh, in_specs=in_specs, out_specs=out_specs, check_vma=False)
```

```python
import math
from functools import partial

import jax
import jax.numpy as jnp
from jax import lax
from jax.experimental import pallas as pl
from jax.experimental.pallas import tpu as pltpu
from jax.sharding import PartitionSpec as P

HID = 1282
BF = jnp.bfloat16
F32 = jnp.float32
EPS = 1e-05
NEAR = 256
MESH = pl.DeviceIdType.MESH


def up_to(size, unit):
    return -(-size // unit) * unit


def mm(left, right, dims=(1, 0)):
    return lax.dot_general(
        left, right, (((dims[0],), (dims[1],)), ((), ())), preferred_element_type=F32
    )


class Sizes:
    def __init__(self, block_input, noise_fields, filter_taps):
        self.steps = block_input.shape[0] * block_input.shape[1]
        self.chans = block_input.shape[2]
        self.noise = noise_fields.shape[2]
        self.inputs = self.chans + self.noise
        self.rows = filter_taps.shape[0]
        self.basis = filter_taps.shape[1]
        self.taps = filter_taps.shape[3]
        self.cells = block_input.shape[3]
        self.lons = self.cells // self.rows
        self.chan_pad = up_to(self.inputs + 1, 16)
        self.chan_main = self.chans // 128 * 128
        self.rest = self.chan_pad - self.chan_main
        self.hid = HID
        self.hid_pad = up_to(HID + 1, 16)
        self.mix = self.basis * self.chan_pad
        self.main = (self.rows - 1) * self.lons
        self.width = self.steps * self.cells
        self.tail = self.steps * self.main


def block_kernel(
    sz, x_hbm, noise_ref, cot_hbm, halo_ref, taps_ref, live_ref, norm_ref, mix_hbm, mixt_hbm,
    up_hbm, down_hbm, out_hbm, grad_hbm, dmix_hbm, dup_hbm, ddown_hbm, dnorm_ref,
    xs, gs, basis_s, normed_s, act_s, gd_s, grad_s, stage, noisy_s, filt_s, filt_e,
    edge_s, mix_s, up_s, down_s,
    in_sem, w_sem, out_sem, send_sem, recv_sem,
):
    chans, cp, cm, rest = sz.chans, sz.chan_pad, sz.chan_main, sz.rest
    hp, lons, main, tail = sz.hid_pad, sz.lons, sz.main, sz.tail
    pair = 2 * lons
    lat = lax.axis_index("lat")
    lat_count = lax.axis_size("lat")
    has_up = lat > 0
    has_down = lat < lat_count - 1

    def fetch(step, slot):
        return (
            pltpu.make_async_copy(x_hbm.at[step], stage.at[slot], in_sem.at[slot, 0]),
            pltpu.make_async_copy(cot_hbm.at[step], stage.at[2 + slot], in_sem.at[slot, 1]),
        )

    for step in range(2):
        for copy in fetch(step, step):
            copy.start()
    weights = [
        pltpu.make_async_copy(src, dst, w_sem.at[i])
        for i, (src, dst) in enumerate(((mix_hbm, mix_s), (up_hbm, up_s), (down_hbm, down_s)))
    ]
    for copy in weights:
        copy.start()
    mixt_s = normed_s.at[:, pl.ds(0, mixt_hbm.shape[1])]
    mixt_copy = pltpu.make_async_copy(mixt_hbm, mixt_s, w_sem.at[3])

    row_in = lax.broadcasted_iota(jnp.int32, (lons, pair), 0)
    lane = lax.broadcasted_iota(jnp.int32, (lons, pair), 1)
    lane_in = lane % lons
    left_half = lane < lons
    half_taps = sz.taps // 2
    circ = []
    circ_t = []
    for t in range(sz.taps):
        circ.append(row_in == (lane_in + (t - half_taps + lons)) % lons)
        circ_t.append(lane_in == (row_in + (t - half_taps + lons)) % lons)
    def tap_block(ext_row_a, a_a, ext_row_b, a_b, k, masks):
        block = jnp.zeros((lons, pair), F32)
        for t in range(sz.taps):
            va = F32(0) if a_a is None else taps_ref[ext_row_a, (k * 3 + a_a) * sz.taps + t]
            vb = F32(0) if a_b is None else taps_ref[ext_row_b, (k * 3 + a_b) * sz.taps + t]
            block = jnp.where(masks[t], jnp.where(left_half, va, vb), block)
        return block.astype(BF)

    def inside(a):
        return a if 0 <= a <= 2 else None

    windows = (sz.rows - 1) // 2
    last = sz.rows - 1

    def build_filters(backward):
        def build(index, _):
            m = index // sz.basis
            k = index % sz.basis
            cols = pl.ds(pl.multiple_of(k * pair, pair), pair)
            for ri in range(4):
                if backward:
                    block = tap_block(
                        2 * m + ri, inside(2 - ri), 2 * m + ri, inside(3 - ri), k, circ_t
                    )
                else:
                    block = tap_block(
                        2 * m + 1, inside(ri), 2 * m + 2, inside(ri - 1), k, circ
                    )
                filt_s[m, pl.ds(ri * lons, lons), cols] = block
            return 0

        def build_last(k, _):
            cols = pl.ds(pl.multiple_of(k * pair, pair), pair)
            for ri in range(4):
                ext = min(last + ri, last + 2) if backward else last + 1
                a = inside(2 - ri) if backward else inside(ri)
                masks = circ_t if backward else circ
                for odd in range(2):
                    filt_e[pl.ds((odd * 4 + ri) * lons, lons), cols] = tap_block(
                        ext, None if odd else a, ext, a if odd else None, k, masks
                    )
            return 0

        lax.fori_loop(0, windows * sz.basis, build, 0)
        lax.fori_loop(0, sz.basis, build_last, 0)

    build_filters(False)

    gain_one, bias_one = norm_ref[0], norm_ref[1]
    gain_two, bias_two = norm_ref[2], norm_ref[3]

    def wide(vec, lanes):
        if lanes <= 128:
            return vec[:, :lanes]
        return jnp.concatenate([vec] * (lanes // 128) + ([vec[:, : lanes % 128]] if lanes % 128 else []), 1)

    def stats(values):
        centre = jnp.sum(values, 0, keepdims=True) * (1.0 / chans)
        shifted = values - centre
        spread = jnp.sum(jnp.square(shifted), 0, keepdims=True) * (1.0 / chans)
        return shifted, lax.rsqrt(spread + EPS)

    def norm_one(values, lanes):
        shifted, inv = stats(values)
        return shifted * inv * wide(gain_one[:chans], lanes) + wide(bias_one[:chans], lanes)

    halos = []
    for side, there in ((0, has_up), (1, has_down)):
        fields = halo_ref[side].astype(F32)
        width = fields.shape[1]
        normed = norm_one(fields[:chans], width)
        noise = fields[chans : sz.inputs]
        full = jnp.concatenate(
            [normed, noise, jnp.zeros((cp - sz.inputs, width), F32)], 0
        )
        edge_s[side] = jnp.where(there, full, 0.0).astype(BF)

    def halo_part(source, step):
        return source[:, step * lons : (step + 1) * lons]

    ones_row = (lax.broadcasted_iota(jnp.int32, (rest, pair), 0) == sz.inputs - cm).astype(F32)

    def run_filter(slot, store):
        for m in range(windows):
            window = noisy_s[slot, :, m * pair : m * pair + 2 * pair]
            result = mm(window, filt_s[m])
            for k in range(sz.basis):
                store(m, k, result[:, k * pair : (k + 1) * pair])

    def run_last(store):
        window = jnp.concatenate(
            [noisy_s[slot, :, windows * pair : windows * pair + 2 * pair] for slot in range(2)], 1
        )
        result = mm(window, filt_e[...])
        for k in range(sz.basis):
            store(k, result[:, k * pair : (k + 1) * pair])

    def put_basis(lanes, k, part, ones):
        basis_s[k * cm : (k + 1) * cm, lanes] = part[:cm].astype(BF)
        low = part[cm:]
        if ones and k == 0:
            low = low + ones_row
        start = sz.basis * cm + k * rest
        basis_s[start : start + rest, lanes] = low.astype(BF)

    zero_lanes = jnp.zeros((cp, lons), BF)
    pad_rows = jnp.zeros((cp - chans, sz.cells), F32)
    pad_pair = jnp.zeros((cp - chans, pair), F32)
    pairs = sz.steps // 2

    def prepare(two, _):
        both = pl.ds(pl.multiple_of(tail + two * pair, pair), pair)
        near = pl.ds(pl.multiple_of(two * pair, pair), pair)
        for slot in range(2):
            step = 2 * two + slot
            for copy in fetch(step, slot):
                copy.wait()
            fields = stage[slot].astype(F32)
            normed = norm_one(fields, sz.cells)
            noise = noise_ref[step].astype(F32)
            own = jnp.concatenate(
                [normed, noise, jnp.zeros((cp - sz.inputs, sz.cells), F32)], 0
            ).astype(BF)
            noisy_s[slot] = jnp.concatenate(
                [
                    halo_part(edge_s[0, :, near], slot),
                    own,
                    halo_part(edge_s[1, :, near], slot),
                    zero_lanes,
                ],
                1,
            )
            lanes = pl.ds(pl.multiple_of(step * main, main), main)
            xs[:, lanes] = jnp.concatenate([fields, pad_rows], 0)[:, :main].astype(BF)
            masked = jnp.concatenate([stage[2 + slot].astype(F32), pad_rows], 0)[:, :main]
            gs[:, lanes] = (masked * live_ref[:, lanes]).astype(BF)

            def keep(m, k, part, step=step):
                start = pl.multiple_of(step * main + m * pair, pair)
                put_basis(pl.ds(start, pair), k, part, True)

            run_filter(slot, keep)
        x_tail = jnp.concatenate([stage[s, :, main:] for s in range(2)], 1).astype(F32)
        xs[:, both] = jnp.concatenate([x_tail, pad_pair], 0).astype(BF)
        g_tail = jnp.concatenate([stage[2 + s, :, main:] for s in range(2)], 1).astype(F32)
        g_tail = jnp.concatenate([g_tail, pad_pair], 0)
        gs[:, both] = (g_tail * live_ref[:, both]).astype(BF)
        run_last(lambda k, part: put_basis(both, k, part, True))

        @pl.when(two + 1 < pairs)
        def _():
            for slot in range(2):
                for copy in fetch(2 * two + 2 + slot, slot):
                    copy.start()

        return 0

    lax.fori_loop(0, pairs, prepare, 0)
    barrier = pltpu.get_barrier_semaphore()

    @pl.when(has_up)
    def _():
        pl.semaphore_signal(barrier, inc=1, device_id={"lat": lat - 1}, device_id_type=MESH)

    @pl.when(has_down)
    def _():
        pl.semaphore_signal(barrier, inc=1, device_id={"lat": lat + 1}, device_id_type=MESH)

    for copy in weights:
        copy.wait()
    dnorm_ref[...] = jnp.zeros_like(dnorm_ref)

    def fold(values):
        total = values[:, :128]
        for i in range(1, values.shape[1] // 128):
            total = total + values[:, i * 128 : (i + 1) * 128]
        return total

    chunks = sz.width // NEAR
    per_step = main // NEAR
    tail_chunk = tail // NEAR
    steps_per_tail = NEAR // lons

    def main_lanes(chunk):
        return pl.ds(pl.multiple_of((chunk % per_step) * NEAR, NEAR), NEAR)

    def put_tail(chunk, put):
        @pl.when(chunk >= tail_chunk)
        def _():
            for part in range(steps_per_tail):
                put(
                    (chunk - tail_chunk) * steps_per_tail + part,
                    pl.ds(main, lons),
                    slice(part * lons, (part + 1) * lons),
                )

    def out_copy(step):
        return pltpu.make_async_copy(stage.at[step], out_hbm.at[step], out_sem.at[0, step])

    def grad_copy(step):
        return pltpu.make_async_copy(grad_s.at[step], grad_hbm.at[:, step, :], out_sem.at[1, step])

    def lanes_of(chunk):
        return pl.ds(pl.multiple_of(chunk * NEAR, NEAR), NEAR)

    def order(index):
        return lax.rem(jnp.minimum(index, chunks - 1) + tail_chunk, chunks)

    def forward_first(chunk):
        lanes = lanes_of(chunk)
        residual = xs[:, lanes].astype(F32) + mm(mix_s[:, : sz.mix], basis_s[:, lanes])
        centre = jnp.sum(residual[:chans], 0, keepdims=True) * (1.0 / chans)
        shifted = residual - centre
        spread = jnp.sum(jnp.square(shifted[:chans]), 0, keepdims=True) * (1.0 / chans)
        inv = lax.rsqrt(spread + EPS)
        hat = shifted * inv
        normed_s[:, lanes] = (hat * wide(gain_two, NEAR) + wide(bias_two, NEAR)).astype(BF)
        return residual, centre, inv

    def forward_chunk(index, held):
        residual, centre, inv = held
        chunk = order(index)
        lanes = lanes_of(chunk)
        grad_low = gs[:, lanes]
        pre = mm(up_s[:, :hp], normed_s[:, lanes], (0, 0))
        grad_hidden = mm(down_s[:, :cp], grad_low)
        phi = 0.5 + 0.5 * lax.erf(pre * 0.7071067811865476)
        density = jnp.exp(pre * pre * -0.5) * 0.3989422804014327
        hidden = pre * phi
        grad_pre = (grad_hidden * (phi + pre * density)).astype(BF)
        low_rows = hp - HID // 16 * 16
        low = lax.broadcasted_iota(jnp.int32, (low_rows, NEAR), 0) == HID - (hp - low_rows)
        hidden = jnp.concatenate(
            [hidden[: hp - low_rows], jnp.where(low, 1.0, hidden[hp - low_rows :])], 0
        ).astype(BF)
        act_s[:hp, lanes] = hidden
        act_s[hp:, lanes] = grad_pre
        branch = mm(down_s[:, :cp], hidden, (0, 0))
        output = ((residual + branch)[:chans] * live_ref[:, lanes]).astype(BF)
        hat = (residual - centre) * inv
        grad_normed = mm(up_s[:, :hp], grad_pre)
        ahead = forward_first(order(index + 1))
        dnorm_ref[2] += fold(grad_normed * hat)
        dnorm_ref[3] += fold(grad_normed)
        scaled = grad_normed * wide(gain_two, NEAR)
        mean_one = jnp.sum(scaled[:chans], 0, keepdims=True) * (1.0 / chans)
        mean_two = jnp.sum((scaled * hat)[:chans], 0, keepdims=True) * (1.0 / chans)
        grad_resid = grad_low.astype(F32) + inv * (scaled - mean_one - hat * mean_two)
        gd_s[:, lanes] = grad_resid.astype(BF)

        def put(step, where, part):
            stage[step, :, where] = output[:, part]
            grad_s[step, :, where] = grad_resid[:chans, part]

        put(jnp.minimum(chunk // per_step, sz.steps - 1), main_lanes(chunk), slice(0, NEAR))
        put_tail(chunk, put)

        @pl.when((chunk < tail_chunk) & (lax.rem(chunk, per_step) == per_step - 1))
        def _():
            out_copy(chunk // per_step).start()

        return ahead

    lax.fori_loop(0, chunks, forward_chunk, forward_first(order(0)))

    rim = pl.ds(0, sz.steps * lons)
    noisy_s[0, :, rim] = jnp.concatenate(
        [gd_s[:, step * main : step * main + lons] for step in range(sz.steps)], 1
    )
    noisy_s[1, :, rim] = gd_s[:, tail:]
    pl.semaphore_wait(barrier, has_up.astype(jnp.int32) + has_down.astype(jnp.int32))

    def send(side, to):
        return pltpu.make_async_remote_copy(
            src_ref=noisy_s.at[side, :, rim],
            dst_ref=edge_s.at[1 - side],
            send_sem=send_sem.at[side],
            recv_sem=recv_sem.at[1 - side],
            device_id={"lat": to},
            device_id_type=MESH,
        )

    @pl.when(has_up)
    def _():
        send(0, lat - 1).start()

    @pl.when(has_down)
    def _():
        send(1, lat + 1).start()

    def blocks(total, size):
        return [(i, min(size, total - i)) for i in range(0, total, size)]

    for start, size in blocks(hp, 512):
        up_s[:, start : start + size] = mm(
            normed_s[...], act_s[hp + start : hp + start + size, :], (1, 1)
        ).astype(BF)
    dup_copy = pltpu.make_async_copy(up_s, dup_hbm, w_sem.at[1])
    dup_copy.start()
    mixt_copy.start()
    for start, size in blocks(hp, 432):
        rows = pl.ds(start, size)
        down_s[rows, :cp] = mm(act_s[rows, :], gs[...], (1, 1)).astype(BF)
    ddown_copy = pltpu.make_async_copy(down_s, ddown_hbm, w_sem.at[2])
    ddown_copy.start()
    for start, size in blocks(sz.mix, 512):
        mix_s[:, start : start + size] = mm(
            gd_s[...], basis_s[start : start + size, :], (1, 1)
        ).astype(BF)
    dmix_copy = pltpu.make_async_copy(mix_s, dmix_hbm, w_sem.at[0])
    dmix_copy.start()

    build_filters(True)

    @pl.when(has_up)
    def _():
        send(0, lat - 1).wait_send()
        send(1, lat - 1).wait_recv()

    @pl.when(has_down)
    def _():
        send(1, lat + 1).wait_send()
        send(0, lat + 1).wait_recv()

    def adjoint(two, _):
        both = pl.ds(pl.multiple_of(tail + two * pair, pair), pair)
        near = pl.ds(pl.multiple_of(two * pair, pair), pair)
        for slot in range(2):
            step = 2 * two + slot
            noisy_s[slot] = jnp.concatenate(
                [
                    halo_part(edge_s[0, :, near], slot),
                    gd_s[:, pl.ds(pl.multiple_of(step * main, main), main)],
                    halo_part(gd_s[:, both], slot),
                    halo_part(edge_s[1, :, near], slot),
                    zero_lanes,
                ],
                1,
            )

            def keep_grad(m, k, part, step=step):
                start = pl.multiple_of(step * main + m * pair, pair)
                put_basis(pl.ds(start, pair), k, part, False)

            run_filter(slot, keep_grad)
        run_last(lambda k, part: put_basis(both, k, part, False))
        return 0

    lax.fori_loop(0, pairs, adjoint, 0)
    mixt_copy.wait()

    def mixed_back(index):
        return mm(normed_s[:, : sz.mix], basis_s[:, lanes_of(order(index))])[:chans]

    def backward_chunk(index, _):
        chunk = order(index)
        lanes = lanes_of(chunk)
        grad_first = mixed_back(index)
        shifted, inv = stats(xs[:, lanes].astype(F32)[:chans])
        hat = shifted * inv
        dnorm_ref[0, :chans] += fold(grad_first * hat)
        dnorm_ref[1, :chans] += fold(grad_first)
        scaled = grad_first * wide(gain_one[:chans], NEAR)
        mean_one = jnp.sum(scaled, 0, keepdims=True) * (1.0 / chans)
        mean_two = jnp.sum(scaled * hat, 0, keepdims=True) * (1.0 / chans)
        added = inv * (scaled - mean_one - hat * mean_two)

        def put_grad(step, where, part):
            grad_s[step, :, where] += added[:, part]

        @pl.when(chunk < tail_chunk)
        def _():
            put_grad(chunk // per_step, main_lanes(chunk), slice(0, NEAR))

        put_tail(chunk, put_grad)

        @pl.when((chunk < tail_chunk) & (lax.rem(chunk, per_step) == per_step - 1))
        def _():
            grad_copy(chunk // per_step).start()

        return 0

    lax.fori_loop(0, chunks, backward_chunk, 0)
    for step in range(sz.steps):
        out_copy(step).wait()
        grad_copy(step).wait()
    for copy in (ddown_copy, dup_copy, dmix_copy):
        copy.wait()


def flip(index, mask):
    for bit in range(mask.bit_length()):
        if mask >> bit & 1:
            index = index + (1 << bit) * (1 - 2 * (index // (1 << bit) % 2))
    return index


def low_bit(mask, bits):
    return (mask & -mask).bit_length() - 1 if mask else bits


def lane_index(rows):
    return lax.broadcasted_iota(jnp.int32, (rows, 128), 1)


def window(flat, start, rows):
    first = start >> 7
    shift = start & 127
    low = flat[pl.ds(first, rows), :]
    high = flat[pl.ds(first + 1, rows), :]
    mixed = jnp.where(lane_index(rows) >= shift, low, high)
    return pltpu.roll(mixed, (128 - shift) & 127, 1)


def gather_kernel(
    sz, parts, params_ref, x_hbm, cot_hbm, noise_ref, taps_ref,
    halo_ref, tap_ref, norm_ref, mix_hbm, mixt_hbm, up_hbm, down_hbm, x_out, cot_out,
    got, flat, lines, x_raw, cot_raw, x_s, cot_s, rim_s, edge_s, tap_s, tap_r, mix_s, mixt_s, up_s, down_s,
    in_sem, z_send, z_recv, x_send, x_recv, y_send, y_recv, c_send, c_recv, e_send, e_recv,
    t_send, t_recv, out_sem, turn_sem,
):
    chans, cp, cm, rest, lons = sz.chans, sz.chan_pad, sz.chan_main, sz.rest, sz.lons
    rows, own_rows, shared, split = parts
    wide = lax.axis_index("wide")
    lat = lax.axis_index("lat")
    lat_count = lax.axis_size("lat")
    total = lax.axis_size("wide")
    heights = total // 4
    core = wide % 2
    side = (wide // 2) % 2
    height = wide // 4
    half = lat % 2
    has_up = lat > 0
    has_down = lat < lat_count - 1

    bits = heights.bit_length() - 1

    def spot(mask, s, c):
        return 4 * flip(height, mask) + 2 * s + c

    raw_copies = [
        pltpu.make_async_copy(x_hbm, x_raw, in_sem.at[0]),
        pltpu.make_async_copy(cot_hbm, cot_raw, in_sem.at[1]),
    ]
    for copy in raw_copies:
        copy.start()
    got[wide, :own_rows] = params_ref[...]

    barrier = pltpu.get_barrier_semaphore()

    def hello(w, l):
        pl.semaphore_signal(barrier, inc=1, device_id=(w, l), device_id_type=MESH)

    for bit in range(bits):
        hello(spot(1 << bit, side, core), lat)
    hello(spot(0, 1 - side, core), lat)
    hello(spot(0, side, 1 - core), lat)

    @pl.when(has_up)
    def _():
        hello(wide, lat - 1)

    @pl.when(has_down)
    def _():
        hello(wide, lat + 1)

    tap_total = taps_ref.shape[1]
    for edge, row in ((0, 0), (1, sz.rows - 1)):
        tap_s[edge] = jnp.zeros(tap_s.shape[1:], F32)
        tap_s[edge, :1, :tap_total] = taps_ref[row : row + 1, :]

    pl.semaphore_wait(
        barrier, bits + 2 + has_up.astype(jnp.int32) + has_down.astype(jnp.int32)
    )

    whole = pl.ds(0, rows)
    mine = pl.ds(pl.multiple_of(half * split, 16), split + shared)
    lead = pl.ds(pl.multiple_of(half * (split + shared), 16), split)
    other = pl.ds(pl.multiple_of((1 - half) * (split + shared), 16), split)

    def message(shard, where, to_wide, to_lat, send, recv):
        return pltpu.make_async_remote_copy(
            src_ref=got.at[shard, where],
            dst_ref=got.at[shard, where],
            send_sem=send,
            recv_sem=recv,
            device_id=(to_wide, to_lat),
            device_id_type=MESH,
        )

    started = []

    def start(copy):
        copy.start()
        started.append(copy)

    def along(mask, bit):
        return message(
            spot(mask, side, core), mine, spot(1 << bit, side, core), lat,
            z_send.at[(mask | 1 << bit) - 1], z_recv.at[(mask | 1 << bit) - 1],
        )

    def arrive(shard, where, sem):
        message(shard, where, wide, lat, z_send.at[0], sem).wait_recv()

    def across(j, shard):
        return message(shard, mine, spot(0, 1 - side, core), lat, x_send.at[j], x_recv.at[j])

    def over(j, shard):
        return message(shard, lead, wide, lat + 1 - 2 * half, y_send.at[j], y_recv.at[j])

    def beside(j, shard, where):
        return message(shard, where, spot(0, side, 1 - core), lat, c_send.at[j], c_recv.at[j])

    for bit in reversed(range(bits)):
        start(along(0, bit))
    start(across(0, wide))
    start(beside(0, wide, whole))

    def turned(i, raw, held, out):
        raw_copies[i].wait()
        held[...] = jnp.swapaxes(raw[...], 0, 1)
        copy = pltpu.make_async_copy(held, out, turn_sem.at[i])
        copy.start()
        return copy

    put_x = turned(0, x_raw, x_s, x_out)
    blank = jnp.zeros((cp - sz.inputs, sz.steps * lons), F32)
    for edge, lanes in ((0, slice(0, lons)), (1, slice(sz.cells - lons, sz.cells))):
        fields = jnp.concatenate([x_s[t, :, lanes] for t in range(sz.steps)], 1).astype(F32)
        noise = jnp.concatenate([noise_ref[t, :, lanes] for t in range(sz.steps)], 1).astype(F32)
        rim_s[edge] = jnp.concatenate([fields, noise, blank], 0).astype(BF)

    def rim(edge, to):
        return pltpu.make_async_remote_copy(
            src_ref=rim_s.at[edge],
            dst_ref=edge_s.at[1 - edge],
            send_sem=e_send.at[edge],
            recv_sem=e_recv.at[1 - edge],
            device_id=(wide, to),
            device_id_type=MESH,
        )

    def tap_rim(edge, to):
        return pltpu.make_async_remote_copy(
            src_ref=tap_s.at[edge],
            dst_ref=tap_r.at[1 - edge],
            send_sem=t_send.at[edge],
            recv_sem=t_recv.at[1 - edge],
            device_id=(wide, to),
            device_id_type=MESH,
        )

    @pl.when(has_up)
    def _():
        rim(0, lat - 1).start()
        tap_rim(0, lat - 1).start()

    @pl.when(has_down)
    def _():
        rim(1, lat + 1).start()
        tap_rim(1, lat + 1).start()

    late = []

    def pass_on(mask, s, where):
        shard = spot(mask, s, core)
        start(over(len(late), shard))
        late.append((mask, s))
        start(beside(len(late), shard, where))

    def from_across(mask):
        arrive(spot(mask, 1 - side, core), mine, x_recv.at[mask])
        pass_on(mask, 1 - side, mine)

    for i in range(1, heights):
        shard = spot(i, side, core)
        arrive(shard, mine, z_recv.at[i - 1])
        for bit in reversed(range(low_bit(i, bits))):
            start(along(i, bit))
        start(across(i, shard))
        pass_on(i, side, mine)
        from_across(i - 1)
        if i == 1:
            put_cot = turned(1, cot_raw, cot_s, cot_out)
    from_across(heights - 1)

    def widen(shard):
        flat[pl.ds(shard * own_rows, own_rows), :] = got[shard, :own_rows].astype(F32)

    def finish(j):
        shard = spot(*late[j], 1 - core)
        arrive(shard, mine, c_recv.at[j + 1])
        arrive(shard, other, c_recv.at[2 * heights + j])
        widen(shard)

    widen(wide)
    arrive(spot(0, side, 1 - core), whole, c_recv.at[0])
    widen(spot(0, side, 1 - core))
    for j, column in enumerate(late):
        shard = spot(*column, core)
        arrive(shard, other, y_recv.at[j])
        start(beside(2 * heights + j, shard, other))
        widen(shard)
        if j:
            finish(j - 1)
    finish(len(late) - 1)
    put_x.wait()
    put_cot.wait()
    for copy in started:
        copy.wait_send()

    @pl.when(has_up)
    def _():
        rim(0, lat - 1).wait_send()
        rim(1, lat - 1).wait_recv()
        tap_rim(0, lat - 1).wait_send()
        tap_rim(1, lat - 1).wait_recv()

    @pl.when(has_down)
    def _():
        rim(1, lat + 1).wait_send()
        rim(0, lat + 1).wait_recv()
        tap_rim(1, lat + 1).wait_send()
        tap_rim(0, lat + 1).wait_recv()

    halo_ref[...] = edge_s[...]
    tap_ref[...] = jnp.zeros_like(tap_ref)
    tap_ref[1 : sz.rows + 1, :tap_total] = taps_ref[...]
    tap_ref[:1] = jnp.where(has_up, tap_r[0, :1], 0.0)
    tap_ref[sz.rows + 1 : sz.rows + 2] = jnp.where(has_down, tap_r[1, :1], 0.0)

    unpack_kernel(
        sz, flat, lines, norm_ref, mix_s, mixt_s, up_s, down_s,
        [
            pltpu.make_async_copy(src, dst, out_sem.at[i])
            for i, (src, dst) in enumerate(
                ((mix_s, mix_hbm), (mixt_s, mixt_hbm), (up_s, up_hbm), (down_s, down_hbm))
            )
        ],
    )


def period(length):
    return 128 // math.gcd(length, 128)


def in_batches(count, first, length, some, step=16):
    again = period(length)
    spots = [(j, (first + j * length) // 128, (first + j * length) % 128) for j in range(again)]

    def body(i, _):
        for j in range(0, again, step):
            some(i * again, i * (again * length // 128), spots[j : j + step])
        return 0

    whole = count // again
    lax.fori_loop(0, whole, body, 0)
    left = count % again
    for j in range(0, left, step):
        some(whole * again, whole * (again * length // 128), spots[j : min(j + step, left)])


def lines_of(flat, lines, first, length, count, group):
    def some(line, row, spots):
        held = []
        for _, top, shift in spots:
            low = flat[pl.ds(row + top, group), :]
            if shift:
                high = flat[pl.ds(row + top + 1, group), :]
                low = pltpu.roll(jnp.where(lane_index(group) >= shift, low, high), 128 - shift, 1)
            held.append(low)
        for (at, _, _), value in zip(spots, held):
            lines[pl.ds(pl.multiple_of((line + at) * group, 8), group), :] = value

    in_batches(count, first, length, some)


def unpack_kernel(sz, flat, lines, norm_ref, mix_ref, mixt_ref, up_ref, down_ref, copies):
    chans, cp, cm, rest, hid, hp = sz.chans, sz.chan_pad, sz.chan_main, sz.rest, sz.hid, sz.hid_pad
    basis, inputs = sz.basis, sz.inputs
    at_disco = 2 * chans
    at_bias = at_disco + chans * basis * inputs
    at_up = at_bias + 3 * chans
    at_down = at_up + (chans + 1) * hid

    def column(start):
        held = window(flat, start, 8)
        full = jnp.concatenate(
            [jnp.broadcast_to(held[s : s + 1], (128, 128)).T for s in range(up_to(cp, 128) // 128)], 0
        )[:cp]
        row = lax.broadcasted_iota(jnp.int32, (cp, 128), 0)
        return jnp.where(row < chans, full, 0.0), row

    for i, start in enumerate((0, chans, at_bias + chans, at_bias + 2 * chans)):
        value, row = column(start)
        norm_ref[i] = jnp.where(row == chans, 1.0, value) if i == 3 else value
    disco_bias, _ = column(at_bias)

    groups = 8
    lines_of(flat, lines, at_disco, inputs, chans * basis, groups)
    stride = basis * groups
    lane = lane_index(chans)
    low = jnp.where(lane == inputs - cm, disco_bias[:chans], 0.0)
    blank = jnp.zeros((cp - cm, 128), BF)

    def clear(ref, size):
        if size < ref.shape[0]:
            ref[size:, :] = jnp.zeros((ref.shape[0] - size, ref.shape[1]), BF)

    def put(ref, lanes, value, size):
        whole = size // 16 * 16
        ref[:whole, lanes] = value[:whole].astype(BF)
        tail = jnp.concatenate(
            [value[whole:size], jnp.zeros((up_to(size, 16) - size, 128), F32)], 0
        )
        ref[whole : up_to(size, 16), lanes] = tail.astype(BF)

    for k in range(basis):
        for s in range(cm // 128):
            value = lines[pl.ds(k * groups + s, chans, stride=stride), :]
            put(mix_ref, slice(k * cm + s * 128, k * cm + s * 128 + 128), value, chans)
        value = lines[pl.ds(k * groups + cm // 128, chans, stride=stride), :]
        value = jnp.where(lane < inputs - cm, value, 0.0)
        low = low + (pltpu.roll(value, k * rest, 1) if k else value)
    put(mix_ref, slice(basis * cm, basis * cm + 128), low, chans)
    clear(mix_ref, up_to(chans, 16))
    copies[0].start()

    for k in range(basis):
        for s in range(cm // 128):
            for r in range(cm // 128):
                block = mix_ref[r * 128 : r * 128 + 128, k * cm + s * 128 : k * cm + s * 128 + 128]
                mixt_ref[s * 128 : s * 128 + 128, k * cm + r * 128 : k * cm + r * 128 + 128] = (
                    block.astype(F32).T.astype(BF)
                )
    for r in range(cm // 128):
        block = low[r * 128 : r * 128 + 128].T
        for k in range(basis):
            mixt_ref[cm:cp, k * cm + r * 128 : k * cm + r * 128 + 128] = block[
                k * rest : (k + 1) * rest
            ].astype(BF)
    for s in range(cm // 128):
        block = jnp.concatenate(
            [
                mix_ref[cm:cp, k * cm + s * 128 : k * cm + s * 128 + 128].astype(F32)
                for k in range(basis)
            ]
            + [jnp.zeros((128 - basis * rest, 128), F32)],
            0,
        )
        mixt_ref[s * 128 : s * 128 + 128, basis * cm : basis * cm + 128] = block.T.astype(BF)
    corner = mix_ref[cm:cp, basis * cm : basis * cm + 128].astype(F32)
    corner = jnp.where(lane_index(cp - cm) % rest == 0, corner, 0.0)
    row = lax.broadcasted_iota(jnp.int32, (cp - cm, 128), 0)
    mixt_ref[cm:cp, basis * cm : basis * cm + 128] = jnp.where(row < chans - cm, corner, 0.0).astype(BF)
    copies[1].start()

    groups = 16
    lines_of(flat, lines, at_up, hid, chans + 1, groups)
    for s in range(up_ref.shape[1] // 128):
        value = lines[pl.ds(s, chans + 1, stride=groups), :]
        keep = hid - s * 128
        if keep < 128:
            value = jnp.where(lane_index(chans + 1) < keep, value, 0.0)
        put(up_ref, slice(s * 128, s * 128 + 128), value, chans + 1)
    clear(up_ref, up_to(chans + 1, 16))
    copies[2].start()
    groups = 8
    lines_of(flat, lines, at_down, chans, hid + 1, groups)
    for s in range(down_ref.shape[1] // 128):
        value = lines[pl.ds(s, hid + 1, stride=groups), :]
        keep = chans - s * 128
        if keep < 128:
            value = jnp.where(lane_index(hid + 1) < keep, value, 0.0)
        put(down_ref, slice(s * 128, s * 128 + 128), value, hid + 1)
    clear(down_ref, up_to(hid + 1, 16))
    copies[3].start()
    for copy in copies:
        copy.wait()


def run_gather(sz, params, x_raw, cot_raw, noise_items, filter_taps, total):
    cp, hp = sz.chan_pad, sz.hid_pad
    own_rows = params.shape[0] // 128
    rows = up_to(own_rows, 16)
    split = rows * 7 // 20 // 16 * 16
    shared = rows - 2 * split
    taps = filter_taps.reshape(sz.rows, -1)
    tap_shape = (up_to(sz.rows + 2, 8), up_to(taps.shape[1], 128))
    heights = total // 4
    items = (sz.steps, sz.chans, sz.cells)
    any_spec = pl.BlockSpec(memory_space=pl.ANY)
    vmem = pl.BlockSpec(memory_space=pltpu.VMEM)
    edges = (2, cp, sz.steps * sz.lons)
    line_rows = max(sz.chans * sz.basis * 8, (sz.chans + 1) * 16, (sz.hid + 1) * 8)
    dma = pltpu.SemaphoreType.DMA
    return pl.pallas_call(
        partial(gather_kernel, sz, (rows, own_rows, shared, split)),
        name="gather",
        out_shape=[
            jax.ShapeDtypeStruct(edges, BF),
            jax.ShapeDtypeStruct(tap_shape, F32),
            jax.ShapeDtypeStruct((4, cp, 128), F32),
            jax.ShapeDtypeStruct((cp, up_to(sz.mix, 128)), BF),
            jax.ShapeDtypeStruct((cp, up_to(sz.mix, 128)), BF),
            jax.ShapeDtypeStruct((cp, up_to(hp, 128)), BF),
            jax.ShapeDtypeStruct((hp, up_to(cp, 128)), BF),
            jax.ShapeDtypeStruct(items, BF),
            jax.ShapeDtypeStruct(items, BF),
        ],
        in_specs=[vmem, any_spec, any_spec, vmem, vmem],
        out_specs=[vmem] * 3 + [any_spec] * 6,
        scratch_shapes=[
            pltpu.VMEM((total, rows, 128), BF),
            pltpu.VMEM((up_to(total * own_rows + 24, 8), 128), F32),
            pltpu.VMEM((line_rows, 128), F32),
            pltpu.VMEM(x_raw.shape, BF),
            pltpu.VMEM(x_raw.shape, BF),
            pltpu.VMEM(items, BF),
            pltpu.VMEM(items, BF),
            pltpu.VMEM(edges, BF),
            pltpu.VMEM(edges, BF),
            pltpu.VMEM((2, 8, tap_shape[1]), F32),
            pltpu.VMEM((2, 8, tap_shape[1]), F32),
            pltpu.VMEM((cp, up_to(sz.mix, 128)), BF),
            pltpu.VMEM((cp, up_to(sz.mix, 128)), BF),
            pltpu.VMEM((cp, up_to(hp, 128)), BF),
            pltpu.VMEM((hp, up_to(cp, 128)), BF),
            dma((2,)),
            dma((heights,)), dma((heights,)),
            dma((heights,)), dma((heights,)),
            dma((2 * heights,)), dma((2 * heights,)),
            dma((4 * heights,)), dma((4 * heights,)),
            dma((2,)), dma((2,)),
            dma((2,)), dma((2,)), dma((4,)), dma((2,)),
        ],
        compiler_params=pltpu.CompilerParams(
            collective_id=1, has_side_effects=True, vmem_limit_bytes=60 * 1024 * 1024
        ),
    )(params.reshape(own_rows, 128), x_raw, cot_raw, noise_items, taps)


def run_block(
    sz, x_items, noise_items, cot_items, taps_ext, live, halo, norms, mix, mixt, up, down
):
    cp, hp = sz.chan_pad, sz.hid_pad
    lons = sz.lons

    live_lanes = jnp.concatenate([jnp.repeat(live, sz.main), jnp.repeat(live, lons)])[None]
    any_spec = pl.BlockSpec(memory_space=pl.ANY)
    vmem = pl.BlockSpec(memory_space=pltpu.VMEM)
    mix_lanes = up_to(sz.mix, 128)
    up_lanes = up_to(hp, 128)
    down_lanes = up_to(cp, 128)
    windows = (sz.rows - 1) // 2
    lon = lons
    flops = 2 * sz.width * (3 * sz.mix * cp + 6 * hp * cp)
    return pl.pallas_call(
        partial(block_kernel, sz),
        name="block",
        out_shape=[
            jax.ShapeDtypeStruct(x_items.shape, BF),
            jax.ShapeDtypeStruct((sz.chans, sz.steps, sz.cells), F32),
            jax.ShapeDtypeStruct((cp, mix_lanes), BF),
            jax.ShapeDtypeStruct((cp, up_lanes), BF),
            jax.ShapeDtypeStruct((hp, down_lanes), BF),
            jax.ShapeDtypeStruct((4, cp, 128), F32),
        ],
        in_specs=[
            any_spec, vmem, any_spec, vmem, pl.BlockSpec(memory_space=pltpu.SMEM), vmem, vmem,
            any_spec, any_spec, any_spec, any_spec,
        ],
        out_specs=[any_spec] * 5 + [vmem],
        scratch_shapes=[
            pltpu.VMEM((cp, sz.width), BF),
            pltpu.VMEM((cp, sz.width), BF),
            pltpu.VMEM((sz.mix, sz.width), BF),
            pltpu.VMEM((cp, sz.width), BF),
            pltpu.VMEM((2 * hp, sz.width), BF),
            pltpu.VMEM((cp, sz.width), BF),
            pltpu.VMEM((sz.steps, sz.chans, sz.cells), F32),
            pltpu.VMEM((4, sz.chans, sz.cells), BF),
            pltpu.VMEM((2, cp, (sz.rows + 3) * lon), BF),
            pltpu.VMEM((windows, 4 * lon, sz.basis * 2 * lon), BF),
            pltpu.VMEM((8 * lon, sz.basis * 2 * lon), BF),
            pltpu.VMEM((2, cp, sz.steps * lon), BF),
            pltpu.VMEM((cp, mix_lanes), BF),
            pltpu.VMEM((cp, up_lanes), BF),
            pltpu.VMEM((hp, down_lanes), BF),
            pltpu.SemaphoreType.DMA((2, 2)),
            pltpu.SemaphoreType.DMA((4,)),
            pltpu.SemaphoreType.DMA((2, sz.steps)),
            pltpu.SemaphoreType.DMA((2,)),
            pltpu.SemaphoreType.DMA((2,)),
        ],
        compiler_params=pltpu.CompilerParams(
            collective_id=0, has_side_effects=True, vmem_limit_bytes=63 * 1024 * 1024
        ),
        cost_estimate=pl.CostEstimate(flops=flops, bytes_accessed=40_000_000, transcendentals=0),
    )(x_items, noise_items, cot_items, halo, taps_ext, live_lanes, norms, mix, mixt, up, down)


def merge(old, shift, length, value, rows):
    lane = lane_index(rows)
    place = lax.broadcasted_iota(jnp.int32, (rows, 128), 0) * 128 + lane
    if shift:
        moved = pltpu.roll(value, shift, 1)
        value = jnp.where(lane >= shift, moved, pltpu.roll(moved, 1, 0))
    return jnp.where((place >= shift) & (place < shift + length), value, old)


def flatten_lines(flat, lines, first, length, count, group):
    for odd in range(2):

        def some(line, row, spots, odd=odd):
            spots = [spot for spot in spots if spot[0] % 2 == odd]
            held = []
            for at, top, shift in spots:
                value = lines[pl.ds(pl.multiple_of((line + at) * group, 8), group), :]
                held.append(merge(flat[pl.ds(row + top, group), :], shift, length, value, group))
            for (_, top, _), value in zip(spots, held):
                flat[pl.ds(row + top, group), :] = value

        in_batches(count, first, length, some, 32)


def pack_kernel(sz, dmix_ref, dup_ref, ddown_ref, dnorm_ref, flat, lines, copies, ready):
    chans, cp, cm, rest, hid = sz.chans, sz.chan_pad, sz.chan_main, sz.rest, sz.hid
    basis, inputs = sz.basis, sz.inputs
    at_disco = 2 * chans
    at_bias = at_disco + chans * basis * inputs
    at_up = at_bias + 3 * chans
    at_down = at_up + (chans + 1) * hid
    used = at_down + (hid + 1) * chans

    def across(columns, pick):
        parts = []
        for s in range(8):
            size = min(128, cp - s * 128)
            if size <= 0:
                parts.append(jnp.zeros((1, 128), F32))
                continue
            block = columns[s * 128 : s * 128 + size]
            if size < 128:
                block = jnp.concatenate([block, jnp.zeros((128 - size, 128), F32)], 0)
            parts.append(pick(block.T))
        return jnp.concatenate(parts, 0)

    def total(block):
        return jnp.sum(block, 0, keepdims=True)

    begin = used // 128
    flat[begin:, :] = jnp.zeros((flat.shape[0] - begin, 128), F32)
    spots = (0, chans, at_bias + chans, at_bias + 2 * chans)
    pieces = [(start, across(dnorm_ref[i], total)) for i, start in enumerate(spots)]
    copies[0].wait()
    low = dmix_ref[:, basis * cm : basis * cm + 128].astype(F32)
    bias_row = inputs - cm
    pieces.append((at_bias, across(low, lambda block: block[bias_row : bias_row + 1])))
    for start, value in pieces:
        rows = pl.ds(start // 128, 8)
        flat[rows, :] = merge(flat[rows, :], start % 128, chans, value, 8)

    groups = 8
    stride = basis * groups
    for k in range(basis):
        for s in range(cm // 128):
            value = dmix_ref[:, k * cm + s * 128 : k * cm + s * 128 + 128].astype(F32)
            lines[pl.ds(k * groups + s, chans, stride=stride), :] = value[:chans]
        value = pltpu.roll(low, 128 - k * rest, 1) if k else low
        lines[pl.ds(k * groups + cm // 128, chans, stride=stride), :] = value[:chans]
    flatten_lines(flat, lines, at_disco, inputs, chans * basis, groups)
    ready(at_bias // 128)

    groups = 16
    copies[1].wait()
    for s in range(up_to(hid, 128) // 128):
        value = dup_ref[:, s * 128 : s * 128 + 128].astype(F32)
        lines[pl.ds(s, chans + 1, stride=groups), :] = value[: chans + 1]
    flatten_lines(flat, lines, at_up, hid, chans + 1, groups)
    ready(at_down // 128)

    groups = 8
    copies[2].wait()
    for s in range(up_to(chans, 128) // 128):
        value = ddown_ref[:, s * 128 : s * 128 + 128].astype(F32)
        lines[pl.ds(s, hid + 1, stride=groups), :] = value[: hid + 1]
    flatten_lines(flat, lines, at_down, chans, hid + 1, groups)
    ready(flat.shape[0])


def reduce_kernel(
    sz, parts, dmix_hbm, dup_hbm, ddown_hbm, dnorm_ref, out_ref,
    flat, lines, dmix_s, dup_s, ddown_s, sums, beside_s, beside_r, over_s, over_r, xa_s, xa_r, xb_s, xb_r,
    za_s, za_r, zb_s, zb_r, fa_s, fa_r, fb_r,
    in_sem, c_send, c_recv, y_send, y_recv, x_send, x_recv, z_send, z_recv, f_send, f_recv,
):
    rows, own_rows, shared, split = parts
    wide = lax.axis_index("wide")
    lat = lax.axis_index("lat")
    total = lax.axis_size("wide")
    heights = total // 4
    core = wide % 2
    side = (wide // 2) % 2
    height = wide // 4
    half = lat % 2
    mate = lat + 1 - 2 * half

    bits = heights.bit_length() - 1

    def spot(mask, s, c):
        return 4 * flip(height, mask) + 2 * s + c

    held = (dmix_s, dup_s, ddown_s)
    copies = [
        pltpu.make_async_copy(src, dst, in_sem.at[i])
        for i, (src, dst) in enumerate(zip((dmix_hbm, dup_hbm, ddown_hbm), held))
    ]
    for item in copies:
        item.start()
    barrier = pltpu.get_barrier_semaphore()

    def hello(w, l):
        pl.semaphore_signal(barrier, inc=1, device_id=(w, l), device_id_type=MESH)

    for bit in range(bits):
        hello(spot(1 << bit, side, core), lat)
    hello(spot(0, 1 - side, core), lat)
    hello(spot(0, side, 1 - core), lat)
    hello(wide, mate)
    shares = pl.ds(split, shared)
    lead = pl.ds(pl.multiple_of(half * (split + shared), 16), split)
    other = pl.ds(pl.multiple_of((1 - half) * (split + shared), 16), split)
    masks = list(reversed(range(heights)))
    columns = [(mask, 1 - side) for mask in masks] + [(mask, side) for mask in masks]
    started = []

    def copy(src, dst, send, recv, to_wide, to_lat):
        return pltpu.make_async_remote_copy(
            src_ref=src, dst_ref=dst, send_sem=send, recv_sem=recv,
            device_id=(to_wide, to_lat), device_id_type=MESH,
        )

    def go(message):
        message.start()
        started.append(message)

    def to_core(j):
        return copy(beside_s.at[j], beside_r.at[j], c_send.at[j], c_recv.at[j], spot(0, side, 1 - core), lat)

    def to_mate(j):
        return copy(over_s.at[j], over_r.at[j], y_send.at[j], y_recv.at[j], wide, mate)

    def to_side(src, dst, j, part):
        return copy(src.at[j], dst.at[j], x_send.at[j, part], x_recv.at[j, part], spot(0, 1 - side, core), lat)

    def to_height(src, dst, mask, part):
        return copy(
            src.at[mask - 1], dst.at[mask - 1], z_send.at[mask - 1, part], z_recv.at[mask - 1, part],
            spot(mask & -mask, side, core), lat,
        )

    def add_heights(src, dst, mask, part, j, where):
        for bit in range(low_bit(mask, bits)):
            sender = mask | 1 << bit
            to_height(src, dst, sender, part).wait_recv()
            sums[j, where] += dst[sender - 1].astype(F32)

    next_pair = [0]

    def ready(limit):
        if next_pair[0] == 0:
            pl.semaphore_wait(barrier, bits + 3)
        while next_pair[0] < 2 * heights:
            two = next_pair[0]
            if (2 * two + 1) * own_rows + rows > limit:
                break
            away = 2 * two + 1 - core
            beside_s[two] = flat[pl.ds(away * own_rows, rows), :].astype(BF)
            go(to_core(two))
            next_pair[0] = two + 1

    pack_kernel(sz, *held, dnorm_ref, flat, lines, copies, ready)
    for j, (mask, s) in enumerate(columns):
        mine = spot(mask, s, core)
        two = mine // 2
        to_core(two).wait_recv()
        sums[j] = flat[pl.ds(mine * own_rows, rows), :] + beside_r[two].astype(F32)
        over_s[j] = sums[j, other].astype(BF)
        go(to_mate(j))
        if j < heights:
            xa_s[j] = sums[j, shares].astype(BF)
            go(to_side(xa_s, xa_r, j, 0))
    for i, mask in enumerate(masks):
        to_mate(i).wait_recv()
        xb_s[i] = (sums[i, lead] + over_r[i].astype(F32)).astype(BF)
        go(to_side(xb_s, xb_r, i, 1))
        j = heights + i
        to_side(xa_s, xa_r, i, 0).wait_recv()
        sums[j, shares] += xa_r[i].astype(F32)
        add_heights(za_s, za_r, mask, 0, j, shares)
        if mask:
            za_s[mask - 1] = sums[j, shares].astype(BF)
            go(to_height(za_s, za_r, mask, 0))
    own = 2 * heights - 1
    fa_s[...] = sums[own, shares].astype(BF)
    last = [
        copy(fa_s, fa_r, f_send.at[0], f_recv.at[0], wide, mate),
        copy(sums.at[own, lead], fb_r, f_send.at[1], f_recv.at[1], wide, mate),
    ]
    go(last[0])
    for i, mask in enumerate(masks):
        j = heights + i
        to_mate(j).wait_recv()
        to_side(xb_s, xb_r, i, 1).wait_recv()
        sums[j, lead] += over_r[j].astype(F32) + xb_r[i].astype(F32)
        add_heights(zb_s, zb_r, mask, 1, j, lead)
        if mask:
            zb_s[mask - 1] = sums[j, lead].astype(BF)
            go(to_height(zb_s, zb_r, mask, 1))
    go(last[1])
    last[0].wait_recv()
    out_ref[shares, :] = fa_s[...].astype(F32) + fa_r[...].astype(F32)
    last[1].wait_recv()
    low, high = sums[own, lead], fb_r[...]
    first = jnp.where(half == 0, low, high)
    second = jnp.where(half == 0, high, low)
    out_ref[:split, :] = first
    out_ref[split + shared :, :] = second[: own_rows - split - shared]
    for message in started:
        message.wait_send()


def run_reduce(sz, own_rows, total, dmix, dup, ddown, dnorm):
    rows = up_to(own_rows, 16)
    split = rows // 4 // 16 * 16
    shared = rows - 2 * split
    heights = total // 4
    vmem = pl.BlockSpec(memory_space=pltpu.VMEM)
    line_rows = max(sz.chans * sz.basis * 8, (sz.chans + 1) * 16, (sz.hid + 1) * 8)
    dma = pltpu.SemaphoreType.DMA
    flat_rows = up_to((total - 1) * own_rows + rows, 8) + 16
    return pl.pallas_call(
        partial(reduce_kernel, sz, (rows, own_rows, shared, split)),
        name="reduce",
        out_shape=jax.ShapeDtypeStruct((own_rows, 128), F32),
        in_specs=[pl.BlockSpec(memory_space=pl.ANY)] * 3 + [vmem],
        out_specs=vmem,
        scratch_shapes=[
            pltpu.VMEM((flat_rows, 128), F32),
            pltpu.VMEM((line_rows, 128), F32),
            pltpu.VMEM(dmix.shape, BF),
            pltpu.VMEM(dup.shape, BF),
            pltpu.VMEM(ddown.shape, BF),
            pltpu.VMEM((2 * heights, rows, 128), F32),
            pltpu.VMEM((2 * heights, rows, 128), BF),
            pltpu.VMEM((2 * heights, rows, 128), BF),
            pltpu.VMEM((2 * heights, split, 128), BF),
            pltpu.VMEM((2 * heights, split, 128), BF),
            pltpu.VMEM((heights, shared, 128), BF),
            pltpu.VMEM((heights, shared, 128), BF),
            pltpu.VMEM((heights, split, 128), BF),
            pltpu.VMEM((heights, split, 128), BF),
            pltpu.VMEM((heights, shared, 128), BF),
            pltpu.VMEM((heights, shared, 128), BF),
            pltpu.VMEM((heights, split, 128), BF),
            pltpu.VMEM((heights, split, 128), BF),
            pltpu.VMEM((shared, 128), BF),
            pltpu.VMEM((shared, 128), BF),
            pltpu.VMEM((split, 128), F32),
            dma((3,)),
            dma((2 * heights,)), dma((2 * heights,)),
            dma((2 * heights,)), dma((2 * heights,)),
            dma((heights, 2)), dma((heights, 2)),
            dma((heights, 2)), dma((heights, 2)),
            dma((2,)), dma((2,)),
        ],
        compiler_params=pltpu.CompilerParams(
            collective_id=2, has_side_effects=True, vmem_limit_bytes=62 * 1024 * 1024
        ),
    )(dmix, dup, ddown, dnorm)


def shards(block_input, noise_fields, filter_taps, rollout, cotangent, params):
    sz = Sizes(block_input, noise_fields, filter_taps)
    chans = sz.chans
    dates, step_total = block_input.shape[:2]
    step_ids = jnp.arange(step_total, dtype=jnp.int32)
    live = (step_ids[None, :] < rollout[:, None]).astype(F32).reshape(sz.steps)
    noise_items = noise_fields.reshape(sz.steps, sz.noise, sz.cells)

    def by_channel(fields):
        return jnp.transpose(fields, (2, 0, 1, 3)).reshape(chans, sz.steps, sz.cells)

    halo, taps_ext, norms, mix, mixt, up, down, x_items, cot_items = run_gather(
        sz,
        params,
        by_channel(block_input),
        by_channel(cotangent),
        noise_items,
        filter_taps,
        lax.axis_size("wide"),
    )
    out, grad, dmix, dup, ddown, dnorm = run_block(
        sz,
        x_items,
        noise_items,
        cot_items,
        taps_ext,
        live,
        halo,
        norms,
        mix,
        mixt,
        up,
        down,
    )
    own = run_reduce(sz, params.shape[0] // 128, lax.axis_size("wide"), dmix, dup, ddown, dnorm)
    param_grad = own.reshape(params.shape)
    return (out.reshape(block_input.shape), jnp.transpose(grad, (1, 0, 2)).reshape(block_input.shape), param_grad)


def solution(mesh):
    in_specs = (
        P("wide", None, None, "lat"),
        P("wide", None, None, "lat"),
        P("lat", None, None, None),
        P("wide"),
        P("wide", None, None, "lat"),
        P("wide"),
    )
    out_specs = (P("wide", None, None, "lat"), P("wide", None, None, "lat"), P("wide"))
    return jax.shard_map(shards, mesh=mesh, in_specs=in_specs, out_specs=out_specs, check_vma=False)
```

```python
import math
from functools import partial

import jax
import jax.numpy as jnp
from jax import lax
from jax.experimental import pallas as pl
from jax.experimental.pallas import tpu as pltpu
from jax.sharding import PartitionSpec as P

HID = 1282
BF = jnp.bfloat16
F32 = jnp.float32
EPS = 1e-05
NEAR = 256
MESH = pl.DeviceIdType.MESH


def up_to(size, unit):
    return -(-size // unit) * unit


def mm(left, right, dims=(1, 0)):
    return lax.dot_general(
        left, right, (((dims[0],), (dims[1],)), ((), ())), preferred_element_type=F32
    )


class Sizes:
    def __init__(self, block_input, noise_fields, filter_taps):
        self.steps = block_input.shape[0] * block_input.shape[1]
        self.chans = block_input.shape[2]
        self.noise = noise_fields.shape[2]
        self.inputs = self.chans + self.noise
        self.rows = filter_taps.shape[0]
        self.basis = filter_taps.shape[1]
        self.taps = filter_taps.shape[3]
        self.cells = block_input.shape[3]
        self.lons = self.cells // self.rows
        self.chan_pad = up_to(self.inputs + 1, 16)
        self.chan_main = self.chans // 128 * 128
        self.rest = self.chan_pad - self.chan_main
        self.hid = HID
        self.hid_pad = up_to(HID + 1, 16)
        self.mix = self.basis * self.chan_pad
        self.main = (self.rows - 1) * self.lons
        self.width = self.steps * self.cells
        self.tail = self.steps * self.main


def block_kernel(
    sz, x_hbm, noise_ref, cot_hbm, halo_ref, taps_ref, live_ref, norm_ref, mix_hbm, mixt_hbm,
    up_hbm, down_hbm, out_hbm, grad_hbm, dmix_hbm, dup_hbm, ddown_hbm, dnorm_ref,
    xs, gs, basis_s, normed_s, act_s, gd_s, grad_s, stage, noisy_s, filt_s, filt_e,
    edge_s, mix_s, up_s, down_s,
    in_sem, w_sem, out_sem, send_sem, recv_sem,
):
    chans, cp, cm, rest = sz.chans, sz.chan_pad, sz.chan_main, sz.rest
    hp, lons, main, tail = sz.hid_pad, sz.lons, sz.main, sz.tail
    pair = 2 * lons
    lat = lax.axis_index("lat")
    lat_count = lax.axis_size("lat")
    has_up = lat > 0
    has_down = lat < lat_count - 1

    def fetch(step, slot):
        return (
            pltpu.make_async_copy(x_hbm.at[step], stage.at[slot], in_sem.at[slot, 0]),
            pltpu.make_async_copy(cot_hbm.at[step], stage.at[2 + slot], in_sem.at[slot, 1]),
        )

    for step in range(2):
        for copy in fetch(step, step):
            copy.start()
    weights = [
        pltpu.make_async_copy(src, dst, w_sem.at[i])
        for i, (src, dst) in enumerate(((mix_hbm, mix_s), (up_hbm, up_s), (down_hbm, down_s)))
    ]
    for copy in weights:
        copy.start()
    mixt_s = normed_s.at[:, pl.ds(0, mixt_hbm.shape[1])]
    mixt_copy = pltpu.make_async_copy(mixt_hbm, mixt_s, w_sem.at[3])

    row_in = lax.broadcasted_iota(jnp.int32, (lons, pair), 0)
    lane = lax.broadcasted_iota(jnp.int32, (lons, pair), 1)
    lane_in = lane % lons
    left_half = lane < lons
    half_taps = sz.taps // 2
    circ = []
    circ_t = []
    for t in range(sz.taps):
        circ.append(row_in == (lane_in + (t - half_taps + lons)) % lons)
        circ_t.append(lane_in == (row_in + (t - half_taps + lons)) % lons)
    def tap_block(ext_row_a, a_a, ext_row_b, a_b, k, masks):
        block = jnp.zeros((lons, pair), F32)
        for t in range(sz.taps):
            va = F32(0) if a_a is None else taps_ref[ext_row_a, (k * 3 + a_a) * sz.taps + t]
            vb = F32(0) if a_b is None else taps_ref[ext_row_b, (k * 3 + a_b) * sz.taps + t]
            block = jnp.where(masks[t], jnp.where(left_half, va, vb), block)
        return block.astype(BF)

    def inside(a):
        return a if 0 <= a <= 2 else None

    windows = (sz.rows - 1) // 2
    last = sz.rows - 1

    def build_filters(backward):
        def build(index, _):
            m = index // sz.basis
            k = index % sz.basis
            cols = pl.ds(pl.multiple_of(k * pair, pair), pair)
            for ri in range(4):
                if backward:
                    block = tap_block(
                        2 * m + ri, inside(2 - ri), 2 * m + ri, inside(3 - ri), k, circ_t
                    )
                else:
                    block = tap_block(
                        2 * m + 1, inside(ri), 2 * m + 2, inside(ri - 1), k, circ
                    )
                filt_s[m, pl.ds(ri * lons, lons), cols] = block
            return 0

        def build_last(k, _):
            cols = pl.ds(pl.multiple_of(k * pair, pair), pair)
            for ri in range(4):
                ext = min(last + ri, last + 2) if backward else last + 1
                a = inside(2 - ri) if backward else inside(ri)
                masks = circ_t if backward else circ
                for odd in range(2):
                    filt_e[pl.ds((odd * 4 + ri) * lons, lons), cols] = tap_block(
                        ext, None if odd else a, ext, a if odd else None, k, masks
                    )
            return 0

        lax.fori_loop(0, windows * sz.basis, build, 0)
        lax.fori_loop(0, sz.basis, build_last, 0)

    build_filters(False)

    gain_one, bias_one = norm_ref[0], norm_ref[1]
    gain_two, bias_two = norm_ref[2], norm_ref[3]

    def wide(vec, lanes):
        if lanes <= 128:
            return vec[:, :lanes]
        return jnp.concatenate([vec] * (lanes // 128) + ([vec[:, : lanes % 128]] if lanes % 128 else []), 1)

    def stats(values):
        centre = jnp.sum(values, 0, keepdims=True) * (1.0 / chans)
        shifted = values - centre
        spread = jnp.sum(jnp.square(shifted), 0, keepdims=True) * (1.0 / chans)
        return shifted, lax.rsqrt(spread + EPS)

    def norm_one(values, lanes):
        shifted, inv = stats(values)
        return shifted * inv * wide(gain_one[:chans], lanes) + wide(bias_one[:chans], lanes)

    halos = []
    for side, there in ((0, has_up), (1, has_down)):
        fields = halo_ref[side].astype(F32)
        width = fields.shape[1]
        normed = norm_one(fields[:chans], width)
        noise = fields[chans : sz.inputs]
        full = jnp.concatenate(
            [normed, noise, jnp.zeros((cp - sz.inputs, width), F32)], 0
        )
        edge_s[side] = jnp.where(there, full, 0.0).astype(BF)

    def halo_part(source, step):
        return source[:, step * lons : (step + 1) * lons]

    ones_row = (lax.broadcasted_iota(jnp.int32, (rest, pair), 0) == sz.inputs - cm).astype(F32)

    def run_filter(slot, store):
        for m in range(windows):
            window = noisy_s[slot, :, m * pair : m * pair + 2 * pair]
            result = mm(window, filt_s[m])
            for k in range(sz.basis):
                store(m, k, result[:, k * pair : (k + 1) * pair])

    def run_last(store):
        window = jnp.concatenate(
            [noisy_s[slot, :, windows * pair : windows * pair + 2 * pair] for slot in range(2)], 1
        )
        result = mm(window, filt_e[...])
        for k in range(sz.basis):
            store(k, result[:, k * pair : (k + 1) * pair])

    def put_basis(lanes, k, part, ones):
        basis_s[k * cm : (k + 1) * cm, lanes] = part[:cm].astype(BF)
        low = part[cm:]
        if ones and k == 0:
            low = low + ones_row
        start = sz.basis * cm + k * rest
        basis_s[start : start + rest, lanes] = low.astype(BF)

    zero_lanes = jnp.zeros((cp, lons), BF)
    pad_rows = jnp.zeros((cp - chans, sz.cells), F32)
    pad_pair = jnp.zeros((cp - chans, pair), F32)
    pairs = sz.steps // 2

    def prepare(two, _):
        both = pl.ds(pl.multiple_of(tail + two * pair, pair), pair)
        near = pl.ds(pl.multiple_of(two * pair, pair), pair)
        for slot in range(2):
            step = 2 * two + slot
            for copy in fetch(step, slot):
                copy.wait()
            fields = stage[slot].astype(F32)
            normed = norm_one(fields, sz.cells)
            noise = noise_ref[step].astype(F32)
            own = jnp.concatenate(
                [normed, noise, jnp.zeros((cp - sz.inputs, sz.cells), F32)], 0
            ).astype(BF)
            noisy_s[slot] = jnp.concatenate(
                [
                    halo_part(edge_s[0, :, near], slot),
                    own,
                    halo_part(edge_s[1, :, near], slot),
                    zero_lanes,
                ],
                1,
            )
            lanes = pl.ds(pl.multiple_of(step * main, main), main)
            xs[:, lanes] = jnp.concatenate([fields, pad_rows], 0)[:, :main].astype(BF)
            masked = jnp.concatenate([stage[2 + slot].astype(F32), pad_rows], 0)[:, :main]
            gs[:, lanes] = (masked * live_ref[:, lanes]).astype(BF)

            def keep(m, k, part, step=step):
                start = pl.multiple_of(step * main + m * pair, pair)
                put_basis(pl.ds(start, pair), k, part, True)

            run_filter(slot, keep)
        x_tail = jnp.concatenate([stage[s, :, main:] for s in range(2)], 1).astype(F32)
        xs[:, both] = jnp.concatenate([x_tail, pad_pair], 0).astype(BF)
        g_tail = jnp.concatenate([stage[2 + s, :, main:] for s in range(2)], 1).astype(F32)
        g_tail = jnp.concatenate([g_tail, pad_pair], 0)
        gs[:, both] = (g_tail * live_ref[:, both]).astype(BF)
        run_last(lambda k, part: put_basis(both, k, part, True))

        @pl.when(two + 1 < pairs)
        def _():
            for slot in range(2):
                for copy in fetch(2 * two + 2 + slot, slot):
                    copy.start()

        return 0

    lax.fori_loop(0, pairs, prepare, 0)
    barrier = pltpu.get_barrier_semaphore()

    @pl.when(has_up)
    def _():
        pl.semaphore_signal(barrier, inc=1, device_id={"lat": lat - 1}, device_id_type=MESH)

    @pl.when(has_down)
    def _():
        pl.semaphore_signal(barrier, inc=1, device_id={"lat": lat + 1}, device_id_type=MESH)

    for copy in weights:
        copy.wait()
    dnorm_ref[...] = jnp.zeros_like(dnorm_ref)

    def fold(values):
        total = values[:, :128]
        for i in range(1, values.shape[1] // 128):
            total = total + values[:, i * 128 : (i + 1) * 128]
        return total

    chunks = sz.width // NEAR
    per_step = main // NEAR
    tail_chunk = tail // NEAR
    steps_per_tail = NEAR // lons

    def main_lanes(chunk):
        return pl.ds(pl.multiple_of((chunk % per_step) * NEAR, NEAR), NEAR)

    def put_tail(chunk, put):
        @pl.when(chunk >= tail_chunk)
        def _():
            for part in range(steps_per_tail):
                put(
                    (chunk - tail_chunk) * steps_per_tail + part,
                    pl.ds(main, lons),
                    slice(part * lons, (part + 1) * lons),
                )

    def out_copy(step):
        return pltpu.make_async_copy(stage.at[step], out_hbm.at[step], out_sem.at[0, step])

    def grad_copy(step):
        return pltpu.make_async_copy(grad_s.at[step], grad_hbm.at[:, step, :], out_sem.at[1, step])

    def lanes_of(chunk):
        return pl.ds(pl.multiple_of(chunk * NEAR, NEAR), NEAR)

    def order(index):
        return lax.rem(jnp.minimum(index, chunks - 1) + tail_chunk, chunks)

    def forward_first(chunk):
        lanes = lanes_of(chunk)
        residual = xs[:, lanes].astype(F32) + mm(mix_s[:, : sz.mix], basis_s[:, lanes])
        centre = jnp.sum(residual[:chans], 0, keepdims=True) * (1.0 / chans)
        shifted = residual - centre
        spread = jnp.sum(jnp.square(shifted[:chans]), 0, keepdims=True) * (1.0 / chans)
        inv = lax.rsqrt(spread + EPS)
        hat = shifted * inv
        normed_s[:, lanes] = (hat * wide(gain_two, NEAR) + wide(bias_two, NEAR)).astype(BF)
        return residual, centre, inv

    def forward_chunk(index, held):
        residual, centre, inv = held
        chunk = order(index)
        lanes = lanes_of(chunk)
        grad_low = gs[:, lanes]
        pre = mm(up_s[:, :hp], normed_s[:, lanes], (0, 0))
        grad_hidden = mm(down_s[:, :cp], grad_low)
        phi = 0.5 + 0.5 * lax.erf(pre * 0.7071067811865476)
        density = jnp.exp(pre * pre * -0.5) * 0.3989422804014327
        hidden = pre * phi
        grad_pre = (grad_hidden * (phi + pre * density)).astype(BF)
        low_rows = hp - HID // 16 * 16
        low = lax.broadcasted_iota(jnp.int32, (low_rows, NEAR), 0) == HID - (hp - low_rows)
        hidden = jnp.concatenate(
            [hidden[: hp - low_rows], jnp.where(low, 1.0, hidden[hp - low_rows :])], 0
        ).astype(BF)
        act_s[:hp, lanes] = hidden
        act_s[hp:, lanes] = grad_pre
        branch = mm(down_s[:, :cp], hidden, (0, 0))
        output = ((residual + branch)[:chans] * live_ref[:, lanes]).astype(BF)
        hat = (residual - centre) * inv
        grad_normed = mm(up_s[:, :hp], grad_pre)
        ahead = forward_first(order(index + 1))
        dnorm_ref[2] += fold(grad_normed * hat)
        dnorm_ref[3] += fold(grad_normed)
        scaled = grad_normed * wide(gain_two, NEAR)
        mean_one = jnp.sum(scaled[:chans], 0, keepdims=True) * (1.0 / chans)
        mean_two = jnp.sum((scaled * hat)[:chans], 0, keepdims=True) * (1.0 / chans)
        grad_resid = grad_low.astype(F32) + inv * (scaled - mean_one - hat * mean_two)
        gd_s[:, lanes] = grad_resid.astype(BF)

        def put(step, where, part):
            stage[step, :, where] = output[:, part]
            grad_s[step, :, where] = grad_resid[:chans, part]

        put(jnp.minimum(chunk // per_step, sz.steps - 1), main_lanes(chunk), slice(0, NEAR))
        put_tail(chunk, put)

        @pl.when((chunk < tail_chunk) & (lax.rem(chunk, per_step) == per_step - 1))
        def _():
            out_copy(chunk // per_step).start()

        return ahead

    lax.fori_loop(0, chunks, forward_chunk, forward_first(order(0)))

    rim = pl.ds(0, sz.steps * lons)
    noisy_s[0, :, rim] = jnp.concatenate(
        [gd_s[:, step * main : step * main + lons] for step in range(sz.steps)], 1
    )
    noisy_s[1, :, rim] = gd_s[:, tail:]
    pl.semaphore_wait(barrier, has_up.astype(jnp.int32) + has_down.astype(jnp.int32))

    def send(side, to):
        return pltpu.make_async_remote_copy(
            src_ref=noisy_s.at[side, :, rim],
            dst_ref=edge_s.at[1 - side],
            send_sem=send_sem.at[side],
            recv_sem=recv_sem.at[1 - side],
            device_id={"lat": to},
            device_id_type=MESH,
        )

    @pl.when(has_up)
    def _():
        send(0, lat - 1).start()

    @pl.when(has_down)
    def _():
        send(1, lat + 1).start()

    def blocks(total, size):
        return [(i, min(size, total - i)) for i in range(0, total, size)]

    for start, size in blocks(hp, 512):
        up_s[:, start : start + size] = mm(
            normed_s[...], act_s[hp + start : hp + start + size, :], (1, 1)
        ).astype(BF)
    dup_copy = pltpu.make_async_copy(up_s, dup_hbm, w_sem.at[1])
    dup_copy.start()
    mixt_copy.start()
    for start, size in blocks(hp, 432):
        rows = pl.ds(start, size)
        down_s[rows, :cp] = mm(act_s[rows, :], gs[...], (1, 1)).astype(BF)
    ddown_copy = pltpu.make_async_copy(down_s, ddown_hbm, w_sem.at[2])
    ddown_copy.start()
    for start, size in blocks(sz.mix, 512):
        mix_s[:, start : start + size] = mm(
            gd_s[...], basis_s[start : start + size, :], (1, 1)
        ).astype(BF)
    dmix_copy = pltpu.make_async_copy(mix_s, dmix_hbm, w_sem.at[0])
    dmix_copy.start()

    build_filters(True)

    @pl.when(has_up)
    def _():
        send(0, lat - 1).wait_send()
        send(1, lat - 1).wait_recv()

    @pl.when(has_down)
    def _():
        send(1, lat + 1).wait_send()
        send(0, lat + 1).wait_recv()

    def adjoint(two, _):
        both = pl.ds(pl.multiple_of(tail + two * pair, pair), pair)
        near = pl.ds(pl.multiple_of(two * pair, pair), pair)
        for slot in range(2):
            step = 2 * two + slot
            noisy_s[slot] = jnp.concatenate(
                [
                    halo_part(edge_s[0, :, near], slot),
                    gd_s[:, pl.ds(pl.multiple_of(step * main, main), main)],
                    halo_part(gd_s[:, both], slot),
                    halo_part(edge_s[1, :, near], slot),
                    zero_lanes,
                ],
                1,
            )

            def keep_grad(m, k, part, step=step):
                start = pl.multiple_of(step * main + m * pair, pair)
                put_basis(pl.ds(start, pair), k, part, False)

            run_filter(slot, keep_grad)
        run_last(lambda k, part: put_basis(both, k, part, False))
        return 0

    lax.fori_loop(0, pairs, adjoint, 0)
    mixt_copy.wait()

    def mixed_back(index):
        return mm(normed_s[:, : sz.mix], basis_s[:, lanes_of(order(index))])[:chans]

    def backward_chunk(index, _):
        chunk = order(index)
        lanes = lanes_of(chunk)
        grad_first = mixed_back(index)
        shifted, inv = stats(xs[:, lanes].astype(F32)[:chans])
        hat = shifted * inv
        dnorm_ref[0, :chans] += fold(grad_first * hat)
        dnorm_ref[1, :chans] += fold(grad_first)
        scaled = grad_first * wide(gain_one[:chans], NEAR)
        mean_one = jnp.sum(scaled, 0, keepdims=True) * (1.0 / chans)
        mean_two = jnp.sum(scaled * hat, 0, keepdims=True) * (1.0 / chans)
        added = inv * (scaled - mean_one - hat * mean_two)

        def put_grad(step, where, part):
            grad_s[step, :, where] += added[:, part]

        @pl.when(chunk < tail_chunk)
        def _():
            put_grad(chunk // per_step, main_lanes(chunk), slice(0, NEAR))

        put_tail(chunk, put_grad)

        @pl.when((chunk < tail_chunk) & (lax.rem(chunk, per_step) == per_step - 1))
        def _():
            grad_copy(chunk // per_step).start()

        return 0

    lax.fori_loop(0, chunks, backward_chunk, 0)
    for step in range(sz.steps):
        out_copy(step).wait()
        grad_copy(step).wait()
    for copy in (ddown_copy, dup_copy, dmix_copy):
        copy.wait()


def flip(index, mask):
    for bit in range(mask.bit_length()):
        if mask >> bit & 1:
            index = index + (1 << bit) * (1 - 2 * (index // (1 << bit) % 2))
    return index


def low_bit(mask, bits):
    return (mask & -mask).bit_length() - 1 if mask else bits


def lane_index(rows):
    return lax.broadcasted_iota(jnp.int32, (rows, 128), 1)


def window(flat, start, rows):
    first = start >> 7
    shift = start & 127
    low = flat[pl.ds(first, rows), :]
    high = flat[pl.ds(first + 1, rows), :]
    mixed = jnp.where(lane_index(rows) >= shift, low, high)
    return pltpu.roll(mixed, (128 - shift) & 127, 1)


def gather_kernel(
    sz, parts, params_ref, x_hbm, cot_hbm, noise_ref, taps_ref,
    halo_ref, tap_ref, norm_ref, mix_hbm, mixt_hbm, up_hbm, down_hbm, x_out, cot_out,
    got, flat, lines, x_raw, cot_raw, x_s, cot_s, rim_s, edge_s, tap_s, tap_r, mix_s, mixt_s, up_s, down_s,
    in_sem, z_send, z_recv, x_send, x_recv, y_send, y_recv, c_send, c_recv, e_send, e_recv,
    t_send, t_recv, out_sem, turn_sem,
):
    chans, cp, cm, rest, lons = sz.chans, sz.chan_pad, sz.chan_main, sz.rest, sz.lons
    rows, own_rows, shared, split = parts
    wide = lax.axis_index("wide")
    lat = lax.axis_index("lat")
    lat_count = lax.axis_size("lat")
    total = lax.axis_size("wide")
    heights = total // 4
    core = wide % 2
    side = (wide // 2) % 2
    height = wide // 4
    half = lat % 2
    has_up = lat > 0
    has_down = lat < lat_count - 1

    bits = heights.bit_length() - 1

    def spot(mask, s, c):
        return 4 * flip(height, mask) + 2 * s + c

    raw_copies = [
        pltpu.make_async_copy(x_hbm, x_raw, in_sem.at[0]),
        pltpu.make_async_copy(cot_hbm, cot_raw, in_sem.at[1]),
    ]
    for copy in raw_copies:
        copy.start()
    got[wide, :own_rows] = params_ref[...]

    barrier = pltpu.get_barrier_semaphore()

    def hello(w, l):
        pl.semaphore_signal(barrier, inc=1, device_id=(w, l), device_id_type=MESH)

    for bit in range(bits):
        hello(spot(1 << bit, side, core), lat)
    hello(spot(0, 1 - side, core), lat)
    hello(spot(0, side, 1 - core), lat)

    @pl.when(has_up)
    def _():
        hello(wide, lat - 1)

    @pl.when(has_down)
    def _():
        hello(wide, lat + 1)

    tap_total = taps_ref.shape[1]
    for edge, row in ((0, 0), (1, sz.rows - 1)):
        tap_s[edge] = jnp.zeros(tap_s.shape[1:], F32)
        tap_s[edge, :1, :tap_total] = taps_ref[row : row + 1, :]

    pl.semaphore_wait(
        barrier, bits + 2 + has_up.astype(jnp.int32) + has_down.astype(jnp.int32)
    )

    whole = pl.ds(0, rows)
    mine = pl.ds(pl.multiple_of(half * split, 16), split + shared)
    lead = pl.ds(pl.multiple_of(half * (split + shared), 16), split)
    other = pl.ds(pl.multiple_of((1 - half) * (split + shared), 16), split)

    def message(shard, where, to_wide, to_lat, send, recv):
        return pltpu.make_async_remote_copy(
            src_ref=got.at[shard, where],
            dst_ref=got.at[shard, where],
            send_sem=send,
            recv_sem=recv,
            device_id=(to_wide, to_lat),
            device_id_type=MESH,
        )

    started = []

    def start(copy):
        copy.start()
        started.append(copy)

    def along(mask, bit):
        return message(
            spot(mask, side, core), mine, spot(1 << bit, side, core), lat,
            z_send.at[(mask | 1 << bit) - 1], z_recv.at[(mask | 1 << bit) - 1],
        )

    def arrive(shard, where, sem):
        message(shard, where, wide, lat, z_send.at[0], sem).wait_recv()

    def across(j, shard):
        return message(shard, mine, spot(0, 1 - side, core), lat, x_send.at[j], x_recv.at[j])

    def over(j, shard):
        return message(shard, lead, wide, lat + 1 - 2 * half, y_send.at[j], y_recv.at[j])

    def beside(j, shard, where):
        return message(shard, where, spot(0, side, 1 - core), lat, c_send.at[j], c_recv.at[j])

    for bit in reversed(range(bits)):
        start(along(0, bit))
    start(across(0, wide))
    start(beside(0, wide, whole))

    def turned(i, raw, held, out):
        raw_copies[i].wait()
        held[...] = jnp.swapaxes(raw[...], 0, 1)
        copy = pltpu.make_async_copy(held, out, turn_sem.at[i])
        copy.start()
        return copy

    put_x = turned(0, x_raw, x_s, x_out)
    blank = jnp.zeros((cp - sz.inputs, sz.steps * lons), F32)
    for edge, lanes in ((0, slice(0, lons)), (1, slice(sz.cells - lons, sz.cells))):
        fields = jnp.concatenate([x_s[t, :, lanes] for t in range(sz.steps)], 1).astype(F32)
        noise = jnp.concatenate([noise_ref[t, :, lanes] for t in range(sz.steps)], 1).astype(F32)
        rim_s[edge] = jnp.concatenate([fields, noise, blank], 0).astype(BF)

    def rim(edge, to):
        return pltpu.make_async_remote_copy(
            src_ref=rim_s.at[edge],
            dst_ref=edge_s.at[1 - edge],
            send_sem=e_send.at[edge],
            recv_sem=e_recv.at[1 - edge],
            device_id=(wide, to),
            device_id_type=MESH,
        )

    def tap_rim(edge, to):
        return pltpu.make_async_remote_copy(
            src_ref=tap_s.at[edge],
            dst_ref=tap_r.at[1 - edge],
            send_sem=t_send.at[edge],
            recv_sem=t_recv.at[1 - edge],
            device_id=(wide, to),
            device_id_type=MESH,
        )

    @pl.when(has_up)
    def _():
        rim(0, lat - 1).start()
        tap_rim(0, lat - 1).start()

    @pl.when(has_down)
    def _():
        rim(1, lat + 1).start()
        tap_rim(1, lat + 1).start()

    late = []

    def pass_on(mask, s, where):
        shard = spot(mask, s, core)
        start(over(len(late), shard))
        late.append((mask, s))
        start(beside(len(late), shard, where))

    def from_across(mask):
        arrive(spot(mask, 1 - side, core), mine, x_recv.at[mask])
        pass_on(mask, 1 - side, mine)

    for i in range(1, heights):
        shard = spot(i, side, core)
        arrive(shard, mine, z_recv.at[i - 1])
        for bit in reversed(range(low_bit(i, bits))):
            start(along(i, bit))
        start(across(i, shard))
        pass_on(i, side, mine)
        from_across(i - 1)
        if i == 1:
            put_cot = turned(1, cot_raw, cot_s, cot_out)
    from_across(heights - 1)

    def widen(shard):
        flat[pl.ds(shard * own_rows, own_rows), :] = got[shard, :own_rows].astype(F32)

    def finish(j):
        shard = spot(*late[j], 1 - core)
        arrive(shard, mine, c_recv.at[j + 1])
        arrive(shard, other, c_recv.at[2 * heights + j])
        widen(shard)

    widen(wide)
    arrive(spot(0, side, 1 - core), whole, c_recv.at[0])
    widen(spot(0, side, 1 - core))
    for j, column in enumerate(late):
        shard = spot(*column, core)
        arrive(shard, other, y_recv.at[j])
        start(beside(2 * heights + j, shard, other))
        widen(shard)
        if j:
            finish(j - 1)
    finish(len(late) - 1)
    put_x.wait()
    put_cot.wait()
    for copy in started:
        copy.wait_send()

    @pl.when(has_up)
    def _():
        rim(0, lat - 1).wait_send()
        rim(1, lat - 1).wait_recv()
        tap_rim(0, lat - 1).wait_send()
        tap_rim(1, lat - 1).wait_recv()

    @pl.when(has_down)
    def _():
        rim(1, lat + 1).wait_send()
        rim(0, lat + 1).wait_recv()
        tap_rim(1, lat + 1).wait_send()
        tap_rim(0, lat + 1).wait_recv()

    halo_ref[...] = edge_s[...]
    tap_ref[...] = jnp.zeros_like(tap_ref)
    tap_ref[1 : sz.rows + 1, :tap_total] = taps_ref[...]
    tap_ref[:1] = jnp.where(has_up, tap_r[0, :1], 0.0)
    tap_ref[sz.rows + 1 : sz.rows + 2] = jnp.where(has_down, tap_r[1, :1], 0.0)

    unpack_kernel(
        sz, flat, lines, norm_ref, mix_s, mixt_s, up_s, down_s,
        [
            pltpu.make_async_copy(src, dst, out_sem.at[i])
            for i, (src, dst) in enumerate(
                ((mix_s, mix_hbm), (mixt_s, mixt_hbm), (up_s, up_hbm), (down_s, down_hbm))
            )
        ],
    )


def period(length):
    return 128 // math.gcd(length, 128)


def in_batches(count, first, length, some, step=16):
    again = period(length)
    spots = [(j, (first + j * length) // 128, (first + j * length) % 128) for j in range(again)]

    def body(i, _):
        for j in range(0, again, step):
            some(i * again, i * (again * length // 128), spots[j : j + step])
        return 0

    whole = count // again
    lax.fori_loop(0, whole, body, 0)
    left = count % again
    for j in range(0, left, step):
        some(whole * again, whole * (again * length // 128), spots[j : min(j + step, left)])


def lines_of(flat, lines, first, length, count, group):
    def some(line, row, spots):
        held = []
        for _, top, shift in spots:
            low = flat[pl.ds(row + top, group), :]
            if shift:
                high = flat[pl.ds(row + top + 1, group), :]
                low = pltpu.roll(jnp.where(lane_index(group) >= shift, low, high), 128 - shift, 1)
            held.append(low)
        for (at, _, _), value in zip(spots, held):
            lines[pl.ds(pl.multiple_of((line + at) * group, 8), group), :] = value

    in_batches(count, first, length, some)


def unpack_kernel(sz, flat, lines, norm_ref, mix_ref, mixt_ref, up_ref, down_ref, copies):
    chans, cp, cm, rest, hid, hp = sz.chans, sz.chan_pad, sz.chan_main, sz.rest, sz.hid, sz.hid_pad
    basis, inputs = sz.basis, sz.inputs
    at_disco = 2 * chans
    at_bias = at_disco + chans * basis * inputs
    at_up = at_bias + 3 * chans
    at_down = at_up + (chans + 1) * hid

    def column(start):
        held = window(flat, start, 8)
        full = jnp.concatenate(
            [jnp.broadcast_to(held[s : s + 1], (128, 128)).T for s in range(up_to(cp, 128) // 128)], 0
        )[:cp]
        row = lax.broadcasted_iota(jnp.int32, (cp, 128), 0)
        return jnp.where(row < chans, full, 0.0), row

    for i, start in enumerate((0, chans, at_bias + chans, at_bias + 2 * chans)):
        value, row = column(start)
        norm_ref[i] = jnp.where(row == chans, 1.0, value) if i == 3 else value
    disco_bias, _ = column(at_bias)

    groups = 8
    lines_of(flat, lines, at_disco, inputs, chans * basis, groups)
    stride = basis * groups
    lane = lane_index(chans)
    low = jnp.where(lane == inputs - cm, disco_bias[:chans], 0.0)
    blank = jnp.zeros((cp - cm, 128), BF)

    def clear(ref, size):
        if size < ref.shape[0]:
            ref[size:, :] = jnp.zeros((ref.shape[0] - size, ref.shape[1]), BF)

    def put(ref, lanes, value, size):
        whole = size // 16 * 16
        ref[:whole, lanes] = value[:whole].astype(BF)
        tail = jnp.concatenate(
            [value[whole:size], jnp.zeros((up_to(size, 16) - size, 128), F32)], 0
        )
        ref[whole : up_to(size, 16), lanes] = tail.astype(BF)

    for k in range(basis):
        for s in range(cm // 128):
            value = lines[pl.ds(k * groups + s, chans, stride=stride), :]
            put(mix_ref, slice(k * cm + s * 128, k * cm + s * 128 + 128), value, chans)
        value = lines[pl.ds(k * groups + cm // 128, chans, stride=stride), :]
        value = jnp.where(lane < inputs - cm, value, 0.0)
        low = low + (pltpu.roll(value, k * rest, 1) if k else value)
    put(mix_ref, slice(basis * cm, basis * cm + 128), low, chans)
    clear(mix_ref, up_to(chans, 16))
    copies[0].start()

    for k in range(basis):
        for s in range(cm // 128):
            for r in range(cm // 128):
                block = mix_ref[r * 128 : r * 128 + 128, k * cm + s * 128 : k * cm + s * 128 + 128]
                mixt_ref[s * 128 : s * 128 + 128, k * cm + r * 128 : k * cm + r * 128 + 128] = (
                    block.astype(F32).T.astype(BF)
                )
    for r in range(cm // 128):
        block = low[r * 128 : r * 128 + 128].T
        for k in range(basis):
            mixt_ref[cm:cp, k * cm + r * 128 : k * cm + r * 128 + 128] = block[
                k * rest : (k + 1) * rest
            ].astype(BF)
    for s in range(cm // 128):
        block = jnp.concatenate(
            [
                mix_ref[cm:cp, k * cm + s * 128 : k * cm + s * 128 + 128].astype(F32)
                for k in range(basis)
            ]
            + [jnp.zeros((128 - basis * rest, 128), F32)],
            0,
        )
        mixt_ref[s * 128 : s * 128 + 128, basis * cm : basis * cm + 128] = block.T.astype(BF)
    corner = mix_ref[cm:cp, basis * cm : basis * cm + 128].astype(F32)
    corner = jnp.where(lane_index(cp - cm) % rest == 0, corner, 0.0)
    row = lax.broadcasted_iota(jnp.int32, (cp - cm, 128), 0)
    mixt_ref[cm:cp, basis * cm : basis * cm + 128] = jnp.where(row < chans - cm, corner, 0.0).astype(BF)
    copies[1].start()

    groups = 16
    lines_of(flat, lines, at_up, hid, chans + 1, groups)
    for s in range(up_ref.shape[1] // 128):
        value = lines[pl.ds(s, chans + 1, stride=groups), :]
        keep = hid - s * 128
        if keep < 128:
            value = jnp.where(lane_index(chans + 1) < keep, value, 0.0)
        put(up_ref, slice(s * 128, s * 128 + 128), value, chans + 1)
    clear(up_ref, up_to(chans + 1, 16))
    copies[2].start()
    groups = 8
    lines_of(flat, lines, at_down, chans, hid + 1, groups)
    for s in range(down_ref.shape[1] // 128):
        value = lines[pl.ds(s, hid + 1, stride=groups), :]
        keep = chans - s * 128
        if keep < 128:
            value = jnp.where(lane_index(hid + 1) < keep, value, 0.0)
        put(down_ref, slice(s * 128, s * 128 + 128), value, hid + 1)
    clear(down_ref, up_to(hid + 1, 16))
    copies[3].start()
    for copy in copies:
        copy.wait()


def run_gather(sz, params, x_raw, cot_raw, noise_items, filter_taps, total):
    cp, hp = sz.chan_pad, sz.hid_pad
    own_rows = params.shape[0] // 128
    rows = up_to(own_rows, 16)
    split = rows * 7 // 20 // 16 * 16
    shared = rows - 2 * split
    taps = filter_taps.reshape(sz.rows, -1)
    tap_shape = (up_to(sz.rows + 2, 8), up_to(taps.shape[1], 128))
    heights = total // 4
    items = (sz.steps, sz.chans, sz.cells)
    any_spec = pl.BlockSpec(memory_space=pl.ANY)
    vmem = pl.BlockSpec(memory_space=pltpu.VMEM)
    edges = (2, cp, sz.steps * sz.lons)
    line_rows = max(sz.chans * sz.basis * 8, (sz.chans + 1) * 16, (sz.hid + 1) * 8)
    dma = pltpu.SemaphoreType.DMA
    return pl.pallas_call(
        partial(gather_kernel, sz, (rows, own_rows, shared, split)),
        name="gather",
        out_shape=[
            jax.ShapeDtypeStruct(edges, BF),
            jax.ShapeDtypeStruct(tap_shape, F32),
            jax.ShapeDtypeStruct((4, cp, 128), F32),
            jax.ShapeDtypeStruct((cp, up_to(sz.mix, 128)), BF),
            jax.ShapeDtypeStruct((cp, up_to(sz.mix, 128)), BF),
            jax.ShapeDtypeStruct((cp, up_to(hp, 128)), BF),
            jax.ShapeDtypeStruct((hp, up_to(cp, 128)), BF),
            jax.ShapeDtypeStruct(items, BF),
            jax.ShapeDtypeStruct(items, BF),
        ],
        in_specs=[vmem, any_spec, any_spec, vmem, vmem],
        out_specs=[vmem] * 3 + [any_spec] * 6,
        scratch_shapes=[
            pltpu.VMEM((total, rows, 128), BF),
            pltpu.VMEM((up_to(total * own_rows + 24, 8), 128), F32),
            pltpu.VMEM((line_rows, 128), F32),
            pltpu.VMEM(x_raw.shape, BF),
            pltpu.VMEM(x_raw.shape, BF),
            pltpu.VMEM(items, BF),
            pltpu.VMEM(items, BF),
            pltpu.VMEM(edges, BF),
            pltpu.VMEM(edges, BF),
            pltpu.VMEM((2, 8, tap_shape[1]), F32),
            pltpu.VMEM((2, 8, tap_shape[1]), F32),
            pltpu.VMEM((cp, up_to(sz.mix, 128)), BF),
            pltpu.VMEM((cp, up_to(sz.mix, 128)), BF),
            pltpu.VMEM((cp, up_to(hp, 128)), BF),
            pltpu.VMEM((hp, up_to(cp, 128)), BF),
            dma((2,)),
            dma((heights,)), dma((heights,)),
            dma((heights,)), dma((heights,)),
            dma((2 * heights,)), dma((2 * heights,)),
            dma((4 * heights,)), dma((4 * heights,)),
            dma((2,)), dma((2,)),
            dma((2,)), dma((2,)), dma((4,)), dma((2,)),
        ],
        compiler_params=pltpu.CompilerParams(
            collective_id=1, has_side_effects=True, vmem_limit_bytes=60 * 1024 * 1024
        ),
    )(params.reshape(own_rows, 128), x_raw, cot_raw, noise_items, taps)


def run_block(
    sz, x_items, noise_items, cot_items, taps_ext, live, halo, norms, mix, mixt, up, down
):
    cp, hp = sz.chan_pad, sz.hid_pad
    lons = sz.lons

    live_lanes = jnp.concatenate([jnp.repeat(live, sz.main), jnp.repeat(live, lons)])[None]
    any_spec = pl.BlockSpec(memory_space=pl.ANY)
    vmem = pl.BlockSpec(memory_space=pltpu.VMEM)
    mix_lanes = up_to(sz.mix, 128)
    up_lanes = up_to(hp, 128)
    down_lanes = up_to(cp, 128)
    windows = (sz.rows - 1) // 2
    lon = lons
    flops = 2 * sz.width * (3 * sz.mix * cp + 6 * hp * cp)
    return pl.pallas_call(
        partial(block_kernel, sz),
        name="block",
        out_shape=[
            jax.ShapeDtypeStruct(x_items.shape, BF),
            jax.ShapeDtypeStruct((sz.chans, sz.steps, sz.cells), F32),
            jax.ShapeDtypeStruct((cp, mix_lanes), BF),
            jax.ShapeDtypeStruct((cp, up_lanes), BF),
            jax.ShapeDtypeStruct((hp, down_lanes), BF),
            jax.ShapeDtypeStruct((4, cp, 128), F32),
        ],
        in_specs=[
            any_spec, vmem, any_spec, vmem, pl.BlockSpec(memory_space=pltpu.SMEM), vmem, vmem,
            any_spec, any_spec, any_spec, any_spec,
        ],
        out_specs=[any_spec] * 5 + [vmem],
        scratch_shapes=[
            pltpu.VMEM((cp, sz.width), BF),
            pltpu.VMEM((cp, sz.width), BF),
            pltpu.VMEM((sz.mix, sz.width), BF),
            pltpu.VMEM((cp, sz.width), BF),
            pltpu.VMEM((2 * hp, sz.width), BF),
            pltpu.VMEM((cp, sz.width), BF),
            pltpu.VMEM((sz.steps, sz.chans, sz.cells), F32),
            pltpu.VMEM((4, sz.chans, sz.cells), BF),
            pltpu.VMEM((2, cp, (sz.rows + 3) * lon), BF),
            pltpu.VMEM((windows, 4 * lon, sz.basis * 2 * lon), BF),
            pltpu.VMEM((8 * lon, sz.basis * 2 * lon), BF),
            pltpu.VMEM((2, cp, sz.steps * lon), BF),
            pltpu.VMEM((cp, mix_lanes), BF),
            pltpu.VMEM((cp, up_lanes), BF),
            pltpu.VMEM((hp, down_lanes), BF),
            pltpu.SemaphoreType.DMA((2, 2)),
            pltpu.SemaphoreType.DMA((4,)),
            pltpu.SemaphoreType.DMA((2, sz.steps)),
            pltpu.SemaphoreType.DMA((2,)),
            pltpu.SemaphoreType.DMA((2,)),
        ],
        compiler_params=pltpu.CompilerParams(
            collective_id=0, has_side_effects=True, vmem_limit_bytes=63 * 1024 * 1024
        ),
        cost_estimate=pl.CostEstimate(flops=flops, bytes_accessed=40_000_000, transcendentals=0),
    )(x_items, noise_items, cot_items, halo, taps_ext, live_lanes, norms, mix, mixt, up, down)


def merge(old, shift, length, value, rows):
    lane = lane_index(rows)
    place = lax.broadcasted_iota(jnp.int32, (rows, 128), 0) * 128 + lane
    if shift:
        moved = pltpu.roll(value, shift, 1)
        value = jnp.where(lane >= shift, moved, pltpu.roll(moved, 1, 0))
    return jnp.where((place >= shift) & (place < shift + length), value, old)


def flatten_lines(flat, lines, first, length, count, group):
    for odd in range(2):

        def some(line, row, spots, odd=odd):
            spots = [spot for spot in spots if spot[0] % 2 == odd]
            held = []
            for at, top, shift in spots:
                value = lines[pl.ds(pl.multiple_of((line + at) * group, 8), group), :]
                held.append(merge(flat[pl.ds(row + top, group), :], shift, length, value, group))
            for (_, top, _), value in zip(spots, held):
                flat[pl.ds(row + top, group), :] = value

        in_batches(count, first, length, some, 32)


def pack_kernel(sz, dmix_ref, dup_ref, ddown_ref, dnorm_ref, flat, lines, copies, ready):
    chans, cp, cm, rest, hid = sz.chans, sz.chan_pad, sz.chan_main, sz.rest, sz.hid
    basis, inputs = sz.basis, sz.inputs
    at_disco = 2 * chans
    at_bias = at_disco + chans * basis * inputs
    at_up = at_bias + 3 * chans
    at_down = at_up + (chans + 1) * hid
    used = at_down + (hid + 1) * chans

    def across(columns, pick):
        parts = []
        for s in range(8):
            size = min(128, cp - s * 128)
            if size <= 0:
                parts.append(jnp.zeros((1, 128), F32))
                continue
            block = columns[s * 128 : s * 128 + size]
            if size < 128:
                block = jnp.concatenate([block, jnp.zeros((128 - size, 128), F32)], 0)
            parts.append(pick(block.T))
        return jnp.concatenate(parts, 0)

    def total(block):
        return jnp.sum(block, 0, keepdims=True)

    begin = used // 128
    flat[begin:, :] = jnp.zeros((flat.shape[0] - begin, 128), F32)
    spots = (0, chans, at_bias + chans, at_bias + 2 * chans)
    pieces = [(start, across(dnorm_ref[i], total)) for i, start in enumerate(spots)]
    copies[0].wait()
    low = dmix_ref[:, basis * cm : basis * cm + 128].astype(F32)
    bias_row = inputs - cm
    pieces.append((at_bias, across(low, lambda block: block[bias_row : bias_row + 1])))
    for start, value in pieces:
        rows = pl.ds(start // 128, 8)
        flat[rows, :] = merge(flat[rows, :], start % 128, chans, value, 8)

    groups = 8
    stride = basis * groups
    for k in range(basis):
        for s in range(cm // 128):
            value = dmix_ref[:, k * cm + s * 128 : k * cm + s * 128 + 128].astype(F32)
            lines[pl.ds(k * groups + s, chans, stride=stride), :] = value[:chans]
        value = pltpu.roll(low, 128 - k * rest, 1) if k else low
        lines[pl.ds(k * groups + cm // 128, chans, stride=stride), :] = value[:chans]
    flatten_lines(flat, lines, at_disco, inputs, chans * basis, groups)
    ready(at_bias // 128)

    groups = 16
    copies[1].wait()
    for s in range(up_to(hid, 128) // 128):
        value = dup_ref[:, s * 128 : s * 128 + 128].astype(F32)
        lines[pl.ds(s, chans + 1, stride=groups), :] = value[: chans + 1]
    flatten_lines(flat, lines, at_up, hid, chans + 1, groups)
    ready(at_down // 128)

    groups = 8
    copies[2].wait()
    for s in range(up_to(chans, 128) // 128):
        value = ddown_ref[:, s * 128 : s * 128 + 128].astype(F32)
        lines[pl.ds(s, hid + 1, stride=groups), :] = value[: hid + 1]
    flatten_lines(flat, lines, at_down, chans, hid + 1, groups)
    ready(flat.shape[0])


def reduce_kernel(
    sz, parts, dmix_hbm, dup_hbm, ddown_hbm, dnorm_ref, block_hbm, out_ref, turned_hbm,
    flat, lines, block_s, turned_s, dmix_s, dup_s, ddown_s, sums, beside_s, beside_r, over_s, over_r, xa_s, xa_r, xb_s, xb_r,
    za_s, za_r, zb_s, zb_r, fa_s, fa_r, fb_r,
    in_sem, turn_sem, c_send, c_recv, y_send, y_recv, x_send, x_recv, z_send, z_recv,
    f_send, f_recv,
):
    rows, own_rows, shared, split = parts
    wide = lax.axis_index("wide")
    lat = lax.axis_index("lat")
    total = lax.axis_size("wide")
    heights = total // 4
    core = wide % 2
    side = (wide // 2) % 2
    height = wide // 4
    half = lat % 2
    mate = lat + 1 - 2 * half

    bits = heights.bit_length() - 1

    def spot(mask, s, c):
        return 4 * flip(height, mask) + 2 * s + c

    held = (dmix_s, dup_s, ddown_s)
    copies = [
        pltpu.make_async_copy(src, dst, in_sem.at[i])
        for i, (src, dst) in enumerate(zip((dmix_hbm, dup_hbm, ddown_hbm), held))
    ]
    copies.append(pltpu.make_async_copy(block_hbm, block_s, in_sem.at[3]))
    for item in copies:
        item.start()
    barrier = pltpu.get_barrier_semaphore()

    def hello(w, l):
        pl.semaphore_signal(barrier, inc=1, device_id=(w, l), device_id_type=MESH)

    for bit in range(bits):
        hello(spot(1 << bit, side, core), lat)
    hello(spot(0, 1 - side, core), lat)
    hello(spot(0, side, 1 - core), lat)
    hello(wide, mate)
    shares = pl.ds(split, shared)
    lead = pl.ds(pl.multiple_of(half * (split + shared), 16), split)
    other = pl.ds(pl.multiple_of((1 - half) * (split + shared), 16), split)
    masks = list(reversed(range(heights)))
    columns = [(mask, 1 - side) for mask in masks] + [(mask, side) for mask in masks]
    started = []

    def copy(src, dst, send, recv, to_wide, to_lat):
        return pltpu.make_async_remote_copy(
            src_ref=src, dst_ref=dst, send_sem=send, recv_sem=recv,
            device_id=(to_wide, to_lat), device_id_type=MESH,
        )

    def go(message):
        message.start()
        started.append(message)

    def to_core(j):
        return copy(beside_s.at[j], beside_r.at[j], c_send.at[j], c_recv.at[j], spot(0, side, 1 - core), lat)

    def to_mate(j):
        return copy(over_s.at[j], over_r.at[j], y_send.at[j], y_recv.at[j], wide, mate)

    def to_side(src, dst, j, part):
        return copy(src.at[j], dst.at[j], x_send.at[j, part], x_recv.at[j, part], spot(0, 1 - side, core), lat)

    def to_height(src, dst, mask, part):
        return copy(
            src.at[mask - 1], dst.at[mask - 1], z_send.at[mask - 1, part], z_recv.at[mask - 1, part],
            spot(mask & -mask, side, core), lat,
        )

    def add_heights(src, dst, mask, part, j, where):
        for bit in range(low_bit(mask, bits)):
            sender = mask | 1 << bit
            to_height(src, dst, sender, part).wait_recv()
            sums[j, where] += dst[sender - 1].astype(F32)

    next_pair = [0]

    def ready(limit):
        if next_pair[0] == 0:
            pl.semaphore_wait(barrier, bits + 3)
        while next_pair[0] < 2 * heights:
            two = next_pair[0]
            if (2 * two + 1) * own_rows + rows > limit:
                break
            away = 2 * two + 1 - core
            beside_s[two] = flat[pl.ds(away * own_rows, rows), :].astype(BF)
            go(to_core(two))
            next_pair[0] = two + 1

    pack_kernel(sz, *held, dnorm_ref, flat, lines, copies, ready)
    for j, (mask, s) in enumerate(columns):
        mine = spot(mask, s, core)
        two = mine // 2
        to_core(two).wait_recv()
        sums[j] = flat[pl.ds(mine * own_rows, rows), :] + beside_r[two].astype(F32)
        over_s[j] = sums[j, other].astype(BF)
        go(to_mate(j))
        if j < heights:
            xa_s[j] = sums[j, shares].astype(BF)
            go(to_side(xa_s, xa_r, j, 0))
    copies[3].wait()
    turned_s[...] = jnp.swapaxes(block_s[...], 0, 1)
    turned = pltpu.make_async_copy(turned_s, turned_hbm, turn_sem)
    turned.start()
    for i, mask in enumerate(masks):
        to_mate(i).wait_recv()
        xb_s[i] = (sums[i, lead] + over_r[i].astype(F32)).astype(BF)
        go(to_side(xb_s, xb_r, i, 1))
        j = heights + i
        to_side(xa_s, xa_r, i, 0).wait_recv()
        sums[j, shares] += xa_r[i].astype(F32)
        add_heights(za_s, za_r, mask, 0, j, shares)
        if mask:
            za_s[mask - 1] = sums[j, shares].astype(BF)
            go(to_height(za_s, za_r, mask, 0))
    own = 2 * heights - 1
    fa_s[...] = sums[own, shares].astype(BF)
    last = [
        copy(fa_s, fa_r, f_send.at[0], f_recv.at[0], wide, mate),
        copy(sums.at[own, lead], fb_r, f_send.at[1], f_recv.at[1], wide, mate),
    ]
    go(last[0])
    for i, mask in enumerate(masks):
        j = heights + i
        to_mate(j).wait_recv()
        to_side(xb_s, xb_r, i, 1).wait_recv()
        sums[j, lead] += over_r[j].astype(F32) + xb_r[i].astype(F32)
        add_heights(zb_s, zb_r, mask, 1, j, lead)
        if mask:
            zb_s[mask - 1] = sums[j, lead].astype(BF)
            go(to_height(zb_s, zb_r, mask, 1))
    go(last[1])
    last[0].wait_recv()
    out_ref[shares, :] = fa_s[...].astype(F32) + fa_r[...].astype(F32)
    last[1].wait_recv()
    low, high = sums[own, lead], fb_r[...]
    first = jnp.where(half == 0, low, high)
    second = jnp.where(half == 0, high, low)
    out_ref[:split, :] = first
    out_ref[split + shared :, :] = second[: own_rows - split - shared]
    turned.wait()
    for message in started:
        message.wait_send()


def run_reduce(sz, own_rows, total, dmix, dup, ddown, dnorm, block_out):
    rows = up_to(own_rows, 16)
    split = rows // 4 // 16 * 16
    shared = rows - 2 * split
    heights = total // 4
    vmem = pl.BlockSpec(memory_space=pltpu.VMEM)
    any_spec = pl.BlockSpec(memory_space=pl.ANY)
    turned_shape = (sz.chans, sz.steps, sz.cells)
    line_rows = max(sz.chans * sz.basis * 8, (sz.chans + 1) * 16, (sz.hid + 1) * 8)
    dma = pltpu.SemaphoreType.DMA
    flat_rows = up_to((total - 1) * own_rows + rows, 8) + 16
    return pl.pallas_call(
        partial(reduce_kernel, sz, (rows, own_rows, shared, split)),
        name="reduce",
        out_shape=[
            jax.ShapeDtypeStruct((own_rows, 128), F32),
            jax.ShapeDtypeStruct(turned_shape, BF),
        ],
        in_specs=[any_spec] * 3 + [vmem, any_spec],
        out_specs=[vmem, any_spec],
        scratch_shapes=[
            pltpu.VMEM((flat_rows, 128), F32),
            pltpu.VMEM((line_rows, 128), F32),
            pltpu.VMEM(block_out.shape, BF),
            pltpu.VMEM(turned_shape, BF),
            pltpu.VMEM(dmix.shape, BF),
            pltpu.VMEM(dup.shape, BF),
            pltpu.VMEM(ddown.shape, BF),
            pltpu.VMEM((2 * heights, rows, 128), F32),
            pltpu.VMEM((2 * heights, rows, 128), BF),
            pltpu.VMEM((2 * heights, rows, 128), BF),
            pltpu.VMEM((2 * heights, split, 128), BF),
            pltpu.VMEM((2 * heights, split, 128), BF),
            pltpu.VMEM((heights, shared, 128), BF),
            pltpu.VMEM((heights, shared, 128), BF),
            pltpu.VMEM((heights, split, 128), BF),
            pltpu.VMEM((heights, split, 128), BF),
            pltpu.VMEM((heights, shared, 128), BF),
            pltpu.VMEM((heights, shared, 128), BF),
            pltpu.VMEM((heights, split, 128), BF),
            pltpu.VMEM((heights, split, 128), BF),
            pltpu.VMEM((shared, 128), BF),
            pltpu.VMEM((shared, 128), BF),
            pltpu.VMEM((split, 128), F32),
            dma((4,)), dma(()),
            dma((2 * heights,)), dma((2 * heights,)),
            dma((2 * heights,)), dma((2 * heights,)),
            dma((heights, 2)), dma((heights, 2)),
            dma((heights, 2)), dma((heights, 2)),
            dma((2,)), dma((2,)),
        ],
        compiler_params=pltpu.CompilerParams(
            collective_id=2, has_side_effects=True, vmem_limit_bytes=62 * 1024 * 1024
        ),
    )(dmix, dup, ddown, dnorm, block_out)


def shards(block_input, noise_fields, filter_taps, rollout, cotangent, params):
    sz = Sizes(block_input, noise_fields, filter_taps)
    chans = sz.chans
    dates, step_total = block_input.shape[:2]
    step_ids = jnp.arange(step_total, dtype=jnp.int32)
    live = (step_ids[None, :] < rollout[:, None]).astype(F32).reshape(sz.steps)
    noise_items = noise_fields.reshape(sz.steps, sz.noise, sz.cells)

    def by_channel(fields):
        return jnp.transpose(fields, (2, 0, 1, 3)).reshape(chans, sz.steps, sz.cells)

    halo, taps_ext, norms, mix, mixt, up, down, x_items, cot_items = run_gather(
        sz,
        params,
        by_channel(block_input),
        by_channel(cotangent),
        noise_items,
        filter_taps,
        lax.axis_size("wide"),
    )
    out, grad, dmix, dup, ddown, dnorm = run_block(
        sz,
        x_items,
        noise_items,
        cot_items,
        taps_ext,
        live,
        halo,
        norms,
        mix,
        mixt,
        up,
        down,
    )
    own, turned = run_reduce(
        sz, params.shape[0] // 128, lax.axis_size("wide"), dmix, dup, ddown, dnorm, out
    )

    def by_step(fields):
        return jnp.transpose(fields, (1, 0, 2)).reshape(block_input.shape)

    return (by_step(turned), by_step(grad), own.reshape(params.shape))


def solution(mesh):
    in_specs = (
        P("wide", None, None, "lat"),
        P("wide", None, None, "lat"),
        P("lat", None, None, None),
        P("wide"),
        P("wide", None, None, "lat"),
        P("wide"),
    )
    out_specs = (P("wide", None, None, "lat"), P("wide", None, None, "lat"), P("wide"))
    return jax.shard_map(shards, mesh=mesh, in_specs=in_specs, out_specs=out_specs, check_vma=False)
```

```python
import math
from functools import partial

import jax
import jax.numpy as jnp
from jax import lax
from jax.experimental import pallas as pl
from jax.experimental.pallas import tpu as pltpu
from jax.sharding import PartitionSpec as P

HID = 1282
BF = jnp.bfloat16
F32 = jnp.float32
EPS = 1e-05
NEAR = 256
MESH = pl.DeviceIdType.MESH


def up_to(size, unit):
    return -(-size // unit) * unit


def mm(left, right, dims=(1, 0)):
    return lax.dot_general(
        left, right, (((dims[0],), (dims[1],)), ((), ())), preferred_element_type=F32
    )


class Sizes:
    def __init__(self, block_input, noise_fields, filter_taps):
        self.steps = block_input.shape[0] * block_input.shape[1]
        self.chans = block_input.shape[2]
        self.noise = noise_fields.shape[2]
        self.inputs = self.chans + self.noise
        self.rows = filter_taps.shape[0]
        self.basis = filter_taps.shape[1]
        self.taps = filter_taps.shape[3]
        self.cells = block_input.shape[3]
        self.lons = self.cells // self.rows
        self.chan_pad = up_to(self.inputs + 1, 16)
        self.chan_main = self.chans // 128 * 128
        self.rest = self.chan_pad - self.chan_main
        self.hid = HID
        self.hid_pad = up_to(HID + 1, 16)
        self.mix = self.basis * self.chan_pad
        self.main = (self.rows - 1) * self.lons
        self.width = self.steps * self.cells
        self.tail = self.steps * self.main


def block_kernel(
    sz, x_hbm, noise_ref, cot_hbm, halo_ref, taps_ref, live_ref, norm_ref, mix_hbm, mixt_hbm,
    up_hbm, down_hbm, out_hbm, grad_hbm, dmix_hbm, dup_hbm, ddown_hbm, dnorm_ref,
    xs, gs, basis_s, normed_s, act_s, gd_s, grad_s, stage, noisy_s, filt_s, filt_e,
    edge_s, mix_s, up_s, down_s,
    in_sem, w_sem, out_sem, send_sem, recv_sem,
):
    chans, cp, cm, rest = sz.chans, sz.chan_pad, sz.chan_main, sz.rest
    hp, lons, main, tail = sz.hid_pad, sz.lons, sz.main, sz.tail
    pair = 2 * lons
    lat = lax.axis_index("lat")
    lat_count = lax.axis_size("lat")
    has_up = lat > 0
    has_down = lat < lat_count - 1

    def fetch(step, slot):
        return (
            pltpu.make_async_copy(x_hbm.at[step], stage.at[slot], in_sem.at[slot, 0]),
            pltpu.make_async_copy(cot_hbm.at[step], stage.at[2 + slot], in_sem.at[slot, 1]),
        )

    for step in range(2):
        for copy in fetch(step, step):
            copy.start()
    weights = [
        pltpu.make_async_copy(src, dst, w_sem.at[i])
        for i, (src, dst) in enumerate(((mix_hbm, mix_s), (up_hbm, up_s), (down_hbm, down_s)))
    ]
    for copy in weights:
        copy.start()
    mixt_s = normed_s.at[:, pl.ds(0, mixt_hbm.shape[1])]
    mixt_copy = pltpu.make_async_copy(mixt_hbm, mixt_s, w_sem.at[3])

    row_in = lax.broadcasted_iota(jnp.int32, (lons, pair), 0)
    lane = lax.broadcasted_iota(jnp.int32, (lons, pair), 1)
    lane_in = lane % lons
    left_half = lane < lons
    half_taps = sz.taps // 2
    circ = []
    circ_t = []
    for t in range(sz.taps):
        circ.append(row_in == (lane_in + (t - half_taps + lons)) % lons)
        circ_t.append(lane_in == (row_in + (t - half_taps + lons)) % lons)
    def tap_block(ext_row_a, a_a, ext_row_b, a_b, k, masks):
        block = jnp.zeros((lons, pair), F32)
        for t in range(sz.taps):
            va = F32(0) if a_a is None else taps_ref[ext_row_a, (k * 3 + a_a) * sz.taps + t]
            vb = F32(0) if a_b is None else taps_ref[ext_row_b, (k * 3 + a_b) * sz.taps + t]
            block = jnp.where(masks[t], jnp.where(left_half, va, vb), block)
        return block.astype(BF)

    def inside(a):
        return a if 0 <= a <= 2 else None

    windows = (sz.rows - 1) // 2
    last = sz.rows - 1

    def build_filters(backward):
        def build(index, _):
            m = index // sz.basis
            k = index % sz.basis
            cols = pl.ds(pl.multiple_of(k * pair, pair), pair)
            for ri in range(4):
                if backward:
                    block = tap_block(
                        2 * m + ri, inside(2 - ri), 2 * m + ri, inside(3 - ri), k, circ_t
                    )
                else:
                    block = tap_block(
                        2 * m + 1, inside(ri), 2 * m + 2, inside(ri - 1), k, circ
                    )
                filt_s[m, pl.ds(ri * lons, lons), cols] = block
            return 0

        def build_last(k, _):
            cols = pl.ds(pl.multiple_of(k * pair, pair), pair)
            for ri in range(4):
                ext = min(last + ri, last + 2) if backward else last + 1
                a = inside(2 - ri) if backward else inside(ri)
                masks = circ_t if backward else circ
                for odd in range(2):
                    filt_e[pl.ds((odd * 4 + ri) * lons, lons), cols] = tap_block(
                        ext, None if odd else a, ext, a if odd else None, k, masks
                    )
            return 0

        lax.fori_loop(0, windows * sz.basis, build, 0)
        lax.fori_loop(0, sz.basis, build_last, 0)

    build_filters(False)

    gain_one, bias_one = norm_ref[0], norm_ref[1]
    gain_two, bias_two = norm_ref[2], norm_ref[3]

    def wide(vec, lanes):
        if lanes <= 128:
            return vec[:, :lanes]
        return jnp.concatenate([vec] * (lanes // 128) + ([vec[:, : lanes % 128]] if lanes % 128 else []), 1)

    def stats(values):
        centre = jnp.sum(values, 0, keepdims=True) * (1.0 / chans)
        shifted = values - centre
        spread = jnp.sum(jnp.square(shifted), 0, keepdims=True) * (1.0 / chans)
        return shifted, lax.rsqrt(spread + EPS)

    def norm_one(values, lanes):
        shifted, inv = stats(values)
        return shifted * inv * wide(gain_one[:chans], lanes) + wide(bias_one[:chans], lanes)

    halos = []
    for side, there in ((0, has_up), (1, has_down)):
        fields = halo_ref[side].astype(F32)
        width = fields.shape[1]
        normed = norm_one(fields[:chans], width)
        noise = fields[chans : sz.inputs]
        full = jnp.concatenate(
            [normed, noise, jnp.zeros((cp - sz.inputs, width), F32)], 0
        )
        edge_s[side] = jnp.where(there, full, 0.0).astype(BF)

    def halo_part(source, step):
        return source[:, step * lons : (step + 1) * lons]

    ones_row = (lax.broadcasted_iota(jnp.int32, (rest, pair), 0) == sz.inputs - cm).astype(F32)

    def run_filter(slot, store):
        for m in range(windows):
            window = noisy_s[slot, :, m * pair : m * pair + 2 * pair]
            result = mm(window, filt_s[m])
            for k in range(sz.basis):
                store(m, k, result[:, k * pair : (k + 1) * pair])

    def run_last(store):
        window = jnp.concatenate(
            [noisy_s[slot, :, windows * pair : windows * pair + 2 * pair] for slot in range(2)], 1
        )
        result = mm(window, filt_e[...])
        for k in range(sz.basis):
            store(k, result[:, k * pair : (k + 1) * pair])

    def put_basis(lanes, k, part, ones):
        basis_s[k * cm : (k + 1) * cm, lanes] = part[:cm].astype(BF)
        low = part[cm:]
        if ones and k == 0:
            low = low + ones_row
        start = sz.basis * cm + k * rest
        basis_s[start : start + rest, lanes] = low.astype(BF)

    zero_lanes = jnp.zeros((cp, lons), BF)
    pad_rows = jnp.zeros((cp - chans, sz.cells), F32)
    pad_pair = jnp.zeros((cp - chans, pair), F32)
    pairs = sz.steps // 2

    def prepare(two, _):
        both = pl.ds(pl.multiple_of(tail + two * pair, pair), pair)
        near = pl.ds(pl.multiple_of(two * pair, pair), pair)
        for slot in range(2):
            step = 2 * two + slot
            for copy in fetch(step, slot):
                copy.wait()
            fields = stage[slot].astype(F32)
            normed = norm_one(fields, sz.cells)
            noise = noise_ref[step].astype(F32)
            own = jnp.concatenate(
                [normed, noise, jnp.zeros((cp - sz.inputs, sz.cells), F32)], 0
            ).astype(BF)
            noisy_s[slot] = jnp.concatenate(
                [
                    halo_part(edge_s[0, :, near], slot),
                    own,
                    halo_part(edge_s[1, :, near], slot),
                    zero_lanes,
                ],
                1,
            )
            lanes = pl.ds(pl.multiple_of(step * main, main), main)
            xs[:, lanes] = jnp.concatenate([fields, pad_rows], 0)[:, :main].astype(BF)
            masked = jnp.concatenate([stage[2 + slot].astype(F32), pad_rows], 0)[:, :main]
            gs[:, lanes] = (masked * live_ref[:, lanes]).astype(BF)

            def keep(m, k, part, step=step):
                start = pl.multiple_of(step * main + m * pair, pair)
                put_basis(pl.ds(start, pair), k, part, True)

            run_filter(slot, keep)
        x_tail = jnp.concatenate([stage[s, :, main:] for s in range(2)], 1).astype(F32)
        xs[:, both] = jnp.concatenate([x_tail, pad_pair], 0).astype(BF)
        g_tail = jnp.concatenate([stage[2 + s, :, main:] for s in range(2)], 1).astype(F32)
        g_tail = jnp.concatenate([g_tail, pad_pair], 0)
        gs[:, both] = (g_tail * live_ref[:, both]).astype(BF)
        run_last(lambda k, part: put_basis(both, k, part, True))

        @pl.when(two + 1 < pairs)
        def _():
            for slot in range(2):
                for copy in fetch(2 * two + 2 + slot, slot):
                    copy.start()

        return 0

    lax.fori_loop(0, pairs, prepare, 0)
    barrier = pltpu.get_barrier_semaphore()

    @pl.when(has_up)
    def _():
        pl.semaphore_signal(barrier, inc=1, device_id={"lat": lat - 1}, device_id_type=MESH)

    @pl.when(has_down)
    def _():
        pl.semaphore_signal(barrier, inc=1, device_id={"lat": lat + 1}, device_id_type=MESH)

    for copy in weights:
        copy.wait()
    dnorm_ref[...] = jnp.zeros_like(dnorm_ref)

    def fold(values):
        total = values[:, :128]
        for i in range(1, values.shape[1] // 128):
            total = total + values[:, i * 128 : (i + 1) * 128]
        return total

    chunks = sz.width // NEAR
    per_step = main // NEAR
    tail_chunk = tail // NEAR
    steps_per_tail = NEAR // lons

    def main_lanes(chunk):
        return pl.ds(pl.multiple_of((chunk % per_step) * NEAR, NEAR), NEAR)

    def put_tail(chunk, put):
        @pl.when(chunk >= tail_chunk)
        def _():
            for part in range(steps_per_tail):
                put(
                    (chunk - tail_chunk) * steps_per_tail + part,
                    pl.ds(main, lons),
                    slice(part * lons, (part + 1) * lons),
                )

    def out_copy(step):
        return pltpu.make_async_copy(stage.at[step], out_hbm.at[step], out_sem.at[0, step])

    def grad_copy(step):
        return pltpu.make_async_copy(grad_s.at[step], grad_hbm.at[:, step, :], out_sem.at[1, step])

    def lanes_of(chunk):
        return pl.ds(pl.multiple_of(chunk * NEAR, NEAR), NEAR)

    def order(index):
        return lax.rem(jnp.minimum(index, chunks - 1) + tail_chunk, chunks)

    def forward_first(chunk):
        lanes = lanes_of(chunk)
        residual = xs[:, lanes].astype(F32) + mm(mix_s[:, : sz.mix], basis_s[:, lanes])
        centre = jnp.sum(residual[:chans], 0, keepdims=True) * (1.0 / chans)
        shifted = residual - centre
        spread = jnp.sum(jnp.square(shifted[:chans]), 0, keepdims=True) * (1.0 / chans)
        inv = lax.rsqrt(spread + EPS)
        hat = shifted * inv
        normed_s[:, lanes] = (hat * wide(gain_two, NEAR) + wide(bias_two, NEAR)).astype(BF)
        return residual, centre, inv

    def forward_chunk(index, held):
        residual, centre, inv = held
        chunk = order(index)
        lanes = lanes_of(chunk)
        grad_low = gs[:, lanes]
        pre = mm(up_s[:, :hp], normed_s[:, lanes], (0, 0))
        grad_hidden = mm(down_s[:, :cp], grad_low)
        phi = 0.5 + 0.5 * lax.erf(pre * 0.7071067811865476)
        density = jnp.exp(pre * pre * -0.5) * 0.3989422804014327
        hidden = pre * phi
        grad_pre = (grad_hidden * (phi + pre * density)).astype(BF)
        low_rows = hp - HID // 16 * 16
        low = lax.broadcasted_iota(jnp.int32, (low_rows, NEAR), 0) == HID - (hp - low_rows)
        hidden = jnp.concatenate(
            [hidden[: hp - low_rows], jnp.where(low, 1.0, hidden[hp - low_rows :])], 0
        ).astype(BF)
        act_s[:hp, lanes] = hidden
        act_s[hp:, lanes] = grad_pre
        branch = mm(down_s[:, :cp], hidden, (0, 0))
        output = ((residual + branch)[:chans] * live_ref[:, lanes]).astype(BF)
        hat = (residual - centre) * inv
        grad_normed = mm(up_s[:, :hp], grad_pre)
        ahead = forward_first(order(index + 1))
        dnorm_ref[2] += fold(grad_normed * hat)
        dnorm_ref[3] += fold(grad_normed)
        scaled = grad_normed * wide(gain_two, NEAR)
        mean_one = jnp.sum(scaled[:chans], 0, keepdims=True) * (1.0 / chans)
        mean_two = jnp.sum((scaled * hat)[:chans], 0, keepdims=True) * (1.0 / chans)
        grad_resid = grad_low.astype(F32) + inv * (scaled - mean_one - hat * mean_two)
        gd_s[:, lanes] = grad_resid.astype(BF)

        def put(step, where, part):
            stage[step, :, where] = output[:, part]
            grad_s[step, :, where] = grad_resid[:chans, part]

        put(jnp.minimum(chunk // per_step, sz.steps - 1), main_lanes(chunk), slice(0, NEAR))
        put_tail(chunk, put)

        @pl.when((chunk < tail_chunk) & (lax.rem(chunk, per_step) == per_step - 1))
        def _():
            out_copy(chunk // per_step).start()

        return ahead

    lax.fori_loop(0, chunks, forward_chunk, forward_first(order(0)))

    rim = pl.ds(0, sz.steps * lons)
    noisy_s[0, :, rim] = jnp.concatenate(
        [gd_s[:, step * main : step * main + lons] for step in range(sz.steps)], 1
    )
    noisy_s[1, :, rim] = gd_s[:, tail:]
    pl.semaphore_wait(barrier, has_up.astype(jnp.int32) + has_down.astype(jnp.int32))

    def send(side, to):
        return pltpu.make_async_remote_copy(
            src_ref=noisy_s.at[side, :, rim],
            dst_ref=edge_s.at[1 - side],
            send_sem=send_sem.at[side],
            recv_sem=recv_sem.at[1 - side],
            device_id={"lat": to},
            device_id_type=MESH,
        )

    @pl.when(has_up)
    def _():
        send(0, lat - 1).start()

    @pl.when(has_down)
    def _():
        send(1, lat + 1).start()

    def blocks(total, size):
        return [(i, min(size, total - i)) for i in range(0, total, size)]

    for start, size in blocks(hp, 512):
        up_s[:, start : start + size] = mm(
            normed_s[...], act_s[hp + start : hp + start + size, :], (1, 1)
        ).astype(BF)
    dup_copy = pltpu.make_async_copy(up_s, dup_hbm, w_sem.at[1])
    dup_copy.start()
    mixt_copy.start()
    for start, size in blocks(hp, 432):
        rows = pl.ds(start, size)
        down_s[rows, :cp] = mm(act_s[rows, :], gs[...], (1, 1)).astype(BF)
    ddown_copy = pltpu.make_async_copy(down_s, ddown_hbm, w_sem.at[2])
    ddown_copy.start()
    for start, size in blocks(sz.mix, 512):
        mix_s[:, start : start + size] = mm(
            gd_s[...], basis_s[start : start + size, :], (1, 1)
        ).astype(BF)
    dmix_copy = pltpu.make_async_copy(mix_s, dmix_hbm, w_sem.at[0])
    dmix_copy.start()

    build_filters(True)

    @pl.when(has_up)
    def _():
        send(0, lat - 1).wait_send()
        send(1, lat - 1).wait_recv()

    @pl.when(has_down)
    def _():
        send(1, lat + 1).wait_send()
        send(0, lat + 1).wait_recv()

    def adjoint(two, _):
        both = pl.ds(pl.multiple_of(tail + two * pair, pair), pair)
        near = pl.ds(pl.multiple_of(two * pair, pair), pair)
        for slot in range(2):
            step = 2 * two + slot
            noisy_s[slot] = jnp.concatenate(
                [
                    halo_part(edge_s[0, :, near], slot),
                    gd_s[:, pl.ds(pl.multiple_of(step * main, main), main)],
                    halo_part(gd_s[:, both], slot),
                    halo_part(edge_s[1, :, near], slot),
                    zero_lanes,
                ],
                1,
            )

            def keep_grad(m, k, part, step=step):
                start = pl.multiple_of(step * main + m * pair, pair)
                put_basis(pl.ds(start, pair), k, part, False)

            run_filter(slot, keep_grad)
        run_last(lambda k, part: put_basis(both, k, part, False))
        return 0

    lax.fori_loop(0, pairs, adjoint, 0)
    mixt_copy.wait()

    def mixed_back(index):
        return mm(normed_s[:, : sz.mix], basis_s[:, lanes_of(order(index))])[:chans]

    def backward_chunk(index, _):
        chunk = order(index)
        lanes = lanes_of(chunk)
        grad_first = mixed_back(index)
        shifted, inv = stats(xs[:, lanes].astype(F32)[:chans])
        hat = shifted * inv
        dnorm_ref[0, :chans] += fold(grad_first * hat)
        dnorm_ref[1, :chans] += fold(grad_first)
        scaled = grad_first * wide(gain_one[:chans], NEAR)
        mean_one = jnp.sum(scaled, 0, keepdims=True) * (1.0 / chans)
        mean_two = jnp.sum(scaled * hat, 0, keepdims=True) * (1.0 / chans)
        added = inv * (scaled - mean_one - hat * mean_two)

        def put_grad(step, where, part):
            grad_s[step, :, where] += added[:, part]

        @pl.when(chunk < tail_chunk)
        def _():
            put_grad(chunk // per_step, main_lanes(chunk), slice(0, NEAR))

        put_tail(chunk, put_grad)

        @pl.when((chunk < tail_chunk) & (lax.rem(chunk, per_step) == per_step - 1))
        def _():
            grad_copy(chunk // per_step).start()

        return 0

    lax.fori_loop(0, chunks, backward_chunk, 0)
    for step in range(sz.steps):
        out_copy(step).wait()
        grad_copy(step).wait()
    for copy in (ddown_copy, dup_copy, dmix_copy):
        copy.wait()


def flip(index, mask):
    for bit in range(mask.bit_length()):
        if mask >> bit & 1:
            index = index + (1 << bit) * (1 - 2 * (index // (1 << bit) % 2))
    return index


def low_bit(mask, bits):
    return (mask & -mask).bit_length() - 1 if mask else bits


def lane_index(rows):
    return lax.broadcasted_iota(jnp.int32, (rows, 128), 1)


def window(flat, start, rows):
    first = start >> 7
    shift = start & 127
    low = flat[pl.ds(first, rows), :]
    high = flat[pl.ds(first + 1, rows), :]
    mixed = jnp.where(lane_index(rows) >= shift, low, high)
    return pltpu.roll(mixed, (128 - shift) & 127, 1)


def gather_kernel(
    sz, parts, params_ref, x_hbm, cot_hbm, noise_ref, taps_ref,
    halo_ref, tap_ref, norm_ref, mix_hbm, mixt_hbm, up_hbm, down_hbm, x_out, cot_out,
    got, flat, lines, x_raw, cot_raw, x_s, cot_s, rim_s, edge_s, tap_s, tap_r, mix_s, mixt_s, up_s, down_s,
    in_sem, z_send, z_recv, x_send, x_recv, y_send, y_recv, c_send, c_recv, e_send, e_recv,
    t_send, t_recv, out_sem, turn_sem,
):
    chans, cp, cm, rest, lons = sz.chans, sz.chan_pad, sz.chan_main, sz.rest, sz.lons
    rows, own_rows, shared, split = parts
    wide = lax.axis_index("wide")
    lat = lax.axis_index("lat")
    lat_count = lax.axis_size("lat")
    total = lax.axis_size("wide")
    heights = total // 4
    core = wide % 2
    side = (wide // 2) % 2
    height = wide // 4
    half = lat % 2
    has_up = lat > 0
    has_down = lat < lat_count - 1

    bits = heights.bit_length() - 1

    def spot(mask, s, c):
        return 4 * flip(height, mask) + 2 * s + c

    raw_copies = [
        pltpu.make_async_copy(x_hbm, x_raw, in_sem.at[0]),
        pltpu.make_async_copy(cot_hbm, cot_raw, in_sem.at[1]),
    ]
    for copy in raw_copies:
        copy.start()
    got[wide, :own_rows] = params_ref[...]

    barrier = pltpu.get_barrier_semaphore()

    def hello(w, l):
        pl.semaphore_signal(barrier, inc=1, device_id=(w, l), device_id_type=MESH)

    for bit in range(bits):
        hello(spot(1 << bit, side, core), lat)
    hello(spot(0, 1 - side, core), lat)
    hello(spot(0, side, 1 - core), lat)

    @pl.when(has_up)
    def _():
        hello(wide, lat - 1)

    @pl.when(has_down)
    def _():
        hello(wide, lat + 1)

    tap_total = taps_ref.shape[1]
    for edge, row in ((0, 0), (1, sz.rows - 1)):
        tap_s[edge] = jnp.zeros(tap_s.shape[1:], F32)
        tap_s[edge, :1, :tap_total] = taps_ref[row : row + 1, :]

    pl.semaphore_wait(
        barrier, bits + 2 + has_up.astype(jnp.int32) + has_down.astype(jnp.int32)
    )

    whole = pl.ds(0, rows)
    mine = pl.ds(pl.multiple_of(half * split, 16), split + shared)
    lead = pl.ds(pl.multiple_of(half * (split + shared), 16), split)
    other = pl.ds(pl.multiple_of((1 - half) * (split + shared), 16), split)

    def message(shard, where, to_wide, to_lat, send, recv):
        return pltpu.make_async_remote_copy(
            src_ref=got.at[shard, where],
            dst_ref=got.at[shard, where],
            send_sem=send,
            recv_sem=recv,
            device_id=(to_wide, to_lat),
            device_id_type=MESH,
        )

    started = []

    def start(copy):
        copy.start()
        started.append(copy)

    def along(mask, bit):
        return message(
            spot(mask, side, core), mine, spot(1 << bit, side, core), lat,
            z_send.at[(mask | 1 << bit) - 1], z_recv.at[(mask | 1 << bit) - 1],
        )

    def arrive(shard, where, sem):
        message(shard, where, wide, lat, z_send.at[0], sem).wait_recv()

    def across(j, shard):
        return message(shard, mine, spot(0, 1 - side, core), lat, x_send.at[j], x_recv.at[j])

    def over(j, shard):
        return message(shard, lead, wide, lat + 1 - 2 * half, y_send.at[j], y_recv.at[j])

    def beside(j, shard, where):
        return message(shard, where, spot(0, side, 1 - core), lat, c_send.at[j], c_recv.at[j])

    for bit in reversed(range(bits)):
        start(along(0, bit))
    start(across(0, wide))
    start(beside(0, wide, whole))

    def turned(i, raw, held, out):
        raw_copies[i].wait()
        held[...] = jnp.swapaxes(raw[...], 0, 1)
        copy = pltpu.make_async_copy(held, out, turn_sem.at[i])
        copy.start()
        return copy

    put_x = turned(0, x_raw, x_s, x_out)
    blank = jnp.zeros((cp - sz.inputs, sz.steps * lons), F32)
    for edge, lanes in ((0, slice(0, lons)), (1, slice(sz.cells - lons, sz.cells))):
        fields = jnp.concatenate([x_s[t, :, lanes] for t in range(sz.steps)], 1).astype(F32)
        noise = jnp.concatenate([noise_ref[t, :, lanes] for t in range(sz.steps)], 1).astype(F32)
        rim_s[edge] = jnp.concatenate([fields, noise, blank], 0).astype(BF)

    def rim(edge, to):
        return pltpu.make_async_remote_copy(
            src_ref=rim_s.at[edge],
            dst_ref=edge_s.at[1 - edge],
            send_sem=e_send.at[edge],
            recv_sem=e_recv.at[1 - edge],
            device_id=(wide, to),
            device_id_type=MESH,
        )

    def tap_rim(edge, to):
        return pltpu.make_async_remote_copy(
            src_ref=tap_s.at[edge],
            dst_ref=tap_r.at[1 - edge],
            send_sem=t_send.at[edge],
            recv_sem=t_recv.at[1 - edge],
            device_id=(wide, to),
            device_id_type=MESH,
        )

    @pl.when(has_up)
    def _():
        rim(0, lat - 1).start()
        tap_rim(0, lat - 1).start()

    @pl.when(has_down)
    def _():
        rim(1, lat + 1).start()
        tap_rim(1, lat + 1).start()

    late = []

    def pass_on(mask, s, where):
        shard = spot(mask, s, core)
        start(over(len(late), shard))
        late.append((mask, s))
        start(beside(len(late), shard, where))

    def from_across(mask):
        arrive(spot(mask, 1 - side, core), mine, x_recv.at[mask])
        pass_on(mask, 1 - side, mine)

    for i in range(1, heights):
        shard = spot(i, side, core)
        arrive(shard, mine, z_recv.at[i - 1])
        for bit in reversed(range(low_bit(i, bits))):
            start(along(i, bit))
        start(across(i, shard))
        pass_on(i, side, mine)
        from_across(i - 1)
        if i == 1:
            put_cot = turned(1, cot_raw, cot_s, cot_out)
    from_across(heights - 1)

    def widen(shard):
        flat[pl.ds(shard * own_rows, own_rows), :] = got[shard, :own_rows].astype(F32)

    def finish(j):
        shard = spot(*late[j], 1 - core)
        arrive(shard, mine, c_recv.at[j + 1])
        arrive(shard, other, c_recv.at[2 * heights + j])
        widen(shard)

    widen(wide)
    arrive(spot(0, side, 1 - core), whole, c_recv.at[0])
    widen(spot(0, side, 1 - core))
    for j, column in enumerate(late):
        shard = spot(*column, core)
        arrive(shard, other, y_recv.at[j])
        start(beside(2 * heights + j, shard, other))
        widen(shard)
        if j:
            finish(j - 1)
    finish(len(late) - 1)
    put_x.wait()
    put_cot.wait()
    for copy in started:
        copy.wait_send()

    @pl.when(has_up)
    def _():
        rim(0, lat - 1).wait_send()
        rim(1, lat - 1).wait_recv()
        tap_rim(0, lat - 1).wait_send()
        tap_rim(1, lat - 1).wait_recv()

    @pl.when(has_down)
    def _():
        rim(1, lat + 1).wait_send()
        rim(0, lat + 1).wait_recv()
        tap_rim(1, lat + 1).wait_send()
        tap_rim(0, lat + 1).wait_recv()

    halo_ref[...] = edge_s[...]
    tap_ref[...] = jnp.zeros_like(tap_ref)
    tap_ref[1 : sz.rows + 1, :tap_total] = taps_ref[...]
    tap_ref[:1] = jnp.where(has_up, tap_r[0, :1], 0.0)
    tap_ref[sz.rows + 1 : sz.rows + 2] = jnp.where(has_down, tap_r[1, :1], 0.0)

    unpack_kernel(
        sz, flat, lines, norm_ref, mix_s, mixt_s, up_s, down_s,
        [
            pltpu.make_async_copy(src, dst, out_sem.at[i])
            for i, (src, dst) in enumerate(
                ((mix_s, mix_hbm), (mixt_s, mixt_hbm), (up_s, up_hbm), (down_s, down_hbm))
            )
        ],
    )


def period(length):
    return 128 // math.gcd(length, 128)


def in_batches(count, first, length, some, step=16):
    again = period(length)
    spots = [(j, (first + j * length) // 128, (first + j * length) % 128) for j in range(again)]

    def body(i, _):
        for j in range(0, again, step):
            some(i * again, i * (again * length // 128), spots[j : j + step])
        return 0

    whole = count // again
    lax.fori_loop(0, whole, body, 0)
    left = count % again
    for j in range(0, left, step):
        some(whole * again, whole * (again * length // 128), spots[j : min(j + step, left)])


def lines_of(flat, lines, first, length, count, group):
    def some(line, row, spots):
        held = []
        for _, top, shift in spots:
            low = flat[pl.ds(row + top, group), :]
            if shift:
                high = flat[pl.ds(row + top + 1, group), :]
                low = pltpu.roll(jnp.where(lane_index(group) >= shift, low, high), 128 - shift, 1)
            held.append(low)
        for (at, _, _), value in zip(spots, held):
            lines[pl.ds(pl.multiple_of((line + at) * group, 8), group), :] = value

    in_batches(count, first, length, some)


def unpack_kernel(sz, flat, lines, norm_ref, mix_ref, mixt_ref, up_ref, down_ref, copies):
    chans, cp, cm, rest, hid, hp = sz.chans, sz.chan_pad, sz.chan_main, sz.rest, sz.hid, sz.hid_pad
    basis, inputs = sz.basis, sz.inputs
    at_disco = 2 * chans
    at_bias = at_disco + chans * basis * inputs
    at_up = at_bias + 3 * chans
    at_down = at_up + (chans + 1) * hid

    def column(start):
        held = window(flat, start, 8)
        full = jnp.concatenate(
            [jnp.broadcast_to(held[s : s + 1], (128, 128)).T for s in range(up_to(cp, 128) // 128)], 0
        )[:cp]
        row = lax.broadcasted_iota(jnp.int32, (cp, 128), 0)
        return jnp.where(row < chans, full, 0.0), row

    for i, start in enumerate((0, chans, at_bias + chans, at_bias + 2 * chans)):
        value, row = column(start)
        norm_ref[i] = jnp.where(row == chans, 1.0, value) if i == 3 else value
    disco_bias, _ = column(at_bias)

    groups = 8
    lines_of(flat, lines, at_disco, inputs, chans * basis, groups)
    stride = basis * groups
    lane = lane_index(chans)
    low = jnp.where(lane == inputs - cm, disco_bias[:chans], 0.0)
    blank = jnp.zeros((cp - cm, 128), BF)

    def clear(ref, size):
        if size < ref.shape[0]:
            ref[size:, :] = jnp.zeros((ref.shape[0] - size, ref.shape[1]), BF)

    def put(ref, lanes, value, size):
        whole = size // 16 * 16
        ref[:whole, lanes] = value[:whole].astype(BF)
        tail = jnp.concatenate(
            [value[whole:size], jnp.zeros((up_to(size, 16) - size, 128), F32)], 0
        )
        ref[whole : up_to(size, 16), lanes] = tail.astype(BF)

    for k in range(basis):
        for s in range(cm // 128):
            value = lines[pl.ds(k * groups + s, chans, stride=stride), :]
            put(mix_ref, slice(k * cm + s * 128, k * cm + s * 128 + 128), value, chans)
        value = lines[pl.ds(k * groups + cm // 128, chans, stride=stride), :]
        value = jnp.where(lane < inputs - cm, value, 0.0)
        low = low + (pltpu.roll(value, k * rest, 1) if k else value)
    put(mix_ref, slice(basis * cm, basis * cm + 128), low, chans)
    clear(mix_ref, up_to(chans, 16))
    copies[0].start()

    for k in range(basis):
        for s in range(cm // 128):
            for r in range(cm // 128):
                block = mix_ref[r * 128 : r * 128 + 128, k * cm + s * 128 : k * cm + s * 128 + 128]
                mixt_ref[s * 128 : s * 128 + 128, k * cm + r * 128 : k * cm + r * 128 + 128] = (
                    block.astype(F32).T.astype(BF)
                )
    for r in range(cm // 128):
        block = low[r * 128 : r * 128 + 128].T
        for k in range(basis):
            mixt_ref[cm:cp, k * cm + r * 128 : k * cm + r * 128 + 128] = block[
                k * rest : (k + 1) * rest
            ].astype(BF)
    for s in range(cm // 128):
        block = jnp.concatenate(
            [
                mix_ref[cm:cp, k * cm + s * 128 : k * cm + s * 128 + 128].astype(F32)
                for k in range(basis)
            ]
            + [jnp.zeros((128 - basis * rest, 128), F32)],
            0,
        )
        mixt_ref[s * 128 : s * 128 + 128, basis * cm : basis * cm + 128] = block.T.astype(BF)
    corner = mix_ref[cm:cp, basis * cm : basis * cm + 128].astype(F32)
    corner = jnp.where(lane_index(cp - cm) % rest == 0, corner, 0.0)
    row = lax.broadcasted_iota(jnp.int32, (cp - cm, 128), 0)
    mixt_ref[cm:cp, basis * cm : basis * cm + 128] = jnp.where(row < chans - cm, corner, 0.0).astype(BF)
    copies[1].start()

    groups = 16
    lines_of(flat, lines, at_up, hid, chans + 1, groups)
    for s in range(up_ref.shape[1] // 128):
        value = lines[pl.ds(s, chans + 1, stride=groups), :]
        keep = hid - s * 128
        if keep < 128:
            value = jnp.where(lane_index(chans + 1) < keep, value, 0.0)
        put(up_ref, slice(s * 128, s * 128 + 128), value, chans + 1)
    clear(up_ref, up_to(chans + 1, 16))
    copies[2].start()
    groups = 8
    lines_of(flat, lines, at_down, chans, hid + 1, groups)
    for s in range(down_ref.shape[1] // 128):
        value = lines[pl.ds(s, hid + 1, stride=groups), :]
        keep = chans - s * 128
        if keep < 128:
            value = jnp.where(lane_index(hid + 1) < keep, value, 0.0)
        put(down_ref, slice(s * 128, s * 128 + 128), value, hid + 1)
    clear(down_ref, up_to(hid + 1, 16))
    copies[3].start()
    for copy in copies:
        copy.wait()


def run_gather(sz, params, x_raw, cot_raw, noise_items, filter_taps, total):
    cp, hp = sz.chan_pad, sz.hid_pad
    own_rows = params.shape[0] // 128
    rows = up_to(own_rows, 16)
    split = rows * 7 // 20 // 16 * 16
    shared = rows - 2 * split
    taps = filter_taps.reshape(sz.rows, -1)
    tap_shape = (up_to(sz.rows + 2, 8), up_to(taps.shape[1], 128))
    heights = total // 4
    items = (sz.steps, sz.chans, sz.cells)
    any_spec = pl.BlockSpec(memory_space=pl.ANY)
    vmem = pl.BlockSpec(memory_space=pltpu.VMEM)
    edges = (2, cp, sz.steps * sz.lons)
    line_rows = max(sz.chans * sz.basis * 8, (sz.chans + 1) * 16, (sz.hid + 1) * 8)
    dma = pltpu.SemaphoreType.DMA
    return pl.pallas_call(
        partial(gather_kernel, sz, (rows, own_rows, shared, split)),
        name="gather",
        out_shape=[
            jax.ShapeDtypeStruct(edges, BF),
            jax.ShapeDtypeStruct(tap_shape, F32),
            jax.ShapeDtypeStruct((4, cp, 128), F32),
            jax.ShapeDtypeStruct((cp, up_to(sz.mix, 128)), BF),
            jax.ShapeDtypeStruct((cp, up_to(sz.mix, 128)), BF),
            jax.ShapeDtypeStruct((cp, up_to(hp, 128)), BF),
            jax.ShapeDtypeStruct((hp, up_to(cp, 128)), BF),
            jax.ShapeDtypeStruct(items, BF),
            jax.ShapeDtypeStruct(items, BF),
        ],
        in_specs=[vmem, any_spec, any_spec, vmem, vmem],
        out_specs=[vmem] * 3 + [any_spec] * 6,
        scratch_shapes=[
            pltpu.VMEM((total, rows, 128), BF),
            pltpu.VMEM((up_to(total * own_rows + 24, 8), 128), F32),
            pltpu.VMEM((line_rows, 128), F32),
            pltpu.VMEM(x_raw.shape, BF),
            pltpu.VMEM(x_raw.shape, BF),
            pltpu.VMEM(items, BF),
            pltpu.VMEM(items, BF),
            pltpu.VMEM(edges, BF),
            pltpu.VMEM(edges, BF),
            pltpu.VMEM((2, 8, tap_shape[1]), F32),
            pltpu.VMEM((2, 8, tap_shape[1]), F32),
            pltpu.VMEM((cp, up_to(sz.mix, 128)), BF),
            pltpu.VMEM((cp, up_to(sz.mix, 128)), BF),
            pltpu.VMEM((cp, up_to(hp, 128)), BF),
            pltpu.VMEM((hp, up_to(cp, 128)), BF),
            dma((2,)),
            dma((heights,)), dma((heights,)),
            dma((heights,)), dma((heights,)),
            dma((2 * heights,)), dma((2 * heights,)),
            dma((4 * heights,)), dma((4 * heights,)),
            dma((2,)), dma((2,)),
            dma((2,)), dma((2,)), dma((4,)), dma((2,)),
        ],
        compiler_params=pltpu.CompilerParams(
            collective_id=1, has_side_effects=True, vmem_limit_bytes=60 * 1024 * 1024
        ),
    )(params.reshape(own_rows, 128), x_raw, cot_raw, noise_items, taps)


def run_block(
    sz, x_items, noise_items, cot_items, taps_ext, live, halo, norms, mix, mixt, up, down
):
    cp, hp = sz.chan_pad, sz.hid_pad
    lons = sz.lons

    live_lanes = jnp.concatenate([jnp.repeat(live, sz.main), jnp.repeat(live, lons)])[None]
    any_spec = pl.BlockSpec(memory_space=pl.ANY)
    vmem = pl.BlockSpec(memory_space=pltpu.VMEM)
    mix_lanes = up_to(sz.mix, 128)
    up_lanes = up_to(hp, 128)
    down_lanes = up_to(cp, 128)
    windows = (sz.rows - 1) // 2
    lon = lons
    flops = 2 * sz.width * (3 * sz.mix * cp + 6 * hp * cp)
    return pl.pallas_call(
        partial(block_kernel, sz),
        name="block",
        out_shape=[
            jax.ShapeDtypeStruct(x_items.shape, BF),
            jax.ShapeDtypeStruct((sz.chans, sz.steps, sz.cells), F32),
            jax.ShapeDtypeStruct((cp, mix_lanes), BF),
            jax.ShapeDtypeStruct((cp, up_lanes), BF),
            jax.ShapeDtypeStruct((hp, down_lanes), BF),
            jax.ShapeDtypeStruct((4, cp, 128), F32),
        ],
        in_specs=[
            any_spec, vmem, any_spec, vmem, pl.BlockSpec(memory_space=pltpu.SMEM), vmem, vmem,
            any_spec, any_spec, any_spec, any_spec,
        ],
        out_specs=[any_spec] * 5 + [vmem],
        scratch_shapes=[
            pltpu.VMEM((cp, sz.width), BF),
            pltpu.VMEM((cp, sz.width), BF),
            pltpu.VMEM((sz.mix, sz.width), BF),
            pltpu.VMEM((cp, sz.width), BF),
            pltpu.VMEM((2 * hp, sz.width), BF),
            pltpu.VMEM((cp, sz.width), BF),
            pltpu.VMEM((sz.steps, sz.chans, sz.cells), F32),
            pltpu.VMEM((4, sz.chans, sz.cells), BF),
            pltpu.VMEM((2, cp, (sz.rows + 3) * lon), BF),
            pltpu.VMEM((windows, 4 * lon, sz.basis * 2 * lon), BF),
            pltpu.VMEM((8 * lon, sz.basis * 2 * lon), BF),
            pltpu.VMEM((2, cp, sz.steps * lon), BF),
            pltpu.VMEM((cp, mix_lanes), BF),
            pltpu.VMEM((cp, up_lanes), BF),
            pltpu.VMEM((hp, down_lanes), BF),
            pltpu.SemaphoreType.DMA((2, 2)),
            pltpu.SemaphoreType.DMA((4,)),
            pltpu.SemaphoreType.DMA((2, sz.steps)),
            pltpu.SemaphoreType.DMA((2,)),
            pltpu.SemaphoreType.DMA((2,)),
        ],
        compiler_params=pltpu.CompilerParams(
            collective_id=0, has_side_effects=True, vmem_limit_bytes=63 * 1024 * 1024
        ),
        cost_estimate=pl.CostEstimate(flops=flops, bytes_accessed=40_000_000, transcendentals=0),
    )(x_items, noise_items, cot_items, halo, taps_ext, live_lanes, norms, mix, mixt, up, down)


def merge(old, shift, length, value, rows):
    lane = lane_index(rows)
    place = lax.broadcasted_iota(jnp.int32, (rows, 128), 0) * 128 + lane
    if shift:
        moved = pltpu.roll(value, shift, 1)
        value = jnp.where(lane >= shift, moved, pltpu.roll(moved, 1, 0))
    return jnp.where((place >= shift) & (place < shift + length), value, old)


def flatten_lines(flat, lines, first, length, count, group):
    for odd in range(2):

        def some(line, row, spots, odd=odd):
            spots = [spot for spot in spots if spot[0] % 2 == odd]
            held = []
            for at, top, shift in spots:
                value = lines[pl.ds(pl.multiple_of((line + at) * group, 8), group), :]
                held.append(merge(flat[pl.ds(row + top, group), :], shift, length, value, group))
            for (_, top, _), value in zip(spots, held):
                flat[pl.ds(row + top, group), :] = value

        in_batches(count, first, length, some, 32)


def pack_kernel(sz, dmix_ref, dup_ref, ddown_ref, dnorm_ref, flat, lines, copies, ready):
    chans, cp, cm, rest, hid = sz.chans, sz.chan_pad, sz.chan_main, sz.rest, sz.hid
    basis, inputs = sz.basis, sz.inputs
    at_disco = 2 * chans
    at_bias = at_disco + chans * basis * inputs
    at_up = at_bias + 3 * chans
    at_down = at_up + (chans + 1) * hid
    used = at_down + (hid + 1) * chans

    def across(columns, pick):
        parts = []
        for s in range(8):
            size = min(128, cp - s * 128)
            if size <= 0:
                parts.append(jnp.zeros((1, 128), F32))
                continue
            block = columns[s * 128 : s * 128 + size]
            if size < 128:
                block = jnp.concatenate([block, jnp.zeros((128 - size, 128), F32)], 0)
            parts.append(pick(block.T))
        return jnp.concatenate(parts, 0)

    def total(block):
        return jnp.sum(block, 0, keepdims=True)

    begin = used // 128
    flat[begin:, :] = jnp.zeros((flat.shape[0] - begin, 128), F32)
    spots = (0, chans, at_bias + chans, at_bias + 2 * chans)
    pieces = [(start, across(dnorm_ref[i], total)) for i, start in enumerate(spots)]
    copies[0].wait()
    low = dmix_ref[:, basis * cm : basis * cm + 128].astype(F32)
    bias_row = inputs - cm
    pieces.append((at_bias, across(low, lambda block: block[bias_row : bias_row + 1])))
    for start, value in pieces:
        rows = pl.ds(start // 128, 8)
        flat[rows, :] = merge(flat[rows, :], start % 128, chans, value, 8)

    groups = 8
    stride = basis * groups
    for k in range(basis):
        for s in range(cm // 128):
            value = dmix_ref[:, k * cm + s * 128 : k * cm + s * 128 + 128].astype(F32)
            lines[pl.ds(k * groups + s, chans, stride=stride), :] = value[:chans]
        value = pltpu.roll(low, 128 - k * rest, 1) if k else low
        lines[pl.ds(k * groups + cm // 128, chans, stride=stride), :] = value[:chans]
    flatten_lines(flat, lines, at_disco, inputs, chans * basis, groups)
    ready(at_bias // 128)

    groups = 16
    copies[1].wait()
    for s in range(up_to(hid, 128) // 128):
        value = dup_ref[:, s * 128 : s * 128 + 128].astype(F32)
        lines[pl.ds(s, chans + 1, stride=groups), :] = value[: chans + 1]
    flatten_lines(flat, lines, at_up, hid, chans + 1, groups)
    ready(at_down // 128)

    groups = 8
    copies[2].wait()
    for s in range(up_to(chans, 128) // 128):
        value = ddown_ref[:, s * 128 : s * 128 + 128].astype(F32)
        lines[pl.ds(s, hid + 1, stride=groups), :] = value[: hid + 1]
    flatten_lines(flat, lines, at_down, chans, hid + 1, groups)
    ready(flat.shape[0])


def reduce_kernel(
    sz, parts, dmix_hbm, dup_hbm, ddown_hbm, dnorm_ref, block_hbm, out_ref, turned_hbm,
    flat, lines, block_s, turned_s, dmix_s, dup_s, ddown_s, sums, beside_s, beside_r, over_s, over_r, xa_s, xa_r, xb_s, xb_r,
    za_s, za_r, zb_s, zb_r, fa_s, fa_r, fb_r,
    in_sem, turn_sem, c_send, c_recv, y_send, y_recv, x_send, x_recv, z_send, z_recv,
    f_send, f_recv,
):
    rows, own_rows, shared, split = parts
    wide = lax.axis_index("wide")
    lat = lax.axis_index("lat")
    total = lax.axis_size("wide")
    heights = total // 4
    core = wide % 2
    side = (wide // 2) % 2
    height = wide // 4
    half = lat % 2
    mate = lat + 1 - 2 * half

    bits = heights.bit_length() - 1

    def spot(mask, s, c):
        return 4 * flip(height, mask) + 2 * s + c

    held = (dmix_s, dup_s, ddown_s)
    copies = [
        pltpu.make_async_copy(src, dst, in_sem.at[i])
        for i, (src, dst) in enumerate(zip((dmix_hbm, dup_hbm, ddown_hbm), held))
    ]
    copies.append(pltpu.make_async_copy(block_hbm, block_s, in_sem.at[3]))
    for item in copies:
        item.start()
    barrier = pltpu.get_barrier_semaphore()

    def hello(w, l):
        pl.semaphore_signal(barrier, inc=1, device_id=(w, l), device_id_type=MESH)

    for bit in range(bits):
        hello(spot(1 << bit, side, core), lat)
    hello(spot(0, 1 - side, core), lat)
    hello(spot(0, side, 1 - core), lat)
    hello(wide, mate)
    shares = pl.ds(split, shared)
    lead = pl.ds(pl.multiple_of(half * (split + shared), 16), split)
    other = pl.ds(pl.multiple_of((1 - half) * (split + shared), 16), split)
    masks = list(reversed(range(heights)))
    columns = [(mask, 1 - side) for mask in masks] + [(mask, side) for mask in masks]
    started = []

    def copy(src, dst, send, recv, to_wide, to_lat):
        return pltpu.make_async_remote_copy(
            src_ref=src, dst_ref=dst, send_sem=send, recv_sem=recv,
            device_id=(to_wide, to_lat), device_id_type=MESH,
        )

    def go(message):
        message.start()
        started.append(message)

    def to_core(j):
        return copy(beside_s.at[j], beside_r.at[j], c_send.at[j], c_recv.at[j], spot(0, side, 1 - core), lat)

    def to_mate(j):
        return copy(over_s.at[j], over_r.at[j], y_send.at[j], y_recv.at[j], wide, mate)

    def to_side(src, dst, j, part):
        return copy(src.at[j], dst.at[j], x_send.at[j, part], x_recv.at[j, part], spot(0, 1 - side, core), lat)

    def to_height(src, dst, mask, part):
        return copy(
            src.at[mask - 1], dst.at[mask - 1], z_send.at[mask - 1, part], z_recv.at[mask - 1, part],
            spot(mask & -mask, side, core), lat,
        )

    def add_heights(src, dst, mask, part, j, where):
        for bit in range(low_bit(mask, bits)):
            sender = mask | 1 << bit
            to_height(src, dst, sender, part).wait_recv()
            sums[j, where] += dst[sender - 1].astype(F32)

    next_pair = [0]

    def ready(limit):
        if next_pair[0] == 0:
            pl.semaphore_wait(barrier, bits + 3)
        while next_pair[0] < 2 * heights:
            two = next_pair[0]
            if (2 * two + 1) * own_rows + rows > limit:
                break
            away = 2 * two + 1 - core
            beside_s[two] = flat[pl.ds(away * own_rows, rows), :].astype(BF)
            go(to_core(two))
            next_pair[0] = two + 1

    pack_kernel(sz, *held, dnorm_ref, flat, lines, copies, ready)
    for j, (mask, s) in enumerate(columns):
        mine = spot(mask, s, core)
        two = mine // 2
        to_core(two).wait_recv()
        sums[j] = flat[pl.ds(mine * own_rows, rows), :] + beside_r[two].astype(F32)
        over_s[j] = sums[j, other].astype(BF)
        go(to_mate(j))
        if j < heights:
            xa_s[j] = sums[j, shares].astype(BF)
            go(to_side(xa_s, xa_r, j, 0))
    copies[3].wait()
    turned_s[...] = jnp.swapaxes(block_s[...], 0, 1)
    turned = pltpu.make_async_copy(turned_s, turned_hbm, turn_sem)
    turned.start()
    for i, mask in enumerate(masks):
        to_mate(i).wait_recv()
        xb_s[i] = (sums[i, lead] + over_r[i].astype(F32)).astype(BF)
        go(to_side(xb_s, xb_r, i, 1))
        j = heights + i
        to_side(xa_s, xa_r, i, 0).wait_recv()
        sums[j, shares] += xa_r[i].astype(F32)
        add_heights(za_s, za_r, mask, 0, j, shares)
        if mask:
            za_s[mask - 1] = sums[j, shares].astype(BF)
            go(to_height(za_s, za_r, mask, 0))
    own = 2 * heights - 1
    fa_s[...] = sums[own, shares].astype(BF)
    last = [
        copy(fa_s, fa_r, f_send.at[0], f_recv.at[0], wide, mate),
        copy(sums.at[own, lead], fb_r, f_send.at[1], f_recv.at[1], wide, mate),
    ]
    go(last[0])
    for i, mask in enumerate(masks):
        j = heights + i
        to_mate(j).wait_recv()
        to_side(xb_s, xb_r, i, 1).wait_recv()
        sums[j, lead] += over_r[j].astype(F32) + xb_r[i].astype(F32)
        add_heights(zb_s, zb_r, mask, 1, j, lead)
        if mask:
            zb_s[mask - 1] = sums[j, lead].astype(BF)
            go(to_height(zb_s, zb_r, mask, 1))
    go(last[1])
    last[0].wait_recv()
    out_ref[shares, :] = fa_s[...].astype(F32) + fa_r[...].astype(F32)
    last[1].wait_recv()
    low, high = sums[own, lead], fb_r[...]
    first = jnp.where(half == 0, low, high)
    second = jnp.where(half == 0, high, low)
    out_ref[:split, :] = first
    out_ref[split + shared :, :] = second[: own_rows - split - shared]
    turned.wait()
    for message in started:
        message.wait_send()


def run_reduce(sz, own_rows, total, dmix, dup, ddown, dnorm, block_out):
    rows = up_to(own_rows, 16)
    split = rows * 3 // 10 // 16 * 16
    shared = rows - 2 * split
    heights = total // 4
    vmem = pl.BlockSpec(memory_space=pltpu.VMEM)
    any_spec = pl.BlockSpec(memory_space=pl.ANY)
    turned_shape = (sz.chans, sz.steps, sz.cells)
    line_rows = max(sz.chans * sz.basis * 8, (sz.chans + 1) * 16, (sz.hid + 1) * 8)
    dma = pltpu.SemaphoreType.DMA
    flat_rows = up_to((total - 1) * own_rows + rows, 8) + 16
    return pl.pallas_call(
        partial(reduce_kernel, sz, (rows, own_rows, shared, split)),
        name="reduce",
        out_shape=[
            jax.ShapeDtypeStruct((own_rows, 128), F32),
            jax.ShapeDtypeStruct(turned_shape, BF),
        ],
        in_specs=[any_spec] * 3 + [vmem, any_spec],
        out_specs=[vmem, any_spec],
        scratch_shapes=[
            pltpu.VMEM((flat_rows, 128), F32),
            pltpu.VMEM((line_rows, 128), F32),
            pltpu.VMEM(block_out.shape, BF),
            pltpu.VMEM(turned_shape, BF),
            pltpu.VMEM(dmix.shape, BF),
            pltpu.VMEM(dup.shape, BF),
            pltpu.VMEM(ddown.shape, BF),
            pltpu.VMEM((2 * heights, rows, 128), F32),
            pltpu.VMEM((2 * heights, rows, 128), BF),
            pltpu.VMEM((2 * heights, rows, 128), BF),
            pltpu.VMEM((2 * heights, split, 128), BF),
            pltpu.VMEM((2 * heights, split, 128), BF),
            pltpu.VMEM((heights, shared, 128), BF),
            pltpu.VMEM((heights, shared, 128), BF),
            pltpu.VMEM((heights, split, 128), BF),
            pltpu.VMEM((heights, split, 128), BF),
            pltpu.VMEM((heights, shared, 128), BF),
            pltpu.VMEM((heights, shared, 128), BF),
            pltpu.VMEM((heights, split, 128), BF),
            pltpu.VMEM((heights, split, 128), BF),
            pltpu.VMEM((shared, 128), BF),
            pltpu.VMEM((shared, 128), BF),
            pltpu.VMEM((split, 128), F32),
            dma((4,)), dma(()),
            dma((2 * heights,)), dma((2 * heights,)),
            dma((2 * heights,)), dma((2 * heights,)),
            dma((heights, 2)), dma((heights, 2)),
            dma((heights, 2)), dma((heights, 2)),
            dma((2,)), dma((2,)),
        ],
        compiler_params=pltpu.CompilerParams(
            collective_id=2, has_side_effects=True, vmem_limit_bytes=62 * 1024 * 1024
        ),
    )(dmix, dup, ddown, dnorm, block_out)


def shards(block_input, noise_fields, filter_taps, rollout, cotangent, params):
    sz = Sizes(block_input, noise_fields, filter_taps)
    chans = sz.chans
    dates, step_total = block_input.shape[:2]
    step_ids = jnp.arange(step_total, dtype=jnp.int32)
    live = (step_ids[None, :] < rollout[:, None]).astype(F32).reshape(sz.steps)
    noise_items = noise_fields.reshape(sz.steps, sz.noise, sz.cells)

    def by_channel(fields):
        return jnp.transpose(fields, (2, 0, 1, 3)).reshape(chans, sz.steps, sz.cells)

    halo, taps_ext, norms, mix, mixt, up, down, x_items, cot_items = run_gather(
        sz,
        params,
        by_channel(block_input),
        by_channel(cotangent),
        noise_items,
        filter_taps,
        lax.axis_size("wide"),
    )
    out, grad, dmix, dup, ddown, dnorm = run_block(
        sz,
        x_items,
        noise_items,
        cot_items,
        taps_ext,
        live,
        halo,
        norms,
        mix,
        mixt,
        up,
        down,
    )
    own, turned = run_reduce(
        sz, params.shape[0] // 128, lax.axis_size("wide"), dmix, dup, ddown, dnorm, out
    )

    def by_step(fields):
        return jnp.transpose(fields, (1, 0, 2)).reshape(block_input.shape)

    return (by_step(turned), by_step(grad), own.reshape(params.shape))


def solution(mesh):
    in_specs = (
        P("wide", None, None, "lat"),
        P("wide", None, None, "lat"),
        P("lat", None, None, None),
        P("wide"),
        P("wide", None, None, "lat"),
        P("wide"),
    )
    out_specs = (P("wide", None, None, "lat"), P("wide", None, None, "lat"), P("wide"))
    return jax.shard_map(shards, mesh=mesh, in_specs=in_specs, out_specs=out_specs, check_vma=False)
```

```python
import math
from functools import partial

import jax
import jax.numpy as jnp
from jax import lax
from jax.experimental import pallas as pl
from jax.experimental.pallas import tpu as pltpu
from jax.sharding import PartitionSpec as P

HID = 1282
BF = jnp.bfloat16
F32 = jnp.float32
EPS = 1e-05
NEAR = 256
MESH = pl.DeviceIdType.MESH


def up_to(size, unit):
    return -(-size // unit) * unit


def mm(left, right, dims=(1, 0)):
    return lax.dot_general(
        left, right, (((dims[0],), (dims[1],)), ((), ())), preferred_element_type=F32
    )


class Sizes:
    def __init__(self, block_input, noise_fields, filter_taps):
        self.steps = block_input.shape[0] * block_input.shape[1]
        self.chans = block_input.shape[2]
        self.noise = noise_fields.shape[2]
        self.inputs = self.chans + self.noise
        self.rows = filter_taps.shape[0]
        self.basis = filter_taps.shape[1]
        self.taps = filter_taps.shape[3]
        self.cells = block_input.shape[3]
        self.lons = self.cells // self.rows
        self.chan_pad = up_to(self.inputs + 1, 16)
        self.chan_main = self.chans // 128 * 128
        self.rest = self.chan_pad - self.chan_main
        self.hid = HID
        self.hid_pad = up_to(HID + 1, 16)
        self.mix = self.basis * self.chan_pad
        self.main = (self.rows - 1) * self.lons
        self.width = self.steps * self.cells
        self.tail = self.steps * self.main


def block_kernel(
    sz, x_hbm, noise_ref, cot_hbm, halo_ref, taps_ref, live_ref, norm_ref, mix_hbm, mixt_hbm,
    up_hbm, down_hbm, out_hbm, grad_hbm, dmix_hbm, dup_hbm, ddown_hbm, dnorm_ref,
    xs, gs, basis_s, normed_s, act_s, gd_s, grad_s, stage, noisy_s, filt_s, filt_e,
    edge_s, mix_s, up_s, down_s,
    in_sem, w_sem, out_sem, send_sem, recv_sem,
):
    chans, cp, cm, rest = sz.chans, sz.chan_pad, sz.chan_main, sz.rest
    hp, lons, main, tail = sz.hid_pad, sz.lons, sz.main, sz.tail
    pair = 2 * lons
    lat = lax.axis_index("lat")
    lat_count = lax.axis_size("lat")
    has_up = lat > 0
    has_down = lat < lat_count - 1

    def fetch(step, slot):
        return (
            pltpu.make_async_copy(x_hbm.at[step], stage.at[slot], in_sem.at[slot, 0]),
            pltpu.make_async_copy(cot_hbm.at[step], stage.at[2 + slot], in_sem.at[slot, 1]),
        )

    for step in range(2):
        for copy in fetch(step, step):
            copy.start()
    weights = [
        pltpu.make_async_copy(src, dst, w_sem.at[i])
        for i, (src, dst) in enumerate(((mix_hbm, mix_s), (up_hbm, up_s), (down_hbm, down_s)))
    ]
    for copy in weights:
        copy.start()
    mixt_s = normed_s.at[:, pl.ds(0, mixt_hbm.shape[1])]
    mixt_copy = pltpu.make_async_copy(mixt_hbm, mixt_s, w_sem.at[3])

    row_in = lax.broadcasted_iota(jnp.int32, (lons, pair), 0)
    lane = lax.broadcasted_iota(jnp.int32, (lons, pair), 1)
    lane_in = lane % lons
    left_half = lane < lons
    half_taps = sz.taps // 2
    circ = []
    circ_t = []
    for t in range(sz.taps):
        circ.append(row_in == (lane_in + (t - half_taps + lons)) % lons)
        circ_t.append(lane_in == (row_in + (t - half_taps + lons)) % lons)
    def tap_block(ext_row_a, a_a, ext_row_b, a_b, k, masks):
        block = jnp.zeros((lons, pair), F32)
        for t in range(sz.taps):
            va = F32(0) if a_a is None else taps_ref[ext_row_a, (k * 3 + a_a) * sz.taps + t]
            vb = F32(0) if a_b is None else taps_ref[ext_row_b, (k * 3 + a_b) * sz.taps + t]
            block = jnp.where(masks[t], jnp.where(left_half, va, vb), block)
        return block.astype(BF)

    def inside(a):
        return a if 0 <= a <= 2 else None

    windows = (sz.rows - 1) // 2
    last = sz.rows - 1

    def build_filters(backward):
        def build(index, _):
            m = index // sz.basis
            k = index % sz.basis
            cols = pl.ds(pl.multiple_of(k * pair, pair), pair)
            for ri in range(4):
                if backward:
                    block = tap_block(
                        2 * m + ri, inside(2 - ri), 2 * m + ri, inside(3 - ri), k, circ_t
                    )
                else:
                    block = tap_block(
                        2 * m + 1, inside(ri), 2 * m + 2, inside(ri - 1), k, circ
                    )
                filt_s[m, pl.ds(ri * lons, lons), cols] = block
            return 0

        def build_last(k, _):
            cols = pl.ds(pl.multiple_of(k * pair, pair), pair)
            for ri in range(4):
                ext = min(last + ri, last + 2) if backward else last + 1
                a = inside(2 - ri) if backward else inside(ri)
                masks = circ_t if backward else circ
                for odd in range(2):
                    filt_e[pl.ds((odd * 4 + ri) * lons, lons), cols] = tap_block(
                        ext, None if odd else a, ext, a if odd else None, k, masks
                    )
            return 0

        lax.fori_loop(0, windows * sz.basis, build, 0)
        lax.fori_loop(0, sz.basis, build_last, 0)

    build_filters(False)

    gain_one, bias_one = norm_ref[0], norm_ref[1]
    gain_two, bias_two = norm_ref[2], norm_ref[3]

    def wide(vec, lanes):
        if lanes <= 128:
            return vec[:, :lanes]
        return jnp.concatenate([vec] * (lanes // 128) + ([vec[:, : lanes % 128]] if lanes % 128 else []), 1)

    def stats(values):
        centre = jnp.sum(values, 0, keepdims=True) * (1.0 / chans)
        shifted = values - centre
        spread = jnp.sum(jnp.square(shifted), 0, keepdims=True) * (1.0 / chans)
        return shifted, lax.rsqrt(spread + EPS)

    def norm_one(values, lanes):
        shifted, inv = stats(values)
        return shifted * inv * wide(gain_one[:chans], lanes) + wide(bias_one[:chans], lanes)

    halos = []
    for side, there in ((0, has_up), (1, has_down)):
        fields = halo_ref[side].astype(F32)
        width = fields.shape[1]
        normed = norm_one(fields[:chans], width)
        noise = fields[chans : sz.inputs]
        full = jnp.concatenate(
            [normed, noise, jnp.zeros((cp - sz.inputs, width), F32)], 0
        )
        edge_s[side] = jnp.where(there, full, 0.0).astype(BF)

    def halo_part(source, step):
        return source[:, step * lons : (step + 1) * lons]

    ones_row = (lax.broadcasted_iota(jnp.int32, (rest, pair), 0) == sz.inputs - cm).astype(F32)

    def run_filter(slot, store):
        for m in range(windows):
            window = noisy_s[slot, :, m * pair : m * pair + 2 * pair]
            result = mm(window, filt_s[m])
            for k in range(sz.basis):
                store(m, k, result[:, k * pair : (k + 1) * pair])

    def run_last(store):
        window = jnp.concatenate(
            [noisy_s[slot, :, windows * pair : windows * pair + 2 * pair] for slot in range(2)], 1
        )
        result = mm(window, filt_e[...])
        for k in range(sz.basis):
            store(k, result[:, k * pair : (k + 1) * pair])

    def put_basis(lanes, k, part, ones):
        basis_s[k * cm : (k + 1) * cm, lanes] = part[:cm].astype(BF)
        low = part[cm:]
        if ones and k == 0:
            low = low + ones_row
        start = sz.basis * cm + k * rest
        basis_s[start : start + rest, lanes] = low.astype(BF)

    zero_lanes = jnp.zeros((cp, lons), BF)
    pad_rows = jnp.zeros((cp - chans, sz.cells), F32)
    pad_pair = jnp.zeros((cp - chans, pair), F32)
    pairs = sz.steps // 2

    def prepare(two, _):
        both = pl.ds(pl.multiple_of(tail + two * pair, pair), pair)
        near = pl.ds(pl.multiple_of(two * pair, pair), pair)
        for slot in range(2):
            step = 2 * two + slot
            for copy in fetch(step, slot):
                copy.wait()
            fields = stage[slot].astype(F32)
            normed = norm_one(fields, sz.cells)
            noise = noise_ref[step].astype(F32)
            own = jnp.concatenate(
                [normed, noise, jnp.zeros((cp - sz.inputs, sz.cells), F32)], 0
            ).astype(BF)
            noisy_s[slot] = jnp.concatenate(
                [
                    halo_part(edge_s[0, :, near], slot),
                    own,
                    halo_part(edge_s[1, :, near], slot),
                    zero_lanes,
                ],
                1,
            )
            lanes = pl.ds(pl.multiple_of(step * main, main), main)
            xs[:, lanes] = jnp.concatenate([fields, pad_rows], 0)[:, :main].astype(BF)
            masked = jnp.concatenate([stage[2 + slot].astype(F32), pad_rows], 0)[:, :main]
            gs[:, lanes] = (masked * live_ref[:, lanes]).astype(BF)

            def keep(m, k, part, step=step):
                start = pl.multiple_of(step * main + m * pair, pair)
                put_basis(pl.ds(start, pair), k, part, True)

            run_filter(slot, keep)
        x_tail = jnp.concatenate([stage[s, :, main:] for s in range(2)], 1).astype(F32)
        xs[:, both] = jnp.concatenate([x_tail, pad_pair], 0).astype(BF)
        g_tail = jnp.concatenate([stage[2 + s, :, main:] for s in range(2)], 1).astype(F32)
        g_tail = jnp.concatenate([g_tail, pad_pair], 0)
        gs[:, both] = (g_tail * live_ref[:, both]).astype(BF)
        run_last(lambda k, part: put_basis(both, k, part, True))

        @pl.when(two + 1 < pairs)
        def _():
            for slot in range(2):
                for copy in fetch(2 * two + 2 + slot, slot):
                    copy.start()

        return 0

    lax.fori_loop(0, pairs, prepare, 0)
    barrier = pltpu.get_barrier_semaphore()

    @pl.when(has_up)
    def _():
        pl.semaphore_signal(barrier, inc=1, device_id={"lat": lat - 1}, device_id_type=MESH)

    @pl.when(has_down)
    def _():
        pl.semaphore_signal(barrier, inc=1, device_id={"lat": lat + 1}, device_id_type=MESH)

    for copy in weights:
        copy.wait()
    dnorm_ref[...] = jnp.zeros_like(dnorm_ref)

    def fold(values):
        total = values[:, :128]
        for i in range(1, values.shape[1] // 128):
            total = total + values[:, i * 128 : (i + 1) * 128]
        return total

    chunks = sz.width // NEAR
    per_step = main // NEAR
    tail_chunk = tail // NEAR
    steps_per_tail = NEAR // lons

    def main_lanes(chunk):
        return pl.ds(pl.multiple_of((chunk % per_step) * NEAR, NEAR), NEAR)

    def put_tail(chunk, put):
        @pl.when(chunk >= tail_chunk)
        def _():
            for part in range(steps_per_tail):
                put(
                    (chunk - tail_chunk) * steps_per_tail + part,
                    pl.ds(main, lons),
                    slice(part * lons, (part + 1) * lons),
                )

    def out_copy(step):
        return pltpu.make_async_copy(stage.at[step], out_hbm.at[step], out_sem.at[0, step])

    def grad_copy(step):
        return pltpu.make_async_copy(grad_s.at[step], grad_hbm.at[:, step, :], out_sem.at[1, step])

    def lanes_of(chunk):
        return pl.ds(pl.multiple_of(chunk * NEAR, NEAR), NEAR)

    def order(index):
        return lax.rem(jnp.minimum(index, chunks - 1) + tail_chunk, chunks)

    def forward_first(chunk):
        lanes = lanes_of(chunk)
        residual = xs[:, lanes].astype(F32) + mm(mix_s[:, : sz.mix], basis_s[:, lanes])
        centre = jnp.sum(residual[:chans], 0, keepdims=True) * (1.0 / chans)
        shifted = residual - centre
        spread = jnp.sum(jnp.square(shifted[:chans]), 0, keepdims=True) * (1.0 / chans)
        inv = lax.rsqrt(spread + EPS)
        hat = shifted * inv
        normed_s[:, lanes] = (hat * wide(gain_two, NEAR) + wide(bias_two, NEAR)).astype(BF)
        return residual, centre, inv

    def forward_chunk(index, held):
        residual, centre, inv = held
        chunk = order(index)
        lanes = lanes_of(chunk)
        grad_low = gs[:, lanes]
        pre = mm(up_s[:, :hp], normed_s[:, lanes], (0, 0))
        grad_hidden = mm(down_s[:, :cp], grad_low)
        phi = 0.5 + 0.5 * lax.erf(pre * 0.7071067811865476)
        density = jnp.exp(pre * pre * -0.5) * 0.3989422804014327
        hidden = pre * phi
        grad_pre = (grad_hidden * (phi + pre * density)).astype(BF)
        low_rows = hp - HID // 16 * 16
        low = lax.broadcasted_iota(jnp.int32, (low_rows, NEAR), 0) == HID - (hp - low_rows)
        hidden = jnp.concatenate(
            [hidden[: hp - low_rows], jnp.where(low, 1.0, hidden[hp - low_rows :])], 0
        ).astype(BF)
        act_s[:hp, lanes] = hidden
        act_s[hp:, lanes] = grad_pre
        branch = mm(down_s[:, :cp], hidden, (0, 0))
        output = ((residual + branch)[:chans] * live_ref[:, lanes]).astype(BF)
        hat = (residual - centre) * inv
        grad_normed = mm(up_s[:, :hp], grad_pre)
        ahead = forward_first(order(index + 1))
        dnorm_ref[2] += fold(grad_normed * hat)
        dnorm_ref[3] += fold(grad_normed)
        scaled = grad_normed * wide(gain_two, NEAR)
        mean_one = jnp.sum(scaled[:chans], 0, keepdims=True) * (1.0 / chans)
        mean_two = jnp.sum((scaled * hat)[:chans], 0, keepdims=True) * (1.0 / chans)
        grad_resid = grad_low.astype(F32) + inv * (scaled - mean_one - hat * mean_two)
        gd_s[:, lanes] = grad_resid.astype(BF)

        def put(step, where, part):
            stage[step, :, where] = output[:, part]
            grad_s[step, :, where] = grad_resid[:chans, part]

        put(jnp.minimum(chunk // per_step, sz.steps - 1), main_lanes(chunk), slice(0, NEAR))
        put_tail(chunk, put)

        @pl.when((chunk < tail_chunk) & (lax.rem(chunk, per_step) == per_step - 1))
        def _():
            out_copy(chunk // per_step).start()

        return ahead

    lax.fori_loop(0, chunks, forward_chunk, forward_first(order(0)))

    rim = pl.ds(0, sz.steps * lons)
    noisy_s[0, :, rim] = jnp.concatenate(
        [gd_s[:, step * main : step * main + lons] for step in range(sz.steps)], 1
    )
    noisy_s[1, :, rim] = gd_s[:, tail:]
    pl.semaphore_wait(barrier, has_up.astype(jnp.int32) + has_down.astype(jnp.int32))

    def send(side, to):
        return pltpu.make_async_remote_copy(
            src_ref=noisy_s.at[side, :, rim],
            dst_ref=edge_s.at[1 - side],
            send_sem=send_sem.at[side],
            recv_sem=recv_sem.at[1 - side],
            device_id={"lat": to},
            device_id_type=MESH,
        )

    @pl.when(has_up)
    def _():
        send(0, lat - 1).start()

    @pl.when(has_down)
    def _():
        send(1, lat + 1).start()

    def blocks(total, size):
        return [(i, min(size, total - i)) for i in range(0, total, size)]

    for start, size in blocks(hp, 512):
        up_s[:, start : start + size] = mm(
            normed_s[...], act_s[hp + start : hp + start + size, :], (1, 1)
        ).astype(BF)
    dup_copy = pltpu.make_async_copy(up_s, dup_hbm, w_sem.at[1])
    dup_copy.start()
    mixt_copy.start()
    for start, size in blocks(hp, 432):
        rows = pl.ds(start, size)
        down_s[rows, :cp] = mm(act_s[rows, :], gs[...], (1, 1)).astype(BF)
    ddown_copy = pltpu.make_async_copy(down_s, ddown_hbm, w_sem.at[2])
    ddown_copy.start()
    for start, size in blocks(sz.mix, 512):
        mix_s[:, start : start + size] = mm(
            gd_s[...], basis_s[start : start + size, :], (1, 1)
        ).astype(BF)
    dmix_copy = pltpu.make_async_copy(mix_s, dmix_hbm, w_sem.at[0])
    dmix_copy.start()

    build_filters(True)

    @pl.when(has_up)
    def _():
        send(0, lat - 1).wait_send()
        send(1, lat - 1).wait_recv()

    @pl.when(has_down)
    def _():
        send(1, lat + 1).wait_send()
        send(0, lat + 1).wait_recv()

    def adjoint(two, _):
        both = pl.ds(pl.multiple_of(tail + two * pair, pair), pair)
        near = pl.ds(pl.multiple_of(two * pair, pair), pair)
        for slot in range(2):
            step = 2 * two + slot
            noisy_s[slot] = jnp.concatenate(
                [
                    halo_part(edge_s[0, :, near], slot),
                    gd_s[:, pl.ds(pl.multiple_of(step * main, main), main)],
                    halo_part(gd_s[:, both], slot),
                    halo_part(edge_s[1, :, near], slot),
                    zero_lanes,
                ],
                1,
            )

            def keep_grad(m, k, part, step=step):
                start = pl.multiple_of(step * main + m * pair, pair)
                put_basis(pl.ds(start, pair), k, part, False)

            run_filter(slot, keep_grad)
        run_last(lambda k, part: put_basis(both, k, part, False))
        return 0

    lax.fori_loop(0, pairs, adjoint, 0)
    mixt_copy.wait()

    def mixed_back(index):
        return mm(normed_s[:, : sz.mix], basis_s[:, lanes_of(order(index))])[:chans]

    def backward_chunk(index, _):
        chunk = order(index)
        lanes = lanes_of(chunk)
        grad_first = mixed_back(index)
        shifted, inv = stats(xs[:, lanes].astype(F32)[:chans])
        hat = shifted * inv
        dnorm_ref[0, :chans] += fold(grad_first * hat)
        dnorm_ref[1, :chans] += fold(grad_first)
        scaled = grad_first * wide(gain_one[:chans], NEAR)
        mean_one = jnp.sum(scaled, 0, keepdims=True) * (1.0 / chans)
        mean_two = jnp.sum(scaled * hat, 0, keepdims=True) * (1.0 / chans)
        added = inv * (scaled - mean_one - hat * mean_two)

        def put_grad(step, where, part):
            grad_s[step, :, where] += added[:, part]

        @pl.when(chunk < tail_chunk)
        def _():
            put_grad(chunk // per_step, main_lanes(chunk), slice(0, NEAR))

        put_tail(chunk, put_grad)

        @pl.when((chunk < tail_chunk) & (lax.rem(chunk, per_step) == per_step - 1))
        def _():
            grad_copy(chunk // per_step).start()

        return 0

    lax.fori_loop(0, chunks, backward_chunk, 0)
    for step in range(sz.steps):
        out_copy(step).wait()
        grad_copy(step).wait()
    for copy in (ddown_copy, dup_copy, dmix_copy):
        copy.wait()


def flip(index, mask):
    for bit in range(mask.bit_length()):
        if mask >> bit & 1:
            index = index + (1 << bit) * (1 - 2 * (index // (1 << bit) % 2))
    return index


def low_bit(mask, bits):
    return (mask & -mask).bit_length() - 1 if mask else bits


def lane_index(rows):
    return lax.broadcasted_iota(jnp.int32, (rows, 128), 1)


def window(flat, start, rows):
    first = start >> 7
    shift = start & 127
    low = flat[pl.ds(first, rows), :]
    high = flat[pl.ds(first + 1, rows), :]
    mixed = jnp.where(lane_index(rows) >= shift, low, high)
    return pltpu.roll(mixed, (128 - shift) & 127, 1)


def gather_kernel(
    sz, parts, params_ref, x_hbm, cot_hbm, noise_ref, taps_ref,
    halo_ref, tap_ref, norm_ref, mix_hbm, mixt_hbm, up_hbm, down_hbm, x_out, cot_out,
    got, flat, lines, x_raw, cot_raw, x_s, cot_s, rim_s, edge_s, tap_s, tap_r, mix_s, mixt_s, up_s, down_s,
    in_sem, z_send, z_recv, x_send, x_recv, y_send, y_recv, c_send, c_recv, e_send, e_recv,
    t_send, t_recv, out_sem, turn_sem,
):
    chans, cp, cm, rest, lons = sz.chans, sz.chan_pad, sz.chan_main, sz.rest, sz.lons
    rows, own_rows, shared, split = parts
    wide = lax.axis_index("wide")
    lat = lax.axis_index("lat")
    lat_count = lax.axis_size("lat")
    total = lax.axis_size("wide")
    heights = total // 4
    core = wide % 2
    side = (wide // 2) % 2
    height = wide // 4
    half = lat % 2
    has_up = lat > 0
    has_down = lat < lat_count - 1

    bits = heights.bit_length() - 1

    def spot(mask, s, c):
        return 4 * flip(height, mask) + 2 * s + c

    raw_copies = [
        pltpu.make_async_copy(x_hbm, x_raw, in_sem.at[0]),
        pltpu.make_async_copy(cot_hbm, cot_raw, in_sem.at[1]),
    ]
    for copy in raw_copies:
        copy.start()
    got[wide, :own_rows] = params_ref[...]

    barrier = pltpu.get_barrier_semaphore()

    def hello(w, l):
        pl.semaphore_signal(barrier, inc=1, device_id=(w, l), device_id_type=MESH)

    for bit in range(bits):
        hello(spot(1 << bit, side, core), lat)
    hello(spot(0, 1 - side, core), lat)
    hello(spot(0, side, 1 - core), lat)

    @pl.when(has_up)
    def _():
        hello(wide, lat - 1)

    @pl.when(has_down)
    def _():
        hello(wide, lat + 1)

    tap_total = taps_ref.shape[1]
    for edge, row in ((0, 0), (1, sz.rows - 1)):
        tap_s[edge] = jnp.zeros(tap_s.shape[1:], F32)
        tap_s[edge, :1, :tap_total] = taps_ref[row : row + 1, :]

    pl.semaphore_wait(
        barrier, bits + 2 + has_up.astype(jnp.int32) + has_down.astype(jnp.int32)
    )

    whole = pl.ds(0, rows)
    mine = pl.ds(pl.multiple_of(half * split, 16), split + shared)
    lead = pl.ds(pl.multiple_of(half * (split + shared), 16), split)
    other = pl.ds(pl.multiple_of((1 - half) * (split + shared), 16), split)

    def message(shard, where, to_wide, to_lat, send, recv):
        return pltpu.make_async_remote_copy(
            src_ref=got.at[shard, where],
            dst_ref=got.at[shard, where],
            send_sem=send,
            recv_sem=recv,
            device_id=(to_wide, to_lat),
            device_id_type=MESH,
        )

    started = []

    def start(copy):
        copy.start()
        started.append(copy)

    def along(mask, bit):
        return message(
            spot(mask, side, core), mine, spot(1 << bit, side, core), lat,
            z_send.at[(mask | 1 << bit) - 1], z_recv.at[(mask | 1 << bit) - 1],
        )

    def arrive(shard, where, sem):
        message(shard, where, wide, lat, z_send.at[0], sem).wait_recv()

    def across(j, shard):
        return message(shard, mine, spot(0, 1 - side, core), lat, x_send.at[j], x_recv.at[j])

    def over(j, shard):
        return message(shard, lead, wide, lat + 1 - 2 * half, y_send.at[j], y_recv.at[j])

    def beside(j, shard, where):
        return message(shard, where, spot(0, side, 1 - core), lat, c_send.at[j], c_recv.at[j])

    for bit in reversed(range(bits)):
        start(along(0, bit))
    start(across(0, wide))
    start(beside(0, wide, whole))

    def turned(i, raw, held, out):
        raw_copies[i].wait()
        held[...] = jnp.swapaxes(raw[...], 0, 1)
        copy = pltpu.make_async_copy(held, out, turn_sem.at[i])
        copy.start()
        return copy

    put_x = turned(0, x_raw, x_s, x_out)
    blank = jnp.zeros((cp - sz.inputs, sz.steps * lons), F32)
    for edge, lanes in ((0, slice(0, lons)), (1, slice(sz.cells - lons, sz.cells))):
        fields = jnp.concatenate([x_s[t, :, lanes] for t in range(sz.steps)], 1).astype(F32)
        noise = jnp.concatenate([noise_ref[t, :, lanes] for t in range(sz.steps)], 1).astype(F32)
        rim_s[edge] = jnp.concatenate([fields, noise, blank], 0).astype(BF)

    def rim(edge, to):
        return pltpu.make_async_remote_copy(
            src_ref=rim_s.at[edge],
            dst_ref=edge_s.at[1 - edge],
            send_sem=e_send.at[edge],
            recv_sem=e_recv.at[1 - edge],
            device_id=(wide, to),
            device_id_type=MESH,
        )

    def tap_rim(edge, to):
        return pltpu.make_async_remote_copy(
            src_ref=tap_s.at[edge],
            dst_ref=tap_r.at[1 - edge],
            send_sem=t_send.at[edge],
            recv_sem=t_recv.at[1 - edge],
            device_id=(wide, to),
            device_id_type=MESH,
        )

    @pl.when(has_up)
    def _():
        rim(0, lat - 1).start()
        tap_rim(0, lat - 1).start()

    @pl.when(has_down)
    def _():
        rim(1, lat + 1).start()
        tap_rim(1, lat + 1).start()

    late = []

    def pass_on(mask, s, where):
        shard = spot(mask, s, core)
        start(over(len(late), shard))
        late.append((mask, s))
        start(beside(len(late), shard, where))

    def from_across(mask):
        arrive(spot(mask, 1 - side, core), mine, x_recv.at[mask])
        pass_on(mask, 1 - side, mine)

    for i in range(1, heights):
        shard = spot(i, side, core)
        arrive(shard, mine, z_recv.at[i - 1])
        for bit in reversed(range(low_bit(i, bits))):
            start(along(i, bit))
        start(across(i, shard))
        pass_on(i, side, mine)
        from_across(i - 1)
        if i == 1:
            put_cot = turned(1, cot_raw, cot_s, cot_out)
    from_across(heights - 1)

    def widen(shard):
        flat[pl.ds(shard * own_rows, own_rows), :] = got[shard, :own_rows].astype(F32)

    def finish(j):
        shard = spot(*late[j], 1 - core)
        arrive(shard, mine, c_recv.at[j + 1])
        arrive(shard, other, c_recv.at[2 * heights + j])
        widen(shard)

    widen(wide)
    arrive(spot(0, side, 1 - core), whole, c_recv.at[0])
    widen(spot(0, side, 1 - core))
    for j, column in enumerate(late):
        shard = spot(*column, core)
        arrive(shard, other, y_recv.at[j])
        start(beside(2 * heights + j, shard, other))
        widen(shard)
        if j:
            finish(j - 1)
    finish(len(late) - 1)
    put_x.wait()
    put_cot.wait()
    for copy in started:
        copy.wait_send()

    @pl.when(has_up)
    def _():
        rim(0, lat - 1).wait_send()
        rim(1, lat - 1).wait_recv()
        tap_rim(0, lat - 1).wait_send()
        tap_rim(1, lat - 1).wait_recv()

    @pl.when(has_down)
    def _():
        rim(1, lat + 1).wait_send()
        rim(0, lat + 1).wait_recv()
        tap_rim(1, lat + 1).wait_send()
        tap_rim(0, lat + 1).wait_recv()

    halo_ref[...] = edge_s[...]
    tap_ref[...] = jnp.zeros_like(tap_ref)
    tap_ref[1 : sz.rows + 1, :tap_total] = taps_ref[...]
    tap_ref[:1] = jnp.where(has_up, tap_r[0, :1], 0.0)
    tap_ref[sz.rows + 1 : sz.rows + 2] = jnp.where(has_down, tap_r[1, :1], 0.0)

    unpack_kernel(
        sz, flat, lines, norm_ref, mix_s, mixt_s, up_s, down_s,
        [
            pltpu.make_async_copy(src, dst, out_sem.at[i])
            for i, (src, dst) in enumerate(
                ((mix_s, mix_hbm), (mixt_s, mixt_hbm), (up_s, up_hbm), (down_s, down_hbm))
            )
        ],
    )


def period(length):
    return 128 // math.gcd(length, 128)


def in_batches(count, first, length, some, step=16):
    again = period(length)
    spots = [(j, (first + j * length) // 128, (first + j * length) % 128) for j in range(again)]

    def body(i, _):
        for j in range(0, again, step):
            some(i * again, i * (again * length // 128), spots[j : j + step])
        return 0

    whole = count // again
    lax.fori_loop(0, whole, body, 0)
    left = count % again
    for j in range(0, left, step):
        some(whole * again, whole * (again * length // 128), spots[j : min(j + step, left)])


def lines_of(flat, lines, first, length, count, group):
    def some(line, row, spots):
        held = []
        for _, top, shift in spots:
            low = flat[pl.ds(row + top, group), :]
            if shift:
                high = flat[pl.ds(row + top + 1, group), :]
                low = pltpu.roll(jnp.where(lane_index(group) >= shift, low, high), 128 - shift, 1)
            held.append(low)
        for (at, _, _), value in zip(spots, held):
            lines[pl.ds(pl.multiple_of((line + at) * group, 8), group), :] = value

    in_batches(count, first, length, some)


def unpack_kernel(sz, flat, lines, norm_ref, mix_ref, mixt_ref, up_ref, down_ref, copies):
    chans, cp, cm, rest, hid, hp = sz.chans, sz.chan_pad, sz.chan_main, sz.rest, sz.hid, sz.hid_pad
    basis, inputs = sz.basis, sz.inputs
    at_disco = 2 * chans
    at_bias = at_disco + chans * basis * inputs
    at_up = at_bias + 3 * chans
    at_down = at_up + (chans + 1) * hid

    def column(start):
        held = window(flat, start, 8)
        full = jnp.concatenate(
            [jnp.broadcast_to(held[s : s + 1], (128, 128)).T for s in range(up_to(cp, 128) // 128)], 0
        )[:cp]
        row = lax.broadcasted_iota(jnp.int32, (cp, 128), 0)
        return jnp.where(row < chans, full, 0.0), row

    for i, start in enumerate((0, chans, at_bias + chans, at_bias + 2 * chans)):
        value, row = column(start)
        norm_ref[i] = jnp.where(row == chans, 1.0, value) if i == 3 else value
    disco_bias, _ = column(at_bias)

    groups = 8
    lines_of(flat, lines, at_disco, inputs, chans * basis, groups)
    stride = basis * groups
    lane = lane_index(chans)
    low = jnp.where(lane == inputs - cm, disco_bias[:chans], 0.0)
    blank = jnp.zeros((cp - cm, 128), BF)

    def clear(ref, size):
        if size < ref.shape[0]:
            ref[size:, :] = jnp.zeros((ref.shape[0] - size, ref.shape[1]), BF)

    def put(ref, lanes, value, size):
        whole = size // 16 * 16
        ref[:whole, lanes] = value[:whole].astype(BF)
        tail = jnp.concatenate(
            [value[whole:size], jnp.zeros((up_to(size, 16) - size, 128), F32)], 0
        )
        ref[whole : up_to(size, 16), lanes] = tail.astype(BF)

    for k in range(basis):
        for s in range(cm // 128):
            value = lines[pl.ds(k * groups + s, chans, stride=stride), :]
            put(mix_ref, slice(k * cm + s * 128, k * cm + s * 128 + 128), value, chans)
        value = lines[pl.ds(k * groups + cm // 128, chans, stride=stride), :]
        value = jnp.where(lane < inputs - cm, value, 0.0)
        low = low + (pltpu.roll(value, k * rest, 1) if k else value)
    put(mix_ref, slice(basis * cm, basis * cm + 128), low, chans)
    clear(mix_ref, up_to(chans, 16))
    copies[0].start()

    for k in range(basis):
        for s in range(cm // 128):
            for r in range(cm // 128):
                block = mix_ref[r * 128 : r * 128 + 128, k * cm + s * 128 : k * cm + s * 128 + 128]
                mixt_ref[s * 128 : s * 128 + 128, k * cm + r * 128 : k * cm + r * 128 + 128] = (
                    block.astype(F32).T.astype(BF)
                )
    for r in range(cm // 128):
        block = low[r * 128 : r * 128 + 128].T
        for k in range(basis):
            mixt_ref[cm:cp, k * cm + r * 128 : k * cm + r * 128 + 128] = block[
                k * rest : (k + 1) * rest
            ].astype(BF)
    for s in range(cm // 128):
        block = jnp.concatenate(
            [
                mix_ref[cm:cp, k * cm + s * 128 : k * cm + s * 128 + 128].astype(F32)
                for k in range(basis)
            ]
            + [jnp.zeros((128 - basis * rest, 128), F32)],
            0,
        )
        mixt_ref[s * 128 : s * 128 + 128, basis * cm : basis * cm + 128] = block.T.astype(BF)
    corner = mix_ref[cm:cp, basis * cm : basis * cm + 128].astype(F32)
    corner = jnp.where(lane_index(cp - cm) % rest == 0, corner, 0.0)
    row = lax.broadcasted_iota(jnp.int32, (cp - cm, 128), 0)
    mixt_ref[cm:cp, basis * cm : basis * cm + 128] = jnp.where(row < chans - cm, corner, 0.0).astype(BF)
    copies[1].start()

    groups = 16
    lines_of(flat, lines, at_up, hid, chans + 1, groups)
    for s in range(up_ref.shape[1] // 128):
        value = lines[pl.ds(s, chans + 1, stride=groups), :]
        keep = hid - s * 128
        if keep < 128:
            value = jnp.where(lane_index(chans + 1) < keep, value, 0.0)
        put(up_ref, slice(s * 128, s * 128 + 128), value, chans + 1)
    clear(up_ref, up_to(chans + 1, 16))
    copies[2].start()
    groups = 8
    lines_of(flat, lines, at_down, chans, hid + 1, groups)
    for s in range(down_ref.shape[1] // 128):
        value = lines[pl.ds(s, hid + 1, stride=groups), :]
        keep = chans - s * 128
        if keep < 128:
            value = jnp.where(lane_index(hid + 1) < keep, value, 0.0)
        put(down_ref, slice(s * 128, s * 128 + 128), value, hid + 1)
    clear(down_ref, up_to(hid + 1, 16))
    copies[3].start()
    for copy in copies:
        copy.wait()


def run_gather(sz, params, x_raw, cot_raw, noise_items, filter_taps, total):
    cp, hp = sz.chan_pad, sz.hid_pad
    own_rows = params.shape[0] // 128
    rows = up_to(own_rows, 16)
    split = rows * 7 // 20 // 16 * 16
    shared = rows - 2 * split
    taps = filter_taps.reshape(sz.rows, -1)
    tap_shape = (up_to(sz.rows + 2, 8), up_to(taps.shape[1], 128))
    heights = total // 4
    items = (sz.steps, sz.chans, sz.cells)
    any_spec = pl.BlockSpec(memory_space=pl.ANY)
    vmem = pl.BlockSpec(memory_space=pltpu.VMEM)
    edges = (2, cp, sz.steps * sz.lons)
    line_rows = max(sz.chans * sz.basis * 8, (sz.chans + 1) * 16, (sz.hid + 1) * 8)
    dma = pltpu.SemaphoreType.DMA
    return pl.pallas_call(
        partial(gather_kernel, sz, (rows, own_rows, shared, split)),
        name="gather",
        out_shape=[
            jax.ShapeDtypeStruct(edges, BF),
            jax.ShapeDtypeStruct(tap_shape, F32),
            jax.ShapeDtypeStruct((4, cp, 128), F32),
            jax.ShapeDtypeStruct((cp, up_to(sz.mix, 128)), BF),
            jax.ShapeDtypeStruct((cp, up_to(sz.mix, 128)), BF),
            jax.ShapeDtypeStruct((cp, up_to(hp, 128)), BF),
            jax.ShapeDtypeStruct((hp, up_to(cp, 128)), BF),
            jax.ShapeDtypeStruct(items, BF),
            jax.ShapeDtypeStruct(items, BF),
        ],
        in_specs=[vmem, any_spec, any_spec, vmem, vmem],
        out_specs=[vmem] * 3 + [any_spec] * 6,
        scratch_shapes=[
            pltpu.VMEM((total, rows, 128), BF),
            pltpu.VMEM((up_to(total * own_rows + 24, 8), 128), F32),
            pltpu.VMEM((line_rows, 128), F32),
            pltpu.VMEM(x_raw.shape, BF),
            pltpu.VMEM(x_raw.shape, BF),
            pltpu.VMEM(items, BF),
            pltpu.VMEM(items, BF),
            pltpu.VMEM(edges, BF),
            pltpu.VMEM(edges, BF),
            pltpu.VMEM((2, 8, tap_shape[1]), F32),
            pltpu.VMEM((2, 8, tap_shape[1]), F32),
            pltpu.VMEM((cp, up_to(sz.mix, 128)), BF),
            pltpu.VMEM((cp, up_to(sz.mix, 128)), BF),
            pltpu.VMEM((cp, up_to(hp, 128)), BF),
            pltpu.VMEM((hp, up_to(cp, 128)), BF),
            dma((2,)),
            dma((heights,)), dma((heights,)),
            dma((heights,)), dma((heights,)),
            dma((2 * heights,)), dma((2 * heights,)),
            dma((4 * heights,)), dma((4 * heights,)),
            dma((2,)), dma((2,)),
            dma((2,)), dma((2,)), dma((4,)), dma((2,)),
        ],
        compiler_params=pltpu.CompilerParams(
            collective_id=1, has_side_effects=True, vmem_limit_bytes=60 * 1024 * 1024
        ),
    )(params.reshape(own_rows, 128), x_raw, cot_raw, noise_items, taps)


def run_block(
    sz, x_items, noise_items, cot_items, taps_ext, live, halo, norms, mix, mixt, up, down
):
    cp, hp = sz.chan_pad, sz.hid_pad
    lons = sz.lons

    live_lanes = jnp.concatenate([jnp.repeat(live, sz.main), jnp.repeat(live, lons)])[None]
    any_spec = pl.BlockSpec(memory_space=pl.ANY)
    vmem = pl.BlockSpec(memory_space=pltpu.VMEM)
    mix_lanes = up_to(sz.mix, 128)
    up_lanes = up_to(hp, 128)
    down_lanes = up_to(cp, 128)
    windows = (sz.rows - 1) // 2
    lon = lons
    flops = 2 * sz.width * (3 * sz.mix * cp + 6 * hp * cp)
    return pl.pallas_call(
        partial(block_kernel, sz),
        name="block",
        out_shape=[
            jax.ShapeDtypeStruct(x_items.shape, BF),
            jax.ShapeDtypeStruct((sz.chans, sz.steps, sz.cells), F32),
            jax.ShapeDtypeStruct((cp, mix_lanes), BF),
            jax.ShapeDtypeStruct((cp, up_lanes), BF),
            jax.ShapeDtypeStruct((hp, down_lanes), BF),
            jax.ShapeDtypeStruct((4, cp, 128), F32),
        ],
        in_specs=[
            any_spec, vmem, any_spec, vmem, pl.BlockSpec(memory_space=pltpu.SMEM), vmem, vmem,
            any_spec, any_spec, any_spec, any_spec,
        ],
        out_specs=[any_spec] * 5 + [vmem],
        scratch_shapes=[
            pltpu.VMEM((cp, sz.width), BF),
            pltpu.VMEM((cp, sz.width), BF),
            pltpu.VMEM((sz.mix, sz.width), BF),
            pltpu.VMEM((cp, sz.width), BF),
            pltpu.VMEM((2 * hp, sz.width), BF),
            pltpu.VMEM((cp, sz.width), BF),
            pltpu.VMEM((sz.steps, sz.chans, sz.cells), F32),
            pltpu.VMEM((4, sz.chans, sz.cells), BF),
            pltpu.VMEM((2, cp, (sz.rows + 3) * lon), BF),
            pltpu.VMEM((windows, 4 * lon, sz.basis * 2 * lon), BF),
            pltpu.VMEM((8 * lon, sz.basis * 2 * lon), BF),
            pltpu.VMEM((2, cp, sz.steps * lon), BF),
            pltpu.VMEM((cp, mix_lanes), BF),
            pltpu.VMEM((cp, up_lanes), BF),
            pltpu.VMEM((hp, down_lanes), BF),
            pltpu.SemaphoreType.DMA((2, 2)),
            pltpu.SemaphoreType.DMA((4,)),
            pltpu.SemaphoreType.DMA((2, sz.steps)),
            pltpu.SemaphoreType.DMA((2,)),
            pltpu.SemaphoreType.DMA((2,)),
        ],
        compiler_params=pltpu.CompilerParams(
            collective_id=0, has_side_effects=True, vmem_limit_bytes=63 * 1024 * 1024
        ),
        cost_estimate=pl.CostEstimate(flops=flops, bytes_accessed=40_000_000, transcendentals=0),
    )(x_items, noise_items, cot_items, halo, taps_ext, live_lanes, norms, mix, mixt, up, down)


def merge(old, shift, length, value, rows):
    lane = lane_index(rows)
    place = lax.broadcasted_iota(jnp.int32, (rows, 128), 0) * 128 + lane
    if shift:
        moved = pltpu.roll(value, shift, 1)
        value = jnp.where(lane >= shift, moved, pltpu.roll(moved, 1, 0))
    return jnp.where((place >= shift) & (place < shift + length), value, old)


def flatten_lines(flat, lines, first, length, count, group):
    for odd in range(2):

        def some(line, row, spots, odd=odd):
            spots = [spot for spot in spots if spot[0] % 2 == odd]
            held = []
            for at, top, shift in spots:
                value = lines[pl.ds(pl.multiple_of((line + at) * group, 8), group), :]
                held.append(merge(flat[pl.ds(row + top, group), :], shift, length, value, group))
            for (_, top, _), value in zip(spots, held):
                flat[pl.ds(row + top, group), :] = value

        in_batches(count, first, length, some, 32)


def pack_kernel(sz, dmix_ref, dup_ref, ddown_ref, dnorm_ref, flat, lines, copies, ready):
    chans, cp, cm, rest, hid = sz.chans, sz.chan_pad, sz.chan_main, sz.rest, sz.hid
    basis, inputs = sz.basis, sz.inputs
    at_disco = 2 * chans
    at_bias = at_disco + chans * basis * inputs
    at_up = at_bias + 3 * chans
    at_down = at_up + (chans + 1) * hid
    used = at_down + (hid + 1) * chans

    def across(columns, pick):
        parts = []
        for s in range(8):
            size = min(128, cp - s * 128)
            if size <= 0:
                parts.append(jnp.zeros((1, 128), F32))
                continue
            block = columns[s * 128 : s * 128 + size]
            if size < 128:
                block = jnp.concatenate([block, jnp.zeros((128 - size, 128), F32)], 0)
            parts.append(pick(block.T))
        return jnp.concatenate(parts, 0)

    def total(block):
        return jnp.sum(block, 0, keepdims=True)

    begin = used // 128
    flat[begin:, :] = jnp.zeros((flat.shape[0] - begin, 128), F32)
    spots = (0, chans, at_bias + chans, at_bias + 2 * chans)
    pieces = [(start, across(dnorm_ref[i], total)) for i, start in enumerate(spots)]
    copies[0].wait()
    low = dmix_ref[:, basis * cm : basis * cm + 128].astype(F32)
    bias_row = inputs - cm
    pieces.append((at_bias, across(low, lambda block: block[bias_row : bias_row + 1])))
    for start, value in pieces:
        rows = pl.ds(start // 128, 8)
        flat[rows, :] = merge(flat[rows, :], start % 128, chans, value, 8)

    groups = 8
    stride = basis * groups
    for k in range(basis):
        for s in range(cm // 128):
            value = dmix_ref[:, k * cm + s * 128 : k * cm + s * 128 + 128].astype(F32)
            lines[pl.ds(k * groups + s, chans, stride=stride), :] = value[:chans]
        value = pltpu.roll(low, 128 - k * rest, 1) if k else low
        lines[pl.ds(k * groups + cm // 128, chans, stride=stride), :] = value[:chans]
    flatten_lines(flat, lines, at_disco, inputs, chans * basis, groups)
    ready(at_bias // 128)

    groups = 16
    copies[1].wait()
    for s in range(up_to(hid, 128) // 128):
        value = dup_ref[:, s * 128 : s * 128 + 128].astype(F32)
        lines[pl.ds(s, chans + 1, stride=groups), :] = value[: chans + 1]
    flatten_lines(flat, lines, at_up, hid, chans + 1, groups)
    ready(at_down // 128)

    groups = 8
    copies[2].wait()
    for s in range(up_to(chans, 128) // 128):
        value = ddown_ref[:, s * 128 : s * 128 + 128].astype(F32)
        lines[pl.ds(s, hid + 1, stride=groups), :] = value[: hid + 1]
    flatten_lines(flat, lines, at_down, chans, hid + 1, groups)
    ready(flat.shape[0])


def reduce_kernel(
    sz, parts, dmix_hbm, dup_hbm, ddown_hbm, dnorm_ref, block_hbm, out_ref, turned_hbm,
    flat, lines, block_s, turned_s, dmix_s, dup_s, ddown_s, sums, beside_s, beside_r, over_s, over_r, xa_s, xa_r, xb_s, xb_r,
    za_s, za_r, zb_s, zb_r, fa_s, fa_r, fb_r,
    in_sem, turn_sem, c_send, c_recv, y_send, y_recv, x_send, x_recv, z_send, z_recv,
    f_send, f_recv,
):
    rows, own_rows, shared, split = parts
    wide = lax.axis_index("wide")
    lat = lax.axis_index("lat")
    total = lax.axis_size("wide")
    heights = total // 4
    core = wide % 2
    side = (wide // 2) % 2
    height = wide // 4
    half = lat % 2
    mate = lat + 1 - 2 * half

    bits = heights.bit_length() - 1

    def spot(mask, s, c):
        return 4 * flip(height, mask) + 2 * s + c

    held = (dmix_s, dup_s, ddown_s)
    copies = [
        pltpu.make_async_copy(src, dst, in_sem.at[i])
        for i, (src, dst) in enumerate(zip((dmix_hbm, dup_hbm, ddown_hbm), held))
    ]
    copies.append(pltpu.make_async_copy(block_hbm, block_s, in_sem.at[3]))
    for item in copies:
        item.start()
    barrier = pltpu.get_barrier_semaphore()

    def hello(w, l):
        pl.semaphore_signal(barrier, inc=1, device_id=(w, l), device_id_type=MESH)

    for bit in range(bits):
        hello(spot(1 << bit, side, core), lat)
    hello(spot(0, 1 - side, core), lat)
    hello(spot(0, side, 1 - core), lat)
    hello(wide, mate)
    shares = pl.ds(split, shared)
    lead = pl.ds(pl.multiple_of(half * (split + shared), 16), split)
    other = pl.ds(pl.multiple_of((1 - half) * (split + shared), 16), split)
    masks = list(reversed(range(heights)))
    columns = [(mask, 1 - side) for mask in masks] + [(mask, side) for mask in masks]
    started = []

    def copy(src, dst, send, recv, to_wide, to_lat):
        return pltpu.make_async_remote_copy(
            src_ref=src, dst_ref=dst, send_sem=send, recv_sem=recv,
            device_id=(to_wide, to_lat), device_id_type=MESH,
        )

    def go(message):
        message.start()
        started.append(message)

    def to_core(j):
        return copy(beside_s.at[j], beside_r.at[j], c_send.at[j], c_recv.at[j], spot(0, side, 1 - core), lat)

    def to_mate(j):
        return copy(over_s.at[j], over_r.at[j], y_send.at[j], y_recv.at[j], wide, mate)

    def to_side(src, dst, j, part):
        return copy(src.at[j], dst.at[j], x_send.at[j, part], x_recv.at[j, part], spot(0, 1 - side, core), lat)

    def to_height(src, dst, mask, part):
        return copy(
            src.at[mask - 1], dst.at[mask - 1], z_send.at[mask - 1, part], z_recv.at[mask - 1, part],
            spot(mask & -mask, side, core), lat,
        )

    def add_heights(src, dst, mask, part, j, where):
        for bit in range(low_bit(mask, bits)):
            sender = mask | 1 << bit
            to_height(src, dst, sender, part).wait_recv()
            sums[j, where] += dst[sender - 1].astype(F32)

    next_pair = [0]

    def ready(limit):
        if next_pair[0] == 0:
            pl.semaphore_wait(barrier, bits + 3)
        while next_pair[0] < 2 * heights:
            two = next_pair[0]
            if (2 * two + 1) * own_rows + rows > limit:
                break
            away = 2 * two + 1 - core
            beside_s[two] = flat[pl.ds(away * own_rows, rows), :].astype(BF)
            go(to_core(two))
            next_pair[0] = two + 1

    pack_kernel(sz, *held, dnorm_ref, flat, lines, copies, ready)
    for j, (mask, s) in enumerate(columns):
        mine = spot(mask, s, core)
        two = mine // 2
        to_core(two).wait_recv()
        sums[j] = flat[pl.ds(mine * own_rows, rows), :] + beside_r[two].astype(F32)
        over_s[j] = sums[j, other].astype(BF)
        go(to_mate(j))
        if j < heights:
            xa_s[j] = sums[j, shares].astype(BF)
            go(to_side(xa_s, xa_r, j, 0))
    copies[3].wait()
    turned_s[...] = jnp.swapaxes(block_s[...], 0, 1)
    turned = pltpu.make_async_copy(turned_s, turned_hbm, turn_sem)
    turned.start()
    for i, mask in enumerate(masks):
        to_mate(i).wait_recv()
        xb_s[i] = (sums[i, lead] + over_r[i].astype(F32)).astype(BF)
        go(to_side(xb_s, xb_r, i, 1))
        j = heights + i
        to_side(xa_s, xa_r, i, 0).wait_recv()
        sums[j, shares] += xa_r[i].astype(F32)
        add_heights(za_s, za_r, mask, 0, j, shares)
        if mask:
            za_s[mask - 1] = sums[j, shares].astype(BF)
            go(to_height(za_s, za_r, mask, 0))
    own = 2 * heights - 1
    fa_s[...] = sums[own, shares].astype(BF)
    last = [
        copy(fa_s, fa_r, f_send.at[0], f_recv.at[0], wide, mate),
        copy(sums.at[own, lead], fb_r, f_send.at[1], f_recv.at[1], wide, mate),
    ]
    go(last[0])
    for i, mask in enumerate(masks):
        j = heights + i
        to_mate(j).wait_recv()
        to_side(xb_s, xb_r, i, 1).wait_recv()
        sums[j, lead] += over_r[j].astype(F32) + xb_r[i].astype(F32)
        add_heights(zb_s, zb_r, mask, 1, j, lead)
        if mask:
            zb_s[mask - 1] = sums[j, lead].astype(BF)
            go(to_height(zb_s, zb_r, mask, 1))
    go(last[1])
    last[0].wait_recv()
    out_ref[shares, :] = fa_s[...].astype(F32) + fa_r[...].astype(F32)
    last[1].wait_recv()
    low, high = sums[own, lead], fb_r[...]
    first = jnp.where(half == 0, low, high)
    second = jnp.where(half == 0, high, low)
    out_ref[:split, :] = first
    out_ref[split + shared :, :] = second[: own_rows - split - shared]
    turned.wait()
    for message in started:
        message.wait_send()


def run_reduce(sz, own_rows, total, dmix, dup, ddown, dnorm, block_out):
    rows = up_to(own_rows, 16)
    split = rows * 7 // 20 // 16 * 16
    shared = rows - 2 * split
    heights = total // 4
    vmem = pl.BlockSpec(memory_space=pltpu.VMEM)
    any_spec = pl.BlockSpec(memory_space=pl.ANY)
    turned_shape = (sz.chans, sz.steps, sz.cells)
    line_rows = max(sz.chans * sz.basis * 8, (sz.chans + 1) * 16, (sz.hid + 1) * 8)
    dma = pltpu.SemaphoreType.DMA
    flat_rows = up_to((total - 1) * own_rows + rows, 8) + 16
    return pl.pallas_call(
        partial(reduce_kernel, sz, (rows, own_rows, shared, split)),
        name="reduce",
        out_shape=[
            jax.ShapeDtypeStruct((own_rows, 128), F32),
            jax.ShapeDtypeStruct(turned_shape, BF),
        ],
        in_specs=[any_spec] * 3 + [vmem, any_spec],
        out_specs=[vmem, any_spec],
        scratch_shapes=[
            pltpu.VMEM((flat_rows, 128), F32),
            pltpu.VMEM((line_rows, 128), F32),
            pltpu.VMEM(block_out.shape, BF),
            pltpu.VMEM(turned_shape, BF),
            pltpu.VMEM(dmix.shape, BF),
            pltpu.VMEM(dup.shape, BF),
            pltpu.VMEM(ddown.shape, BF),
            pltpu.VMEM((2 * heights, rows, 128), F32),
            pltpu.VMEM((2 * heights, rows, 128), BF),
            pltpu.VMEM((2 * heights, rows, 128), BF),
            pltpu.VMEM((2 * heights, split, 128), BF),
            pltpu.VMEM((2 * heights, split, 128), BF),
            pltpu.VMEM((heights, shared, 128), BF),
            pltpu.VMEM((heights, shared, 128), BF),
            pltpu.VMEM((heights, split, 128), BF),
            pltpu.VMEM((heights, split, 128), BF),
            pltpu.VMEM((heights, shared, 128), BF),
            pltpu.VMEM((heights, shared, 128), BF),
            pltpu.VMEM((heights, split, 128), BF),
            pltpu.VMEM((heights, split, 128), BF),
            pltpu.VMEM((shared, 128), BF),
            pltpu.VMEM((shared, 128), BF),
            pltpu.VMEM((split, 128), F32),
            dma((4,)), dma(()),
            dma((2 * heights,)), dma((2 * heights,)),
            dma((2 * heights,)), dma((2 * heights,)),
            dma((heights, 2)), dma((heights, 2)),
            dma((heights, 2)), dma((heights, 2)),
            dma((2,)), dma((2,)),
        ],
        compiler_params=pltpu.CompilerParams(
            collective_id=2, has_side_effects=True, vmem_limit_bytes=62 * 1024 * 1024
        ),
    )(dmix, dup, ddown, dnorm, block_out)


def shards(block_input, noise_fields, filter_taps, rollout, cotangent, params):
    sz = Sizes(block_input, noise_fields, filter_taps)
    chans = sz.chans
    dates, step_total = block_input.shape[:2]
    step_ids = jnp.arange(step_total, dtype=jnp.int32)
    live = (step_ids[None, :] < rollout[:, None]).astype(F32).reshape(sz.steps)
    noise_items = noise_fields.reshape(sz.steps, sz.noise, sz.cells)

    def by_channel(fields):
        return jnp.transpose(fields, (2, 0, 1, 3)).reshape(chans, sz.steps, sz.cells)

    halo, taps_ext, norms, mix, mixt, up, down, x_items, cot_items = run_gather(
        sz,
        params,
        by_channel(block_input),
        by_channel(cotangent),
        noise_items,
        filter_taps,
        lax.axis_size("wide"),
    )
    out, grad, dmix, dup, ddown, dnorm = run_block(
        sz,
        x_items,
        noise_items,
        cot_items,
        taps_ext,
        live,
        halo,
        norms,
        mix,
        mixt,
        up,
        down,
    )
    own, turned = run_reduce(
        sz, params.shape[0] // 128, lax.axis_size("wide"), dmix, dup, ddown, dnorm, out
    )

    def by_step(fields):
        return jnp.transpose(fields, (1, 0, 2)).reshape(block_input.shape)

    return (by_step(turned), by_step(grad), own.reshape(params.shape))


def solution(mesh):
    in_specs = (
        P("wide", None, None, "lat"),
        P("wide", None, None, "lat"),
        P("lat", None, None, None),
        P("wide"),
        P("wide", None, None, "lat"),
        P("wide"),
    )
    out_specs = (P("wide", None, None, "lat"), P("wide", None, None, "lat"), P("wide"))
    return jax.shard_map(shards, mesh=mesh, in_specs=in_specs, out_specs=out_specs, check_vma=False)
```
